32 devices in a mesh: section: 2 (over core), dp: 4 (over y, x), seq: 4 (over z).
Axes of the slice: x: 2, y: 2, z: 4, core: 2. Of those that a mesh axis runs over, the one named last changes fastest.
Arguments:
- inputs: bfloat16 [8, 1024, 1088], P('dp', 'seq'), may hold values from -6 to 6
- cotangent: bfloat16 [8, 1024, 1088], P('dp', 'seq'), may hold values from -6 to 6
- first_gain: bfloat16 [2, 1088], P('section', ('dp', 'seq')), may hold values from 0.5 to 1.5
- first_shift: bfloat16 [2, 1088], P('section', ('dp', 'seq')), may hold values from -1.75 to 1.75
- joint_weight: bfloat16 [2, 1088, 3264], P('section', ('dp', 'seq')), may hold values from -0.1875 to 0.1875
- query_bias: bfloat16 [2, 1088], P('section', ('dp', 'seq')), may hold values from -3 to 3
- value_bias: bfloat16 [2, 1088], P('section', ('dp', 'seq')), may hold values from -0.3125 to 0.3125
- output_weight: bfloat16 [2, 1088, 1088], P('section', ('dp', 'seq')), may hold values from -0.75 to 0.75
- output_bias: bfloat16 [2, 1088], P('section', ('dp', 'seq')), may hold values from -1.75 to 1.75
- second_gain: bfloat16 [2, 1088], P('section', ('dp', 'seq')), may hold values from 0.5 to 1.5
- second_shift: bfloat16 [2, 1088], P('section', ('dp', 'seq')), may hold values from -1.75 to 1.75
- expand_weight: bfloat16 [2, 1088, 4352], P('section', ('dp', 'seq')), may hold values from -0.1875 to 0.1875
- expand_bias: bfloat16 [2, 4352], P('section', ('dp', 'seq')), may hold values from -3 to 3
- reduce_weight: bfloat16 [2, 4352, 1088], P('section', ('dp', 'seq')), may hold values from -0.09375 to 0.09375
- reduce_bias: bfloat16 [2, 1088], P('section', ('dp', 'seq')), may hold values from -1.75 to 1.75
Outputs:
- layer_outputs: bfloat16 [2, 8, 1024, 1088], P('section', 'dp', 'seq')
- input_grads: bfloat16 [2, 8, 1024, 1088], P('section', 'dp', 'seq')
- grad_first_gain: float32 [2, 1088], P('section', ('dp', 'seq'))
- grad_first_shift: float32 [2, 1088], P('section', ('dp', 'seq'))
- grad_joint_weight: float32 [2, 1088, 3264], P('section', ('dp', 'seq'))
- grad_query_bias: float32 [2, 1088], P('section', ('dp', 'seq'))
- grad_value_bias: float32 [2, 1088], P('section', ('dp', 'seq'))
- grad_output_weight: float32 [2, 1088, 1088], P('section', ('dp', 'seq'))
- grad_output_bias: float32 [2, 1088], P('section', ('dp', 'seq'))
- grad_second_gain: float32 [2, 1088], P('section', ('dp', 'seq'))
- grad_second_shift: float32 [2, 1088], P('section', ('dp', 'seq'))
- grad_expand_weight: float32 [2, 1088, 4352], P('section', ('dp', 'seq'))
- grad_expand_bias: float32 [2, 4352], P('section', ('dp', 'seq'))
- grad_reduce_weight: float32 [2, 4352, 1088], P('section', ('dp', 'seq'))
- grad_reduce_bias: float32 [2, 1088], P('section', ('dp', 'seq'))
The draws below stay inside these ranges and needn't reach their ends.
All inputs are finite; a program needn't handle non-finite values.
Results may differ from the reference program's by a relative error of at most 0.028.
Values may be sent and summed in bfloat16 or wider, within the bound.
A program may use at most 320 MiB of HBM per device.

```python
import jax
import jax.numpy as jnp
from jax import lax

HEADS = 17
HDIM = 64
D = 1088
FF = 4352
SEQLEN = 1024
BLK = 256
SEQS = 8
N_SECTION = 2


def block_scale(rng, shape, split, smallest, high):
    def one(dim, blocks):
        draws = jax.random.uniform(jax.random.fold_in(jax.random.fold_in(rng, 6), dim), (blocks,), jnp.float32, smallest / len(split), high / len(split))
        return jnp.repeat(jnp.exp(draws), shape[dim] // blocks).reshape((-1,) + (1,) * (len(shape) - dim - 1))

    gain = one(*split[0])
    for cut in split[1:]:
        gain = gain * one(*cut)
    return gain


def scatter_about(key, extent, width, reach, shards=(), kind=jnp.bfloat16):
    factor_of = block_scale(key, extent, shards, -0.22, 0.18) if shards else 1.0
    values = jax.random.normal(key, extent, jnp.float32) * width * factor_of
    return jnp.minimum(jnp.maximum(values, -reach), reach).astype(kind)


def setup_inputs(seed: int = 0) -> dict:
    seeds = jax.random.split(jax.random.key(seed), 16)
    return {
        "inputs": scatter_about(seeds[0], (SEQS, SEQLEN, D), 1.0, 6.0, ((0, 4), (1, 4))),
        "cotangent": scatter_about(seeds[1], (SEQS, SEQLEN, D), 1.0, 6.0, ((0, 4), (1, 4))),
        "first_gain": jnp.clip(1.0 + 0.1 * jax.random.normal(seeds[2], (N_SECTION, D), jnp.float32), 0.5, 1.5).astype(jnp.bfloat16),
        "first_shift": scatter_about(seeds[3], (N_SECTION, D), 0.3, 1.75, ((0, 2), (1, 16))),
        "joint_weight": scatter_about(seeds[4], (N_SECTION, D, 3 * D), D ** -0.5, 0.1875, ((0, 2), (1, 16))),
        "query_bias": scatter_about(seeds[5], (N_SECTION, D), 0.5, 3.0, ((0, 2), (1, 16))),
        "value_bias": scatter_about(seeds[6], (N_SECTION, D), 0.05, 0.3125, ((0, 2), (1, 16))),
        "output_weight": scatter_about(seeds[7], (N_SECTION, D, D), (max(16, D // 16)) ** -0.5, 0.75, ((0, 2), (1, 16))),
        "output_bias": scatter_about(seeds[8], (N_SECTION, D), 0.3, 1.75, ((0, 2), (1, 16))),
        "second_gain": jnp.clip(1.0 + 0.1 * jax.random.normal(seeds[9], (N_SECTION, D), jnp.float32), 0.5, 1.5).astype(jnp.bfloat16),
        "second_shift": scatter_about(seeds[10], (N_SECTION, D), 0.3, 1.75, ((0, 2), (1, 16))),
        "expand_weight": scatter_about(seeds[11], (N_SECTION, D, FF), D ** -0.5, 0.1875, ((0, 2), (1, 16))),
        "expand_bias": scatter_about(seeds[12], (N_SECTION, FF), 0.5, 3.0, ((0, 2), (1, 16))),
        "reduce_weight": scatter_about(seeds[13], (N_SECTION, FF, D), FF ** -0.5, 0.09375, ((0, 2), (1, 16))),
        "reduce_bias": scatter_about(seeds[14], (N_SECTION, D), 0.3, 1.75, ((0, 2), (1, 16))),
    }


epsilon = 1e-05
far_below = -1e+30
highest = lax.Precision.HIGHEST

@jax.custom_vjp
def low(v):
    return lax.optimization_barrier(v.astype(jnp.bfloat16)).astype(jnp.float32)

@jax.custom_vjp
def low_back(v):
    return v

def low_keep(v):
    return (low(v), None)

def low_pass(kept, grad):
    return (grad,)

def back_keep(v):
    return (v, None)

def back_low(kept, grad):
    return (low(grad),)
low.defvjp(low_keep, low_pass)
low_back.defvjp(back_keep, back_low)

def normalize(values, scales, offsets):
    centre = lax.optimization_barrier(jnp.mean(values, axis=-1, keepdims=True))
    centred = values - centre
    unit_rows = centred * lax.rsqrt(lax.optimization_barrier(jnp.mean(centred * centred, axis=-1, keepdims=True)) + epsilon)
    return unit_rows * scales + offsets

def attend(query, keys, values):
    length = keys.shape[0]
    block_count = length // BLK
    scale_factor = HDIM ** (-0.5)
    key_blocks = keys.reshape(block_count, BLK, HEADS, HDIM)
    value_blocks = values.reshape(block_count, BLK, HEADS, HDIM)

    def one_block(element):
        rows_here, block_number = element
        scores = low_back(jnp.einsum('qhd,bkhd->qhbk', rows_here, key_blocks, precision=highest) * scale_factor)
        highest_score = lax.optimization_barrier(jnp.max(scores, axis=-1))
        allowed = jnp.arange(block_count, dtype=jnp.int32) <= block_number
        exponent = jnp.exp(scores - highest_score[..., None]) * allowed[None, None, :, None].astype(jnp.float32)
        weights = low(exponent)
        block_out = low_back(jnp.einsum('qhbk,bkhd->qhbd', weights, value_blocks, precision=highest))
        levels = jnp.where(allowed[None, None, :], highest_score, far_below)
        factor = jnp.exp(levels - lax.optimization_barrier(jnp.max(levels, axis=-1, keepdims=True)))
        running_sum = lax.optimization_barrier(jnp.sum(factor * lax.optimization_barrier(jnp.sum(exponent, axis=-1)), axis=-1))
        weighted = lax.optimization_barrier(jnp.sum(factor[..., None] * block_out, axis=2))
        return weighted / running_sum[..., None]
    blocks_out = lax.map(jax.checkpoint(one_block), (query.reshape(block_count, BLK, HEADS, HDIM), jnp.arange(block_count, dtype=jnp.int32)))
    return blocks_out.reshape(length, HEADS * HDIM)

def layer(source, params):
    first_gain, first_shift, joint_weight, query_bias, value_bias, output_weight, output_bias, second_gain, second_shift, expand_weight, expand_bias, reduce_weight, reduce_bias = params
    feature_width = HEADS * HDIM
    length = source.shape[0]
    normed = low(normalize(source, first_gain, first_shift))
    mixture = jnp.dot(normed, joint_weight, precision=highest, preferred_element_type=jnp.float32)
    query = low(low_back(mixture[:, :feature_width] + query_bias))
    keys = low(low_back(mixture[:, feature_width:2 * feature_width]))
    values = low(low_back(mixture[:, 2 * feature_width:] + value_bias))
    shaped = (length, HEADS, HDIM)
    attended = low(attend(query.reshape(shaped), keys.reshape(shaped), values.reshape(shaped)))
    middle = source + low_back(jnp.dot(attended, output_weight, precision=highest, preferred_element_type=jnp.float32) + output_bias)
    second = low(normalize(middle, second_gain, second_shift))
    hidden = low_back(jnp.dot(second, expand_weight, precision=highest, preferred_element_type=jnp.float32) + expand_bias)
    active = low(jax.nn.gelu(hidden, approximate=False))
    return middle + low_back(jnp.dot(active, reduce_weight, precision=highest, preferred_element_type=jnp.float32) + reduce_bias)

def reference(inputs, cotangent, first_gain, first_shift, joint_weight, query_bias, value_bias, output_weight, output_bias, second_gain, second_shift, expand_weight, expand_bias, reduce_weight, reduce_bias):
    stacked = tuple((piece.astype(jnp.float32) for piece in (first_gain, first_shift, joint_weight, query_bias, value_bias, output_weight, output_bias, second_gain, second_shift, expand_weight, expand_bias, reduce_weight, reduce_bias)))
    lower_params = tuple((piece[0] for piece in stacked))
    upper_params = tuple((piece[1] for piece in stacked))

    def one_sequence(carried, couple):
        source, incoming = couple
        lower_out, lower_pull = jax.vjp(layer, source.astype(jnp.float32), lower_params)
        sent = low(lower_out)
        upper_out, upper_pull = jax.vjp(layer, sent, upper_params)
        upper_back, upper_grads = upper_pull(incoming.astype(jnp.float32))
        returned = low(upper_back)
        lower_back, lower_grads = lower_pull(returned)
        carried = (jax.tree.map(jnp.add, carried[0], lower_grads), jax.tree.map(jnp.add, carried[1], upper_grads))
        return (carried, (sent, upper_out, lower_back, returned))
    initial = (tuple((jnp.zeros_like(piece) for piece in lower_params)), tuple((jnp.zeros_like(piece) for piece in upper_params)))
    (lower_sums, upper_sums), (sent, upper_out, lower_back, returned) = lax.scan(one_sequence, initial, (inputs, cotangent))
    layer_outputs = jnp.stack([sent, upper_out]).astype(jnp.bfloat16)
    input_grads = jnp.stack([lower_back, returned]).astype(jnp.bfloat16)
    grads = tuple((jnp.stack([lower_part, upper_part]) for lower_part, upper_part in zip(lower_sums, upper_sums)))
    return (layer_outputs, input_grads, grads[0], grads[1], grads[2], grads[3], grads[4], grads[5], grads[6], grads[7], grads[8], grads[9], grads[10], grads[11], grads[12])
```

```python
from functools import partial

import jax
import jax.numpy as jnp
from jax import lax
from jax.sharding import PartitionSpec as P

HEADS = 17
HDIM = 64
BLK = 256


epsilon = 1e-05
far_below = -1e30


def passed_along(value, axis, steps):
    count = lax.axis_size(axis)
    first, last = (max(0, -steps), min(count, count - steps))
    return lax.ppermute(value, axis, [(source, source + steps) for source in range(first, last)])


def normalize(values, scales, offsets):
    centre = jnp.mean(values, axis=-1, keepdims=True)
    centred = values - centre
    inverse = lax.rsqrt(jnp.mean(centred * centred, axis=-1, keepdims=True) + epsilon)
    unit_rows = centred * inverse
    return (unit_rows * scales + offsets, unit_rows, inverse)


def normalize_back(upstream, unit_rows, inverse):
    return inverse * (
        upstream
        - jnp.mean(upstream, axis=-1, keepdims=True)
        - unit_rows * jnp.mean(upstream * unit_rows, axis=-1, keepdims=True)
    )


def score_block(query, key_block, block_index, row_block):
    scores = jnp.einsum(
        "qhd,khd->qhk", query, key_block, preferred_element_type=jnp.float32
    ) * HDIM ** (-0.5)
    highest = jnp.max(scores, axis=-1)
    allowed = (block_index <= row_block)[:, None]
    exponent = jnp.exp(scores - highest[..., None]) * allowed[..., None].astype(jnp.float32)
    levels = jnp.where(allowed, highest, far_below)
    return (exponent, levels)


def attend_forward(query, keys_all, values_all, row_block):
    length = keys_all.shape[0]
    row_count = query.shape[0]
    key_shaped = keys_all.reshape(length, HEADS, HDIM)
    value_shaped = values_all.reshape(length, HEADS, HDIM)
    block_limit = row_block[-1] + 1

    def advance(block_index, carried):
        running_peak, running_sum, weighted = carried
        key_block = lax.dynamic_slice_in_dim(key_shaped, block_index * BLK, BLK, 0)
        value_block = lax.dynamic_slice_in_dim(value_shaped, block_index * BLK, BLK, 0)
        exponent, levels = score_block(query, key_block, block_index, row_block)
        weights = exponent.astype(jnp.bfloat16)
        block_out = jnp.einsum(
            "qhk,khd->qhd", weights, value_block, preferred_element_type=jnp.float32
        )
        newest_peak = jnp.maximum(running_peak, levels)
        shrink_old = jnp.exp(running_peak - newest_peak)
        shrink_new = jnp.exp(levels - newest_peak)
        running_sum = running_sum * shrink_old + shrink_new * jnp.sum(exponent, axis=-1)
        weighted = weighted * shrink_old[..., None] + shrink_new[..., None] * block_out
        return (newest_peak, running_sum, weighted)

    initial = (
        jnp.full((row_count, HEADS), far_below, jnp.float32),
        jnp.zeros((row_count, HEADS), jnp.float32),
        jnp.zeros((row_count, HEADS, HDIM), jnp.float32),
    )
    running_peak, running_sum, weighted = lax.fori_loop(0, block_limit, advance, initial)
    return (weighted / running_sum[..., None], running_peak + jnp.log(running_sum))


def attend_backward(query, keys_all, values_all, row_block, attended, log_total, grad_attended):
    length = keys_all.shape[0]
    key_shaped = keys_all.reshape(length, HEADS, HDIM)
    value_shaped = values_all.reshape(length, HEADS, HDIM)
    block_limit = row_block[-1] + 1
    delta = jnp.sum(grad_attended * attended, axis=-1)

    def advance(block_index, carried):
        grad_query, grad_keys, grad_values = carried
        key_block = lax.dynamic_slice_in_dim(key_shaped, block_index * BLK, BLK, 0)
        value_block = lax.dynamic_slice_in_dim(value_shaped, block_index * BLK, BLK, 0)
        exponent, levels = score_block(query, key_block, block_index, row_block)
        weights = exponent.astype(jnp.bfloat16)
        factor = jnp.exp(levels - log_total)
        scaled = (factor[..., None] * grad_attended).astype(jnp.bfloat16)
        grad_weights = jnp.einsum(
            "qhd,khd->qhk", scaled, value_block, preferred_element_type=jnp.float32
        )
        grad_scores = (exponent * (grad_weights - (factor * delta)[..., None])).astype(jnp.bfloat16)
        grad_query = grad_query + jnp.einsum(
            "qhk,khd->qhd", grad_scores, key_block, preferred_element_type=jnp.float32
        )
        grad_key = jnp.einsum(
            "qhk,qhd->khd", grad_scores, query, preferred_element_type=jnp.float32
        )
        grad_value = jnp.einsum("qhk,qhd->khd", weights, scaled, preferred_element_type=jnp.float32)
        grad_keys = lax.dynamic_update_slice_in_dim(grad_keys, grad_key, block_index * BLK, 0)
        grad_values = lax.dynamic_update_slice_in_dim(grad_values, grad_value, block_index * BLK, 0)
        return (grad_query, grad_keys, grad_values)

    initial = (
        jnp.zeros(query.shape, jnp.float32),
        jnp.zeros((length, HEADS, HDIM), jnp.float32),
        jnp.zeros((length, HEADS, HDIM), jnp.float32),
    )
    grad_query, grad_keys, grad_values = lax.fori_loop(0, block_limit, advance, initial)
    return (
        grad_query,
        grad_keys.reshape(length, HEADS * HDIM),
        grad_values.reshape(length, HEADS * HDIM),
    )


def project(source, params):
    feature_width = HEADS * HDIM
    normed, unit_rows, inverse = normalize(
        source, params[0].astype(jnp.float32), params[1].astype(jnp.float32)
    )
    normed_low = normed.astype(jnp.bfloat16)
    mixture = jnp.dot(normed_low, params[2], preferred_element_type=jnp.float32)
    query_low = (mixture[:, :feature_width] + params[3].astype(jnp.float32)).astype(jnp.bfloat16)
    keys_low = mixture[:, feature_width : 2 * feature_width].astype(jnp.bfloat16)
    values_low = (mixture[:, 2 * feature_width :] + params[4].astype(jnp.float32)).astype(
        jnp.bfloat16
    )
    return (unit_rows, inverse, normed_low, query_low, keys_low, values_low)


def complete(source, params, projected, gathered, row_block):
    row_count = source.shape[0]
    query = projected[3].reshape(row_count, HEADS, HDIM)
    attended, log_total = attend_forward(query, gathered[0], gathered[1], row_block)
    attended_low = attended.reshape(row_count, HEADS * HDIM).astype(jnp.bfloat16)
    middle = source + (
        jnp.dot(attended_low, params[5], preferred_element_type=jnp.float32)
        + params[6].astype(jnp.float32)
    )
    second, unit_second, inverse_second = normalize(
        middle, params[7].astype(jnp.float32), params[8].astype(jnp.float32)
    )
    second_low = second.astype(jnp.bfloat16)
    hidden = jnp.dot(second_low, params[9], preferred_element_type=jnp.float32) + params[10].astype(
        jnp.float32
    )
    active, gelu_pull = jax.vjp(partial(jax.nn.gelu, approximate=False), hidden)
    active_low = active.astype(jnp.bfloat16)
    result = middle + (
        jnp.dot(active_low, params[11], preferred_element_type=jnp.float32)
        + params[12].astype(jnp.float32)
    )
    saved = (
        query,
        attended,
        log_total,
        attended_low,
        unit_second,
        inverse_second,
        second_low,
        gelu_pull,
        active_low,
    )
    return (result, saved)


def layer_backward(source, upstream, params, projected, gathered, row_block):
    unit_first, inverse_first, normed_low, query_low, keys_low, values_low = projected
    row_count = source.shape[0]
    feature_width = HEADS * HDIM
    result, saved = complete(source, params, projected, gathered, row_block)
    (
        query,
        attended,
        log_total,
        attended_low,
        unit_second,
        inverse_second,
        second_low,
        gelu_pull,
        active_low,
    ) = saved
    top_low = upstream.astype(jnp.bfloat16)
    grad_reduce_bias = jnp.sum(top_low.astype(jnp.float32), axis=0)
    grad_reduce_weight = jnp.einsum(
        "tf,td->fd", active_low, top_low, preferred_element_type=jnp.float32
    )
    grad_active = jnp.einsum("td,fd->tf", top_low, params[11], preferred_element_type=jnp.float32)
    grad_hidden_low = gelu_pull(grad_active)[0].astype(jnp.bfloat16)
    grad_expand_bias = jnp.sum(grad_hidden_low.astype(jnp.float32), axis=0)
    grad_expand_weight = jnp.einsum(
        "td,tf->df", second_low, grad_hidden_low, preferred_element_type=jnp.float32
    )
    grad_second = jnp.einsum(
        "tf,df->td", grad_hidden_low, params[9], preferred_element_type=jnp.float32
    )
    grad_second_gain = jnp.sum(grad_second * unit_second, axis=0)
    grad_second_shift = jnp.sum(grad_second, axis=0)
    grad_middle = upstream + normalize_back(
        grad_second * params[7].astype(jnp.float32), unit_second, inverse_second
    )
    branch_low = grad_middle.astype(jnp.bfloat16)
    grad_output_bias = jnp.sum(branch_low.astype(jnp.float32), axis=0)
    grad_output_weight = jnp.einsum(
        "td,te->de", attended_low, branch_low, preferred_element_type=jnp.float32
    )
    grad_attended = jnp.einsum(
        "te,de->td", branch_low, params[5], preferred_element_type=jnp.float32
    )
    grad_query, grad_keys_full, grad_values_full = attend_backward(
        query,
        gathered[0],
        gathered[1],
        row_block,
        attended,
        log_total,
        grad_attended.reshape(row_count, HEADS, HDIM),
    )
    grad_keys, grad_values = (
        lax.psum_scatter(grad_keys_full, "seq", scatter_dimension=0, tiled=True),
        lax.psum_scatter(grad_values_full, "seq", scatter_dimension=0, tiled=True),
    )
    scale_factor = HDIM ** (-0.5)
    grad_mixture = jnp.concatenate(
        [
            grad_query.reshape(row_count, feature_width) * scale_factor,
            grad_keys * scale_factor,
            grad_values,
        ],
        axis=1,
    ).astype(jnp.bfloat16)
    grad_query_bias = jnp.sum(grad_mixture[:, :feature_width].astype(jnp.float32), axis=0)
    grad_value_bias = jnp.sum(grad_mixture[:, 2 * feature_width :].astype(jnp.float32), axis=0)
    grad_joint_weight = jnp.einsum(
        "td,te->de", normed_low, grad_mixture, preferred_element_type=jnp.float32
    )
    grad_normed = jnp.einsum(
        "te,de->td", grad_mixture, params[2], preferred_element_type=jnp.float32
    )
    grad_first_gain = jnp.sum(grad_normed * unit_first, axis=0)
    grad_first_shift = jnp.sum(grad_normed, axis=0)
    grad_source = grad_middle + normalize_back(
        grad_normed * params[0].astype(jnp.float32), unit_first, inverse_first
    )
    grads = (
        grad_first_gain,
        grad_first_shift,
        grad_joint_weight,
        grad_query_bias,
        grad_value_bias,
        grad_output_weight,
        grad_output_bias,
        grad_second_gain,
        grad_second_shift,
        grad_expand_weight,
        grad_expand_bias,
        grad_reduce_weight,
        grad_reduce_bias,
    )
    return (grad_source.astype(jnp.bfloat16), grads)


def body(
    inputs,
    cotangent,
    first_gain,
    first_shift,
    joint_weight,
    query_bias,
    value_bias,
    output_weight,
    output_bias,
    second_gain,
    second_shift,
    expand_weight,
    expand_bias,
    reduce_weight,
    reduce_bias,
):
    section_index = lax.axis_index("section")
    micro_count = inputs.shape[0]
    row_count = inputs.shape[1]
    first_row = lax.axis_index("seq") * row_count
    row_block = (first_row + jnp.arange(row_count, dtype=jnp.int32)) // BLK
    owned = (
        first_gain[0],
        first_shift[0],
        joint_weight[0],
        query_bias[0],
        value_bias[0],
        output_weight[0],
        output_bias[0],
        second_gain[0],
        second_shift[0],
        expand_weight[0],
        expand_bias[0],
        reduce_weight[0],
        reduce_bias[0],
    )
    forward_params = (
        lax.all_gather(first_gain[0], ("dp", "seq"), axis=0, tiled=True),
        lax.all_gather(first_shift[0], ("dp", "seq"), axis=0, tiled=True),
        lax.all_gather(joint_weight[0], ("dp", "seq"), axis=0, tiled=True),
        lax.all_gather(query_bias[0], ("dp", "seq"), axis=0, tiled=True),
        lax.all_gather(value_bias[0], ("dp", "seq"), axis=0, tiled=True),
        lax.all_gather(output_weight[0], ("dp", "seq"), axis=0, tiled=True),
        lax.all_gather(output_bias[0], ("dp", "seq"), axis=0, tiled=True),
        lax.all_gather(second_gain[0], ("dp", "seq"), axis=0, tiled=True),
        lax.all_gather(second_shift[0], ("dp", "seq"), axis=0, tiled=True),
        lax.all_gather(expand_weight[0], ("dp", "seq"), axis=0, tiled=True),
        lax.all_gather(expand_bias[0], ("dp", "seq"), axis=0, tiled=True),
        lax.all_gather(reduce_weight[0], ("dp", "seq"), axis=0, tiled=True),
        lax.all_gather(reduce_bias[0], ("dp", "seq"), axis=0, tiled=True),
    )
    incoming = jnp.zeros(inputs.shape[1:], jnp.bfloat16)
    section_inputs = []
    produced = []
    key_sets = []
    for tick_index in range(micro_count + 1):
        section_input = jnp.where(
            section_index == 0, inputs[min(tick_index, micro_count - 1)], incoming
        )
        source = section_input.astype(jnp.float32)
        projected = project(source, forward_params)
        gathered = (
            lax.all_gather(projected[4], "seq", axis=0, tiled=True),
            lax.all_gather(projected[5], "seq", axis=0, tiled=True),
        )
        result, unused = complete(source, forward_params, projected, gathered, row_block)
        result_low = result.astype(jnp.bfloat16)
        section_inputs.append(section_input)
        produced.append(result_low)
        key_sets.append(gathered)
        if tick_index < micro_count:
            incoming = passed_along(result_low, "section", 1)
    backward_params = (
        lax.all_gather(first_gain[0], ("dp", "seq"), axis=0, tiled=True),
        lax.all_gather(first_shift[0], ("dp", "seq"), axis=0, tiled=True),
        lax.all_gather(joint_weight[0], ("dp", "seq"), axis=0, tiled=True),
        lax.all_gather(query_bias[0], ("dp", "seq"), axis=0, tiled=True),
        lax.all_gather(value_bias[0], ("dp", "seq"), axis=0, tiled=True),
        lax.all_gather(output_weight[0], ("dp", "seq"), axis=0, tiled=True),
        lax.all_gather(output_bias[0], ("dp", "seq"), axis=0, tiled=True),
        lax.all_gather(second_gain[0], ("dp", "seq"), axis=0, tiled=True),
        lax.all_gather(second_shift[0], ("dp", "seq"), axis=0, tiled=True),
        lax.all_gather(expand_weight[0], ("dp", "seq"), axis=0, tiled=True),
        lax.all_gather(expand_bias[0], ("dp", "seq"), axis=0, tiled=True),
        lax.all_gather(reduce_weight[0], ("dp", "seq"), axis=0, tiled=True),
        lax.all_gather(reduce_bias[0], ("dp", "seq"), axis=0, tiled=True),
    )
    totals = tuple((jnp.zeros(piece.shape, jnp.float32) for piece in backward_params))
    shares = tuple((jnp.zeros(piece.shape, jnp.float32) for piece in owned))
    returning = jnp.zeros(inputs.shape[1:], jnp.bfloat16)
    sent_back = []
    for tick_index in range(micro_count + 1):
        upper_pick = min(tick_index + 1, micro_count)
        lower_pick = max(tick_index - 1, 0)
        section_input = jnp.where(
            section_index == 1, section_inputs[upper_pick], section_inputs[lower_pick]
        )
        upstream = jnp.where(
            section_index == 1, cotangent[min(tick_index, micro_count - 1)], returning
        ).astype(jnp.float32)
        weight_valid = jnp.where(
            section_index == 1,
            1.0 if tick_index < micro_count else 0.0,
            1.0 if tick_index >= 1 else 0.0,
        ).astype(jnp.float32)
        source = section_input.astype(jnp.float32)
        projected = project(source, backward_params)
        gathered = (
            lax.all_gather(projected[4], "seq", axis=0, tiled=True),
            lax.all_gather(projected[5], "seq", axis=0, tiled=True),
        )
        grad_source, grads = layer_backward(
            source, upstream, backward_params, projected, gathered, row_block
        )
        masked = tuple((update * weight_valid for update in grads))
        totals = tuple((running + update for running, update in zip(totals, masked)))
        sent_back.append(grad_source)
        if tick_index < micro_count:
            returning = passed_along(grad_source, "section", -1)
    layer_outputs = jnp.stack(
        [
            jnp.where(section_index == 0, produced[position], produced[position + 1])
            for position in range(micro_count)
        ]
    )[None]
    input_grads = jnp.stack(
        [
            jnp.where(section_index == 1, sent_back[position], sent_back[position + 1])
            for position in range(micro_count)
        ]
    )[None]
    (
        sum_first_gain,
        sum_first_shift,
        sum_joint_weight,
        sum_query_bias,
        sum_value_bias,
        sum_output_weight,
        sum_output_bias,
        sum_second_gain,
        sum_second_shift,
        sum_expand_weight,
        sum_expand_bias,
        sum_reduce_weight,
        sum_reduce_bias,
    ) = totals
    shares = (
        lax.psum_scatter(sum_first_gain, ("dp", "seq"), scatter_dimension=0, tiled=True),
        lax.psum_scatter(sum_first_shift, ("dp", "seq"), scatter_dimension=0, tiled=True),
        lax.psum_scatter(sum_joint_weight, ("dp", "seq"), scatter_dimension=0, tiled=True),
        lax.psum_scatter(sum_query_bias, ("dp", "seq"), scatter_dimension=0, tiled=True),
        lax.psum_scatter(sum_value_bias, ("dp", "seq"), scatter_dimension=0, tiled=True),
        lax.psum_scatter(sum_output_weight, ("dp", "seq"), scatter_dimension=0, tiled=True),
        lax.psum_scatter(sum_output_bias, ("dp", "seq"), scatter_dimension=0, tiled=True),
        lax.psum_scatter(sum_second_gain, ("dp", "seq"), scatter_dimension=0, tiled=True),
        lax.psum_scatter(sum_second_shift, ("dp", "seq"), scatter_dimension=0, tiled=True),
        lax.psum_scatter(sum_expand_weight, ("dp", "seq"), scatter_dimension=0, tiled=True),
        lax.psum_scatter(sum_expand_bias, ("dp", "seq"), scatter_dimension=0, tiled=True),
        lax.psum_scatter(sum_reduce_weight, ("dp", "seq"), scatter_dimension=0, tiled=True),
        lax.psum_scatter(sum_reduce_bias, ("dp", "seq"), scatter_dimension=0, tiled=True),
    )
    return (layer_outputs, input_grads) + tuple((portion[None] for portion in shares))


def swapped(value, axis, bits):
    count = lax.axis_size(axis)
    return lax.ppermute(value, axis, [(source, source ^ bits) for source in range(count)])


def after(value, *earlier):
    return lax.optimization_barrier((value,) + earlier)[0]


def natural_four(pieces, place):
    odd, far = (place & 1) == 1, (place & 2) == 2
    first = [
        jnp.where(odd, pieces[1], pieces[0]),
        jnp.where(odd, pieces[0], pieces[1]),
        jnp.where(odd, pieces[3], pieces[2]),
        jnp.where(odd, pieces[2], pieces[3]),
    ]
    return [jnp.where(far, first[index ^ 2], first[index]) for index in range(4)]


def gather_page(shard, core, ring, line):
    rows, columns = shard.shape
    column = [shard] + [swapped(shard, "seq", bits) for bits in (1, 2, 3)]
    block = jnp.concatenate(natural_four(column, line), axis=0)
    tall = block.shape[0]
    across = swapped(block, "dp", 1)
    along = swapped(block, "dp", 2)
    corner_top = swapped(across[: tall // 2], "dp", 2)
    corner_bottom = swapped(along[tall // 2 :], "dp", 1)
    corner = jnp.concatenate([corner_top, corner_bottom], axis=0)
    whole = jnp.zeros((2, 4, tall, columns), shard.dtype)
    pieces = (block, across, along, corner)
    for bits, piece in enumerate(pieces):
        whole = lax.dynamic_update_slice(whole, piece[None, None], (core, ring ^ bits, 0, 0))
    for bits, piece in enumerate(pieces):
        other = swapped(piece, "section", 1)
        whole = lax.dynamic_update_slice(whole, other[None, None], (core ^ 1, ring ^ bits, 0, 0))
    return whole.reshape(2, 4 * tall, columns), column[3], corner


def gather_weights(attention_page, expand, reduce, core, ring, line):
    other = swapped(jnp.where(core == 0, expand, attention_page), "section", 1)
    lower = jnp.where(core == 0, attention_page, other)
    upper = jnp.where(core == 0, other, expand)
    lower_pages, held, done = gather_page(lower, core, ring, line)
    reduce_pages, held, done = gather_page(after(reduce, held), core, ring, line)
    upper_pages, held, done = gather_page(after(upper, held), core, ring, line)
    return lower_pages, reduce_pages, upper_pages


def gather_small(pieces):
    packed = jnp.concatenate([piece.reshape(-1) for piece in pieces]).reshape(12, -1)
    packed = jnp.pad(packed, ((0, 4), (0, 128 - packed.shape[1])))
    full = lax.all_gather(packed, ("section", "dp", "seq"), axis=0, tiled=True)
    width = pieces[0].shape[0]
    return full.reshape(2, 16, 16, 128)[:, :, :12, :width]


def small_of(full, layer):
    part = full[layer].astype(jnp.float32)
    vectors = [part[:, row].reshape(1, -1) for row in range(8)]
    return vectors[:6], part[:, 8:].reshape(1, -1), vectors[6], vectors[7]


def attention_forward(query, sources, low_chunk):
    half = query.shape[0] // 2
    split = (half, HEADS, HDIM)
    query_low, query_high = query[:half].reshape(split), query[half:].reshape(split)
    first = low_chunk == 0
    queries = jnp.stack(
        [query_low, query_high, query_high, query_high, jnp.where(first, query_high, query_low)]
    )

    def of_blocks(which):
        def block(near, part):
            return jnp.concatenate(
                [sources[near][other][which][part] for other in (0, 1)], axis=0
            ).reshape(2 * half, HEADS, HDIM)

        last = jnp.where(first, block(1, 1), block(1, 0))
        return jnp.stack([block(0, 0), block(0, 0), block(0, 1), block(1, 0), last])

    keys, values = of_blocks(0), of_blocks(1)
    scores = jnp.einsum("uqhd,ukhd->uhqk", queries, keys, preferred_element_type=jnp.float32)
    scores = scores * HDIM ** (-0.5)
    levels = jnp.max(scores, axis=-1)
    exponent = jnp.exp(scores - levels[..., None])
    weights = exponent.astype(jnp.bfloat16)
    out = jnp.einsum("uhqk,ukhd->uhqd", weights, values, preferred_element_type=jnp.float32)
    sums = jnp.sum(exponent, axis=-1)
    last_low = jnp.where(first, far_below, levels[4])
    last_high = jnp.where(first, levels[4], far_below)
    peak_low = jnp.maximum(levels[0], last_low)
    peak_high = jnp.maximum(jnp.maximum(levels[1], levels[2]), jnp.maximum(levels[3], last_high))
    parts_low = [(levels[0], 0), (last_low, 4)]
    parts_high = [(levels[1], 1), (levels[2], 2), (levels[3], 3), (last_high, 4)]
    attended, logs = [], []
    for peak, parts in ((peak_low, parts_low), (peak_high, parts_high)):
        total = sum(jnp.exp(level - peak) * sums[unit] for level, unit in parts)
        mixed = sum(jnp.exp(level - peak)[..., None] * out[unit] for level, unit in parts)
        attended.append(mixed / total[..., None])
        logs.append(peak + jnp.log(total))
    attended_heads = jnp.stack(attended)
    log_low, log_high = logs
    log_units = jnp.stack(
        [log_low, log_high, log_high, log_high, jnp.where(first, log_high, log_low)]
    )
    rows = attended_heads.transpose(0, 2, 1, 3).reshape(2 * half, HEADS * HDIM)
    factor = jnp.exp(levels - log_units)
    return rows, (queries, keys, values, exponent, weights, factor)


def attention_backward(attended, grad_attended, saved, core, low_chunk):
    queries, keys, values, exponent, weights, factor = saved
    half = attended.shape[0] // 2
    first = low_chunk == 0
    split = (2, half, HEADS, HDIM)
    delta_rows = jnp.sum((grad_attended * attended).reshape(split), axis=-1).transpose(0, 2, 1)
    grad_rows = grad_attended.reshape(split).transpose(0, 2, 1, 3)

    def units(rows):
        return jnp.stack(
            [rows[0], rows[1], rows[1], rows[1], jnp.where(first, rows[1], rows[0])]
        )

    delta, grads = units(delta_rows), units(grad_rows)
    scaled = (factor[..., None] * grads).astype(jnp.bfloat16)
    grad_weights = jnp.einsum("uhqd,ukhd->uhqk", scaled, values, preferred_element_type=jnp.float32)
    grad_scores = (exponent * (grad_weights - (factor * delta)[..., None])).astype(jnp.bfloat16)
    grad_query = jnp.einsum("uhqk,ukhd->uqhd", grad_scores, keys, preferred_element_type=jnp.float32)
    grad_keys = jnp.einsum("uhqk,uqhd->ukhd", grad_scores, queries, preferred_element_type=jnp.float32)
    grad_values = jnp.einsum("uhqk,uhqd->ukhd", weights, scaled, preferred_element_type=jnp.float32)
    low = grad_query[0] + jnp.where(first, 0.0, grad_query[4])
    high = grad_query[1] + grad_query[2] + grad_query[3] + jnp.where(first, grad_query[4], 0.0)
    width = HEADS * HDIM
    grad_query_rows = jnp.concatenate([low, high], axis=0).reshape(2 * half, width)
    both = jnp.concatenate(
        [grad_keys.reshape(5, 2 * half, width), grad_values.reshape(5, 2 * half, width)], axis=2
    )
    near = jnp.stack([both[0] + both[1], both[2]])
    away = jnp.stack(
        [both[3] + jnp.where(first, 0.0, both[4]), jnp.where(first, both[4], 0.0)]
    )
    near = near.reshape(2, 2, half, 2 * width)
    away = away.reshape(2, 2, half, 2 * width)
    away_other = swapped(away[:, 1].astype(jnp.bfloat16), "section", 1)
    near_other = swapped(near[:, 1].astype(jnp.bfloat16), "section", 1)
    away_sum = (away[:, 0] + away_other.astype(jnp.float32)).astype(jnp.bfloat16)
    arrived = swapped(away_sum, "seq", 1)
    own = near[:, 0] + near_other.astype(jnp.float32) + arrived.astype(jnp.float32)
    own = own.reshape(2 * half, 2 * width)
    return grad_query_rows, own[:, :width], own[:, width:]


def layer_forward(source, small, expand_bias, gain_two, weights, core, low_chunk):
    first_gain, first_shift, query_bias, value_bias, output_bias, reduce_bias = small
    second_gain, second_shift = gain_two
    joint, output, expand, reduce = weights
    width = HEADS * HDIM
    half = source.shape[0] // 2
    normed, unit_first, inverse_first = normalize(source, first_gain, first_shift)
    normed_low = normed.astype(jnp.bfloat16)
    both = jnp.dot(normed_low, joint[:, width:], preferred_element_type=jnp.float32)
    keys_low = both[:, :width].astype(jnp.bfloat16)
    values_low = (both[:, width:] + value_bias).astype(jnp.bfloat16)
    here = jnp.concatenate([keys_low, values_low], axis=1)
    away = swapped(here, "seq", 1)
    here_other = swapped(here, "section", 1)
    away_other = swapped(away, "section", 1)
    query = jnp.dot(normed_low, joint[:, :width], preferred_element_type=jnp.float32)
    query_low = (query + query_bias).astype(jnp.bfloat16)

    def parts(piece):
        return (
            piece[:, :width].reshape(2, half, width),
            piece[:, width:].reshape(2, half, width),
        )

    sources = ((parts(here), parts(here_other)), (parts(away), parts(away_other)))
    attended, kept = attention_forward(query_low, sources, low_chunk)
    attended_low = attended.astype(jnp.bfloat16)
    middle = source + (
        jnp.dot(attended_low, output, preferred_element_type=jnp.float32) + output_bias
    )
    second, unit_second, inverse_second = normalize(middle, second_gain, second_shift)
    second_low = second.astype(jnp.bfloat16)
    hidden = jnp.dot(second_low, expand, preferred_element_type=jnp.float32) + expand_bias
    active, gelu_pull = jax.vjp(partial(jax.nn.gelu, approximate=False), hidden)
    active_low = active.astype(jnp.bfloat16)
    result = middle + (
        jnp.dot(active_low, reduce, preferred_element_type=jnp.float32) + reduce_bias
    )
    saved = (
        unit_first,
        inverse_first,
        normed_low,
        attended,
        kept,
        attended_low,
        unit_second,
        inverse_second,
        second_low,
        gelu_pull,
        active_low,
    )
    return result.astype(jnp.bfloat16), saved


def scatter_sum(halves, ring, line):
    def of_ring(bits):
        return lax.dynamic_index_in_dim(halves, ring ^ bits, 0, keepdims=False)

    corner = of_ring(3)
    got_top = swapped(corner[:2], "dp", 1)
    got_bottom = swapped(corner[2:], "dp", 2)
    across, along = of_ring(1), of_ring(2)

    def add(left, right):
        return (left.astype(jnp.float32) + right.astype(jnp.float32)).astype(jnp.bfloat16)

    to_across = jnp.concatenate([across[:2], add(across[2:], got_bottom)], axis=0)
    to_along = jnp.concatenate([add(along[:2], got_top), along[2:]], axis=0)
    from_across = swapped(to_across, "dp", 1)
    from_along = swapped(to_along, "dp", 2)
    own = (
        of_ring(0).astype(jnp.float32)
        + from_across.astype(jnp.float32)
        + from_along.astype(jnp.float32)
    ).astype(jnp.bfloat16)

    def of_line(bits):
        return lax.dynamic_index_in_dim(own, line ^ bits, 0, keepdims=False)

    total = of_line(0).astype(jnp.float32)
    for bits in (1, 2, 3):
        total = total + swapped(of_line(bits), "seq", bits).astype(jnp.float32)
    return total


def column_halves(left, right, core):
    half = right.shape[1] // 2

    def product(which):
        part = lax.dynamic_slice_in_dim(right, which * half, half, 1)
        return jnp.einsum("td,te->de", left, part, preferred_element_type=jnp.float32)

    arrived = swapped(product(core ^ 1).astype(jnp.bfloat16), "section", 1)
    total = (product(core) + arrived.astype(jnp.float32)).astype(jnp.bfloat16)
    return total.reshape(4, 4, total.shape[0] // 16, half)


def row_halves(left, right, core):
    whole = jnp.einsum("tf,td->fd", left, right, preferred_element_type=jnp.float32)
    whole = whole.astype(jnp.bfloat16)
    whole = whole.reshape(4, 4, 2, whole.shape[0] // 32, whole.shape[1])

    def part(which):
        return lax.dynamic_index_in_dim(whole, which, 2, keepdims=False)

    arrived = swapped(part(core ^ 1), "section", 1)
    return (part(core).astype(jnp.float32) + arrived.astype(jnp.float32)).astype(jnp.bfloat16)


def layer_gradient(upstream_low, saved, small, gain_two, weights, core, ring, line, low_chunk):
    (
        unit_first,
        inverse_first,
        normed_low,
        attended,
        kept,
        attended_low,
        unit_second,
        inverse_second,
        second_low,
        gelu_pull,
        active_low,
    ) = saved
    joint, output, expand, reduce = weights
    first_gain = small[0]
    second_gain = gain_two[0]
    upstream = upstream_low.astype(jnp.float32)
    sum_reduce_bias = jnp.sum(upstream, axis=0)
    share_reduce = scatter_sum(row_halves(active_low, upstream_low, core), ring, line)
    grad_active = jnp.einsum("td,fd->tf", upstream_low, reduce, preferred_element_type=jnp.float32)
    grad_hidden_low = gelu_pull(grad_active)[0].astype(jnp.bfloat16)
    sum_expand_bias = jnp.sum(grad_hidden_low.astype(jnp.float32), axis=0)
    share_expand = scatter_sum(column_halves(second_low, grad_hidden_low, core), ring, line)
    grad_second = jnp.einsum("tf,df->td", grad_hidden_low, expand, preferred_element_type=jnp.float32)
    sum_second_gain = jnp.sum(grad_second * unit_second, axis=0)
    sum_second_shift = jnp.sum(grad_second, axis=0)
    grad_middle = upstream + normalize_back(grad_second * second_gain, unit_second, inverse_second)
    branch_low = grad_middle.astype(jnp.bfloat16)
    sum_output_bias = jnp.sum(branch_low.astype(jnp.float32), axis=0)
    share_output = scatter_sum(column_halves(attended_low, branch_low, core), ring, line)
    grad_attended = jnp.einsum("te,de->td", branch_low, output, preferred_element_type=jnp.float32)
    grad_query, grad_keys, grad_values = attention_backward(
        attended, grad_attended, kept, core, low_chunk
    )
    scale_factor = HDIM ** (-0.5)
    grad_mixture = jnp.concatenate(
        [grad_query * scale_factor, grad_keys * scale_factor, grad_values], axis=1
    ).astype(jnp.bfloat16)
    width = HEADS * HDIM
    sums = jnp.sum(grad_mixture.astype(jnp.float32), axis=0)
    share_joint = scatter_sum(column_halves(normed_low, grad_mixture, core), ring, line)
    grad_normed = jnp.einsum("te,de->td", grad_mixture, joint, preferred_element_type=jnp.float32)
    sum_first_gain = jnp.sum(grad_normed * unit_first, axis=0)
    sum_first_shift = jnp.sum(grad_normed, axis=0)
    grad_source = grad_middle + normalize_back(grad_normed * first_gain, unit_first, inverse_first)
    vectors = (
        sum_first_gain,
        sum_first_shift,
        sums[:width],
        sums[2 * width :],
        sum_output_bias,
        sum_reduce_bias,
        sum_second_gain,
        sum_second_shift,
    )
    packed = jnp.stack([vector.reshape(16, -1) for vector in vectors], axis=1)
    packed = jnp.concatenate([packed, sum_expand_bias.reshape(16, 4, -1)], axis=1)
    return (
        grad_source.astype(jnp.bfloat16),
        (share_joint, share_output, share_expand, share_reduce),
        packed,
    )


def sum_small(lower, upper, core, ring, line):
    mine = jnp.where(core == 0, lower, upper)
    mine = mine + swapped(jnp.where(core == 0, upper, lower), "section", 1)
    mine = mine.reshape((4, 4) + mine.shape[1:])

    def scatter(value, axis, place):
        def part(bits):
            return lax.dynamic_index_in_dim(value, place ^ bits, 0, keepdims=False)

        return part(0) + sum(swapped(part(bits), axis, bits) for bits in (1, 2, 3))

    return scatter(scatter(mine, "dp", ring), "seq", line)


def to_rows(array, core, line):
    half = array.shape[1] // 2
    which = line // 2

    def part(index):
        return lax.dynamic_slice(
            array, (index, core * half, 0), (1, half, array.shape[2])
        )[0]

    mine, arrived = part(which), swapped(part(1 - which), "seq", 3)
    low_side = which == 0
    return jnp.concatenate(
        [jnp.where(low_side, mine, arrived), jnp.where(low_side, arrived, mine)], axis=0
    )


def from_rows(lower, upper, core, line):
    half = lower.shape[0] // 2
    low_side = line // 2 == 0
    both = jnp.stack([lower, upper])
    mine = jnp.where(low_side, both[:, :half], both[:, half:])
    arrived = swapped(jnp.where(low_side, both[:, half:], both[:, :half]), "seq", 3)
    pair = jnp.stack(
        [jnp.where(low_side, mine, arrived), jnp.where(low_side, arrived, mine)], axis=1
    )
    kept = jnp.where(core == 0, pair[0], pair[1])
    other = swapped(jnp.where(core == 0, pair[1], pair[0]), "section", 1)
    return jnp.concatenate(
        [jnp.where(core == 0, kept, other), jnp.where(core == 0, other, kept)], axis=1
    )[None]


def joined_shares(lower, upper, core, axis):
    kept = jnp.where(core == 0, lower, upper)
    other = swapped(jnp.where(core == 0, upper, lower), "section", 1)
    return jnp.concatenate(
        [jnp.where(core == 0, kept, other), jnp.where(core == 0, other, kept)], axis=axis
    )[None]


def four_by_four(
    inputs,
    cotangent,
    first_gain,
    first_shift,
    joint_weight,
    query_bias,
    value_bias,
    output_weight,
    output_bias,
    second_gain,
    second_shift,
    expand_weight,
    expand_bias,
    reduce_weight,
    reduce_bias,
):
    core = lax.axis_index("section")
    ring = lax.axis_index("dp")
    line = lax.axis_index("seq")
    low_chunk = jnp.where(line < 2, line, 3 - line)
    width = HEADS * HDIM
    full_small = gather_small(
        (
            first_gain[0],
            first_shift[0],
            query_bias[0],
            value_bias[0],
            output_bias[0],
            reduce_bias[0],
            second_gain[0],
            second_shift[0],
            expand_bias[0],
        )
    )
    rows = to_rows(inputs, core, line)
    attention_page = jnp.concatenate([joint_weight[0], output_weight[0]], axis=1)
    lower_pages, reduce_pages, upper_pages = gather_weights(
        attention_page, expand_weight[0], reduce_weight[0], core, ring, line
    )
    top = to_rows(cotangent, core, line)
    layers = []
    for layer, pages in enumerate((lower_pages, upper_pages)):
        small, wide, gain, shift = small_of(full_small, layer)
        weights = (
            pages[0][:, : 3 * width],
            pages[0][:, 3 * width :],
            pages[1],
            reduce_pages[layer],
        )
        layers.append((small, wide, (gain, shift), weights))
    small, wide, gains, weights = layers[0]
    middle_rows, saved_lower = layer_forward(
        rows.astype(jnp.float32), small, wide, gains, weights, core, low_chunk
    )
    small, wide, gains, weights = layers[1]
    final_rows, saved_upper = layer_forward(
        middle_rows.astype(jnp.float32), small, wide, gains, weights, core, low_chunk
    )
    layer_outputs = from_rows(middle_rows, final_rows, core, line)
    upper_grad, upper_shares, upper_small = layer_gradient(
        top, saved_upper, small, gains, weights, core, ring, line, low_chunk
    )
    small, wide, gains, weights = layers[0]
    lower_grad, lower_shares, lower_small = layer_gradient(
        upper_grad, saved_lower, small, gains, weights, core, ring, line, low_chunk
    )
    input_grads = from_rows(lower_grad, upper_grad, core, line)
    grad_joint, grad_output, grad_expand, grad_reduce = (
        joined_shares(lower, upper, core, axis)
        for lower, upper, axis in zip(lower_shares, upper_shares, (1, 1, 1, 0))
    )
    vectors = sum_small(lower_small, upper_small, core, ring, line)
    return (
        layer_outputs,
        input_grads,
        vectors[0][None],
        vectors[1][None],
        grad_joint,
        vectors[2][None],
        vectors[3][None],
        grad_output,
        vectors[4][None],
        vectors[6][None],
        vectors[7][None],
        grad_expand,
        vectors[8:].reshape(1, -1),
        grad_reduce,
        vectors[5][None],
    )


def fits(mesh):
    return dict(mesh.shape) == {"section": 2, "dp": 4, "seq": 4}


def solution(mesh):
    return jax.shard_map(
        four_by_four if fits(mesh) else body,
        mesh=mesh,
        in_specs=(
            P("dp", "seq", None),
            P("dp", "seq", None),
            P("section", ("dp", "seq")),
            P("section", ("dp", "seq")),
            P("section", ("dp", "seq"), None),
            P("section", ("dp", "seq")),
            P("section", ("dp", "seq")),
            P("section", ("dp", "seq"), None),
            P("section", ("dp", "seq")),
            P("section", ("dp", "seq")),
            P("section", ("dp", "seq")),
            P("section", ("dp", "seq"), None),
            P("section", ("dp", "seq")),
            P("section", ("dp", "seq"), None),
            P("section", ("dp", "seq")),
        ),
        out_specs=(
            P("section", "dp", "seq", None),
            P("section", "dp", "seq", None),
            P("section", ("dp", "seq")),
            P("section", ("dp", "seq")),
            P("section", ("dp", "seq"), None),
            P("section", ("dp", "seq")),
            P("section", ("dp", "seq")),
            P("section", ("dp", "seq"), None),
            P("section", ("dp", "seq")),
            P("section", ("dp", "seq")),
            P("section", ("dp", "seq")),
            P("section", ("dp", "seq"), None),
            P("section", ("dp", "seq")),
            P("section", ("dp", "seq"), None),
            P("section", ("dp", "seq")),
        ),
        check_vma=False,
    )
```

```python
from functools import partial

import jax
import jax.numpy as jnp
from jax import lax
from jax.experimental import pallas as pl
from jax.experimental.pallas import tpu as pltpu
from jax.sharding import PartitionSpec as P

HEADS = 17
HDIM = 64
BLK = 256
WIDE = 1152
F32, LOW = jnp.float32, jnp.bfloat16
SECTION, RING, LINE = "section", "dp", "seq"
OWNERS = (RING, LINE)
EAST, NORTH, LEVEL, SIBLING, CORNER, ONCE = range(6)


epsilon = 1e-05
far_below = -1e30


def passed_along(value, axis, steps):
    count = lax.axis_size(axis)
    first, last = (max(0, -steps), min(count, count - steps))
    return lax.ppermute(value, axis, [(source, source + steps) for source in range(first, last)])


def normalize(values, scales, offsets):
    centre = jnp.mean(values, axis=-1, keepdims=True)
    centred = values - centre
    inverse = lax.rsqrt(jnp.mean(centred * centred, axis=-1, keepdims=True) + epsilon)
    unit_rows = centred * inverse
    return (unit_rows * scales + offsets, unit_rows, inverse)


def normalize_back(upstream, unit_rows, inverse):
    return inverse * (
        upstream
        - jnp.mean(upstream, axis=-1, keepdims=True)
        - unit_rows * jnp.mean(upstream * unit_rows, axis=-1, keepdims=True)
    )


def score_block(query, key_block, block_index, row_block):
    scores = jnp.einsum(
        "qhd,khd->qhk", query, key_block, preferred_element_type=jnp.float32
    ) * HDIM ** (-0.5)
    highest = jnp.max(scores, axis=-1)
    allowed = (block_index <= row_block)[:, None]
    exponent = jnp.exp(scores - highest[..., None]) * allowed[..., None].astype(jnp.float32)
    levels = jnp.where(allowed, highest, far_below)
    return (exponent, levels)


def attend_forward(query, keys_all, values_all, row_block):
    length = keys_all.shape[0]
    row_count = query.shape[0]
    key_shaped = keys_all.reshape(length, HEADS, HDIM)
    value_shaped = values_all.reshape(length, HEADS, HDIM)
    block_limit = row_block[-1] + 1

    def advance(block_index, carried):
        running_peak, running_sum, weighted = carried
        key_block = lax.dynamic_slice_in_dim(key_shaped, block_index * BLK, BLK, 0)
        value_block = lax.dynamic_slice_in_dim(value_shaped, block_index * BLK, BLK, 0)
        exponent, levels = score_block(query, key_block, block_index, row_block)
        weights = exponent.astype(jnp.bfloat16)
        block_out = jnp.einsum(
            "qhk,khd->qhd", weights, value_block, preferred_element_type=jnp.float32
        )
        newest_peak = jnp.maximum(running_peak, levels)
        shrink_old = jnp.exp(running_peak - newest_peak)
        shrink_new = jnp.exp(levels - newest_peak)
        running_sum = running_sum * shrink_old + shrink_new * jnp.sum(exponent, axis=-1)
        weighted = weighted * shrink_old[..., None] + shrink_new[..., None] * block_out
        return (newest_peak, running_sum, weighted)

    initial = (
        jnp.full((row_count, HEADS), far_below, jnp.float32),
        jnp.zeros((row_count, HEADS), jnp.float32),
        jnp.zeros((row_count, HEADS, HDIM), jnp.float32),
    )
    running_peak, running_sum, weighted = lax.fori_loop(0, block_limit, advance, initial)
    return (weighted / running_sum[..., None], running_peak + jnp.log(running_sum))


def attend_backward(query, keys_all, values_all, row_block, attended, log_total, grad_attended):
    length = keys_all.shape[0]
    key_shaped = keys_all.reshape(length, HEADS, HDIM)
    value_shaped = values_all.reshape(length, HEADS, HDIM)
    block_limit = row_block[-1] + 1
    delta = jnp.sum(grad_attended * attended, axis=-1)

    def advance(block_index, carried):
        grad_query, grad_keys, grad_values = carried
        key_block = lax.dynamic_slice_in_dim(key_shaped, block_index * BLK, BLK, 0)
        value_block = lax.dynamic_slice_in_dim(value_shaped, block_index * BLK, BLK, 0)
        exponent, levels = score_block(query, key_block, block_index, row_block)
        weights = exponent.astype(jnp.bfloat16)
        factor = jnp.exp(levels - log_total)
        scaled = (factor[..., None] * grad_attended).astype(jnp.bfloat16)
        grad_weights = jnp.einsum(
            "qhd,khd->qhk", scaled, value_block, preferred_element_type=jnp.float32
        )
        grad_scores = (exponent * (grad_weights - (factor * delta)[..., None])).astype(jnp.bfloat16)
        grad_query = grad_query + jnp.einsum(
            "qhk,khd->qhd", grad_scores, key_block, preferred_element_type=jnp.float32
        )
        grad_key = jnp.einsum(
            "qhk,qhd->khd", grad_scores, query, preferred_element_type=jnp.float32
        )
        grad_value = jnp.einsum("qhk,qhd->khd", weights, scaled, preferred_element_type=jnp.float32)
        grad_keys = lax.dynamic_update_slice_in_dim(grad_keys, grad_key, block_index * BLK, 0)
        grad_values = lax.dynamic_update_slice_in_dim(grad_values, grad_value, block_index * BLK, 0)
        return (grad_query, grad_keys, grad_values)

    initial = (
        jnp.zeros(query.shape, jnp.float32),
        jnp.zeros((length, HEADS, HDIM), jnp.float32),
        jnp.zeros((length, HEADS, HDIM), jnp.float32),
    )
    grad_query, grad_keys, grad_values = lax.fori_loop(0, block_limit, advance, initial)
    return (
        grad_query,
        grad_keys.reshape(length, HEADS * HDIM),
        grad_values.reshape(length, HEADS * HDIM),
    )


def project(source, params):
    feature_width = HEADS * HDIM
    normed, unit_rows, inverse = normalize(
        source, params[0].astype(jnp.float32), params[1].astype(jnp.float32)
    )
    normed_low = normed.astype(jnp.bfloat16)
    mixture = jnp.dot(normed_low, params[2], preferred_element_type=jnp.float32)
    query_low = (mixture[:, :feature_width] + params[3].astype(jnp.float32)).astype(jnp.bfloat16)
    keys_low = mixture[:, feature_width : 2 * feature_width].astype(jnp.bfloat16)
    values_low = (mixture[:, 2 * feature_width :] + params[4].astype(jnp.float32)).astype(
        jnp.bfloat16
    )
    return (unit_rows, inverse, normed_low, query_low, keys_low, values_low)


def complete(source, params, projected, gathered, row_block):
    row_count = source.shape[0]
    query = projected[3].reshape(row_count, HEADS, HDIM)
    attended, log_total = attend_forward(query, gathered[0], gathered[1], row_block)
    attended_low = attended.reshape(row_count, HEADS * HDIM).astype(jnp.bfloat16)
    middle = source + (
        jnp.dot(attended_low, params[5], preferred_element_type=jnp.float32)
        + params[6].astype(jnp.float32)
    )
    second, unit_second, inverse_second = normalize(
        middle, params[7].astype(jnp.float32), params[8].astype(jnp.float32)
    )
    second_low = second.astype(jnp.bfloat16)
    hidden = jnp.dot(second_low, params[9], preferred_element_type=jnp.float32) + params[10].astype(
        jnp.float32
    )
    active, gelu_pull = jax.vjp(partial(jax.nn.gelu, approximate=False), hidden)
    active_low = active.astype(jnp.bfloat16)
    result = middle + (
        jnp.dot(active_low, params[11], preferred_element_type=jnp.float32)
        + params[12].astype(jnp.float32)
    )
    saved = (
        query,
        attended,
        log_total,
        attended_low,
        unit_second,
        inverse_second,
        second_low,
        gelu_pull,
        active_low,
    )
    return (result, saved)


def layer_backward(source, upstream, params, projected, gathered, row_block):
    unit_first, inverse_first, normed_low, query_low, keys_low, values_low = projected
    row_count = source.shape[0]
    feature_width = HEADS * HDIM
    result, saved = complete(source, params, projected, gathered, row_block)
    (
        query,
        attended,
        log_total,
        attended_low,
        unit_second,
        inverse_second,
        second_low,
        gelu_pull,
        active_low,
    ) = saved
    top_low = upstream.astype(jnp.bfloat16)
    grad_reduce_bias = jnp.sum(top_low.astype(jnp.float32), axis=0)
    grad_reduce_weight = jnp.einsum(
        "tf,td->fd", active_low, top_low, preferred_element_type=jnp.float32
    )
    grad_active = jnp.einsum("td,fd->tf", top_low, params[11], preferred_element_type=jnp.float32)
    grad_hidden_low = gelu_pull(grad_active)[0].astype(jnp.bfloat16)
    grad_expand_bias = jnp.sum(grad_hidden_low.astype(jnp.float32), axis=0)
    grad_expand_weight = jnp.einsum(
        "td,tf->df", second_low, grad_hidden_low, preferred_element_type=jnp.float32
    )
    grad_second = jnp.einsum(
        "tf,df->td", grad_hidden_low, params[9], preferred_element_type=jnp.float32
    )
    grad_second_gain = jnp.sum(grad_second * unit_second, axis=0)
    grad_second_shift = jnp.sum(grad_second, axis=0)
    grad_middle = upstream + normalize_back(
        grad_second * params[7].astype(jnp.float32), unit_second, inverse_second
    )
    branch_low = grad_middle.astype(jnp.bfloat16)
    grad_output_bias = jnp.sum(branch_low.astype(jnp.float32), axis=0)
    grad_output_weight = jnp.einsum(
        "td,te->de", attended_low, branch_low, preferred_element_type=jnp.float32
    )
    grad_attended = jnp.einsum(
        "te,de->td", branch_low, params[5], preferred_element_type=jnp.float32
    )
    grad_query, grad_keys_full, grad_values_full = attend_backward(
        query,
        gathered[0],
        gathered[1],
        row_block,
        attended,
        log_total,
        grad_attended.reshape(row_count, HEADS, HDIM),
    )
    grad_keys, grad_values = (
        lax.psum_scatter(grad_keys_full, LINE, scatter_dimension=0, tiled=True),
        lax.psum_scatter(grad_values_full, LINE, scatter_dimension=0, tiled=True),
    )
    scale_factor = HDIM ** (-0.5)
    grad_mixture = jnp.concatenate(
        [
            grad_query.reshape(row_count, feature_width) * scale_factor,
            grad_keys * scale_factor,
            grad_values,
        ],
        axis=1,
    ).astype(jnp.bfloat16)
    grad_query_bias = jnp.sum(grad_mixture[:, :feature_width].astype(jnp.float32), axis=0)
    grad_value_bias = jnp.sum(grad_mixture[:, 2 * feature_width :].astype(jnp.float32), axis=0)
    grad_joint_weight = jnp.einsum(
        "td,te->de", normed_low, grad_mixture, preferred_element_type=jnp.float32
    )
    grad_normed = jnp.einsum(
        "te,de->td", grad_mixture, params[2], preferred_element_type=jnp.float32
    )
    grad_first_gain = jnp.sum(grad_normed * unit_first, axis=0)
    grad_first_shift = jnp.sum(grad_normed, axis=0)
    grad_source = grad_middle + normalize_back(
        grad_normed * params[0].astype(jnp.float32), unit_first, inverse_first
    )
    grads = (
        grad_first_gain,
        grad_first_shift,
        grad_joint_weight,
        grad_query_bias,
        grad_value_bias,
        grad_output_weight,
        grad_output_bias,
        grad_second_gain,
        grad_second_shift,
        grad_expand_weight,
        grad_expand_bias,
        grad_reduce_weight,
        grad_reduce_bias,
    )
    return (grad_source.astype(jnp.bfloat16), grads)


def body(
    inputs,
    cotangent,
    first_gain,
    first_shift,
    joint_weight,
    query_bias,
    value_bias,
    output_weight,
    output_bias,
    second_gain,
    second_shift,
    expand_weight,
    expand_bias,
    reduce_weight,
    reduce_bias,
):
    section_index = lax.axis_index(SECTION)
    micro_count = inputs.shape[0]
    row_count = inputs.shape[1]
    first_row = lax.axis_index(LINE) * row_count
    row_block = (first_row + jnp.arange(row_count, dtype=jnp.int32)) // BLK
    owned = (
        first_gain[0],
        first_shift[0],
        joint_weight[0],
        query_bias[0],
        value_bias[0],
        output_weight[0],
        output_bias[0],
        second_gain[0],
        second_shift[0],
        expand_weight[0],
        expand_bias[0],
        reduce_weight[0],
        reduce_bias[0],
    )
    forward_params = (
        lax.all_gather(first_gain[0], OWNERS, axis=0, tiled=True),
        lax.all_gather(first_shift[0], OWNERS, axis=0, tiled=True),
        lax.all_gather(joint_weight[0], OWNERS, axis=0, tiled=True),
        lax.all_gather(query_bias[0], OWNERS, axis=0, tiled=True),
        lax.all_gather(value_bias[0], OWNERS, axis=0, tiled=True),
        lax.all_gather(output_weight[0], OWNERS, axis=0, tiled=True),
        lax.all_gather(output_bias[0], OWNERS, axis=0, tiled=True),
        lax.all_gather(second_gain[0], OWNERS, axis=0, tiled=True),
        lax.all_gather(second_shift[0], OWNERS, axis=0, tiled=True),
        lax.all_gather(expand_weight[0], OWNERS, axis=0, tiled=True),
        lax.all_gather(expand_bias[0], OWNERS, axis=0, tiled=True),
        lax.all_gather(reduce_weight[0], OWNERS, axis=0, tiled=True),
        lax.all_gather(reduce_bias[0], OWNERS, axis=0, tiled=True),
    )
    incoming = jnp.zeros(inputs.shape[1:], jnp.bfloat16)
    section_inputs = []
    produced = []
    key_sets = []
    for tick_index in range(micro_count + 1):
        section_input = jnp.where(
            section_index == 0, inputs[min(tick_index, micro_count - 1)], incoming
        )
        source = section_input.astype(jnp.float32)
        projected = project(source, forward_params)
        gathered = (
            lax.all_gather(projected[4], LINE, axis=0, tiled=True),
            lax.all_gather(projected[5], LINE, axis=0, tiled=True),
        )
        result, unused = complete(source, forward_params, projected, gathered, row_block)
        result_low = result.astype(jnp.bfloat16)
        section_inputs.append(section_input)
        produced.append(result_low)
        key_sets.append(gathered)
        if tick_index < micro_count:
            incoming = passed_along(result_low, SECTION, 1)
    backward_params = (
        lax.all_gather(first_gain[0], OWNERS, axis=0, tiled=True),
        lax.all_gather(first_shift[0], OWNERS, axis=0, tiled=True),
        lax.all_gather(joint_weight[0], OWNERS, axis=0, tiled=True),
        lax.all_gather(query_bias[0], OWNERS, axis=0, tiled=True),
        lax.all_gather(value_bias[0], OWNERS, axis=0, tiled=True),
        lax.all_gather(output_weight[0], OWNERS, axis=0, tiled=True),
        lax.all_gather(output_bias[0], OWNERS, axis=0, tiled=True),
        lax.all_gather(second_gain[0], OWNERS, axis=0, tiled=True),
        lax.all_gather(second_shift[0], OWNERS, axis=0, tiled=True),
        lax.all_gather(expand_weight[0], OWNERS, axis=0, tiled=True),
        lax.all_gather(expand_bias[0], OWNERS, axis=0, tiled=True),
        lax.all_gather(reduce_weight[0], OWNERS, axis=0, tiled=True),
        lax.all_gather(reduce_bias[0], OWNERS, axis=0, tiled=True),
    )
    totals = tuple((jnp.zeros(piece.shape, jnp.float32) for piece in backward_params))
    shares = tuple((jnp.zeros(piece.shape, jnp.float32) for piece in owned))
    returning = jnp.zeros(inputs.shape[1:], jnp.bfloat16)
    sent_back = []
    for tick_index in range(micro_count + 1):
        upper_pick = min(tick_index + 1, micro_count)
        lower_pick = max(tick_index - 1, 0)
        section_input = jnp.where(
            section_index == 1, section_inputs[upper_pick], section_inputs[lower_pick]
        )
        upstream = jnp.where(
            section_index == 1, cotangent[min(tick_index, micro_count - 1)], returning
        ).astype(jnp.float32)
        weight_valid = jnp.where(
            section_index == 1,
            1.0 if tick_index < micro_count else 0.0,
            1.0 if tick_index >= 1 else 0.0,
        ).astype(jnp.float32)
        source = section_input.astype(jnp.float32)
        projected = project(source, backward_params)
        gathered = (
            lax.all_gather(projected[4], LINE, axis=0, tiled=True),
            lax.all_gather(projected[5], LINE, axis=0, tiled=True),
        )
        grad_source, grads = layer_backward(
            source, upstream, backward_params, projected, gathered, row_block
        )
        masked = tuple((update * weight_valid for update in grads))
        totals = tuple((running + update for running, update in zip(totals, masked)))
        sent_back.append(grad_source)
        if tick_index < micro_count:
            returning = passed_along(grad_source, SECTION, -1)
    layer_outputs = jnp.stack(
        [
            jnp.where(section_index == 0, produced[position], produced[position + 1])
            for position in range(micro_count)
        ]
    )[None]
    input_grads = jnp.stack(
        [
            jnp.where(section_index == 1, sent_back[position], sent_back[position + 1])
            for position in range(micro_count)
        ]
    )[None]
    (
        sum_first_gain,
        sum_first_shift,
        sum_joint_weight,
        sum_query_bias,
        sum_value_bias,
        sum_output_weight,
        sum_output_bias,
        sum_second_gain,
        sum_second_shift,
        sum_expand_weight,
        sum_expand_bias,
        sum_reduce_weight,
        sum_reduce_bias,
    ) = totals
    shares = (
        lax.psum_scatter(sum_first_gain, OWNERS, scatter_dimension=0, tiled=True),
        lax.psum_scatter(sum_first_shift, OWNERS, scatter_dimension=0, tiled=True),
        lax.psum_scatter(sum_joint_weight, OWNERS, scatter_dimension=0, tiled=True),
        lax.psum_scatter(sum_query_bias, OWNERS, scatter_dimension=0, tiled=True),
        lax.psum_scatter(sum_value_bias, OWNERS, scatter_dimension=0, tiled=True),
        lax.psum_scatter(sum_output_weight, OWNERS, scatter_dimension=0, tiled=True),
        lax.psum_scatter(sum_output_bias, OWNERS, scatter_dimension=0, tiled=True),
        lax.psum_scatter(sum_second_gain, OWNERS, scatter_dimension=0, tiled=True),
        lax.psum_scatter(sum_second_shift, OWNERS, scatter_dimension=0, tiled=True),
        lax.psum_scatter(sum_expand_weight, OWNERS, scatter_dimension=0, tiled=True),
        lax.psum_scatter(sum_expand_bias, OWNERS, scatter_dimension=0, tiled=True),
        lax.psum_scatter(sum_reduce_weight, OWNERS, scatter_dimension=0, tiled=True),
        lax.psum_scatter(sum_reduce_bias, OWNERS, scatter_dimension=0, tiled=True),
    )
    return (layer_outputs, input_grads) + tuple((portion[None] for portion in shares))


def swapped(value, axis, bits):
    count = lax.axis_size(axis)
    return lax.ppermute(value, axis, [(source, source ^ bits) for source in range(count)])


def to_rows(array, core, line):
    half = array.shape[1] // 2
    which = line // 2

    def part(index):
        return lax.dynamic_slice(
            array, (index, core * half, 0), (1, half, array.shape[2])
        )[0]

    mine, arrived = part(which), swapped(part(1 - which), LINE, 3)
    low_side = which == 0
    return jnp.concatenate(
        [jnp.where(low_side, mine, arrived), jnp.where(low_side, arrived, mine)], axis=0
    )


def from_rows(lower, upper, core, line):
    half = lower.shape[0] // 2
    low_side = line // 2 == 0
    both = jnp.stack([lower, upper])
    mine = jnp.where(low_side, both[:, :half], both[:, half:])
    arrived = swapped(jnp.where(low_side, both[:, half:], both[:, :half]), LINE, 3)
    pair = jnp.stack(
        [jnp.where(low_side, mine, arrived), jnp.where(low_side, arrived, mine)], axis=1
    )
    kept = jnp.where(core == 0, pair[0], pair[1])
    other = swapped(jnp.where(core == 0, pair[1], pair[0]), SECTION, 1)
    return jnp.concatenate(
        [jnp.where(core == 0, kept, other), jnp.where(core == 0, other, kept)], axis=1
    )[None]


def flip(place, bits):
    return {1: place + 1 - 2 * (place % 2), 2: (place + 2) % 4, 3: 3 - place}[bits]


def places():
    core, ring, line = (lax.axis_index(name) for name in (SECTION, RING, LINE))
    rings = [ring] + [flip(ring, bits) for bits in (1, 2, 3)]
    lines = [line] + [flip(line, bits) for bits in (1, 2, 3)]
    toward = {
        EAST: {RING: rings[1]},
        NORTH: {RING: rings[2]},
        (LEVEL, 1): {LINE: lines[1]},
        (LEVEL, 2): {LINE: lines[2]},
        (LEVEL, 3): {LINE: lines[3]},
        SIBLING: {SECTION: 1 - core},
    }
    return core, rings, lines, toward


def greet(toward):
    barrier = pltpu.get_barrier_semaphore()
    for to in toward.values():
        pl.semaphore_signal(barrier, inc=1, device_id=to, device_id_type=pl.DeviceIdType.MESH)
    pl.semaphore_wait(barrier, len(toward))


def remote_copy(source, target, send_sem, recv_sem, to):
    return pltpu.make_async_remote_copy(
        src_ref=source,
        dst_ref=target,
        send_sem=send_sem,
        recv_sem=recv_sem,
        device_id=to,
        device_id_type=pl.DeviceIdType.MESH,
    )


def per_core(core, act):
    for index in (0, 1):

        @pl.when(core == index)
        def _():
            act(index)


GATHER_KINDS = (
    [(LEVEL, k) for k in (1, 2, 3)]
    + [(name, k) for name in (EAST, NORTH, CORNER) for k in range(4)]
    + [(SIBLING, k) for k in range(4)]
)
GATHER_NUMBER = {kind: index for index, kind in enumerate(GATHER_KINDS)}


def gather_kernel(slots, *refs):
    shards, refs = refs[:slots], refs[slots:]
    outs, refs = [refs[2 * t : 2 * t + 2] for t in range(slots)], refs[2 * slots :]
    send_sem, recv_sem, copy_sem = refs
    core, rings, lines, toward = places()
    greet(toward)
    sent, copied = [], []

    def copy_of(t, source, target, to, kind):
        index = t * len(GATHER_KINDS) + GATHER_NUMBER[kind]
        return remote_copy(source, target, send_sem.at[index], recv_sem.at[index], toward[to])

    def place(t, page, dd, k):
        return outs[t][page].at[rings[dd] * 4 + lines[k]]

    def send(t, dd, k, to, kind, own=False):
        def act(page):
            target = place(t, page, dd, k)
            copy_of(t, shards[t] if own else target, target, to, kind).start()

        per_core(core, act)
        sent.append(copy_of(t, place(t, 0, dd, k), place(t, 0, dd, k), to, kind))

    def arrive(t, dd, k, to, kind):
        def act(page):
            target = place(t, page, dd, k)
            copy_of(t, target, target, to, kind).wait_recv()

        per_core(core, act)

    def group(t, page, dd):
        return outs[t][page].at[pl.ds(rings[dd] * 4, 4)]

    def sibling(t, dd):
        def act(page):
            copy_of(t, group(t, page, dd), group(t, page, dd), SIBLING, (SIBLING, dd)).start()

        per_core(core, act)
        sent.append(copy_of(t, group(t, 0, dd), group(t, 0, dd), SIBLING, (SIBLING, dd)))

    def begin_line(t):
        for k in (1, 2, 3):
            send(t, 0, 0, (LEVEL, k), (LEVEL, k), own=True)

    def begin_ring(t):
        send(t, 0, 0, EAST, (EAST, 0), own=True)
        send(t, 0, 0, NORTH, (NORTH, 0), own=True)

        def act(page):
            pltpu.make_async_copy(shards[t], place(t, page, 0, 0), copy_sem.at[t]).start()

        per_core(core, act)

    def own_ready(t):
        def act(page):
            pltpu.make_async_copy(shards[t], place(t, page, 0, 0), copy_sem.at[t]).wait()

        per_core(core, act)

    def from_line(t, k):
        arrive(t, 0, k, (LEVEL, k), (LEVEL, k))
        send(t, 0, k, EAST, (EAST, k))
        send(t, 0, k, NORTH, (NORTH, k))

    def from_ring(t, k):
        arrive(t, 1, k, EAST, (EAST, k))
        if k < 2:
            send(t, 1, k, NORTH, (CORNER, k))
        arrive(t, 2, k, NORTH, (NORTH, k))
        if k >= 2:
            send(t, 2, k, EAST, (CORNER, k))

    begin_line(0)
    begin_ring(0)
    for t in range(slots):
        from_ring(t, 0)
        from_line(t, 1)
        from_line(t, 2)
        from_line(t, 3)
        own_ready(t)
        sibling(t, 0)
        if t + 1 < slots:
            begin_line(t + 1)
        from_ring(t, 1)
        if t + 1 < slots:
            begin_ring(t + 1)
        from_ring(t, 2)
        from_ring(t, 3)
        sibling(t, 1)
        sibling(t, 2)
        for k in range(4):
            arrive(t, 3, k, NORTH if k < 2 else EAST, (CORNER, k))
        sibling(t, 3)
    for t in range(slots):
        for dd in range(4):

            def act(page):
                target = group(t, 1 - page, dd)
                copy_of(t, target, target, SIBLING, (SIBLING, dd)).wait_recv()

            per_core(core, act)
    for copy in sent:
        copy.wait_send()


def gather_pages(shards):
    slots = len(shards)
    count = slots * len(GATHER_KINDS)
    whole = [
        jax.ShapeDtypeStruct((16,) + shard.shape, shard.dtype) for shard in shards for _ in (0, 1)
    ]
    anywhere = pl.BlockSpec(memory_space=pl.ANY)
    out = pl.pallas_call(
        partial(gather_kernel, slots),
        out_shape=tuple(whole),
        in_specs=[anywhere] * slots,
        out_specs=tuple(anywhere for _ in whole),
        scratch_shapes=[
            pltpu.SemaphoreType.DMA((count,)),
            pltpu.SemaphoreType.DMA((count,)),
            pltpu.SemaphoreType.DMA((slots,)),
        ],
        compiler_params=pltpu.CompilerParams(collective_id=0, has_side_effects=True),
        name="gather_pages",
    )(*shards)
    return [out[2 * t : 2 * t + 2] for t in range(slots)]


KINDS = (
    [(CORNER, dd) for dd in range(4)]
    + [(ONCE, k) for k in range(4)]
    + [(EAST, k) for k in range(4)]
    + [(NORTH, k) for k in range(4)]
    + [(LEVEL, k) for k in (1, 2, 3)]
)
NUMBER = {kind: i for i, kind in enumerate(KINDS)}
DEPTH = 8

def scatter_kernel(slots, *refs):
    n = len(slots)
    pages = [(refs[2 * t], refs[2 * t + 1]) for t in range(n)]
    refs = refs[2 * n :]
    finals, refs = refs[:n], refs[n:]
    lands, refs = [refs[5 * t : 5 * t + 5] for t in range(n)], refs[5 * n :]
    shapes = sorted(set(slots))
    work = {}
    for i, shape in enumerate(shapes):
        work[shape] = refs[3 * i : 3 * i + 3]
    refs = refs[3 * len(shapes) :]
    send_sem, recv_sem, load_sem, out_sem = refs
    core, rings, lines, toward = places()
    greet(toward)

    def remote(t, src, dst, to, kind):
        i = t * len(KINDS) + NUMBER[kind]
        return pltpu.make_async_remote_copy(
            src_ref=src, dst_ref=dst, send_sem=send_sem.at[i], recv_sem=recv_sem.at[i],
            device_id=toward[to], device_id_type=pl.DeviceIdType.MESH)

    def by_core(make):
        def start(pair):
            for index in (0, 1):
                @pl.when(core == index)
                def _():
                    make(pair[index]).start()
        return start

    pending = []

    def give(t, dd):
        dst = lands[t][0].at[pl.ds(rings[dd] * 4, 4)]
        pair = (pages[t][1], pages[t][0])
        by_core(lambda ref: remote(t, ref.at[pl.ds(rings[dd] * 4, 4)], dst, SIBLING, (CORNER, dd)))(pair)
        pending.append(remote(t, dst, dst, SIBLING, (CORNER, dd)))

    def arrived(t, ref, to, kind):
        remote(t, ref, ref, to, kind).wait_recv()

    task = [0]
    used = {shape: [None] * DEPTH for shape in shapes}
    count = {shape: 0 for shape in shapes}

    def total_of(t, dd, k, extra):
        shape = slots[t]
        loads = work[shape][0]
        slot = task[0] % 2
        task[0] += 1
        index = rings[dd] * 4 + lines[k]
        buf = lambda j: loads.at[slot, j]
        sem = lambda j: load_sem.at[slot * 4 + j]
        by_core(lambda ref: pltpu.make_async_copy(ref.at[index], buf(0), sem(0)))(pages[t])
        copies = [pltpu.make_async_copy(buf(0), buf(0), sem(0))]
        sources = [lands[t][0].at[index]] + extra
        for j, source in enumerate(sources):
            copy = pltpu.make_async_copy(source, buf(j + 1), sem(j + 1))
            copy.start()
            copies.append(copy)
        for copy in copies:
            copy.wait()
        return loads, slot, len(copies)

    def add_up(shape, loads, slot, terms, store):
        rows, columns = shape
        if rows == 72:
            def step(i, _):
                at = pl.ds(pl.multiple_of(i * 256, 256), 256)
                value = loads[slot, 0, :, at].astype(jnp.float32)
                for j in range(1, terms):
                    value = value + loads[slot, j, :, at].astype(jnp.float32)
                store((slice(None), at), value)
                return 0
            lax.fori_loop(0, columns // 256, step, 0)
        else:
            def step(i, _):
                at = pl.ds(pl.multiple_of(i * 16, 16), 16)
                value = loads[slot, 0, at, :].astype(jnp.float32)
                for j in range(1, terms):
                    value = value + loads[slot, j, at, :].astype(jnp.float32)
                store((at, slice(None)), value)
                return 0
            lax.fori_loop(0, rows // 16, step, 0)

    def sum_and_send(t, dd, k, extra, dst, to, kind):
        shape = slots[t]
        loads, slot, terms = total_of(t, dd, k, extra)
        place = count[shape] % DEPTH
        count[shape] += 1
        if used[shape][place] is not None:
            used[shape][place].wait_send()
        out = work[shape][1]
        def store(at, value):
            out[(place,) + at] = value.astype(jnp.bfloat16)
        add_up(shape, loads, slot, terms, store)
        copy = remote(t, out.at[place], dst, to, kind)
        copy.start()
        used[shape][place] = copy

    def first(t):
        one = lands[t][1]
        arrived(t, lands[t][0].at[pl.ds(rings[3] * 4, 4)], SIBLING, (CORNER, 3))
        for k in (0, 2, 1, 3):
            to = EAST if k < 2 else NORTH
            sum_and_send(t, 3, k, [], one.at[k], to, (ONCE, k))

    def second(t):
        one, land_x, land_y = lands[t][1:4]
        arrived(t, lands[t][0].at[pl.ds(rings[1] * 4, 4)], SIBLING, (CORNER, 1))
        arrived(t, lands[t][0].at[pl.ds(rings[2] * 4, 4)], SIBLING, (CORNER, 2))
        order = ((1, 0), (2, 3), (1, 1), (2, 2), (1, 3), (2, 0), (1, 2), (2, 1))
        for dd, k in order:
            to, land = (EAST, land_x) if dd == 1 else (NORTH, land_y)
            extra = []
            if (dd == 1) == (k >= 2):
                arrived(t, one.at[k], NORTH if k >= 2 else EAST, (ONCE, k))
                extra = [one.at[k]]
            sum_and_send(t, dd, k, extra, land.at[k], to, (to, k))

    held = {}

    def third(t):
        land_x, land_y, land_z = lands[t][2:5]
        arrived(t, lands[t][0].at[pl.ds(rings[0] * 4, 4)], SIBLING, (CORNER, 0))
        for k in (3, 2, 1, 0):
            arrived(t, land_x.at[k], EAST, (EAST, k))
            arrived(t, land_y.at[k], NORTH, (NORTH, k))
            extra = [land_x.at[k], land_y.at[k]]
            if k:
                sum_and_send(t, 0, k, extra, land_z.at[k], (LEVEL, k), (LEVEL, k))
            else:
                shape = slots[t]
                loads, slot, terms = total_of(t, 0, 0, extra)
                total = work[shape][2]
                def store(at, value):
                    total[at] = value
                add_up(shape, loads, slot, terms, store)

    def last(t):
        shape = slots[t]
        land_z = lands[t][4]
        loads, _, total = work[shape]
        slot = task[0] % 2
        task[0] += 1
        copies = []
        for k in (1, 2, 3):
            arrived(t, land_z.at[k], (LEVEL, k), (LEVEL, k))
            copy = pltpu.make_async_copy(land_z.at[k], loads.at[slot, k - 1], load_sem.at[slot * 4 + k - 1])
            copy.start()
            copies.append(copy)
        for copy in copies:
            copy.wait()
        def store(at, value):
            total[at] = total[at] + value
        add_up(shape, loads, slot, 3, store)
        copy = pltpu.make_async_copy(total, finals[t], out_sem)
        copy.start()
        copy.wait()

    for dd in (3, 1, 2, 0):
        give(0, dd)
    for t in range(n + 1):
        if t < n:
            first(t)
            if t + 1 < n:
                for dd in (3, 1, 2, 0):
                    give(t + 1, dd)
        if t > 0:
            third(t - 1)
        if t < n:
            second(t)
        if t > 0:
            last(t - 1)
    for copy in pending:
        copy.wait_send()
    for shape in shapes:
        for copy in used[shape]:
            if copy is not None:
                copy.wait_send()

def scatter(pairs, name="scatter_gradients", collective=1):
    slots = [tuple(a.shape[1:]) for a, _ in pairs]
    n = len(slots)
    shapes = sorted(set(slots))
    out = [jax.ShapeDtypeStruct(s, jnp.float32) for s in slots]
    for s in slots:
        out += [jax.ShapeDtypeStruct((m,) + s, jnp.bfloat16) for m in (16, 4, 4, 4, 4)]
    scratch = []
    for s in shapes:
        scratch += [pltpu.VMEM((2, 4) + s, jnp.bfloat16), pltpu.VMEM((DEPTH,) + s, jnp.bfloat16), pltpu.VMEM(s, jnp.float32)]
    m = n * len(KINDS)
    scratch += [pltpu.SemaphoreType.DMA((m,)), pltpu.SemaphoreType.DMA((m,)), pltpu.SemaphoreType.DMA((8,)), pltpu.SemaphoreType.DMA(())]
    res = pl.pallas_call(
        partial(scatter_kernel, slots),
        out_shape=tuple(out),
        in_specs=[pl.BlockSpec(memory_space=pl.ANY)] * (2 * n),
        out_specs=tuple(pl.BlockSpec(memory_space=pl.ANY) for _ in out),
        scratch_shapes=scratch,
        compiler_params=pltpu.CompilerParams(collective_id=collective, has_side_effects=True, vmem_limit_bytes=48 << 20),
        name=name,
    )(*[x for pair in pairs for x in pair])
    return res[:n]


def mm(left, right):
    return jnp.dot(left, right, preferred_element_type=F32)


def mm_nt(left, right):
    return lax.dot_general(left, right, (((1,), (1,)), ((), ())), preferred_element_type=F32)


def mm_tn(left, right):
    return lax.dot_general(left, right, (((0,), (0,)), ((), ())), preferred_element_type=F32)


def normal_parts(values):
    centre = jnp.mean(values, axis=-1, keepdims=True)
    centred = values - centre
    inverse = lax.rsqrt(jnp.mean(centred * centred, axis=-1, keepdims=True) + epsilon)
    return centred * inverse, inverse


def normal_back(upstream, unit, inverse):
    return inverse * (
        upstream
        - jnp.mean(upstream, axis=-1, keepdims=True)
        - unit * jnp.mean(upstream * unit, axis=-1, keepdims=True)
    )


def close_up(rows, table):
    high = rows.astype(LOW)
    rest = (rows - high.astype(F32)).astype(LOW)
    return mm_nt(high, table) + mm_nt(rest, table)


def whole(shape):
    zeros = (0,) * len(shape)
    return pl.BlockSpec(shape, lambda *_: zeros)


def project_kernel(steps, width, x, gain, shift, query_bias, value_bias, table, page,
                   normed_out, query_out, pair_out, mixture):
    step = pl.program_id(0)
    tile = page.shape[1]

    @pl.when(step == 0)
    def _():
        unit, _ = normal_parts(x[...].astype(F32))
        normed = (unit * gain[...] + shift[...]).astype(LOW)
        normed_out[...] = mm(normed, table[...]).astype(LOW)

    mixture[:, pl.ds(pl.multiple_of(step * tile, tile), tile)] = mm(normed_out[...], page[...])

    @pl.when(step == steps - 1)
    def _():
        blank = jnp.zeros((x.shape[0], WIDE - width), LOW)
        query = ((mixture[:, :width] + query_bias[...]).astype(LOW).astype(F32) * HDIM ** (-0.5)).astype(LOW)
        query_out[:, :width] = query
        query_out[:, width:] = blank
        pair_out[0, :, :width] = mixture[:, width : 2 * width].astype(LOW)
        pair_out[0, :, width:] = blank
        pair_out[1, :, :width] = (mixture[:, 2 * width : 3 * width] + value_bias[...]).astype(LOW)
        pair_out[1, :, width:] = blank


def project_rows(x, gain, shift, query_bias, value_bias, table, page):
    rows, width = x.shape
    tile, steps = 640, 6
    return pl.pallas_call(
        partial(project_kernel, steps, width),
        grid=(steps,),
        in_specs=[whole(x.shape)] + [whole((1, width))] * 4 + [whole(table.shape)]
        + [pl.BlockSpec((page.shape[0], tile), lambda i: (0, i))],
        out_specs=(whole((rows, WIDE)), whole((rows, WIDE)), whole((2, rows, WIDE))),
        out_shape=(
            jax.ShapeDtypeStruct((rows, WIDE), LOW),
            jax.ShapeDtypeStruct((rows, WIDE), LOW),
            jax.ShapeDtypeStruct((2, rows, WIDE), LOW),
        ),
        scratch_shapes=[pltpu.VMEM((rows, tile * steps), F32)],
        compiler_params=pltpu.CompilerParams(vmem_limit_bytes=48 << 20),
        name="project_rows",
    )(x, gain, shift, query_bias, value_bias, table, page)


def head_pair(rows):
    lane = lax.broadcasted_iota(jnp.int32, rows.shape, 1)
    zero = jnp.zeros_like(rows)
    return jnp.concatenate(
        [jnp.where(lane < HDIM, rows, zero), jnp.where(lane < HDIM, zero, rows)], axis=0
    )


def from_pair(turned):
    n = turned.shape[1] // 2
    own = jnp.concatenate([turned[:HDIM, :n], turned[HDIM:, n:]], axis=0)
    return own.T


def attend_kernel(x, here, beside, away, corner, first_ref, attended_out, log_out):
    first = first_ref[0] == 0
    half = x.shape[0] // 2
    low, high = head_pair(x[:half]), head_pair(x[half:])
    last_rows = jnp.where(first, high, low)

    def block(kind, near, part):
        at = pl.ds(part * half, half)
        one, two = (here, beside) if near == 0 else (away, corner)
        return jnp.concatenate([one[kind, at], two[kind, at]], axis=0)

    def last_block(kind):
        return jnp.where(first, block(kind, 1, 1), block(kind, 1, 0))

    units = [
        (low, (0, 0)), (high, (0, 0)), (high, (0, 1)), (high, (1, 0)), (last_rows, None),
    ]
    parts = []
    for rows, which in units:
        keys = last_block(0) if which is None else block(0, *which)
        values = last_block(1) if which is None else block(1, *which)
        scores = mm_nt(keys, rows)
        level = jnp.max(scores, axis=0, keepdims=True)
        exponent = jnp.exp(scores - level)
        parts.append(
            (level, jnp.sum(exponent, axis=0, keepdims=True), mm_tn(values, exponent.astype(LOW)))
        )
    last = parts[4]
    low_last = (jnp.where(first, far_below, last[0]),) + last[1:]
    high_last = (jnp.where(first, last[0], far_below),) + last[1:]
    for place, group in enumerate(([parts[0], low_last], parts[1:4] + [high_last])):
        peak = group[0][0]
        for level, _, _ in group[1:]:
            peak = jnp.maximum(peak, level)
        total, mixed = 0.0, 0.0
        for level, sums, out in group:
            share = jnp.exp(level - peak)
            total = total + share * sums
            mixed = mixed + share * out
        attended_out[place * half : (place + 1) * half] = from_pair(mixed / total)
        log_out[0, place : place + 1] = peak + jnp.log(total)


def attend(query, here, beside, away, corner, low_chunk):
    rows = query.shape[0]
    pairs = WIDE // 128
    flat = pl.BlockSpec((rows, 128), lambda p: (0, p))
    both = pl.BlockSpec((2, rows, 128), lambda p: (0, 0, p))
    return pl.pallas_call(
        attend_kernel,
        grid=(pairs,),
        in_specs=[flat] + [both] * 4 + [pl.BlockSpec(memory_space=pltpu.SMEM)],
        out_specs=(flat, pl.BlockSpec((1, 2, rows), lambda p: (p, 0, 0))),
        out_shape=(
            jax.ShapeDtypeStruct((rows, WIDE), F32),
            jax.ShapeDtypeStruct((pairs, 2, rows), F32),
        ),
        compiler_params=pltpu.CompilerParams(vmem_limit_bytes=48 << 20),
        name="attend",
    )(query, here, beside, away, corner, low_chunk.reshape(1))


def attend_back_kernel(query, grad, attended, logs, here, beside, away, corner, first_ref,
                       query_out, here_out, beside_out, away_out, corner_out):
    first = first_ref[0] == 0
    half = query.shape[0] // 2

    def rows_of(place):
        at = slice(place * half, (place + 1) * half)
        rows, grads = head_pair(query[at]), head_pair(grad[at])
        product = (grad[at].astype(F32) * attended[at]).T
        delta = jnp.concatenate(
            [jnp.sum(product[:HDIM], axis=0, keepdims=True), jnp.sum(product[HDIM:], axis=0, keepdims=True)],
            axis=1,
        )
        return rows, grads, logs[0, place : place + 1], delta

    low, high = rows_of(0), rows_of(1)
    last_rows = tuple(jnp.where(first, b, a) for a, b in zip(low, high))

    def block(kind, near, part):
        at = pl.ds(part * half, half)
        one, two = (here, beside) if near == 0 else (away, corner)
        return jnp.concatenate([one[kind, at], two[kind, at]], axis=0)

    def back(rows, keys, values):
        queries, grads, log, delta = rows
        weights = jnp.exp(mm_nt(keys, queries) - log)
        pulled = (weights * (mm_nt(values, grads) - delta)).astype(LOW)
        return (
            mm_tn(keys, pulled),
            mm(pulled, queries),
            mm(weights.astype(LOW), grads),
        )

    def put(near, part, grad_keys, grad_values):
        one, two = (here_out, beside_out) if near == 0 else (away_out, corner_out)
        at = pl.ds(part * half, half)
        for kind, value in ((0, grad_keys), (1, grad_values)):
            one[kind, at] = value[:half].astype(one.dtype)
            two[kind, at] = value[half:].astype(two.dtype)

    keys, values = block(0, 0, 0), block(1, 0, 0)
    low_query, keys_a, values_a = back(low, keys, values)
    high_query, keys_b, values_b = back(high, keys, values)
    put(0, 0, keys_a + keys_b, values_a + values_b)
    more, keys_a, values_a = back(high, block(0, 0, 1), block(1, 0, 1))
    high_query = high_query + more
    put(0, 1, keys_a, values_a)
    more, keys_a, values_a = back(high, block(0, 1, 0), block(1, 1, 0))
    high_query = high_query + more
    keys = jnp.where(first, block(0, 1, 1), block(0, 1, 0))
    values = jnp.where(first, block(1, 1, 1), block(1, 1, 0))
    more, keys_b, values_b = back(last_rows, keys, values)
    zero = jnp.zeros_like(keys_b)
    put(1, 0, keys_a + jnp.where(first, zero, keys_b), values_a + jnp.where(first, zero, values_b))
    put(1, 1, jnp.where(first, keys_b, zero), jnp.where(first, values_b, zero))
    empty = jnp.zeros_like(more)
    low_query = low_query + jnp.where(first, empty, more)
    high_query = high_query + jnp.where(first, more, empty)
    scale_factor = HDIM ** (-0.5)
    query_out[:half] = (from_pair(low_query) * scale_factor).astype(LOW)
    query_out[half:] = (from_pair(high_query) * scale_factor).astype(LOW)


def attend_back(query, grad, attended, logs, here, beside, away, corner, low_chunk):
    rows = query.shape[0]
    pairs = WIDE // 128
    flat = pl.BlockSpec((rows, 128), lambda p: (0, p))
    both = pl.BlockSpec((2, rows, 128), lambda p: (0, 0, p))
    shape = (2, rows, WIDE)
    return pl.pallas_call(
        attend_back_kernel,
        grid=(pairs,),
        in_specs=[flat, flat, flat, pl.BlockSpec((1, 2, rows), lambda p: (p, 0, 0))] + [both] * 4
        + [pl.BlockSpec(memory_space=pltpu.SMEM)],
        out_specs=(flat, both, both, both, both),
        out_shape=(jax.ShapeDtypeStruct((rows, WIDE), LOW), jax.ShapeDtypeStruct(shape, F32))
        + tuple(jax.ShapeDtypeStruct(shape, LOW) for _ in range(3)),
        compiler_params=pltpu.CompilerParams(vmem_limit_bytes=48 << 20),
        name="attend_back",
    )(query, grad, attended, logs, here, beside, away, corner, low_chunk.reshape(1))


def feed_kernel(steps, width, x, attended, gain, shift, output_bias, reduce_bias, table, page, expand,
                expand_bias, reduce, attended_out, middle_out, second_out, active_out, slope_out,
                result_out, result_low_out, output, sem):
    step = pl.program_id(0)
    lead = 4 * width - WIDE
    extra = 3 * width - lead

    @pl.when(step == 0)
    def _():
        copy = pltpu.make_async_copy(page.at[:, pl.ds(lead, WIDE)], output, sem)
        copy.start()
        attended_out[...] = mm(attended[:, :width].astype(LOW), table[...]).astype(LOW)
        copy.wait()
        blended = mm(attended_out[...], output[...])
        middle = x[...].astype(F32) + (blended[:, extra:] + output_bias[...])
        middle_out[...] = middle
        unit, _ = normal_parts(middle)
        second = (unit * gain[...] + shift[...]).astype(LOW)
        second_out[...] = mm(second, table[...]).astype(LOW)
        result_out[...] = middle + reduce_bias[...]

    hidden = mm(second_out[...], expand[...]) + expand_bias[...]
    below = 0.5 + 0.5 * lax.erf(hidden * 0.7071067811865476)
    active = (hidden * below).astype(LOW)
    active_out[...] = active
    slope = below + hidden * (0.3989422804014327 * jnp.exp(-0.5 * hidden * hidden))
    slope_out[...] = slope.astype(LOW)
    result_out[...] += mm(active, reduce[...])

    @pl.when(step == steps - 1)
    def _():
        result_low_out[...] = result_out[...].astype(LOW)


def feed(x, attended, gain, shift, output_bias, reduce_bias, table, page, expand, expand_bias, reduce):
    rows, width = x.shape
    inner = expand.shape[1]
    tile = 256
    steps = inner // tile
    flat = whole((rows, width))
    wide = whole((rows, WIDE))
    column = pl.BlockSpec((rows, tile), lambda i: (0, i))
    outs = pl.pallas_call(
        partial(feed_kernel, steps, width),
        grid=(steps,),
        in_specs=[flat, wide] + [whole((1, width))] * 4
        + [whole(table.shape), pl.BlockSpec(memory_space=pl.ANY)]
        + [pl.BlockSpec((WIDE, tile), lambda i: (0, i)), pl.BlockSpec((1, tile), lambda i: (0, i)),
           pl.BlockSpec((tile, width), lambda i: (i, 0))],
        out_specs=(wide, flat, wide, column, column, flat, flat),
        out_shape=(
            jax.ShapeDtypeStruct((rows, WIDE), LOW),
            jax.ShapeDtypeStruct((rows, width), F32),
            jax.ShapeDtypeStruct((rows, WIDE), LOW),
            jax.ShapeDtypeStruct((rows, inner), LOW),
            jax.ShapeDtypeStruct((rows, inner), LOW),
            jax.ShapeDtypeStruct((rows, width), F32),
            jax.ShapeDtypeStruct((rows, width), LOW),
        ),
        scratch_shapes=[pltpu.VMEM((WIDE, WIDE), LOW), pltpu.SemaphoreType.DMA(())],
        compiler_params=pltpu.CompilerParams(vmem_limit_bytes=48 << 20),
        name="feed",
    )(x, attended, gain, shift, output_bias, reduce_bias, table, page, expand, expand_bias, reduce)
    attended_low, middle, second_low, active, slope, _, result = outs
    return attended_low, middle, second_low, active, slope, result


def feed_back_kernel(steps, width, top, slope, middle, gain, table, page, expand, reduce,
                     hidden_out, bias_out, middle_out, branch_out, attended_out, sums_out,
                     second, output, sem):
    step = pl.program_id(0)
    lead = 4 * width - WIDE
    extra = 3 * width - lead
    rows = top.shape[0]

    @pl.when(step == 0)
    def _():
        pltpu.make_async_copy(page.at[:, pl.ds(lead, WIDE)], output, sem).start()
        second[...] = jnp.zeros_like(second)

    hidden = (mm_nt(top[...], reduce[...]) * slope[...].astype(F32)).astype(LOW)
    hidden_out[...] = hidden
    bias_out[...] = jnp.sum(hidden.astype(F32), axis=0, keepdims=True)
    second[...] += mm_nt(hidden, expand[...])

    @pl.when(step == steps - 1)
    def _():
        pltpu.make_async_copy(page.at[:, pl.ds(lead, WIDE)], output, sem).wait()
        upstream = top[...].astype(F32)
        grad_second = close_up(second[...], table[...])
        unit, inverse = normal_parts(middle[...])
        grad_middle = upstream + normal_back(grad_second * gain[...], unit, inverse)
        middle_out[...] = grad_middle
        branch = grad_middle.astype(LOW)
        branch_out[...] = branch
        full = jnp.concatenate([jnp.zeros((rows, extra), LOW), branch], axis=1)
        pulled = mm_nt(full, output[...]).astype(LOW)
        attended_out[:, :width] = mm_nt(pulled, table[...]).astype(LOW)
        attended_out[:, width:] = jnp.zeros((rows, WIDE - width), LOW)

        def row(value):
            return jnp.sum(value, axis=0, keepdims=True)

        sums_out[0:1] = row(grad_second * unit)
        sums_out[1:2] = row(grad_second)
        sums_out[2:3] = row(branch.astype(F32))
        sums_out[3:4] = row(upstream)
        sums_out[4:8] = jnp.zeros((4, width), F32)


def feed_back(top, slope, middle, gain, table, page, expand, reduce):
    rows, width = top.shape
    inner = expand.shape[1]
    tile = 256
    steps = inner // tile
    flat = whole((rows, width))
    wide = whole((rows, WIDE))
    column = pl.BlockSpec((rows, tile), lambda i: (0, i))
    return pl.pallas_call(
        partial(feed_back_kernel, steps, width),
        grid=(steps,),
        in_specs=[flat, column, flat, whole((1, width)), whole(table.shape),
                  pl.BlockSpec(memory_space=pl.ANY),
                  pl.BlockSpec((WIDE, tile), lambda i: (0, i)),
                  pl.BlockSpec((tile, width), lambda i: (i, 0))],
        out_specs=(column, pl.BlockSpec((1, tile), lambda i: (0, i)), flat, flat, wide, whole((8, width))),
        out_shape=(
            jax.ShapeDtypeStruct((rows, inner), LOW),
            jax.ShapeDtypeStruct((1, inner), F32),
            jax.ShapeDtypeStruct((rows, width), F32),
            jax.ShapeDtypeStruct((rows, width), LOW),
            jax.ShapeDtypeStruct((rows, WIDE), LOW),
            jax.ShapeDtypeStruct((8, width), F32),
        ),
        scratch_shapes=[pltpu.VMEM((rows, WIDE), F32), pltpu.VMEM((WIDE, WIDE), LOW), pltpu.SemaphoreType.DMA(())],
        compiler_params=pltpu.CompilerParams(vmem_limit_bytes=48 << 20),
        name="feed_back",
    )(top, slope, middle, gain, table, page, expand, reduce)


def project_back_kernel(steps, width, query, pair, branch, x, middle, gain, table, page,
                        mixture_out, result_out, sums_out, mixture, normed):
    step = pl.program_id(0)
    tile = page.shape[1]
    rows = x.shape[0]

    @pl.when(step == 0)
    def _():
        mixture[:, :width] = query[:, :width].astype(F32)
        mixture[:, width : 2 * width] = pair[0, :, :width].astype(F32)
        mixture[:, 2 * width : 3 * width] = pair[1, :, :width].astype(F32)
        mixture[:, 3 * width :] = jnp.zeros((rows, width), F32)
        normed[...] = jnp.zeros_like(normed)

    part = mixture[:, pl.ds(pl.multiple_of(step * tile, tile), tile)].astype(LOW)
    normed[...] += mm_nt(part, page[...])

    @pl.when(step == steps - 1)
    def _():
        grad_normed = close_up(normed[...], table[...])
        unit, inverse = normal_parts(x[...].astype(F32))
        result_out[...] = (middle[...] + normal_back(grad_normed * gain[...], unit, inverse)).astype(LOW)

        def row(value):
            return jnp.sum(value, axis=0, keepdims=True)

        sums_out[0:1] = row(grad_normed * unit)
        sums_out[1:2] = row(grad_normed)
        sums_out[2:3] = row(query[:, :width].astype(F32))
        sums_out[3:4] = row(pair[1, :, :width].astype(F32))
        sums_out[4:8] = jnp.zeros((4, width), F32)
        mixture[:, 3 * width :] = branch[...].astype(F32)
        mixture_out[...] = mixture[...].astype(LOW)


def project_back(query, pair, branch, x, middle, gain, table, page):
    rows, width = x.shape
    tile, steps = 640, 6
    flat = whole((rows, width))
    return pl.pallas_call(
        partial(project_back_kernel, steps, width),
        grid=(steps,),
        in_specs=[whole((rows, WIDE)), whole((2, rows, WIDE)), flat, flat, flat, whole((1, width)),
                  whole(table.shape), pl.BlockSpec((WIDE, tile), lambda i: (0, i))],
        out_specs=(whole((rows, 4 * width)), flat, whole((8, width))),
        out_shape=(
            jax.ShapeDtypeStruct((rows, 4 * width), LOW),
            jax.ShapeDtypeStruct((rows, width), LOW),
            jax.ShapeDtypeStruct((8, width), F32),
        ),
        scratch_shapes=[pltpu.VMEM((rows, 4 * width), F32), pltpu.VMEM((rows, WIDE), F32)],
        compiler_params=pltpu.CompilerParams(vmem_limit_bytes=48 << 20),
        name="project_back",
    )(query, pair, branch, x, middle, gain, table, page)


def page_kernel(width, normed, attended, mixture, small, out, left_one, left_two):
    step = pl.program_id(0)
    tile = mixture.shape[1]
    edge = 3 * width

    @pl.when(step == 0)
    def _():
        left_one[...] = normed[...].T
        left_two[...] = attended[...].T

    def put(value):
        value = value.reshape(16, 72, tile)
        row = lax.broadcasted_iota(jnp.int32, value.shape, 1)
        out[...] = jnp.where(row == 68, small[...], value).astype(LOW)

    @pl.when((step + 1) * tile <= edge)
    def _():
        put(mm(left_one[...], mixture[...]))

    @pl.when(step * tile >= edge)
    def _():
        put(mm(left_two[...], mixture[...]))

    @pl.when(((step + 1) * tile > edge) & (step * tile < edge))
    def _():
        column = step * tile + lax.broadcasted_iota(jnp.int32, mixture.shape, 1)
        value = mixture[...]
        zero = jnp.zeros_like(value)
        put(mm(left_one[...], jnp.where(column < edge, value, zero))
            + mm(left_two[...], jnp.where(column < edge, zero, value)))


def attention_page(normed, attended, mixture, small):
    rows, total = mixture.shape
    tile = 256
    return pl.pallas_call(
        partial(page_kernel, total // 4),
        grid=(total // tile,),
        in_specs=[whole((rows, WIDE)), whole((rows, WIDE)), pl.BlockSpec((rows, tile), lambda i: (0, i)),
                  pl.BlockSpec((16, 1, tile), lambda i: (0, 0, i))],
        out_specs=pl.BlockSpec((16, 72, tile), lambda i: (0, 0, i)),
        out_shape=jax.ShapeDtypeStruct((16, 72, total), LOW),
        scratch_shapes=[pltpu.VMEM((WIDE, rows), LOW), pltpu.VMEM((WIDE, rows), LOW)],
        compiler_params=pltpu.CompilerParams(vmem_limit_bytes=48 << 20),
        name="attention_page",
    )(normed, attended, mixture, small)


def spread(width):
    row = lax.broadcasted_iota(jnp.int32, (width, 16 * 72), 0)
    column = lax.broadcasted_iota(jnp.int32, (width, 16 * 72), 1)
    same = (row // 68 == column // 72) & (row % 68 == column % 72)
    return same.astype(LOW)


def small_of(page):
    part = page[:, 68, : 12 * 68].astype(F32).reshape(16, 12, 68)
    vectors = [part[:, row].reshape(1, -1) for row in range(8)]
    return vectors, part[:, 8:].reshape(1, -1)


def layer_forward(source, small, wide, weights, low_chunk, table):
    page, expand, reduce = weights
    first_gain, first_shift, query_bias, value_bias, output_bias, reduce_bias, gain, shift = small
    normed, query, here = project_rows(
        source, first_gain, first_shift, query_bias, value_bias, table, page
    )
    away = swapped(here, LINE, 1)
    beside = swapped(here, SECTION, 1)
    corner = swapped(away, SECTION, 1)
    pairs = (here, beside, away, corner)
    attended, logs = attend(query, *pairs, low_chunk)
    attended_low, middle, second, active, slope, result = feed(
        source, attended, gain, shift, output_bias, reduce_bias, table, page, expand, wide, reduce
    )
    saved = (source, normed, query, pairs, attended, logs, attended_low, middle, second, active, slope)
    return result, saved


def layer_gradient(top, saved, small, weights, low_chunk, table):
    source, normed, query, pairs, attended, logs, attended_low, middle, second, active, slope = saved
    page, expand, reduce = weights
    width = top.shape[1]
    grad_hidden, sum_wide, grad_middle, branch, grad_attended, late = feed_back(
        top, slope, middle, small[6], table, page, expand, reduce
    )
    grad_query, near, beside, away, corner = attend_back(
        query, grad_attended, attended, logs, *pairs, low_chunk
    )
    away = (away.astype(F32) + swapped(corner, SECTION, 1).astype(F32)).astype(LOW)
    near = near + swapped(beside, SECTION, 1).astype(F32)
    near = (near + swapped(away, LINE, 1).astype(F32)).astype(LOW)
    mixture, result, early = project_back(
        grad_query, near, branch, source, grad_middle, small[0], table, page
    )
    order = (early[0], early[1], early[2], early[3], late[2], late[3], late[0], late[1])
    packed = jnp.stack([vector.reshape(16, -1) for vector in order], axis=1)
    packed = jnp.concatenate([packed, sum_wide.reshape(16, 4, -1)], axis=1)
    packed = packed.reshape(16, 1, -1).astype(LOW)
    packed = jnp.pad(packed, ((0, 0), (0, 0), (0, 4 * width - packed.shape[2])))
    page_attention = attention_page(normed, attended_low, mixture, packed)
    page_expand = mm_tn(second, grad_hidden).astype(LOW).reshape(16, 72, -1)
    page_reduce = mm_tn(active, top).astype(LOW).reshape(16, -1, width)
    return result, page_attention, page_expand, page_reduce


def four_by_four(
    inputs,
    cotangent,
    first_gain,
    first_shift,
    joint_weight,
    query_bias,
    value_bias,
    output_weight,
    output_bias,
    second_gain,
    second_shift,
    expand_weight,
    expand_bias,
    reduce_weight,
    reduce_bias,
):
    core = lax.axis_index(SECTION)
    line = lax.axis_index(LINE)
    low_chunk = jnp.where(line < 2, line, 3 - line)
    width = HEADS * HDIM
    packed = jnp.concatenate(
        [
            first_gain[0],
            first_shift[0],
            query_bias[0],
            value_bias[0],
            output_bias[0],
            reduce_bias[0],
            second_gain[0],
            second_shift[0],
            expand_bias[0],
        ]
    )
    packed = jnp.pad(packed[None], ((0, 3), (0, 4 * width - packed.shape[0])))
    attention_shard = jnp.concatenate(
        [jnp.concatenate([joint_weight[0], output_weight[0]], axis=1), packed], axis=0
    )
    expand_shard = jnp.pad(expand_weight[0], ((0, 4), (0, 0)))
    other = swapped(jnp.where(core == 0, expand_shard, attention_shard), SECTION, 1)
    lower = jnp.where(core == 0, attention_shard, other)
    upper = jnp.where(core == 0, other, expand_shard)
    rows = to_rows(inputs, core, line)
    top = to_rows(cotangent, core, line)
    lower_pages, reduce_pages, upper_pages = gather_pages((lower, reduce_weight[0], upper))
    table = spread(width)
    layers = []
    for layer, pages in enumerate((lower_pages, upper_pages)):
        small, wide = small_of(pages[0])
        weights = (
            pages[0].reshape(-1, 4 * width),
            pages[1].reshape(-1, 4 * width),
            reduce_pages[layer].reshape(-1, width),
        )
        layers.append((small, wide, weights))
    small, wide, weights = layers[0]
    middle_rows, saved_lower = layer_forward(rows, small, wide, weights, low_chunk, table)
    small, wide, weights = layers[1]
    final_rows, saved_upper = layer_forward(middle_rows, small, wide, weights, low_chunk, table)
    layer_outputs = from_rows(middle_rows, final_rows, core, line)
    upper_grad, upper_attention, upper_expand, upper_reduce = layer_gradient(
        top, saved_upper, small, weights, low_chunk, table
    )
    small, wide, weights = layers[0]
    lower_grad, lower_attention, lower_expand, lower_reduce = layer_gradient(
        upper_grad, saved_lower, small, weights, low_chunk, table
    )
    input_grads = from_rows(lower_grad, upper_grad, core, line)
    lower_sum, reduce_sum, upper_sum = scatter(
        [
            (lower_attention, lower_expand),
            (lower_reduce, upper_reduce),
            (upper_attention, upper_expand),
        ]
    )
    kept = jnp.where(core == 0, lower_sum, upper_sum)
    other = swapped(jnp.where(core == 0, upper_sum, lower_sum), SECTION, 1)
    attention_sum = jnp.where(core == 0, kept, other)
    expand_sum = jnp.where(core == 0, other, kept)
    vectors = attention_sum[68, : 12 * 68].reshape(12, 68)
    return (
        layer_outputs,
        input_grads,
        vectors[0][None],
        vectors[1][None],
        attention_sum[None, :68, : 3 * width],
        vectors[2][None],
        vectors[3][None],
        attention_sum[None, :68, 3 * width :],
        vectors[4][None],
        vectors[6][None],
        vectors[7][None],
        expand_sum[None, :68],
        vectors[8:].reshape(1, -1),
        reduce_sum[None],
        vectors[5][None],
    )


def fits(mesh):
    return dict(mesh.shape) == {SECTION: 2, RING: 4, LINE: 4}


def solution(mesh):
    return jax.shard_map(
        four_by_four if fits(mesh) else body,
        mesh=mesh,
        in_specs=(
            P(RING, LINE, None),
            P(RING, LINE, None),
            P(SECTION, OWNERS),
            P(SECTION, OWNERS),
            P(SECTION, OWNERS, None),
            P(SECTION, OWNERS),
            P(SECTION, OWNERS),
            P(SECTION, OWNERS, None),
            P(SECTION, OWNERS),
            P(SECTION, OWNERS),
            P(SECTION, OWNERS),
            P(SECTION, OWNERS, None),
            P(SECTION, OWNERS),
            P(SECTION, OWNERS, None),
            P(SECTION, OWNERS),
        ),
        out_specs=(
            P(SECTION, RING, LINE, None),
            P(SECTION, RING, LINE, None),
            P(SECTION, OWNERS),
            P(SECTION, OWNERS),
            P(SECTION, OWNERS, None),
            P(SECTION, OWNERS),
            P(SECTION, OWNERS),
            P(SECTION, OWNERS, None),
            P(SECTION, OWNERS),
            P(SECTION, OWNERS),
            P(SECTION, OWNERS),
            P(SECTION, OWNERS, None),
            P(SECTION, OWNERS),
            P(SECTION, OWNERS, None),
            P(SECTION, OWNERS),
        ),
        check_vma=False,
    )
```

```python
from functools import partial

import jax
import jax.numpy as jnp
from jax import lax
from jax.experimental import pallas as pl
from jax.experimental.pallas import tpu as pltpu
from jax.sharding import PartitionSpec as P

HEADS = 17
HDIM = 64
BLK = 256
WIDE = 1152
F32, LOW = jnp.float32, jnp.bfloat16
SECTION, RING, LINE = "section", "dp", "seq"
OWNERS = (RING, LINE)
EAST, NORTH, LEVEL, SIBLING, CORNER, ONCE = range(6)


epsilon = 1e-05
far_below = -1e30


def passed_along(value, axis, steps):
    count = lax.axis_size(axis)
    first, last = (max(0, -steps), min(count, count - steps))
    return lax.ppermute(value, axis, [(source, source + steps) for source in range(first, last)])


def normalize(values, scales, offsets):
    centre = jnp.mean(values, axis=-1, keepdims=True)
    centred = values - centre
    inverse = lax.rsqrt(jnp.mean(centred * centred, axis=-1, keepdims=True) + epsilon)
    unit_rows = centred * inverse
    return (unit_rows * scales + offsets, unit_rows, inverse)


def normalize_back(upstream, unit_rows, inverse):
    return inverse * (
        upstream
        - jnp.mean(upstream, axis=-1, keepdims=True)
        - unit_rows * jnp.mean(upstream * unit_rows, axis=-1, keepdims=True)
    )


def score_block(query, key_block, block_index, row_block):
    scores = jnp.einsum(
        "qhd,khd->qhk", query, key_block, preferred_element_type=jnp.float32
    ) * HDIM ** (-0.5)
    highest = jnp.max(scores, axis=-1)
    allowed = (block_index <= row_block)[:, None]
    exponent = jnp.exp(scores - highest[..., None]) * allowed[..., None].astype(jnp.float32)
    levels = jnp.where(allowed, highest, far_below)
    return (exponent, levels)


def attend_forward(query, keys_all, values_all, row_block):
    length = keys_all.shape[0]
    row_count = query.shape[0]
    key_shaped = keys_all.reshape(length, HEADS, HDIM)
    value_shaped = values_all.reshape(length, HEADS, HDIM)
    block_limit = row_block[-1] + 1

    def advance(block_index, carried):
        running_peak, running_sum, weighted = carried
        key_block = lax.dynamic_slice_in_dim(key_shaped, block_index * BLK, BLK, 0)
        value_block = lax.dynamic_slice_in_dim(value_shaped, block_index * BLK, BLK, 0)
        exponent, levels = score_block(query, key_block, block_index, row_block)
        weights = exponent.astype(jnp.bfloat16)
        block_out = jnp.einsum(
            "qhk,khd->qhd", weights, value_block, preferred_element_type=jnp.float32
        )
        newest_peak = jnp.maximum(running_peak, levels)
        shrink_old = jnp.exp(running_peak - newest_peak)
        shrink_new = jnp.exp(levels - newest_peak)
        running_sum = running_sum * shrink_old + shrink_new * jnp.sum(exponent, axis=-1)
        weighted = weighted * shrink_old[..., None] + shrink_new[..., None] * block_out
        return (newest_peak, running_sum, weighted)

    initial = (
        jnp.full((row_count, HEADS), far_below, jnp.float32),
        jnp.zeros((row_count, HEADS), jnp.float32),
        jnp.zeros((row_count, HEADS, HDIM), jnp.float32),
    )
    running_peak, running_sum, weighted = lax.fori_loop(0, block_limit, advance, initial)
    return (weighted / running_sum[..., None], running_peak + jnp.log(running_sum))


def attend_backward(query, keys_all, values_all, row_block, attended, log_total, grad_attended):
    length = keys_all.shape[0]
    key_shaped = keys_all.reshape(length, HEADS, HDIM)
    value_shaped = values_all.reshape(length, HEADS, HDIM)
    block_limit = row_block[-1] + 1
    delta = jnp.sum(grad_attended * attended, axis=-1)

    def advance(block_index, carried):
        grad_query, grad_keys, grad_values = carried
        key_block = lax.dynamic_slice_in_dim(key_shaped, block_index * BLK, BLK, 0)
        value_block = lax.dynamic_slice_in_dim(value_shaped, block_index * BLK, BLK, 0)
        exponent, levels = score_block(query, key_block, block_index, row_block)
        weights = exponent.astype(jnp.bfloat16)
        factor = jnp.exp(levels - log_total)
        scaled = (factor[..., None] * grad_attended).astype(jnp.bfloat16)
        grad_weights = jnp.einsum(
            "qhd,khd->qhk", scaled, value_block, preferred_element_type=jnp.float32
        )
        grad_scores = (exponent * (grad_weights - (factor * delta)[..., None])).astype(jnp.bfloat16)
        grad_query = grad_query + jnp.einsum(
            "qhk,khd->qhd", grad_scores, key_block, preferred_element_type=jnp.float32
        )
        grad_key = jnp.einsum(
            "qhk,qhd->khd", grad_scores, query, preferred_element_type=jnp.float32
        )
        grad_value = jnp.einsum("qhk,qhd->khd", weights, scaled, preferred_element_type=jnp.float32)
        grad_keys = lax.dynamic_update_slice_in_dim(grad_keys, grad_key, block_index * BLK, 0)
        grad_values = lax.dynamic_update_slice_in_dim(grad_values, grad_value, block_index * BLK, 0)
        return (grad_query, grad_keys, grad_values)

    initial = (
        jnp.zeros(query.shape, jnp.float32),
        jnp.zeros((length, HEADS, HDIM), jnp.float32),
        jnp.zeros((length, HEADS, HDIM), jnp.float32),
    )
    grad_query, grad_keys, grad_values = lax.fori_loop(0, block_limit, advance, initial)
    return (
        grad_query,
        grad_keys.reshape(length, HEADS * HDIM),
        grad_values.reshape(length, HEADS * HDIM),
    )


def project(source, params):
    feature_width = HEADS * HDIM
    normed, unit_rows, inverse = normalize(
        source, params[0].astype(jnp.float32), params[1].astype(jnp.float32)
    )
    normed_low = normed.astype(jnp.bfloat16)
    mixture = jnp.dot(normed_low, params[2], preferred_element_type=jnp.float32)
    query_low = (mixture[:, :feature_width] + params[3].astype(jnp.float32)).astype(jnp.bfloat16)
    keys_low = mixture[:, feature_width : 2 * feature_width].astype(jnp.bfloat16)
    values_low = (mixture[:, 2 * feature_width :] + params[4].astype(jnp.float32)).astype(
        jnp.bfloat16
    )
    return (unit_rows, inverse, normed_low, query_low, keys_low, values_low)


def complete(source, params, projected, gathered, row_block):
    row_count = source.shape[0]
    query = projected[3].reshape(row_count, HEADS, HDIM)
    attended, log_total = attend_forward(query, gathered[0], gathered[1], row_block)
    attended_low = attended.reshape(row_count, HEADS * HDIM).astype(jnp.bfloat16)
    middle = source + (
        jnp.dot(attended_low, params[5], preferred_element_type=jnp.float32)
        + params[6].astype(jnp.float32)
    )
    second, unit_second, inverse_second = normalize(
        middle, params[7].astype(jnp.float32), params[8].astype(jnp.float32)
    )
    second_low = second.astype(jnp.bfloat16)
    hidden = jnp.dot(second_low, params[9], preferred_element_type=jnp.float32) + params[10].astype(
        jnp.float32
    )
    active, gelu_pull = jax.vjp(partial(jax.nn.gelu, approximate=False), hidden)
    active_low = active.astype(jnp.bfloat16)
    result = middle + (
        jnp.dot(active_low, params[11], preferred_element_type=jnp.float32)
        + params[12].astype(jnp.float32)
    )
    saved = (
        query,
        attended,
        log_total,
        attended_low,
        unit_second,
        inverse_second,
        second_low,
        gelu_pull,
        active_low,
    )
    return (result, saved)


def layer_backward(source, upstream, params, projected, gathered, row_block):
    unit_first, inverse_first, normed_low, query_low, keys_low, values_low = projected
    row_count = source.shape[0]
    feature_width = HEADS * HDIM
    result, saved = complete(source, params, projected, gathered, row_block)
    (
        query,
        attended,
        log_total,
        attended_low,
        unit_second,
        inverse_second,
        second_low,
        gelu_pull,
        active_low,
    ) = saved
    top_low = upstream.astype(jnp.bfloat16)
    grad_reduce_bias = jnp.sum(top_low.astype(jnp.float32), axis=0)
    grad_reduce_weight = jnp.einsum(
        "tf,td->fd", active_low, top_low, preferred_element_type=jnp.float32
    )
    grad_active = jnp.einsum("td,fd->tf", top_low, params[11], preferred_element_type=jnp.float32)
    grad_hidden_low = gelu_pull(grad_active)[0].astype(jnp.bfloat16)
    grad_expand_bias = jnp.sum(grad_hidden_low.astype(jnp.float32), axis=0)
    grad_expand_weight = jnp.einsum(
        "td,tf->df", second_low, grad_hidden_low, preferred_element_type=jnp.float32
    )
    grad_second = jnp.einsum(
        "tf,df->td", grad_hidden_low, params[9], preferred_element_type=jnp.float32
    )
    grad_second_gain = jnp.sum(grad_second * unit_second, axis=0)
    grad_second_shift = jnp.sum(grad_second, axis=0)
    grad_middle = upstream + normalize_back(
        grad_second * params[7].astype(jnp.float32), unit_second, inverse_second
    )
    branch_low = grad_middle.astype(jnp.bfloat16)
    grad_output_bias = jnp.sum(branch_low.astype(jnp.float32), axis=0)
    grad_output_weight = jnp.einsum(
        "td,te->de", attended_low, branch_low, preferred_element_type=jnp.float32
    )
    grad_attended = jnp.einsum(
        "te,de->td", branch_low, params[5], preferred_element_type=jnp.float32
    )
    grad_query, grad_keys_full, grad_values_full = attend_backward(
        query,
        gathered[0],
        gathered[1],
        row_block,
        attended,
        log_total,
        grad_attended.reshape(row_count, HEADS, HDIM),
    )
    grad_keys, grad_values = (
        lax.psum_scatter(grad_keys_full, LINE, scatter_dimension=0, tiled=True),
        lax.psum_scatter(grad_values_full, LINE, scatter_dimension=0, tiled=True),
    )
    scale_factor = HDIM ** (-0.5)
    grad_mixture = jnp.concatenate(
        [
            grad_query.reshape(row_count, feature_width) * scale_factor,
            grad_keys * scale_factor,
            grad_values,
        ],
        axis=1,
    ).astype(jnp.bfloat16)
    grad_query_bias = jnp.sum(grad_mixture[:, :feature_width].astype(jnp.float32), axis=0)
    grad_value_bias = jnp.sum(grad_mixture[:, 2 * feature_width :].astype(jnp.float32), axis=0)
    grad_joint_weight = jnp.einsum(
        "td,te->de", normed_low, grad_mixture, preferred_element_type=jnp.float32
    )
    grad_normed = jnp.einsum(
        "te,de->td", grad_mixture, params[2], preferred_element_type=jnp.float32
    )
    grad_first_gain = jnp.sum(grad_normed * unit_first, axis=0)
    grad_first_shift = jnp.sum(grad_normed, axis=0)
    grad_source = grad_middle + normalize_back(
        grad_normed * params[0].astype(jnp.float32), unit_first, inverse_first
    )
    grads = (
        grad_first_gain,
        grad_first_shift,
        grad_joint_weight,
        grad_query_bias,
        grad_value_bias,
        grad_output_weight,
        grad_output_bias,
        grad_second_gain,
        grad_second_shift,
        grad_expand_weight,
        grad_expand_bias,
        grad_reduce_weight,
        grad_reduce_bias,
    )
    return (grad_source.astype(jnp.bfloat16), grads)


def body(
    inputs,
    cotangent,
    first_gain,
    first_shift,
    joint_weight,
    query_bias,
    value_bias,
    output_weight,
    output_bias,
    second_gain,
    second_shift,
    expand_weight,
    expand_bias,
    reduce_weight,
    reduce_bias,
):
    section_index = lax.axis_index(SECTION)
    micro_count = inputs.shape[0]
    row_count = inputs.shape[1]
    first_row = lax.axis_index(LINE) * row_count
    row_block = (first_row + jnp.arange(row_count, dtype=jnp.int32)) // BLK
    owned = (
        first_gain[0],
        first_shift[0],
        joint_weight[0],
        query_bias[0],
        value_bias[0],
        output_weight[0],
        output_bias[0],
        second_gain[0],
        second_shift[0],
        expand_weight[0],
        expand_bias[0],
        reduce_weight[0],
        reduce_bias[0],
    )
    forward_params = (
        lax.all_gather(first_gain[0], OWNERS, axis=0, tiled=True),
        lax.all_gather(first_shift[0], OWNERS, axis=0, tiled=True),
        lax.all_gather(joint_weight[0], OWNERS, axis=0, tiled=True),
        lax.all_gather(query_bias[0], OWNERS, axis=0, tiled=True),
        lax.all_gather(value_bias[0], OWNERS, axis=0, tiled=True),
        lax.all_gather(output_weight[0], OWNERS, axis=0, tiled=True),
        lax.all_gather(output_bias[0], OWNERS, axis=0, tiled=True),
        lax.all_gather(second_gain[0], OWNERS, axis=0, tiled=True),
        lax.all_gather(second_shift[0], OWNERS, axis=0, tiled=True),
        lax.all_gather(expand_weight[0], OWNERS, axis=0, tiled=True),
        lax.all_gather(expand_bias[0], OWNERS, axis=0, tiled=True),
        lax.all_gather(reduce_weight[0], OWNERS, axis=0, tiled=True),
        lax.all_gather(reduce_bias[0], OWNERS, axis=0, tiled=True),
    )
    incoming = jnp.zeros(inputs.shape[1:], jnp.bfloat16)
    section_inputs = []
    produced = []
    key_sets = []
    for tick_index in range(micro_count + 1):
        section_input = jnp.where(
            section_index == 0, inputs[min(tick_index, micro_count - 1)], incoming
        )
        source = section_input.astype(jnp.float32)
        projected = project(source, forward_params)
        gathered = (
            lax.all_gather(projected[4], LINE, axis=0, tiled=True),
            lax.all_gather(projected[5], LINE, axis=0, tiled=True),
        )
        result, unused = complete(source, forward_params, projected, gathered, row_block)
        result_low = result.astype(jnp.bfloat16)
        section_inputs.append(section_input)
        produced.append(result_low)
        key_sets.append(gathered)
        if tick_index < micro_count:
            incoming = passed_along(result_low, SECTION, 1)
    backward_params = (
        lax.all_gather(first_gain[0], OWNERS, axis=0, tiled=True),
        lax.all_gather(first_shift[0], OWNERS, axis=0, tiled=True),
        lax.all_gather(joint_weight[0], OWNERS, axis=0, tiled=True),
        lax.all_gather(query_bias[0], OWNERS, axis=0, tiled=True),
        lax.all_gather(value_bias[0], OWNERS, axis=0, tiled=True),
        lax.all_gather(output_weight[0], OWNERS, axis=0, tiled=True),
        lax.all_gather(output_bias[0], OWNERS, axis=0, tiled=True),
        lax.all_gather(second_gain[0], OWNERS, axis=0, tiled=True),
        lax.all_gather(second_shift[0], OWNERS, axis=0, tiled=True),
        lax.all_gather(expand_weight[0], OWNERS, axis=0, tiled=True),
        lax.all_gather(expand_bias[0], OWNERS, axis=0, tiled=True),
        lax.all_gather(reduce_weight[0], OWNERS, axis=0, tiled=True),
        lax.all_gather(reduce_bias[0], OWNERS, axis=0, tiled=True),
    )
    totals = tuple((jnp.zeros(piece.shape, jnp.float32) for piece in backward_params))
    shares = tuple((jnp.zeros(piece.shape, jnp.float32) for piece in owned))
    returning = jnp.zeros(inputs.shape[1:], jnp.bfloat16)
    sent_back = []
    for tick_index in range(micro_count + 1):
        upper_pick = min(tick_index + 1, micro_count)
        lower_pick = max(tick_index - 1, 0)
        section_input = jnp.where(
            section_index == 1, section_inputs[upper_pick], section_inputs[lower_pick]
        )
        upstream = jnp.where(
            section_index == 1, cotangent[min(tick_index, micro_count - 1)], returning
        ).astype(jnp.float32)
        weight_valid = jnp.where(
            section_index == 1,
            1.0 if tick_index < micro_count else 0.0,
            1.0 if tick_index >= 1 else 0.0,
        ).astype(jnp.float32)
        source = section_input.astype(jnp.float32)
        projected = project(source, backward_params)
        gathered = (
            lax.all_gather(projected[4], LINE, axis=0, tiled=True),
            lax.all_gather(projected[5], LINE, axis=0, tiled=True),
        )
        grad_source, grads = layer_backward(
            source, upstream, backward_params, projected, gathered, row_block
        )
        masked = tuple((update * weight_valid for update in grads))
        totals = tuple((running + update for running, update in zip(totals, masked)))
        sent_back.append(grad_source)
        if tick_index < micro_count:
            returning = passed_along(grad_source, SECTION, -1)
    layer_outputs = jnp.stack(
        [
            jnp.where(section_index == 0, produced[position], produced[position + 1])
            for position in range(micro_count)
        ]
    )[None]
    input_grads = jnp.stack(
        [
            jnp.where(section_index == 1, sent_back[position], sent_back[position + 1])
            for position in range(micro_count)
        ]
    )[None]
    (
        sum_first_gain,
        sum_first_shift,
        sum_joint_weight,
        sum_query_bias,
        sum_value_bias,
        sum_output_weight,
        sum_output_bias,
        sum_second_gain,
        sum_second_shift,
        sum_expand_weight,
        sum_expand_bias,
        sum_reduce_weight,
        sum_reduce_bias,
    ) = totals
    shares = (
        lax.psum_scatter(sum_first_gain, OWNERS, scatter_dimension=0, tiled=True),
        lax.psum_scatter(sum_first_shift, OWNERS, scatter_dimension=0, tiled=True),
        lax.psum_scatter(sum_joint_weight, OWNERS, scatter_dimension=0, tiled=True),
        lax.psum_scatter(sum_query_bias, OWNERS, scatter_dimension=0, tiled=True),
        lax.psum_scatter(sum_value_bias, OWNERS, scatter_dimension=0, tiled=True),
        lax.psum_scatter(sum_output_weight, OWNERS, scatter_dimension=0, tiled=True),
        lax.psum_scatter(sum_output_bias, OWNERS, scatter_dimension=0, tiled=True),
        lax.psum_scatter(sum_second_gain, OWNERS, scatter_dimension=0, tiled=True),
        lax.psum_scatter(sum_second_shift, OWNERS, scatter_dimension=0, tiled=True),
        lax.psum_scatter(sum_expand_weight, OWNERS, scatter_dimension=0, tiled=True),
        lax.psum_scatter(sum_expand_bias, OWNERS, scatter_dimension=0, tiled=True),
        lax.psum_scatter(sum_reduce_weight, OWNERS, scatter_dimension=0, tiled=True),
        lax.psum_scatter(sum_reduce_bias, OWNERS, scatter_dimension=0, tiled=True),
    )
    return (layer_outputs, input_grads) + tuple((portion[None] for portion in shares))


def swapped(value, axis, bits):
    count = lax.axis_size(axis)
    return lax.ppermute(value, axis, [(source, source ^ bits) for source in range(count)])


def to_rows(array, core, line):
    half = array.shape[1] // 2
    which = line // 2

    def part(index):
        return lax.dynamic_slice(
            array, (index, core * half, 0), (1, half, array.shape[2])
        )[0]

    mine, arrived = part(which), swapped(part(1 - which), LINE, 3)
    low_side = which == 0
    return jnp.concatenate(
        [jnp.where(low_side, mine, arrived), jnp.where(low_side, arrived, mine)], axis=0
    )


def from_rows(lower, upper, core, line):
    half = lower.shape[0] // 2
    low_side = line // 2 == 0
    both = jnp.stack([lower, upper])
    mine = jnp.where(low_side, both[:, :half], both[:, half:])
    arrived = swapped(jnp.where(low_side, both[:, half:], both[:, :half]), LINE, 3)
    pair = jnp.stack(
        [jnp.where(low_side, mine, arrived), jnp.where(low_side, arrived, mine)], axis=1
    )
    kept = jnp.where(core == 0, pair[0], pair[1])
    other = swapped(jnp.where(core == 0, pair[1], pair[0]), SECTION, 1)
    return jnp.concatenate(
        [jnp.where(core == 0, kept, other), jnp.where(core == 0, other, kept)], axis=1
    )[None]


def flip(place, bits):
    return {1: place + 1 - 2 * (place % 2), 2: (place + 2) % 4, 3: 3 - place}[bits]


def places():
    core, ring, line = (lax.axis_index(name) for name in (SECTION, RING, LINE))
    rings = [ring] + [flip(ring, bits) for bits in (1, 2, 3)]
    lines = [line] + [flip(line, bits) for bits in (1, 2, 3)]
    toward = {
        EAST: {RING: rings[1]},
        NORTH: {RING: rings[2]},
        (LEVEL, 1): {LINE: lines[1]},
        (LEVEL, 2): {LINE: lines[2]},
        (LEVEL, 3): {LINE: lines[3]},
        SIBLING: {SECTION: 1 - core},
    }
    return core, rings, lines, toward


def greet(toward):
    barrier = pltpu.get_barrier_semaphore()
    for to in toward.values():
        pl.semaphore_signal(barrier, inc=1, device_id=to, device_id_type=pl.DeviceIdType.MESH)
    pl.semaphore_wait(barrier, len(toward))


def remote_copy(source, target, send_sem, recv_sem, to):
    return pltpu.make_async_remote_copy(
        src_ref=source,
        dst_ref=target,
        send_sem=send_sem,
        recv_sem=recv_sem,
        device_id=to,
        device_id_type=pl.DeviceIdType.MESH,
    )


def per_core(core, act):
    for index in (0, 1):

        @pl.when(core == index)
        def _():
            act(index)


GATHER_KINDS = (
    [(LEVEL, k) for k in (1, 2, 3)]
    + [(name, k) for name in (EAST, NORTH, CORNER) for k in range(4)]
    + [(SIBLING, k) for k in range(4)]
)
GATHER_NUMBER = {kind: index for index, kind in enumerate(GATHER_KINDS)}


KINDS = (
    [(CORNER, dd) for dd in range(4)]
    + [(ONCE, k) for k in range(4)]
    + [(EAST, k) for k in range(4)]
    + [(NORTH, k) for k in range(4)]
    + [(LEVEL, k) for k in (1, 2, 3)]
)
NUMBER = {kind: i for i, kind in enumerate(KINDS)}
DEPTH = 8

def scatter_kernel(slots, *refs):
    n = len(slots)
    pages = [(refs[2 * t], refs[2 * t + 1]) for t in range(n)]
    refs = refs[2 * n :]
    finals, refs = refs[:n], refs[n:]
    lands, refs = [refs[5 * t : 5 * t + 5] for t in range(n)], refs[5 * n :]
    shapes = sorted(set(slots))
    work = {}
    for i, shape in enumerate(shapes):
        work[shape] = refs[3 * i : 3 * i + 3]
    refs = refs[3 * len(shapes) :]
    send_sem, recv_sem, load_sem, out_sem = refs
    core, rings, lines, toward = places()
    greet(toward)

    def remote(t, src, dst, to, kind):
        i = t * len(KINDS) + NUMBER[kind]
        return pltpu.make_async_remote_copy(
            src_ref=src, dst_ref=dst, send_sem=send_sem.at[i], recv_sem=recv_sem.at[i],
            device_id=toward[to], device_id_type=pl.DeviceIdType.MESH)

    def by_core(make):
        def start(pair):
            for index in (0, 1):
                @pl.when(core == index)
                def _():
                    make(pair[index]).start()
        return start

    pending = []

    def give(t, dd):
        dst = lands[t][0].at[pl.ds(rings[dd] * 4, 4)]
        pair = (pages[t][1], pages[t][0])
        by_core(lambda ref: remote(t, ref.at[pl.ds(rings[dd] * 4, 4)], dst, SIBLING, (CORNER, dd)))(pair)
        pending.append(remote(t, dst, dst, SIBLING, (CORNER, dd)))

    def arrived(t, ref, to, kind):
        remote(t, ref, ref, to, kind).wait_recv()

    task = [0]
    used = {shape: [None] * DEPTH for shape in shapes}
    count = {shape: 0 for shape in shapes}

    def total_of(t, dd, k, extra):
        shape = slots[t]
        loads = work[shape][0]
        slot = task[0] % 2
        task[0] += 1
        index = rings[dd] * 4 + lines[k]
        buf = lambda j: loads.at[slot, j]
        sem = lambda j: load_sem.at[slot * 4 + j]
        by_core(lambda ref: pltpu.make_async_copy(ref.at[index], buf(0), sem(0)))(pages[t])
        copies = [pltpu.make_async_copy(buf(0), buf(0), sem(0))]
        sources = [lands[t][0].at[index]] + extra
        for j, source in enumerate(sources):
            copy = pltpu.make_async_copy(source, buf(j + 1), sem(j + 1))
            copy.start()
            copies.append(copy)
        for copy in copies:
            copy.wait()
        return loads, slot, len(copies)

    def add_up(shape, loads, slot, terms, store):
        rows, columns = shape
        if rows == 72:
            def step(i, _):
                at = pl.ds(pl.multiple_of(i * 256, 256), 256)
                value = loads[slot, 0, :, at].astype(jnp.float32)
                for j in range(1, terms):
                    value = value + loads[slot, j, :, at].astype(jnp.float32)
                store((slice(None), at), value)
                return 0
            lax.fori_loop(0, columns // 256, step, 0)
        else:
            def step(i, _):
                at = pl.ds(pl.multiple_of(i * 16, 16), 16)
                value = loads[slot, 0, at, :].astype(jnp.float32)
                for j in range(1, terms):
                    value = value + loads[slot, j, at, :].astype(jnp.float32)
                store((at, slice(None)), value)
                return 0
            lax.fori_loop(0, rows // 16, step, 0)

    def sum_and_send(t, dd, k, extra, dst, to, kind):
        shape = slots[t]
        loads, slot, terms = total_of(t, dd, k, extra)
        place = count[shape] % DEPTH
        count[shape] += 1
        if used[shape][place] is not None:
            used[shape][place].wait_send()
        out = work[shape][1]
        def store(at, value):
            out[(place,) + at] = value.astype(jnp.bfloat16)
        add_up(shape, loads, slot, terms, store)
        copy = remote(t, out.at[place], dst, to, kind)
        copy.start()
        used[shape][place] = copy

    def first(t):
        one = lands[t][1]
        arrived(t, lands[t][0].at[pl.ds(rings[3] * 4, 4)], SIBLING, (CORNER, 3))
        for k in (0, 2, 1, 3):
            to = EAST if k < 2 else NORTH
            sum_and_send(t, 3, k, [], one.at[k], to, (ONCE, k))

    def second(t):
        one, land_x, land_y = lands[t][1:4]
        arrived(t, lands[t][0].at[pl.ds(rings[1] * 4, 4)], SIBLING, (CORNER, 1))
        arrived(t, lands[t][0].at[pl.ds(rings[2] * 4, 4)], SIBLING, (CORNER, 2))
        order = ((1, 0), (2, 3), (1, 1), (2, 2), (1, 3), (2, 0), (1, 2), (2, 1))
        for dd, k in order:
            to, land = (EAST, land_x) if dd == 1 else (NORTH, land_y)
            extra = []
            if (dd == 1) == (k >= 2):
                arrived(t, one.at[k], NORTH if k >= 2 else EAST, (ONCE, k))
                extra = [one.at[k]]
            sum_and_send(t, dd, k, extra, land.at[k], to, (to, k))

    held = {}

    def third(t):
        land_x, land_y, land_z = lands[t][2:5]
        arrived(t, lands[t][0].at[pl.ds(rings[0] * 4, 4)], SIBLING, (CORNER, 0))
        for k in (3, 2, 1, 0):
            arrived(t, land_x.at[k], EAST, (EAST, k))
            arrived(t, land_y.at[k], NORTH, (NORTH, k))
            extra = [land_x.at[k], land_y.at[k]]
            if k:
                sum_and_send(t, 0, k, extra, land_z.at[k], (LEVEL, k), (LEVEL, k))
            else:
                shape = slots[t]
                loads, slot, terms = total_of(t, 0, 0, extra)
                total = work[shape][2]
                def store(at, value):
                    total[at] = value
                add_up(shape, loads, slot, terms, store)

    def last(t):
        shape = slots[t]
        land_z = lands[t][4]
        loads, _, total = work[shape]
        slot = task[0] % 2
        task[0] += 1
        copies = []
        for k in (1, 2, 3):
            arrived(t, land_z.at[k], (LEVEL, k), (LEVEL, k))
            copy = pltpu.make_async_copy(land_z.at[k], loads.at[slot, k - 1], load_sem.at[slot * 4 + k - 1])
            copy.start()
            copies.append(copy)
        for copy in copies:
            copy.wait()
        def store(at, value):
            total[at] = total[at] + value
        add_up(shape, loads, slot, 3, store)
        copy = pltpu.make_async_copy(total, finals[t], out_sem)
        copy.start()
        copy.wait()

    for dd in (3, 1, 2, 0):
        give(0, dd)
    for t in range(n + 1):
        if t < n:
            first(t)
            if t + 1 < n:
                for dd in (3, 1, 2, 0):
                    give(t + 1, dd)
        if t > 0:
            third(t - 1)
        if t < n:
            second(t)
        if t > 0:
            last(t - 1)
    for copy in pending:
        copy.wait_send()
    for shape in shapes:
        for copy in used[shape]:
            if copy is not None:
                copy.wait_send()

def scatter(pairs, name="scatter_gradients", collective=1):
    slots = [tuple(a.shape[1:]) for a, _ in pairs]
    n = len(slots)
    shapes = sorted(set(slots))
    out = [jax.ShapeDtypeStruct(s, jnp.float32) for s in slots]
    for s in slots:
        out += [jax.ShapeDtypeStruct((m,) + s, jnp.bfloat16) for m in (16, 4, 4, 4, 4)]
    scratch = []
    for s in shapes:
        scratch += [pltpu.VMEM((2, 4) + s, jnp.bfloat16), pltpu.VMEM((DEPTH,) + s, jnp.bfloat16), pltpu.VMEM(s, jnp.float32)]
    m = n * len(KINDS)
    scratch += [pltpu.SemaphoreType.DMA((m,)), pltpu.SemaphoreType.DMA((m,)), pltpu.SemaphoreType.DMA((8,)), pltpu.SemaphoreType.DMA(())]
    res = pl.pallas_call(
        partial(scatter_kernel, slots),
        out_shape=tuple(out),
        in_specs=[pl.BlockSpec(memory_space=pl.ANY)] * (2 * n),
        out_specs=tuple(pl.BlockSpec(memory_space=pl.ANY) for _ in out),
        scratch_shapes=scratch,
        compiler_params=pltpu.CompilerParams(collective_id=collective, has_side_effects=True, vmem_limit_bytes=48 << 20),
        name=name,
    )(*[x for pair in pairs for x in pair])
    return res[:n]


def mm(left, right):
    return jnp.dot(left, right, preferred_element_type=F32)


def mm_nt(left, right):
    return lax.dot_general(left, right, (((1,), (1,)), ((), ())), preferred_element_type=F32)


def mm_tn(left, right):
    return lax.dot_general(left, right, (((0,), (0,)), ((), ())), preferred_element_type=F32)


def normal_parts(values):
    centre = jnp.mean(values, axis=-1, keepdims=True)
    centred = values - centre
    inverse = lax.rsqrt(jnp.mean(centred * centred, axis=-1, keepdims=True) + epsilon)
    return centred * inverse, inverse


def normal_back(upstream, unit, inverse):
    return inverse * (
        upstream
        - jnp.mean(upstream, axis=-1, keepdims=True)
        - unit * jnp.mean(upstream * unit, axis=-1, keepdims=True)
    )


def close_up(rows, table):
    high = rows.astype(LOW)
    rest = (rows - high.astype(F32)).astype(LOW)
    return mm_nt(high, table) + mm_nt(rest, table)


def whole(shape):
    zeros = (0,) * len(shape)
    return pl.BlockSpec(shape, lambda *_: zeros)


def head_pair(rows):
    lane = lax.broadcasted_iota(jnp.int32, rows.shape, 1)
    zero = jnp.zeros_like(rows)
    return jnp.concatenate(
        [jnp.where(lane < HDIM, rows, zero), jnp.where(lane < HDIM, zero, rows)], axis=0
    )


def from_pair(turned):
    n = turned.shape[1] // 2
    own = jnp.concatenate([turned[:HDIM, :n], turned[HDIM:, n:]], axis=0)
    return own.T


def attend_back_kernel(query, grad, attended, logs, here, beside, away, corner, first_ref,
                       query_out, here_out, beside_out, away_out, corner_out):
    first = first_ref[0] == 0
    half = query.shape[0] // 2

    def rows_of(place):
        at = slice(place * half, (place + 1) * half)
        rows, grads = head_pair(query[at]), head_pair(grad[at])
        product = (grad[at].astype(F32) * attended[at]).T
        delta = jnp.concatenate(
            [jnp.sum(product[:HDIM], axis=0, keepdims=True), jnp.sum(product[HDIM:], axis=0, keepdims=True)],
            axis=1,
        )
        return rows, grads, logs[0, place : place + 1], delta

    low, high = rows_of(0), rows_of(1)
    last_rows = tuple(jnp.where(first, b, a) for a, b in zip(low, high))

    def block(kind, near, part):
        at = pl.ds(part * half, half)
        one, two = (here, beside) if near == 0 else (away, corner)
        return jnp.concatenate([one[kind, at], two[kind, at]], axis=0)

    def back(rows, keys, values):
        queries, grads, log, delta = rows
        weights = jnp.exp(mm_nt(keys, queries) - log)
        pulled = (weights * (mm_nt(values, grads) - delta)).astype(LOW)
        return (
            mm_tn(keys, pulled),
            mm(pulled, queries),
            mm(weights.astype(LOW), grads),
        )

    def put(near, part, grad_keys, grad_values):
        one, two = (here_out, beside_out) if near == 0 else (away_out, corner_out)
        at = pl.ds(part * half, half)
        for kind, value in ((0, grad_keys), (1, grad_values)):
            one[kind, at] = value[:half].astype(one.dtype)
            two[kind, at] = value[half:].astype(two.dtype)

    keys, values = block(0, 0, 0), block(1, 0, 0)
    low_query, keys_a, values_a = back(low, keys, values)
    high_query, keys_b, values_b = back(high, keys, values)
    put(0, 0, keys_a + keys_b, values_a + values_b)
    more, keys_a, values_a = back(high, block(0, 0, 1), block(1, 0, 1))
    high_query = high_query + more
    put(0, 1, keys_a, values_a)
    more, keys_a, values_a = back(high, block(0, 1, 0), block(1, 1, 0))
    high_query = high_query + more
    keys = jnp.where(first, block(0, 1, 1), block(0, 1, 0))
    values = jnp.where(first, block(1, 1, 1), block(1, 1, 0))
    more, keys_b, values_b = back(last_rows, keys, values)
    zero = jnp.zeros_like(keys_b)
    put(1, 0, keys_a + jnp.where(first, zero, keys_b), values_a + jnp.where(first, zero, values_b))
    put(1, 1, jnp.where(first, keys_b, zero), jnp.where(first, values_b, zero))
    empty = jnp.zeros_like(more)
    low_query = low_query + jnp.where(first, empty, more)
    high_query = high_query + jnp.where(first, more, empty)
    scale_factor = HDIM ** (-0.5)
    query_out[:half] = (from_pair(low_query) * scale_factor).astype(LOW)
    query_out[half:] = (from_pair(high_query) * scale_factor).astype(LOW)


def attend_back(query, grad, attended, logs, here, beside, away, corner, low_chunk):
    rows = query.shape[0]
    pairs = WIDE // 128
    flat = pl.BlockSpec((rows, 128), lambda p: (0, p))
    both = pl.BlockSpec((2, rows, 128), lambda p: (0, 0, p))
    shape = (2, rows, WIDE)
    return pl.pallas_call(
        attend_back_kernel,
        grid=(pairs,),
        in_specs=[flat, flat, flat, pl.BlockSpec((1, 2, rows), lambda p: (p, 0, 0))] + [both] * 4
        + [pl.BlockSpec(memory_space=pltpu.SMEM)],
        out_specs=(flat, both, both, both, both),
        out_shape=(jax.ShapeDtypeStruct((rows, WIDE), LOW), jax.ShapeDtypeStruct(shape, F32))
        + tuple(jax.ShapeDtypeStruct(shape, LOW) for _ in range(3)),
        compiler_params=pltpu.CompilerParams(vmem_limit_bytes=48 << 20),
        name="attend_back",
    )(query, grad, attended, logs, here, beside, away, corner, low_chunk.reshape(1))


def feed_back_kernel(steps, width, top, slope, middle, gain, table, page, expand, reduce,
                     hidden_out, bias_out, middle_out, branch_out, attended_out, sums_out,
                     second, output, sem):
    step = pl.program_id(0)
    lead = 4 * width - WIDE
    extra = 3 * width - lead
    rows = top.shape[0]

    @pl.when(step == 0)
    def _():
        pltpu.make_async_copy(page.at[:, pl.ds(lead, WIDE)], output, sem).start()
        second[...] = jnp.zeros_like(second)

    hidden = (mm_nt(top[...], reduce[...]) * slope[...].astype(F32)).astype(LOW)
    hidden_out[...] = hidden
    bias_out[...] = jnp.sum(hidden.astype(F32), axis=0, keepdims=True)
    second[...] += mm_nt(hidden, expand[...])

    @pl.when(step == steps - 1)
    def _():
        pltpu.make_async_copy(page.at[:, pl.ds(lead, WIDE)], output, sem).wait()
        upstream = top[...].astype(F32)
        grad_second = close_up(second[...], table[...])
        unit, inverse = normal_parts(middle[...])
        grad_middle = upstream + normal_back(grad_second * gain[...], unit, inverse)
        middle_out[...] = grad_middle
        branch = grad_middle.astype(LOW)
        branch_out[...] = branch
        full = jnp.concatenate([jnp.zeros((rows, extra), LOW), branch], axis=1)
        pulled = mm_nt(full, output[...]).astype(LOW)
        attended_out[:, :width] = mm_nt(pulled, table[...]).astype(LOW)
        attended_out[:, width:] = jnp.zeros((rows, WIDE - width), LOW)

        def row(value):
            return jnp.sum(value, axis=0, keepdims=True)

        sums_out[0:1] = row(grad_second * unit)
        sums_out[1:2] = row(grad_second)
        sums_out[2:3] = row(branch.astype(F32))
        sums_out[3:4] = row(upstream)
        sums_out[4:8] = jnp.zeros((4, width), F32)


def feed_back(top, slope, middle, gain, table, page, expand, reduce):
    rows, width = top.shape
    inner = expand.shape[1]
    tile = 256
    steps = inner // tile
    flat = whole((rows, width))
    wide = whole((rows, WIDE))
    column = pl.BlockSpec((rows, tile), lambda i: (0, i))
    return pl.pallas_call(
        partial(feed_back_kernel, steps, width),
        grid=(steps,),
        in_specs=[flat, column, flat, whole((1, width)), whole(table.shape),
                  pl.BlockSpec(memory_space=pl.ANY),
                  pl.BlockSpec((WIDE, tile), lambda i: (0, i)),
                  pl.BlockSpec((tile, width), lambda i: (i, 0))],
        out_specs=(column, pl.BlockSpec((1, tile), lambda i: (0, i)), flat, flat, wide, whole((8, width))),
        out_shape=(
            jax.ShapeDtypeStruct((rows, inner), LOW),
            jax.ShapeDtypeStruct((1, inner), F32),
            jax.ShapeDtypeStruct((rows, width), F32),
            jax.ShapeDtypeStruct((rows, width), LOW),
            jax.ShapeDtypeStruct((rows, WIDE), LOW),
            jax.ShapeDtypeStruct((8, width), F32),
        ),
        scratch_shapes=[pltpu.VMEM((rows, WIDE), F32), pltpu.VMEM((WIDE, WIDE), LOW), pltpu.SemaphoreType.DMA(())],
        compiler_params=pltpu.CompilerParams(vmem_limit_bytes=48 << 20),
        name="feed_back",
    )(top, slope, middle, gain, table, page, expand, reduce)


def project_back_kernel(steps, width, query, pair, branch, x, middle, gain, table, page,
                        mixture_out, result_out, sums_out, mixture, normed):
    step = pl.program_id(0)
    tile = page.shape[1]
    rows = x.shape[0]

    @pl.when(step == 0)
    def _():
        mixture[:, :width] = query[:, :width].astype(F32)
        mixture[:, width : 2 * width] = pair[0, :, :width].astype(F32)
        mixture[:, 2 * width : 3 * width] = pair[1, :, :width].astype(F32)
        mixture[:, 3 * width :] = jnp.zeros((rows, width), F32)
        normed[...] = jnp.zeros_like(normed)

    part = mixture[:, pl.ds(pl.multiple_of(step * tile, tile), tile)].astype(LOW)
    normed[...] += mm_nt(part, page[...])

    @pl.when(step == steps - 1)
    def _():
        grad_normed = close_up(normed[...], table[...])
        unit, inverse = normal_parts(x[...].astype(F32))
        result_out[...] = (middle[...] + normal_back(grad_normed * gain[...], unit, inverse)).astype(LOW)

        def row(value):
            return jnp.sum(value, axis=0, keepdims=True)

        sums_out[0:1] = row(grad_normed * unit)
        sums_out[1:2] = row(grad_normed)
        sums_out[2:3] = row(query[:, :width].astype(F32))
        sums_out[3:4] = row(pair[1, :, :width].astype(F32))
        sums_out[4:8] = jnp.zeros((4, width), F32)
        mixture[:, 3 * width :] = branch[...].astype(F32)
        mixture_out[...] = mixture[...].astype(LOW)


def project_back(query, pair, branch, x, middle, gain, table, page):
    rows, width = x.shape
    tile, steps = 640, 6
    flat = whole((rows, width))
    return pl.pallas_call(
        partial(project_back_kernel, steps, width),
        grid=(steps,),
        in_specs=[whole((rows, WIDE)), whole((2, rows, WIDE)), flat, flat, flat, whole((1, width)),
                  whole(table.shape), pl.BlockSpec((WIDE, tile), lambda i: (0, i))],
        out_specs=(whole((rows, 4 * width)), flat, whole((8, width))),
        out_shape=(
            jax.ShapeDtypeStruct((rows, 4 * width), LOW),
            jax.ShapeDtypeStruct((rows, width), LOW),
            jax.ShapeDtypeStruct((8, width), F32),
        ),
        scratch_shapes=[pltpu.VMEM((rows, 4 * width), F32), pltpu.VMEM((rows, WIDE), F32)],
        compiler_params=pltpu.CompilerParams(vmem_limit_bytes=48 << 20),
        name="project_back",
    )(query, pair, branch, x, middle, gain, table, page)


def page_kernel(width, normed, attended, mixture, small, out, left_one, left_two):
    step = pl.program_id(0)
    tile = mixture.shape[1]
    edge = 3 * width

    @pl.when(step == 0)
    def _():
        left_one[...] = normed[...].T
        left_two[...] = attended[...].T

    def put(value):
        value = value.reshape(16, 72, tile)
        row = lax.broadcasted_iota(jnp.int32, value.shape, 1)
        out[...] = jnp.where(row == 68, small[...], value).astype(LOW)

    @pl.when((step + 1) * tile <= edge)
    def _():
        put(mm(left_one[...], mixture[...]))

    @pl.when(step * tile >= edge)
    def _():
        put(mm(left_two[...], mixture[...]))

    @pl.when(((step + 1) * tile > edge) & (step * tile < edge))
    def _():
        column = step * tile + lax.broadcasted_iota(jnp.int32, mixture.shape, 1)
        value = mixture[...]
        zero = jnp.zeros_like(value)
        put(mm(left_one[...], jnp.where(column < edge, value, zero))
            + mm(left_two[...], jnp.where(column < edge, zero, value)))


def attention_page(normed, attended, mixture, small):
    rows, total = mixture.shape
    tile = 256
    return pl.pallas_call(
        partial(page_kernel, total // 4),
        grid=(total // tile,),
        in_specs=[whole((rows, WIDE)), whole((rows, WIDE)), pl.BlockSpec((rows, tile), lambda i: (0, i)),
                  pl.BlockSpec((16, 1, tile), lambda i: (0, 0, i))],
        out_specs=pl.BlockSpec((16, 72, tile), lambda i: (0, 0, i)),
        out_shape=jax.ShapeDtypeStruct((16, 72, total), LOW),
        scratch_shapes=[pltpu.VMEM((WIDE, rows), LOW), pltpu.VMEM((WIDE, rows), LOW)],
        compiler_params=pltpu.CompilerParams(vmem_limit_bytes=48 << 20),
        name="attention_page",
    )(normed, attended, mixture, small)


LEAD_ROWS = 144


def gather_tasks(shards, outs, halved, send_sem, recv_sem, copy_sem, place_of):
    core, rings, lines, toward = place_of
    slots = len(shards)
    sent = []

    def rows_of(t, page):
        if not halved[t]:
            return None
        total = shards[t].shape[0]
        return pl.ds(0, LEAD_ROWS) if page == 0 else pl.ds(LEAD_ROWS, total - LEAD_ROWS)

    def out_of(t, page):
        return outs[t][0] if halved[t] else outs[t][page]

    def place(t, page, dd, k):
        index, rows = rings[dd] * 4 + lines[k], rows_of(t, page)
        return out_of(t, page).at[index] if rows is None else out_of(t, page).at[index, rows]

    def own(t, page):
        rows = rows_of(t, page)
        return shards[t] if rows is None else shards[t].at[rows]

    def group(t, page, dd):
        at, rows = pl.ds(rings[dd] * 4, 4), rows_of(t, page)
        return out_of(t, page).at[at] if rows is None else out_of(t, page).at[at, rows]

    def copy_of(t, source, target, to, kind):
        index = t * len(GATHER_KINDS) + GATHER_NUMBER[kind]
        return remote_copy(source, target, send_sem.at[index], recv_sem.at[index], toward[to])

    def send(t, dd, k, to, kind, mine=False):
        def act(page):
            target = place(t, page, dd, k)
            copy_of(t, own(t, page) if mine else target, target, to, kind).start()

        per_core(core, act)
        sent.append((t, lambda page: copy_of(t, place(t, page, dd, k), place(t, page, dd, k), to, kind)))

    def arrive(t, dd, k, to, kind):
        def act(page):
            target = place(t, page, dd, k)
            copy_of(t, target, target, to, kind).wait_recv()

        per_core(core, act)

    def sibling(t, dd):
        def copy(page):
            return copy_of(t, group(t, page, dd), group(t, page, dd), SIBLING, (SIBLING, dd))

        per_core(core, lambda page: copy(page).start())
        sent.append((t, copy))

    def begin_line(t):
        for k in (1, 2, 3):
            send(t, 0, 0, (LEVEL, k), (LEVEL, k), mine=True)

    def local(t, page):
        return pltpu.make_async_copy(own(t, page), place(t, page, 0, 0), copy_sem.at[t])

    def begin_ring(t):
        send(t, 0, 0, EAST, (EAST, 0), mine=True)
        send(t, 0, 0, NORTH, (NORTH, 0), mine=True)
        per_core(core, lambda page: local(t, page).start())

    def own_ready(t):
        per_core(core, lambda page: local(t, page).wait())

    def from_line(t, k):
        arrive(t, 0, k, (LEVEL, k), (LEVEL, k))
        send(t, 0, k, EAST, (EAST, k))
        send(t, 0, k, NORTH, (NORTH, k))

    def from_east(t, k):
        arrive(t, 1, k, EAST, (EAST, k))
        if k < 2:
            send(t, 1, k, NORTH, (CORNER, k))

    def from_north(t, k):
        arrive(t, 2, k, NORTH, (NORTH, k))
        if k >= 2:
            send(t, 2, k, EAST, (CORNER, k))

    def from_corner(t, k):
        arrive(t, 3, k, NORTH if k < 2 else EAST, (CORNER, k))

    def last(t, dd):
        def act(page):
            target = group(t, 1 - page, dd)
            copy_of(t, target, target, SIBLING, (SIBLING, dd)).wait_recv()

        per_core(core, act)

    tasks = []

    def then(function, *given):
        tasks.append(lambda: function(*given))

    then(begin_line, 0)
    then(begin_ring, 0)
    for t in range(slots):
        then(from_east, t, 0)
        then(from_north, t, 0)
        then(from_line, t, 1)
        then(from_line, t, 2)
        then(from_line, t, 3)
        then(own_ready, t)
        then(sibling, t, 0)
        if t + 1 < slots:
            then(begin_line, t + 1)
        then(from_east, t, 1)
        then(from_north, t, 1)
        if t + 1 < slots:
            then(begin_ring, t + 1)
        for k in (2, 3):
            then(from_east, t, k)
            then(from_north, t, k)
        then(sibling, t, 1)
        then(sibling, t, 2)
        for k in range(4):
            then(from_corner, t, k)
        then(sibling, t, 3)
    for t in range(slots):
        for dd in range(4):
            then(last, t, dd)

    def drain():
        for _, copy in sent:
            per_core(core, lambda page: copy(page).wait_send())

    tasks.append(drain)
    return tasks


HALVED = (False, True)


def gather_kernel(*refs):
    shards, refs = refs[:2], refs[2:]
    outs, refs = [refs[0:2], refs[2:3]], refs[3:]
    place_of = places()
    greet(place_of[3])
    for task in gather_tasks(shards, outs, HALVED, *refs, place_of):
        task()


def gather_shapes(shards):
    pages, reduce = ((16,) + shard.shape for shard in shards)
    return [jax.ShapeDtypeStruct(shape, LOW) for shape in (pages, pages, reduce)]


def gather_semaphores():
    count = 2 * len(GATHER_KINDS)
    return [pltpu.SemaphoreType.DMA((count,)), pltpu.SemaphoreType.DMA((count,)), pltpu.SemaphoreType.DMA((2,))]


def gather_pages(shards):
    anywhere = pl.BlockSpec(memory_space=pl.ANY)
    return pl.pallas_call(
        gather_kernel,
        out_shape=tuple(gather_shapes(shards)),
        in_specs=[anywhere] * 2,
        out_specs=(anywhere,) * 3,
        scratch_shapes=gather_semaphores(),
        compiler_params=pltpu.CompilerParams(collective_id=0, has_side_effects=True),
        name="gather_pages",
    )(*shards)


def low_place(line):
    return jnp.where(line < 2, line, 3 - line)


def forward_kernel(extra, *refs):
    x, vectors, wide, table, page_hbm, expand_hbm, reduce_hbm = refs[:7]
    refs = refs[7:]
    if extra:
        shards, refs = refs[:2], refs[2:]
    (normed_out, query_out, here, beside, away, corner, attended_out, log_out, attended_low, middle_out,
     second_out, active_out, slope_out, result_out) = refs[:14]
    refs = refs[14:]
    if extra:
        outs, refs = [refs[0:2], refs[2:3]], refs[3:]
    page, expand, reduce, mixture, result, mixed, stats, page_sem, expand_sem, reduce_sem, pair_send, pair_recv = refs[:12]
    place_of = places()
    core, rings, lines, toward = place_of
    rows, width = x.shape
    half = rows // 2
    first = low_place(lines[0]) == 0

    def page_copy(i):
        at = pl.ds(pl.multiple_of(i * 256, 256), 256)
        return pltpu.make_async_copy(page_hbm.at[:, at], page.at[:, at], page_sem.at[i])

    def expand_copy(i):
        at = pl.ds(pl.multiple_of(i * 256, 256), 256)
        return pltpu.make_async_copy(expand_hbm.at[:, at], expand.at[:, at], expand_sem.at[i])

    def reduce_copy(i):
        at = pl.ds(pl.multiple_of(i * 256, 256), 256)
        return pltpu.make_async_copy(reduce_hbm.at[at], reduce.at[at], reduce_sem.at[i])

    tiles = page.shape[1] // 256

    def begin(make):
        def step(i, _):
            make(i).start()
            return 0

        lax.fori_loop(0, tiles, step, 0)

    begin(page_copy)
    begin(expand_copy)
    begin(reduce_copy)
    greet(toward)
    todo = list(gather_tasks(shards, outs, HALVED, *refs[12:15], place_of)) if extra else []

    def progress(count):
        for _ in range(count):
            if todo:
                todo.pop(0)()

    progress(2)
    unit, _ = normal_parts(x[...].astype(F32))
    normed = (unit * vectors[0:1] + vectors[1:2]).astype(LOW)
    normed_out[...] = mm(normed, table[...]).astype(LOW)

    def column(i, _):
        page_copy(i).wait()
        at = pl.ds(pl.multiple_of(i * 256, 256), 256)
        mixture[:, at] = mm(normed_out[...], page[:, at])
        return 0

    lax.fori_loop(0, 13, column, 0)
    blank = jnp.zeros((rows, WIDE - width), LOW)
    here[0, :, :width] = mixture[:, width : 2 * width].astype(LOW)
    here[0, :, width:] = blank
    here[1, :, :width] = (mixture[:, 2 * width : 3 * width] + vectors[3:4]).astype(LOW)
    here[1, :, width:] = blank

    def pair_copy(source, target, to, number):
        return remote_copy(source, target, pair_send.at[number], pair_recv.at[number], toward[to])

    to_away = pair_copy(here, away, (LEVEL, 1), 0)
    to_beside = pair_copy(here, beside, SIBLING, 1)
    to_corner = pair_copy(away, corner, SIBLING, 2)
    to_away.start()
    to_beside.start()
    query = ((mixture[:, :width] + vectors[2:3]).astype(LOW).astype(F32) * HDIM ** (-0.5)).astype(LOW)
    query_out[:, :width] = query
    query_out[:, width:] = blank
    progress(2)
    to_beside.wait_recv()

    def block(kind, near, part, at):
        rows_at = pl.ds(part * half, half)
        one, two = (here, beside) if near == 0 else (away, corner)
        return jnp.concatenate([one[kind, rows_at, at], two[kind, rows_at, at]], axis=0)

    def one_unit(queries, keys, values):
        scores = mm_nt(keys, queries)
        level = jnp.max(scores, axis=0, keepdims=True)
        exponent = jnp.exp(scores - level)
        return level, jnp.sum(exponent, axis=0, keepdims=True), mm_tn(values, exponent.astype(LOW))

    def merge(units):
        peak = units[0][0]
        for level, _, _ in units[1:]:
            peak = jnp.maximum(peak, level)
        total, out = 0.0, 0.0
        for level, sums, part in units:
            share = jnp.exp(level - peak)
            total = total + share * sums
            out = out + share * part
        return peak, total, out

    def local_pair(p, _):
        at = pl.ds(pl.multiple_of(p * 128, 128), 128)
        low, high = head_pair(query_out[:half, at]), head_pair(query_out[half:, at])
        keys, values = block(0, 0, 0, at), block(1, 0, 0, at)
        bottom = one_unit(low, keys, values)
        top = merge([one_unit(high, keys, values), one_unit(high, block(0, 0, 1, at), block(1, 0, 1, at))])
        for place, (level, sums, out) in enumerate((bottom, top)):
            stats[p, 2 * place : 2 * place + 1] = level
            stats[p, 2 * place + 1 : 2 * place + 2] = sums
            mixed[p, place] = out
        return 0

    for begin_at in (0, 3, 6):
        lax.fori_loop(begin_at, begin_at + 3, local_pair, 0)
        progress(1)
    to_away.wait_recv()
    to_corner.start()
    progress(1)
    to_corner.wait_recv()

    def far_pair(p, _):
        at = pl.ds(pl.multiple_of(p * 128, 128), 128)
        low, high = head_pair(query_out[:half, at]), head_pair(query_out[half:, at])
        keys, values = block(0, 1, 0, at), block(1, 1, 0, at)
        last_keys = jnp.where(first, block(0, 1, 1, at), keys)
        last_values = jnp.where(first, block(1, 1, 1, at), values)
        near = one_unit(high, keys, values)
        last = one_unit(jnp.where(first, high, low), last_keys, last_values)
        low_last = (jnp.where(first, far_below, last[0]),) + last[1:]
        high_last = (jnp.where(first, last[0], far_below),) + last[1:]

        def before(place):
            return (stats[p, 2 * place : 2 * place + 1], stats[p, 2 * place + 1 : 2 * place + 2], mixed[p, place])

        for place, units in enumerate(([before(0), low_last], [before(1), near, high_last])):
            peak, total, out = merge(units)
            attended_out[place * half : (place + 1) * half, at] = from_pair(out / total)
            log_out[p, place : place + 1] = peak + jnp.log(total)
        return 0

    for begin_at in (0, 3, 6):
        lax.fori_loop(begin_at, begin_at + 3, far_pair, 0)
        progress(1)

    def late(i, _):
        page_copy(i).wait()
        return 0

    lax.fori_loop(13, tiles, late, 0)
    lead = 4 * width - WIDE
    attended_low[...] = mm(attended_out[:, :width].astype(LOW), table[...]).astype(LOW)
    blended = mm(attended_low[...], page[:, lead:])
    middle = x[...].astype(F32) + (blended[:, 3 * width - lead :] + vectors[4:5])
    middle_out[...] = middle
    unit, _ = normal_parts(middle)
    second = (unit * vectors[6:7] + vectors[7:8]).astype(LOW)
    second_out[...] = mm(second, table[...]).astype(LOW)
    result[...] = middle + vectors[5:6]

    def inner(i, _):
        at = pl.ds(pl.multiple_of(i * 256, 256), 256)
        expand_copy(i).wait()
        hidden = mm(second_out[...], expand[:, at]) + wide[:, at]
        below = 0.5 + 0.5 * lax.erf(hidden * 0.7071067811865476)
        active = (hidden * below).astype(LOW)
        active_out[:, at] = active
        slope_out[:, at] = (below + hidden * (0.3989422804014327 * jnp.exp(-0.5 * hidden * hidden))).astype(LOW)
        reduce_copy(i).wait()
        result[...] += mm(active, reduce[at])
        return 0

    for begin_at in range(0, tiles, 4):
        lax.fori_loop(begin_at, min(begin_at + 4, tiles), inner, 0)
        progress(2)
    result_out[...] = result[...].astype(LOW)
    progress(len(todo))
    for copy in (to_away, to_beside, to_corner):
        copy.wait_send()


def forward(x, vectors, wide, table, page, expand, reduce, shards=None):
    rows, width = x.shape
    inner = expand.shape[1]
    pairs = WIDE // 128
    anywhere = pl.BlockSpec(memory_space=pl.ANY)
    inside = pl.BlockSpec(memory_space=pltpu.VMEM)

    def shape(*dims, kind=LOW):
        return jax.ShapeDtypeStruct(dims, kind)

    pair = shape(2, rows, WIDE)
    outs = [
        shape(rows, WIDE), shape(rows, WIDE), pair, pair, pair, pair, shape(rows, WIDE, kind=F32),
        shape(pairs, 2, rows, kind=F32), shape(rows, WIDE), shape(rows, width, kind=F32),
        shape(rows, WIDE), shape(rows, inner), shape(rows, inner), shape(rows, width),
    ]
    extra = shards is not None
    count = len(outs)
    scratch = [
        pltpu.VMEM(page.shape, LOW), pltpu.VMEM(expand.shape, LOW), pltpu.VMEM(reduce.shape, LOW),
        pltpu.VMEM((rows, 13 * 256), F32), pltpu.VMEM((rows, width), F32),
        pltpu.VMEM((pairs, 2, 128, rows), F32), pltpu.VMEM((pairs, 4, rows), F32),
        pltpu.SemaphoreType.DMA((inner // 256,)), pltpu.SemaphoreType.DMA((inner // 256,)),
        pltpu.SemaphoreType.DMA((inner // 256,)), pltpu.SemaphoreType.DMA((3,)), pltpu.SemaphoreType.DMA((3,)),
    ]
    if extra:
        outs += gather_shapes(shards)
        scratch += gather_semaphores()
    res = pl.pallas_call(
        partial(forward_kernel, extra),
        out_shape=tuple(outs),
        in_specs=[inside] * 4 + [anywhere] * 3 + ([anywhere] * 2 if extra else []),
        out_specs=(inside,) * count + (anywhere,) * (len(outs) - count),
        scratch_shapes=scratch,
        compiler_params=pltpu.CompilerParams(
            collective_id=2 if extra else 3, has_side_effects=True, vmem_limit_bytes=60 << 20
        ),
        name="forward_gather" if extra else "forward",
    )(x, vectors, wide, table, page, expand, reduce, *(shards if extra else ()))
    return res[:count], res[count:]


def spread(width):
    row = lax.broadcasted_iota(jnp.int32, (width, 16 * 72), 0)
    column = lax.broadcasted_iota(jnp.int32, (width, 16 * 72), 1)
    same = (row // 68 == column // 72) & (row % 68 == column % 72)
    return same.astype(LOW)


def small_of(page):
    part = page[:, 68, : 12 * 68].astype(F32).reshape(16, 12, 68).transpose(1, 0, 2)
    return part[:8].reshape(8, -1), part[8:].transpose(1, 0, 2).reshape(1, -1)


def layer_forward(source, small, wide, weights, table, shards=None):
    saved, gathered = forward(source, small, wide, table, *weights, shards=shards)
    return saved[13], (source,) + tuple(saved[:13]), gathered


def layer_gradient(top, saved, small, weights, low_chunk, table):
    source, normed, query = saved[:3]
    pairs = saved[3:7]
    attended, logs, attended_low, middle, second, active, slope = saved[7:]
    page, expand, reduce = weights
    width = top.shape[1]
    grad_hidden, sum_wide, grad_middle, branch, grad_attended, late = feed_back(
        top, slope, middle, small[6:7], table, page, expand, reduce
    )
    grad_query, near, beside, away, corner = attend_back(
        query, grad_attended, attended, logs, *pairs, low_chunk
    )
    away = (away.astype(F32) + swapped(corner, SECTION, 1).astype(F32)).astype(LOW)
    near = near + swapped(beside, SECTION, 1).astype(F32)
    near = (near + swapped(away, LINE, 1).astype(F32)).astype(LOW)
    mixture, result, early = project_back(
        grad_query, near, branch, source, grad_middle, small[:1], table, page
    )
    order = (early[0], early[1], early[2], early[3], late[2], late[3], late[0], late[1])
    packed = jnp.stack([vector.reshape(16, -1) for vector in order], axis=1)
    packed = jnp.concatenate([packed, sum_wide.reshape(16, 4, -1)], axis=1)
    packed = packed.reshape(16, 1, -1).astype(LOW)
    packed = jnp.pad(packed, ((0, 0), (0, 0), (0, 4 * width - packed.shape[2])))
    page_attention = attention_page(normed, attended_low, mixture, packed)
    page_expand = mm_tn(second, grad_hidden).astype(LOW).reshape(16, 72, -1)
    page_reduce = mm_tn(active, top).astype(LOW).reshape(16, -1, width)
    return result, page_attention, page_expand, page_reduce


def four_by_four(
    inputs,
    cotangent,
    first_gain,
    first_shift,
    joint_weight,
    query_bias,
    value_bias,
    output_weight,
    output_bias,
    second_gain,
    second_shift,
    expand_weight,
    expand_bias,
    reduce_weight,
    reduce_bias,
):
    core = lax.axis_index(SECTION)
    line = lax.axis_index(LINE)
    low_chunk = jnp.where(line < 2, line, 3 - line)
    width = HEADS * HDIM
    packed = jnp.concatenate(
        [
            first_gain[0],
            first_shift[0],
            query_bias[0],
            value_bias[0],
            output_bias[0],
            reduce_bias[0],
            second_gain[0],
            second_shift[0],
            expand_bias[0],
        ]
    )
    packed = jnp.pad(packed[None], ((0, 3), (0, 4 * width - packed.shape[0])))
    attention_shard = jnp.concatenate(
        [jnp.concatenate([joint_weight[0], output_weight[0]], axis=1), packed], axis=0
    )
    expand_shard = jnp.pad(expand_weight[0], ((0, 4), (0, 0)))
    other = swapped(jnp.where(core == 0, expand_shard, attention_shard), SECTION, 1)
    lower = jnp.where(core == 0, attention_shard, other)
    upper = jnp.where(core == 0, other, expand_shard)
    reduce_other = swapped(reduce_weight[0], SECTION, 1)
    lower_reduce = jnp.where(core == 0, reduce_weight[0], reduce_other)
    upper_reduce = jnp.where(core == 0, reduce_other, reduce_weight[0])
    rows = to_rows(inputs, core, line)
    top = to_rows(cotangent, core, line)
    table = spread(width)

    def prepared(pages):
        small, wide = small_of(pages[0])
        weights = (
            pages[0].reshape(-1, 4 * width),
            pages[1].reshape(-1, 4 * width),
            pages[2].reshape(-1, width),
        )
        return small, wide, weights

    layers = [prepared(gather_pages((lower, lower_reduce)))]
    small, wide, weights = layers[0]
    middle_rows, saved_lower, upper_pages = layer_forward(
        rows, small, wide, weights, table, (upper, upper_reduce)
    )
    layers.append(prepared(upper_pages))
    small, wide, weights = layers[1]
    final_rows, saved_upper, _ = layer_forward(middle_rows, small, wide, weights, table)
    layer_outputs = from_rows(middle_rows, final_rows, core, line)
    upper_grad, upper_attention, upper_expand, upper_reduce = layer_gradient(
        top, saved_upper, small, weights, low_chunk, table
    )
    small, wide, weights = layers[0]
    lower_grad, lower_attention, lower_expand, lower_reduce = layer_gradient(
        upper_grad, saved_lower, small, weights, low_chunk, table
    )
    input_grads = from_rows(lower_grad, upper_grad, core, line)
    lower_sum, reduce_sum, upper_sum = scatter(
        [
            (lower_attention, lower_expand),
            (lower_reduce, upper_reduce),
            (upper_attention, upper_expand),
        ]
    )
    kept = jnp.where(core == 0, lower_sum, upper_sum)
    other = swapped(jnp.where(core == 0, upper_sum, lower_sum), SECTION, 1)
    attention_sum = jnp.where(core == 0, kept, other)
    expand_sum = jnp.where(core == 0, other, kept)
    vectors = attention_sum[68, : 12 * 68].reshape(12, 68)
    return (
        layer_outputs,
        input_grads,
        vectors[0][None],
        vectors[1][None],
        attention_sum[None, :68, : 3 * width],
        vectors[2][None],
        vectors[3][None],
        attention_sum[None, :68, 3 * width :],
        vectors[4][None],
        vectors[6][None],
        vectors[7][None],
        expand_sum[None, :68],
        vectors[8:].reshape(1, -1),
        reduce_sum[None],
        vectors[5][None],
    )


def fits(mesh):
    return dict(mesh.shape) == {SECTION: 2, RING: 4, LINE: 4}


def solution(mesh):
    return jax.shard_map(
        four_by_four if fits(mesh) else body,
        mesh=mesh,
        in_specs=(
            P(RING, LINE, None),
            P(RING, LINE, None),
            P(SECTION, OWNERS),
            P(SECTION, OWNERS),
            P(SECTION, OWNERS, None),
            P(SECTION, OWNERS),
            P(SECTION, OWNERS),
            P(SECTION, OWNERS, None),
            P(SECTION, OWNERS),
            P(SECTION, OWNERS),
            P(SECTION, OWNERS),
            P(SECTION, OWNERS, None),
            P(SECTION, OWNERS),
            P(SECTION, OWNERS, None),
            P(SECTION, OWNERS),
        ),
        out_specs=(
            P(SECTION, RING, LINE, None),
            P(SECTION, RING, LINE, None),
            P(SECTION, OWNERS),
            P(SECTION, OWNERS),
            P(SECTION, OWNERS, None),
            P(SECTION, OWNERS),
            P(SECTION, OWNERS),
            P(SECTION, OWNERS, None),
            P(SECTION, OWNERS),
            P(SECTION, OWNERS),
            P(SECTION, OWNERS),
            P(SECTION, OWNERS, None),
            P(SECTION, OWNERS),
            P(SECTION, OWNERS, None),
            P(SECTION, OWNERS),
        ),
        check_vma=False,
    )
```

```python
from functools import partial

import jax
import jax.numpy as jnp
from jax import lax
from jax.experimental import pallas as pl
from jax.experimental.pallas import tpu as pltpu
from jax.sharding import PartitionSpec as P

HEADS = 17
HDIM = 64
BLK = 256
WIDE = 1152
F32, LOW = jnp.float32, jnp.bfloat16
SECTION, RING, LINE = "section", "dp", "seq"
OWNERS = (RING, LINE)
EAST, NORTH, LEVEL, SIBLING, CORNER, ONCE = range(6)


epsilon = 1e-05
far_below = -1e30


def passed_along(value, axis, steps):
    count = lax.axis_size(axis)
    first, last = (max(0, -steps), min(count, count - steps))
    return lax.ppermute(value, axis, [(source, source + steps) for source in range(first, last)])


def normalize(values, scales, offsets):
    centre = jnp.mean(values, axis=-1, keepdims=True)
    centred = values - centre
    inverse = lax.rsqrt(jnp.mean(centred * centred, axis=-1, keepdims=True) + epsilon)
    unit_rows = centred * inverse
    return (unit_rows * scales + offsets, unit_rows, inverse)


def normalize_back(upstream, unit_rows, inverse):
    return inverse * (
        upstream
        - jnp.mean(upstream, axis=-1, keepdims=True)
        - unit_rows * jnp.mean(upstream * unit_rows, axis=-1, keepdims=True)
    )


def score_block(query, key_block, block_index, row_block):
    scores = jnp.einsum(
        "qhd,khd->qhk", query, key_block, preferred_element_type=jnp.float32
    ) * HDIM ** (-0.5)
    highest = jnp.max(scores, axis=-1)
    allowed = (block_index <= row_block)[:, None]
    exponent = jnp.exp(scores - highest[..., None]) * allowed[..., None].astype(jnp.float32)
    levels = jnp.where(allowed, highest, far_below)
    return (exponent, levels)


def attend_forward(query, keys_all, values_all, row_block):
    length = keys_all.shape[0]
    row_count = query.shape[0]
    key_shaped = keys_all.reshape(length, HEADS, HDIM)
    value_shaped = values_all.reshape(length, HEADS, HDIM)
    block_limit = row_block[-1] + 1

    def advance(block_index, carried):
        running_peak, running_sum, weighted = carried
        key_block = lax.dynamic_slice_in_dim(key_shaped, block_index * BLK, BLK, 0)
        value_block = lax.dynamic_slice_in_dim(value_shaped, block_index * BLK, BLK, 0)
        exponent, levels = score_block(query, key_block, block_index, row_block)
        weights = exponent.astype(jnp.bfloat16)
        block_out = jnp.einsum(
            "qhk,khd->qhd", weights, value_block, preferred_element_type=jnp.float32
        )
        newest_peak = jnp.maximum(running_peak, levels)
        shrink_old = jnp.exp(running_peak - newest_peak)
        shrink_new = jnp.exp(levels - newest_peak)
        running_sum = running_sum * shrink_old + shrink_new * jnp.sum(exponent, axis=-1)
        weighted = weighted * shrink_old[..., None] + shrink_new[..., None] * block_out
        return (newest_peak, running_sum, weighted)

    initial = (
        jnp.full((row_count, HEADS), far_below, jnp.float32),
        jnp.zeros((row_count, HEADS), jnp.float32),
        jnp.zeros((row_count, HEADS, HDIM), jnp.float32),
    )
    running_peak, running_sum, weighted = lax.fori_loop(0, block_limit, advance, initial)
    return (weighted / running_sum[..., None], running_peak + jnp.log(running_sum))


def attend_backward(query, keys_all, values_all, row_block, attended, log_total, grad_attended):
    length = keys_all.shape[0]
    key_shaped = keys_all.reshape(length, HEADS, HDIM)
    value_shaped = values_all.reshape(length, HEADS, HDIM)
    block_limit = row_block[-1] + 1
    delta = jnp.sum(grad_attended * attended, axis=-1)

    def advance(block_index, carried):
        grad_query, grad_keys, grad_values = carried
        key_block = lax.dynamic_slice_in_dim(key_shaped, block_index * BLK, BLK, 0)
        value_block = lax.dynamic_slice_in_dim(value_shaped, block_index * BLK, BLK, 0)
        exponent, levels = score_block(query, key_block, block_index, row_block)
        weights = exponent.astype(jnp.bfloat16)
        factor = jnp.exp(levels - log_total)
        scaled = (factor[..., None] * grad_attended).astype(jnp.bfloat16)
        grad_weights = jnp.einsum(
            "qhd,khd->qhk", scaled, value_block, preferred_element_type=jnp.float32
        )
        grad_scores = (exponent * (grad_weights - (factor * delta)[..., None])).astype(jnp.bfloat16)
        grad_query = grad_query + jnp.einsum(
            "qhk,khd->qhd", grad_scores, key_block, preferred_element_type=jnp.float32
        )
        grad_key = jnp.einsum(
            "qhk,qhd->khd", grad_scores, query, preferred_element_type=jnp.float32
        )
        grad_value = jnp.einsum("qhk,qhd->khd", weights, scaled, preferred_element_type=jnp.float32)
        grad_keys = lax.dynamic_update_slice_in_dim(grad_keys, grad_key, block_index * BLK, 0)
        grad_values = lax.dynamic_update_slice_in_dim(grad_values, grad_value, block_index * BLK, 0)
        return (grad_query, grad_keys, grad_values)

    initial = (
        jnp.zeros(query.shape, jnp.float32),
        jnp.zeros((length, HEADS, HDIM), jnp.float32),
        jnp.zeros((length, HEADS, HDIM), jnp.float32),
    )
    grad_query, grad_keys, grad_values = lax.fori_loop(0, block_limit, advance, initial)
    return (
        grad_query,
        grad_keys.reshape(length, HEADS * HDIM),
        grad_values.reshape(length, HEADS * HDIM),
    )


def project(source, params):
    feature_width = HEADS * HDIM
    normed, unit_rows, inverse = normalize(
        source, params[0].astype(jnp.float32), params[1].astype(jnp.float32)
    )
    normed_low = normed.astype(jnp.bfloat16)
    mixture = jnp.dot(normed_low, params[2], preferred_element_type=jnp.float32)
    query_low = (mixture[:, :feature_width] + params[3].astype(jnp.float32)).astype(jnp.bfloat16)
    keys_low = mixture[:, feature_width : 2 * feature_width].astype(jnp.bfloat16)
    values_low = (mixture[:, 2 * feature_width :] + params[4].astype(jnp.float32)).astype(
        jnp.bfloat16
    )
    return (unit_rows, inverse, normed_low, query_low, keys_low, values_low)


def complete(source, params, projected, gathered, row_block):
    row_count = source.shape[0]
    query = projected[3].reshape(row_count, HEADS, HDIM)
    attended, log_total = attend_forward(query, gathered[0], gathered[1], row_block)
    attended_low = attended.reshape(row_count, HEADS * HDIM).astype(jnp.bfloat16)
    middle = source + (
        jnp.dot(attended_low, params[5], preferred_element_type=jnp.float32)
        + params[6].astype(jnp.float32)
    )
    second, unit_second, inverse_second = normalize(
        middle, params[7].astype(jnp.float32), params[8].astype(jnp.float32)
    )
    second_low = second.astype(jnp.bfloat16)
    hidden = jnp.dot(second_low, params[9], preferred_element_type=jnp.float32) + params[10].astype(
        jnp.float32
    )
    active, gelu_pull = jax.vjp(partial(jax.nn.gelu, approximate=False), hidden)
    active_low = active.astype(jnp.bfloat16)
    result = middle + (
        jnp.dot(active_low, params[11], preferred_element_type=jnp.float32)
        + params[12].astype(jnp.float32)
    )
    saved = (
        query,
        attended,
        log_total,
        attended_low,
        unit_second,
        inverse_second,
        second_low,
        gelu_pull,
        active_low,
    )
    return (result, saved)


def layer_backward(source, upstream, params, projected, gathered, row_block):
    unit_first, inverse_first, normed_low, query_low, keys_low, values_low = projected
    row_count = source.shape[0]
    feature_width = HEADS * HDIM
    result, saved = complete(source, params, projected, gathered, row_block)
    (
        query,
        attended,
        log_total,
        attended_low,
        unit_second,
        inverse_second,
        second_low,
        gelu_pull,
        active_low,
    ) = saved
    top_low = upstream.astype(jnp.bfloat16)
    grad_reduce_bias = jnp.sum(top_low.astype(jnp.float32), axis=0)
    grad_reduce_weight = jnp.einsum(
        "tf,td->fd", active_low, top_low, preferred_element_type=jnp.float32
    )
    grad_active = jnp.einsum("td,fd->tf", top_low, params[11], preferred_element_type=jnp.float32)
    grad_hidden_low = gelu_pull(grad_active)[0].astype(jnp.bfloat16)
    grad_expand_bias = jnp.sum(grad_hidden_low.astype(jnp.float32), axis=0)
    grad_expand_weight = jnp.einsum(
        "td,tf->df", second_low, grad_hidden_low, preferred_element_type=jnp.float32
    )
    grad_second = jnp.einsum(
        "tf,df->td", grad_hidden_low, params[9], preferred_element_type=jnp.float32
    )
    grad_second_gain = jnp.sum(grad_second * unit_second, axis=0)
    grad_second_shift = jnp.sum(grad_second, axis=0)
    grad_middle = upstream + normalize_back(
        grad_second * params[7].astype(jnp.float32), unit_second, inverse_second
    )
    branch_low = grad_middle.astype(jnp.bfloat16)
    grad_output_bias = jnp.sum(branch_low.astype(jnp.float32), axis=0)
    grad_output_weight = jnp.einsum(
        "td,te->de", attended_low, branch_low, preferred_element_type=jnp.float32
    )
    grad_attended = jnp.einsum(
        "te,de->td", branch_low, params[5], preferred_element_type=jnp.float32
    )
    grad_query, grad_keys_full, grad_values_full = attend_backward(
        query,
        gathered[0],
        gathered[1],
        row_block,
        attended,
        log_total,
        grad_attended.reshape(row_count, HEADS, HDIM),
    )
    grad_keys, grad_values = (
        lax.psum_scatter(grad_keys_full, LINE, scatter_dimension=0, tiled=True),
        lax.psum_scatter(grad_values_full, LINE, scatter_dimension=0, tiled=True),
    )
    scale_factor = HDIM ** (-0.5)
    grad_mixture = jnp.concatenate(
        [
            grad_query.reshape(row_count, feature_width) * scale_factor,
            grad_keys * scale_factor,
            grad_values,
        ],
        axis=1,
    ).astype(jnp.bfloat16)
    grad_query_bias = jnp.sum(grad_mixture[:, :feature_width].astype(jnp.float32), axis=0)
    grad_value_bias = jnp.sum(grad_mixture[:, 2 * feature_width :].astype(jnp.float32), axis=0)
    grad_joint_weight = jnp.einsum(
        "td,te->de", normed_low, grad_mixture, preferred_element_type=jnp.float32
    )
    grad_normed = jnp.einsum(
        "te,de->td", grad_mixture, params[2], preferred_element_type=jnp.float32
    )
    grad_first_gain = jnp.sum(grad_normed * unit_first, axis=0)
    grad_first_shift = jnp.sum(grad_normed, axis=0)
    grad_source = grad_middle + normalize_back(
        grad_normed * params[0].astype(jnp.float32), unit_first, inverse_first
    )
    grads = (
        grad_first_gain,
        grad_first_shift,
        grad_joint_weight,
        grad_query_bias,
        grad_value_bias,
        grad_output_weight,
        grad_output_bias,
        grad_second_gain,
        grad_second_shift,
        grad_expand_weight,
        grad_expand_bias,
        grad_reduce_weight,
        grad_reduce_bias,
    )
    return (grad_source.astype(jnp.bfloat16), grads)


def body(
    inputs,
    cotangent,
    first_gain,
    first_shift,
    joint_weight,
    query_bias,
    value_bias,
    output_weight,
    output_bias,
    second_gain,
    second_shift,
    expand_weight,
    expand_bias,
    reduce_weight,
    reduce_bias,
):
    section_index = lax.axis_index(SECTION)
    micro_count = inputs.shape[0]
    row_count = inputs.shape[1]
    first_row = lax.axis_index(LINE) * row_count
    row_block = (first_row + jnp.arange(row_count, dtype=jnp.int32)) // BLK
    owned = (
        first_gain[0],
        first_shift[0],
        joint_weight[0],
        query_bias[0],
        value_bias[0],
        output_weight[0],
        output_bias[0],
        second_gain[0],
        second_shift[0],
        expand_weight[0],
        expand_bias[0],
        reduce_weight[0],
        reduce_bias[0],
    )
    forward_params = (
        lax.all_gather(first_gain[0], OWNERS, axis=0, tiled=True),
        lax.all_gather(first_shift[0], OWNERS, axis=0, tiled=True),
        lax.all_gather(joint_weight[0], OWNERS, axis=0, tiled=True),
        lax.all_gather(query_bias[0], OWNERS, axis=0, tiled=True),
        lax.all_gather(value_bias[0], OWNERS, axis=0, tiled=True),
        lax.all_gather(output_weight[0], OWNERS, axis=0, tiled=True),
        lax.all_gather(output_bias[0], OWNERS, axis=0, tiled=True),
        lax.all_gather(second_gain[0], OWNERS, axis=0, tiled=True),
        lax.all_gather(second_shift[0], OWNERS, axis=0, tiled=True),
        lax.all_gather(expand_weight[0], OWNERS, axis=0, tiled=True),
        lax.all_gather(expand_bias[0], OWNERS, axis=0, tiled=True),
        lax.all_gather(reduce_weight[0], OWNERS, axis=0, tiled=True),
        lax.all_gather(reduce_bias[0], OWNERS, axis=0, tiled=True),
    )
    incoming = jnp.zeros(inputs.shape[1:], jnp.bfloat16)
    section_inputs = []
    produced = []
    key_sets = []
    for tick_index in range(micro_count + 1):
        section_input = jnp.where(
            section_index == 0, inputs[min(tick_index, micro_count - 1)], incoming
        )
        source = section_input.astype(jnp.float32)
        projected = project(source, forward_params)
        gathered = (
            lax.all_gather(projected[4], LINE, axis=0, tiled=True),
            lax.all_gather(projected[5], LINE, axis=0, tiled=True),
        )
        result, unused = complete(source, forward_params, projected, gathered, row_block)
        result_low = result.astype(jnp.bfloat16)
        section_inputs.append(section_input)
        produced.append(result_low)
        key_sets.append(gathered)
        if tick_index < micro_count:
            incoming = passed_along(result_low, SECTION, 1)
    backward_params = (
        lax.all_gather(first_gain[0], OWNERS, axis=0, tiled=True),
        lax.all_gather(first_shift[0], OWNERS, axis=0, tiled=True),
        lax.all_gather(joint_weight[0], OWNERS, axis=0, tiled=True),
        lax.all_gather(query_bias[0], OWNERS, axis=0, tiled=True),
        lax.all_gather(value_bias[0], OWNERS, axis=0, tiled=True),
        lax.all_gather(output_weight[0], OWNERS, axis=0, tiled=True),
        lax.all_gather(output_bias[0], OWNERS, axis=0, tiled=True),
        lax.all_gather(second_gain[0], OWNERS, axis=0, tiled=True),
        lax.all_gather(second_shift[0], OWNERS, axis=0, tiled=True),
        lax.all_gather(expand_weight[0], OWNERS, axis=0, tiled=True),
        lax.all_gather(expand_bias[0], OWNERS, axis=0, tiled=True),
        lax.all_gather(reduce_weight[0], OWNERS, axis=0, tiled=True),
        lax.all_gather(reduce_bias[0], OWNERS, axis=0, tiled=True),
    )
    totals = tuple((jnp.zeros(piece.shape, jnp.float32) for piece in backward_params))
    shares = tuple((jnp.zeros(piece.shape, jnp.float32) for piece in owned))
    returning = jnp.zeros(inputs.shape[1:], jnp.bfloat16)
    sent_back = []
    for tick_index in range(micro_count + 1):
        upper_pick = min(tick_index + 1, micro_count)
        lower_pick = max(tick_index - 1, 0)
        section_input = jnp.where(
            section_index == 1, section_inputs[upper_pick], section_inputs[lower_pick]
        )
        upstream = jnp.where(
            section_index == 1, cotangent[min(tick_index, micro_count - 1)], returning
        ).astype(jnp.float32)
        weight_valid = jnp.where(
            section_index == 1,
            1.0 if tick_index < micro_count else 0.0,
            1.0 if tick_index >= 1 else 0.0,
        ).astype(jnp.float32)
        source = section_input.astype(jnp.float32)
        projected = project(source, backward_params)
        gathered = (
            lax.all_gather(projected[4], LINE, axis=0, tiled=True),
            lax.all_gather(projected[5], LINE, axis=0, tiled=True),
        )
        grad_source, grads = layer_backward(
            source, upstream, backward_params, projected, gathered, row_block
        )
        masked = tuple((update * weight_valid for update in grads))
        totals = tuple((running + update for running, update in zip(totals, masked)))
        sent_back.append(grad_source)
        if tick_index < micro_count:
            returning = passed_along(grad_source, SECTION, -1)
    layer_outputs = jnp.stack(
        [
            jnp.where(section_index == 0, produced[position], produced[position + 1])
            for position in range(micro_count)
        ]
    )[None]
    input_grads = jnp.stack(
        [
            jnp.where(section_index == 1, sent_back[position], sent_back[position + 1])
            for position in range(micro_count)
        ]
    )[None]
    (
        sum_first_gain,
        sum_first_shift,
        sum_joint_weight,
        sum_query_bias,
        sum_value_bias,
        sum_output_weight,
        sum_output_bias,
        sum_second_gain,
        sum_second_shift,
        sum_expand_weight,
        sum_expand_bias,
        sum_reduce_weight,
        sum_reduce_bias,
    ) = totals
    shares = (
        lax.psum_scatter(sum_first_gain, OWNERS, scatter_dimension=0, tiled=True),
        lax.psum_scatter(sum_first_shift, OWNERS, scatter_dimension=0, tiled=True),
        lax.psum_scatter(sum_joint_weight, OWNERS, scatter_dimension=0, tiled=True),
        lax.psum_scatter(sum_query_bias, OWNERS, scatter_dimension=0, tiled=True),
        lax.psum_scatter(sum_value_bias, OWNERS, scatter_dimension=0, tiled=True),
        lax.psum_scatter(sum_output_weight, OWNERS, scatter_dimension=0, tiled=True),
        lax.psum_scatter(sum_output_bias, OWNERS, scatter_dimension=0, tiled=True),
        lax.psum_scatter(sum_second_gain, OWNERS, scatter_dimension=0, tiled=True),
        lax.psum_scatter(sum_second_shift, OWNERS, scatter_dimension=0, tiled=True),
        lax.psum_scatter(sum_expand_weight, OWNERS, scatter_dimension=0, tiled=True),
        lax.psum_scatter(sum_expand_bias, OWNERS, scatter_dimension=0, tiled=True),
        lax.psum_scatter(sum_reduce_weight, OWNERS, scatter_dimension=0, tiled=True),
        lax.psum_scatter(sum_reduce_bias, OWNERS, scatter_dimension=0, tiled=True),
    )
    return (layer_outputs, input_grads) + tuple((portion[None] for portion in shares))


def swapped(value, axis, bits):
    count = lax.axis_size(axis)
    return lax.ppermute(value, axis, [(source, source ^ bits) for source in range(count)])


def to_rows(array, core, line):
    half = array.shape[1] // 2
    which = line // 2

    def part(index):
        return lax.dynamic_slice(
            array, (index, core * half, 0), (1, half, array.shape[2])
        )[0]

    mine, arrived = part(which), swapped(part(1 - which), LINE, 3)
    low_side = which == 0
    return jnp.concatenate(
        [jnp.where(low_side, mine, arrived), jnp.where(low_side, arrived, mine)], axis=0
    )


def from_rows(lower, upper, core, line):
    half = lower.shape[0] // 2
    low_side = line // 2 == 0
    both = jnp.stack([lower, upper])
    mine = jnp.where(low_side, both[:, :half], both[:, half:])
    arrived = swapped(jnp.where(low_side, both[:, half:], both[:, :half]), LINE, 3)
    pair = jnp.stack(
        [jnp.where(low_side, mine, arrived), jnp.where(low_side, arrived, mine)], axis=1
    )
    kept = jnp.where(core == 0, pair[0], pair[1])
    other = swapped(jnp.where(core == 0, pair[1], pair[0]), SECTION, 1)
    return jnp.concatenate(
        [jnp.where(core == 0, kept, other), jnp.where(core == 0, other, kept)], axis=1
    )[None]


def flip(place, bits):
    return {1: place + 1 - 2 * (place % 2), 2: (place + 2) % 4, 3: 3 - place}[bits]


def places():
    core, ring, line = (lax.axis_index(name) for name in (SECTION, RING, LINE))
    rings = [ring] + [flip(ring, bits) for bits in (1, 2, 3)]
    lines = [line] + [flip(line, bits) for bits in (1, 2, 3)]
    toward = {
        EAST: {RING: rings[1]},
        NORTH: {RING: rings[2]},
        (LEVEL, 1): {LINE: lines[1]},
        (LEVEL, 2): {LINE: lines[2]},
        (LEVEL, 3): {LINE: lines[3]},
        SIBLING: {SECTION: 1 - core},
    }
    return core, rings, lines, toward


def greet(toward):
    barrier = pltpu.get_barrier_semaphore()
    for to in toward.values():
        pl.semaphore_signal(barrier, inc=1, device_id=to, device_id_type=pl.DeviceIdType.MESH)
    pl.semaphore_wait(barrier, len(toward))


def remote_copy(source, target, send_sem, recv_sem, to):
    return pltpu.make_async_remote_copy(
        src_ref=source,
        dst_ref=target,
        send_sem=send_sem,
        recv_sem=recv_sem,
        device_id=to,
        device_id_type=pl.DeviceIdType.MESH,
    )


def per_core(core, act):
    for index in (0, 1):

        @pl.when(core == index)
        def _():
            act(index)


GATHER_KINDS = (
    [(LEVEL, k) for k in (1, 2, 3)]
    + [(name, k) for name in (EAST, NORTH, CORNER) for k in range(4)]
    + [(SIBLING, k) for k in range(4)]
)
GATHER_NUMBER = {kind: index for index, kind in enumerate(GATHER_KINDS)}


def mm(left, right):
    return jnp.dot(left, right, preferred_element_type=F32)


def mm_nt(left, right):
    return lax.dot_general(left, right, (((1,), (1,)), ((), ())), preferred_element_type=F32)


def mm_tn(left, right):
    return lax.dot_general(left, right, (((0,), (0,)), ((), ())), preferred_element_type=F32)


def normal_parts(values):
    centre = jnp.mean(values, axis=-1, keepdims=True)
    centred = values - centre
    inverse = lax.rsqrt(jnp.mean(centred * centred, axis=-1, keepdims=True) + epsilon)
    return centred * inverse, inverse


def normal_back(upstream, unit, inverse):
    return inverse * (
        upstream
        - jnp.mean(upstream, axis=-1, keepdims=True)
        - unit * jnp.mean(upstream * unit, axis=-1, keepdims=True)
    )


def close_up(rows, table):
    high = rows.astype(LOW)
    rest = (rows - high.astype(F32)).astype(LOW)
    return mm_nt(high, table) + mm_nt(rest, table)


def head_pair(rows):
    lane = lax.broadcasted_iota(jnp.int32, rows.shape, 1)
    zero = jnp.zeros_like(rows)
    return jnp.concatenate(
        [jnp.where(lane < HDIM, rows, zero), jnp.where(lane < HDIM, zero, rows)], axis=0
    )


def from_pair(turned):
    n = turned.shape[1] // 2
    own = jnp.concatenate([turned[:HDIM, :n], turned[HDIM:, n:]], axis=0)
    return own.T


LEAD_ROWS = 144


def gather_tasks(shards, outs, halved, send_sem, recv_sem, copy_sem, place_of):
    core, rings, lines, toward = place_of
    slots = len(shards)
    sent = []

    def rows_of(t, page):
        if not halved[t]:
            return None
        total = shards[t].shape[0]
        return pl.ds(0, LEAD_ROWS) if page == 0 else pl.ds(LEAD_ROWS, total - LEAD_ROWS)

    def out_of(t, page):
        return outs[t][0] if halved[t] else outs[t][page]

    def place(t, page, dd, k):
        index, rows = rings[dd] * 4 + lines[k], rows_of(t, page)
        return out_of(t, page).at[index] if rows is None else out_of(t, page).at[index, rows]

    def own(t, page):
        rows = rows_of(t, page)
        return shards[t] if rows is None else shards[t].at[rows]

    def group(t, page, dd):
        at, rows = pl.ds(rings[dd] * 4, 4), rows_of(t, page)
        return out_of(t, page).at[at] if rows is None else out_of(t, page).at[at, rows]

    def copy_of(t, source, target, to, kind):
        index = t * len(GATHER_KINDS) + GATHER_NUMBER[kind]
        return remote_copy(source, target, send_sem.at[index], recv_sem.at[index], toward[to])

    def send(t, dd, k, to, kind, mine=False):
        def act(page):
            target = place(t, page, dd, k)
            copy_of(t, own(t, page) if mine else target, target, to, kind).start()

        per_core(core, act)
        sent.append((t, lambda page: copy_of(t, place(t, page, dd, k), place(t, page, dd, k), to, kind)))

    def arrive(t, dd, k, to, kind):
        def act(page):
            target = place(t, page, dd, k)
            copy_of(t, target, target, to, kind).wait_recv()

        per_core(core, act)

    def sibling(t, dd):
        def copy(page):
            return copy_of(t, group(t, page, dd), group(t, page, dd), SIBLING, (SIBLING, dd))

        per_core(core, lambda page: copy(page).start())
        sent.append((t, copy))

    def begin_line(t):
        for k in (1, 2, 3):
            send(t, 0, 0, (LEVEL, k), (LEVEL, k), mine=True)

    def local(t, page):
        return pltpu.make_async_copy(own(t, page), place(t, page, 0, 0), copy_sem.at[t])

    def begin_ring(t):
        send(t, 0, 0, EAST, (EAST, 0), mine=True)
        send(t, 0, 0, NORTH, (NORTH, 0), mine=True)
        per_core(core, lambda page: local(t, page).start())

    def own_ready(t):
        per_core(core, lambda page: local(t, page).wait())

    def from_line(t, k):
        arrive(t, 0, k, (LEVEL, k), (LEVEL, k))
        send(t, 0, k, EAST, (EAST, k))
        send(t, 0, k, NORTH, (NORTH, k))

    def from_east(t, k):
        arrive(t, 1, k, EAST, (EAST, k))
        if k < 2:
            send(t, 1, k, NORTH, (CORNER, k))

    def from_north(t, k):
        arrive(t, 2, k, NORTH, (NORTH, k))
        if k >= 2:
            send(t, 2, k, EAST, (CORNER, k))

    def from_corner(t, k):
        arrive(t, 3, k, NORTH if k < 2 else EAST, (CORNER, k))

    def last(t, dd):
        def act(page):
            target = group(t, 1 - page, dd)
            copy_of(t, target, target, SIBLING, (SIBLING, dd)).wait_recv()

        per_core(core, act)

    tasks = []

    def then(function, *given):
        tasks.append(lambda: function(*given))

    then(begin_line, 0)
    then(begin_ring, 0)
    for t in range(slots):
        then(from_east, t, 0)
        then(from_north, t, 0)
        then(from_line, t, 1)
        then(from_line, t, 2)
        then(from_line, t, 3)
        then(own_ready, t)
        then(sibling, t, 0)
        if t + 1 < slots:
            then(begin_line, t + 1)
        then(from_east, t, 1)
        then(from_north, t, 1)
        if t + 1 < slots:
            then(begin_ring, t + 1)
        for k in (2, 3):
            then(from_east, t, k)
            then(from_north, t, k)
        then(sibling, t, 1)
        then(sibling, t, 2)
        for k in range(4):
            then(from_corner, t, k)
        then(sibling, t, 3)
    for t in range(slots):
        for dd in range(4):
            then(last, t, dd)

    def drain():
        for _, copy in sent:
            per_core(core, lambda page: copy(page).wait_send())

    tasks.append(drain)
    return tasks


HALVED = (False, True)


def gather_kernel(*refs):
    shards, refs = refs[:2], refs[2:]
    outs, refs = [refs[0:2], refs[2:3]], refs[3:]
    place_of = places()
    greet(place_of[3])
    for task in gather_tasks(shards, outs, HALVED, *refs, place_of):
        task()


def gather_shapes(shards):
    pages, reduce = ((16,) + shard.shape for shard in shards)
    return [jax.ShapeDtypeStruct(shape, LOW) for shape in (pages, pages, reduce)]


def gather_semaphores():
    count = 2 * len(GATHER_KINDS)
    return [pltpu.SemaphoreType.DMA((count,)), pltpu.SemaphoreType.DMA((count,)), pltpu.SemaphoreType.DMA((2,))]


def gather_pages(shards):
    anywhere = pl.BlockSpec(memory_space=pl.ANY)
    return pl.pallas_call(
        gather_kernel,
        out_shape=tuple(gather_shapes(shards)),
        in_specs=[anywhere] * 2,
        out_specs=(anywhere,) * 3,
        scratch_shapes=gather_semaphores(),
        compiler_params=pltpu.CompilerParams(collective_id=0, has_side_effects=True),
        name="gather_pages",
    )(*shards)


def low_place(line):
    return jnp.where(line < 2, line, 3 - line)


def forward_kernel(extra, *refs):
    x, vectors, wide, table, page_hbm, expand_hbm, reduce_hbm = refs[:7]
    refs = refs[7:]
    if extra:
        shards, refs = refs[:2], refs[2:]
    (normed_out, query_out, here, beside, away, corner, attended_out, log_out, attended_low, middle_out,
     second_out, active_out, slope_out, result_out) = refs[:14]
    refs = refs[14:]
    if extra:
        outs, refs = [refs[0:2], refs[2:3]], refs[3:]
    page, expand, reduce, mixture, result, mixed, stats, page_sem, expand_sem, reduce_sem, pair_send, pair_recv = refs[:12]
    place_of = places()
    core, rings, lines, toward = place_of
    rows, width = x.shape
    half = rows // 2
    first = low_place(lines[0]) == 0

    def page_copy(i):
        at = pl.ds(pl.multiple_of(i * 256, 256), 256)
        return pltpu.make_async_copy(page_hbm.at[:, at], page.at[:, at], page_sem.at[i])

    def expand_copy(i):
        at = pl.ds(pl.multiple_of(i * 256, 256), 256)
        return pltpu.make_async_copy(expand_hbm.at[:, at], expand.at[:, at], expand_sem.at[i])

    def reduce_copy(i):
        at = pl.ds(pl.multiple_of(i * 256, 256), 256)
        return pltpu.make_async_copy(reduce_hbm.at[at], reduce.at[at], reduce_sem.at[i])

    tiles = page.shape[1] // 256

    def begin(make):
        def step(i, _):
            make(i).start()
            return 0

        lax.fori_loop(0, tiles, step, 0)

    begin(page_copy)
    begin(expand_copy)
    begin(reduce_copy)
    greet(toward)
    todo = list(gather_tasks(shards, outs, HALVED, *refs[12:15], place_of)) if extra else []

    def progress(count):
        for _ in range(count):
            if todo:
                todo.pop(0)()

    progress(2)
    unit, _ = normal_parts(x[...].astype(F32))
    normed = (unit * vectors[0:1] + vectors[1:2]).astype(LOW)
    normed_out[...] = mm(normed, table[...]).astype(LOW)

    def column(i, _):
        page_copy(i).wait()
        at = pl.ds(pl.multiple_of(i * 256, 256), 256)
        mixture[:, at] = mm(normed_out[...], page[:, at])
        return 0

    lax.fori_loop(0, 13, column, 0)
    blank = jnp.zeros((rows, WIDE - width), LOW)
    here[0, :, :width] = mixture[:, width : 2 * width].astype(LOW)
    here[0, :, width:] = blank
    here[1, :, :width] = (mixture[:, 2 * width : 3 * width] + vectors[3:4]).astype(LOW)
    here[1, :, width:] = blank

    def pair_copy(source, target, to, number):
        return remote_copy(source, target, pair_send.at[number], pair_recv.at[number], toward[to])

    to_away = pair_copy(here, away, (LEVEL, 1), 0)
    to_beside = pair_copy(here, beside, SIBLING, 1)
    to_corner = pair_copy(away, corner, SIBLING, 2)
    to_away.start()
    to_beside.start()
    query = ((mixture[:, :width] + vectors[2:3]).astype(LOW).astype(F32) * HDIM ** (-0.5)).astype(LOW)
    query_out[:, :width] = query
    query_out[:, width:] = blank
    progress(2)
    to_beside.wait_recv()

    def block(kind, near, part, at):
        rows_at = pl.ds(part * half, half)
        one, two = (here, beside) if near == 0 else (away, corner)
        return jnp.concatenate([one[kind, rows_at, at], two[kind, rows_at, at]], axis=0)

    def one_unit(queries, keys, values):
        scores = mm_nt(keys, queries)
        level = jnp.max(scores, axis=0, keepdims=True)
        exponent = jnp.exp(scores - level)
        return level, jnp.sum(exponent, axis=0, keepdims=True), mm_tn(values, exponent.astype(LOW))

    def merge(units):
        peak = units[0][0]
        for level, _, _ in units[1:]:
            peak = jnp.maximum(peak, level)
        total, out = 0.0, 0.0
        for level, sums, part in units:
            share = jnp.exp(level - peak)
            total = total + share * sums
            out = out + share * part
        return peak, total, out

    def local_pair(p, _):
        at = pl.ds(pl.multiple_of(p * 128, 128), 128)
        low, high = head_pair(query_out[:half, at]), head_pair(query_out[half:, at])
        keys, values = block(0, 0, 0, at), block(1, 0, 0, at)
        bottom = one_unit(low, keys, values)
        top = merge([one_unit(high, keys, values), one_unit(high, block(0, 0, 1, at), block(1, 0, 1, at))])
        for place, (level, sums, out) in enumerate((bottom, top)):
            stats[p, 2 * place : 2 * place + 1] = level
            stats[p, 2 * place + 1 : 2 * place + 2] = sums
            mixed[p, place] = out
        return 0

    for begin_at in (0, 3, 6):
        lax.fori_loop(begin_at, begin_at + 3, local_pair, 0)
        progress(1)
    to_away.wait_recv()
    to_corner.start()
    progress(1)
    to_corner.wait_recv()

    def far_pair(p, _):
        at = pl.ds(pl.multiple_of(p * 128, 128), 128)
        low, high = head_pair(query_out[:half, at]), head_pair(query_out[half:, at])
        keys, values = block(0, 1, 0, at), block(1, 1, 0, at)
        last_keys = jnp.where(first, block(0, 1, 1, at), keys)
        last_values = jnp.where(first, block(1, 1, 1, at), values)
        near = one_unit(high, keys, values)
        last = one_unit(jnp.where(first, high, low), last_keys, last_values)
        low_last = (jnp.where(first, far_below, last[0]),) + last[1:]
        high_last = (jnp.where(first, last[0], far_below),) + last[1:]

        def before(place):
            return (stats[p, 2 * place : 2 * place + 1], stats[p, 2 * place + 1 : 2 * place + 2], mixed[p, place])

        for place, units in enumerate(([before(0), low_last], [before(1), near, high_last])):
            peak, total, out = merge(units)
            attended_out[place * half : (place + 1) * half, at] = from_pair(out / total)
            log_out[p, place : place + 1] = peak + jnp.log(total)
        return 0

    for begin_at in (0, 3, 6):
        lax.fori_loop(begin_at, begin_at + 3, far_pair, 0)
        progress(1)

    def late(i, _):
        page_copy(i).wait()
        return 0

    lax.fori_loop(13, tiles, late, 0)
    lead = 4 * width - WIDE
    attended_low[...] = mm(attended_out[:, :width].astype(LOW), table[...]).astype(LOW)
    blended = mm(attended_low[...], page[:, lead:])
    middle = x[...].astype(F32) + (blended[:, 3 * width - lead :] + vectors[4:5])
    middle_out[...] = middle
    unit, _ = normal_parts(middle)
    second = (unit * vectors[6:7] + vectors[7:8]).astype(LOW)
    second_out[...] = mm(second, table[...]).astype(LOW)
    result[...] = middle + vectors[5:6]

    def inner(i, _):
        at = pl.ds(pl.multiple_of(i * 256, 256), 256)
        expand_copy(i).wait()
        hidden = mm(second_out[...], expand[:, at]) + wide[:, at]
        below = 0.5 + 0.5 * lax.erf(hidden * 0.7071067811865476)
        active = (hidden * below).astype(LOW)
        active_out[:, at] = active
        slope_out[:, at] = (below + hidden * (0.3989422804014327 * jnp.exp(-0.5 * hidden * hidden))).astype(LOW)
        reduce_copy(i).wait()
        result[...] += mm(active, reduce[at])
        return 0

    for begin_at in range(0, tiles, 4):
        lax.fori_loop(begin_at, min(begin_at + 4, tiles), inner, 0)
        progress(2)
    result_out[...] = result[...].astype(LOW)
    progress(len(todo))
    for copy in (to_away, to_beside, to_corner):
        copy.wait_send()


def forward(x, vectors, wide, table, page, expand, reduce, shards=None):
    rows, width = x.shape
    inner = expand.shape[1]
    pairs = WIDE // 128
    anywhere = pl.BlockSpec(memory_space=pl.ANY)
    inside = pl.BlockSpec(memory_space=pltpu.VMEM)

    def shape(*dims, kind=LOW):
        return jax.ShapeDtypeStruct(dims, kind)

    pair = shape(2, rows, WIDE)
    outs = [
        shape(rows, WIDE), shape(rows, WIDE), pair, pair, pair, pair, shape(rows, WIDE, kind=F32),
        shape(pairs, 2, rows, kind=F32), shape(rows, WIDE), shape(rows, width, kind=F32),
        shape(rows, WIDE), shape(rows, inner), shape(rows, inner), shape(rows, width),
    ]
    extra = shards is not None
    count = len(outs)
    scratch = [
        pltpu.VMEM(page.shape, LOW), pltpu.VMEM(expand.shape, LOW), pltpu.VMEM(reduce.shape, LOW),
        pltpu.VMEM((rows, 13 * 256), F32), pltpu.VMEM((rows, width), F32),
        pltpu.VMEM((pairs, 2, 128, rows), F32), pltpu.VMEM((pairs, 4, rows), F32),
        pltpu.SemaphoreType.DMA((inner // 256,)), pltpu.SemaphoreType.DMA((inner // 256,)),
        pltpu.SemaphoreType.DMA((inner // 256,)), pltpu.SemaphoreType.DMA((3,)), pltpu.SemaphoreType.DMA((3,)),
    ]
    if extra:
        outs += gather_shapes(shards)
        scratch += gather_semaphores()
    res = pl.pallas_call(
        partial(forward_kernel, extra),
        out_shape=tuple(outs),
        in_specs=[inside] * 4 + [anywhere] * 3 + ([anywhere] * 2 if extra else []),
        out_specs=(inside,) * count + (anywhere,) * (len(outs) - count),
        scratch_shapes=scratch,
        compiler_params=pltpu.CompilerParams(
            collective_id=2 if extra else 3, has_side_effects=True, vmem_limit_bytes=60 << 20
        ),
        name="forward_gather" if extra else "forward",
    )(x, vectors, wide, table, page, expand, reduce, *(shards if extra else ()))
    return res[:count], res[count:]


COLUMNS, ROWS, TINY = range(3)
SIZES = {COLUMNS: (72, 2176), ROWS: (144, 1088), TINY: (8, 128)}
DEPTH = 6
SCATTER_KINDS = (
    [(SIBLING, dd) for dd in range(4)]
    + [(ONCE, k) for k in range(4)]
    + [(EAST, k) for k in range(4)]
    + [(NORTH, k) for k in range(4)]
    + [(LEVEL, k) for k in (1, 2, 3)]
    + [(CORNER, 0)]
)
SCATTER_NUMBER = {kind: index for index, kind in enumerate(SCATTER_KINDS)}


def kind_type(kind):
    return F32 if kind == TINY else LOW


def landing_shapes(kind):
    return [jax.ShapeDtypeStruct((many,) + SIZES[kind], kind_type(kind)) for many in (16, 4, 4, 4, 4)]


def final_shape(kind):
    return jax.ShapeDtypeStruct({COLUMNS: (72, 4352), ROWS: (272, 1088), TINY: (16, 128)}[kind], F32)


def work_shapes(kinds):
    shapes = []
    for kind in sorted(set(kinds)):
        size, held = SIZES[kind], kind_type(kind)
        shapes += [pltpu.VMEM((2, 4) + size, held), pltpu.VMEM((DEPTH,) + size, held), pltpu.VMEM(size, F32)]
    count = len(kinds) * len(SCATTER_KINDS)
    return shapes + [
        pltpu.SemaphoreType.DMA((count,)), pltpu.SemaphoreType.DMA((count,)),
        pltpu.SemaphoreType.DMA((8,)), pltpu.SemaphoreType.DMA(()),
    ]


class Scatter:
    def __init__(self, kinds, pages, lands, finals, owners, refs, place_of):
        self.kinds, self.pages, self.lands, self.finals, self.owners = kinds, pages, lands, finals, owners
        self.core, self.rings, self.lines, self.toward = place_of
        self.work = {}
        for index, kind in enumerate(sorted(set(kinds))):
            self.work[kind] = refs[3 * index : 3 * index + 3]
        self.send_sem, self.recv_sem, self.load_sem, self.out_sem = refs[3 * len(self.work) :]
        self.turn = 0
        self.used = {kind: [None] * DEPTH for kind in self.work}
        self.count = {kind: 0 for kind in self.work}
        self.given, self.final_sent = [], []

    def remote(self, t, source, target, to, kind):
        index = t * len(SCATTER_KINDS) + SCATTER_NUMBER[kind]
        return remote_copy(source, target, self.send_sem.at[index], self.recv_sem.at[index], self.toward[to])

    def part(self, t, core, index, many=None):
        page, at = self.pages[t], index if many is None else pl.ds(index, many)
        if self.kinds[t] == COLUMNS:
            return page.at[at, :, pl.ds(pl.multiple_of(core * 2176, 128), 2176)]
        if self.kinds[t] == ROWS:
            return page.at[pl.ds(pl.multiple_of(index * 272 + core * 128, 16), 144)]
        return page.at[at, pl.ds(pl.multiple_of(core * 8, 8), 8)]

    def landed(self, t, dd):
        return self.lands[t][0].at[pl.ds(self.rings[dd] * 4, 4)]

    def give(self, t, dd):
        base = self.rings[dd] * 4
        if self.kinds[t] == ROWS:
            for k in range(4):
                self.remote(t, self.part(t, 1 - self.core, base + k), self.lands[t][0].at[base + k], SIBLING, (SIBLING, dd)).start()
        else:
            self.remote(t, self.part(t, 1 - self.core, base, 4), self.landed(t, dd), SIBLING, (SIBLING, dd)).start()
        self.given.append(self.remote(t, self.landed(t, dd), self.landed(t, dd), SIBLING, (SIBLING, dd)))

    def arrived(self, t, ref, to, kind):
        self.remote(t, ref, ref, to, kind).wait_recv()

    def load(self, t, sources):
        loads = self.work[self.kinds[t]][0]
        slot = self.turn % 2
        self.turn += 1
        copies = []
        for j, source in enumerate(sources):
            copies.append(pltpu.make_async_copy(source, loads.at[slot, j], self.load_sem.at[slot * 4 + j]))
        for copy in copies:
            copy.start()
        for copy in copies:
            copy.wait()
        return loads, slot, len(copies)

    def add_up(self, t, loaded, store):
        loads, slot, terms = loaded
        rows, columns = SIZES[self.kinds[t]]
        wide = self.kinds[t] != ROWS
        piece = min(256, columns) if wide else 16

        def step(i, _):
            at = pl.ds(pl.multiple_of(i * piece, piece), piece)
            where = (slice(None), at) if wide else (at, slice(None))
            value = loads[(slot, 0) + where].astype(F32)
            for j in range(1, terms):
                value = value + loads[(slot, j) + where].astype(F32)
            store(where, value)
            return 0

        steps = (columns if wide else rows) // piece
        lax.fori_loop(0, steps, step, 0)
        if wide and steps * piece < columns:
            where = (slice(None), pl.ds(steps * piece, columns - steps * piece))
            value = loads[(slot, 0) + where].astype(F32)
            for j in range(1, terms):
                value = value + loads[(slot, j) + where].astype(F32)
            store(where, value)

    def sources(self, t, dd, k, extra):
        index = self.rings[dd] * 4 + self.lines[k]
        return [self.part(t, self.core, index), self.lands[t][0].at[index]] + extra

    def sum_and_send(self, t, dd, k, extra, target, to, kind):
        form = self.kinds[t]
        loaded = self.load(t, self.sources(t, dd, k, extra))
        place = self.count[form] % DEPTH
        self.count[form] += 1
        if self.used[form][place] is not None:
            self.used[form][place].wait_send()
        out = self.work[form][1]

        def store(where, value):
            out[(place,) + where] = value.astype(out.dtype)

        self.add_up(t, loaded, store)
        copy = self.remote(t, out.at[place], target, to, kind)
        copy.start()
        self.used[form][place] = copy

    def first(self, t, k):
        if k == 0:
            self.arrived(t, self.landed(t, 3), SIBLING, (SIBLING, 3))
        self.sum_and_send(t, 3, k, [], self.lands[t][1].at[k], EAST if k < 2 else NORTH, (ONCE, k))

    def second(self, t, dd, k):
        if (dd, k) in ((1, 0), (2, 3)):
            self.arrived(t, self.landed(t, dd), SIBLING, (SIBLING, dd))
        to, land = (EAST, self.lands[t][2]) if dd == 1 else (NORTH, self.lands[t][3])
        extra = []
        if (dd == 1) == (k >= 2):
            one = self.lands[t][1].at[k]
            self.arrived(t, one, NORTH if k >= 2 else EAST, (ONCE, k))
            extra = [one]
        self.sum_and_send(t, dd, k, extra, land.at[k], to, (to, k))

    def third(self, t, k):
        if k == 3:
            self.arrived(t, self.landed(t, 0), SIBLING, (SIBLING, 0))
        extra = []
        for to, land in ((EAST, self.lands[t][2]), (NORTH, self.lands[t][3])):
            self.arrived(t, land.at[k], to, (to, k))
            extra.append(land.at[k])
        if k:
            self.sum_and_send(t, 0, k, extra, self.lands[t][4].at[k], (LEVEL, k), (LEVEL, k))
        else:
            loaded = self.load(t, self.sources(t, 0, 0, extra))
            total = self.work[self.kinds[t]][2]

            def store(where, value):
                total[where] = value

            self.add_up(t, loaded, store)

    def final_part(self, t, core):
        if self.kinds[t] == COLUMNS:
            return (slice(None), slice(None)), (slice(None), pl.ds(2176 * core, 2176))
        if self.kinds[t] == ROWS:
            return (pl.ds(16 * core, 144 - 16 * core),), (pl.ds(144 * core, 144 - 16 * core),)
        return (slice(None),), (pl.ds(8 * core, 8),)

    def last(self, t):
        land = self.lands[t][4]
        for k in (1, 2, 3):
            self.arrived(t, land.at[k], (LEVEL, k), (LEVEL, k))
        loaded = self.load(t, [land.at[k] for k in (1, 2, 3)])
        total = self.work[self.kinds[t]][2]

        def store(where, value):
            total[where] = total[where] + value

        self.add_up(t, loaded, store)
        owner = self.owners[t]

        def act(core):
            inner, outer = self.final_part(t, core)
            source, target = total.at[inner], self.finals[t].at[outer]
            if core == owner:
                copy = pltpu.make_async_copy(source, target, self.out_sem)
                copy.start()
                copy.wait()
                theirs = self.finals[t].at[self.final_part(t, 1 - core)[1]]
                self.remote(t, theirs, theirs, SIBLING, (CORNER, 0)).wait_recv()
            else:
                copy = self.remote(t, source, target, SIBLING, (CORNER, 0))
                copy.start()
                copy.wait_send()

        per_core(self.core, act)

    def steps(self, t):
        def of(function, *given):
            return lambda: function(*given)

        return (
            [of(self.give, t, dd) for dd in (3, 1, 2, 0)],
            [of(self.first, t, k) for k in (0, 2, 1, 3)],
            [of(self.second, t, dd, k) for dd, k in ((1, 0), (2, 3), (1, 1), (2, 2), (1, 3), (2, 0), (1, 2), (2, 1))],
            [of(self.third, t, k) for k in (3, 2, 1, 0)],
            [of(self.last, t)],
        )

    def drain(self):
        for copy in self.given:
            copy.wait_send()
        for held in self.used.values():
            for copy in held:
                if copy is not None:
                    copy.wait_send()


def backward_kernel(carried, *refs):
    (top, x, vectors, table, normed_in, query, here, beside, away, corner, attended, logs, attended_low, middle,
     second, active, slope) = refs[:17]
    page_hbm, expand_hbm, reduce_hbm = refs[17:20]
    refs = refs[20:]
    if carried:
        carried_page, refs = refs[0], refs[1:]
    result_out, page_reduce, page_expand, page_attention, page_small = refs[:5]
    refs = refs[5:]
    kinds = (COLUMNS, ROWS, COLUMNS, COLUMNS, TINY) if carried else (ROWS, COLUMNS, TINY)
    owners = (1, 0, 0, 0, 0) if carried else (1, 1, 1)
    pages = (carried_page, page_reduce, page_expand, page_attention, page_small) if carried else (page_reduce, page_expand, page_small)
    n = len(kinds)
    finals, refs = refs[:n], refs[n:]
    lands, refs = [refs[5 * t : 5 * t + 5] for t in range(n)], refs[5 * n :]
    (reduce_ring, expand_ring, output, second_sum, left_one, left_two, stage_wide, stage_tall, wide_sum, query_sum,
     here_sum, beside_give, away_give, corner_give, beside_got, away_got, corner_got, pair, mixture, grad_middle,
     grad_attended, sums, small, reduce_sem, expand_sem, output_sem, wide_sem, tall_sem, pair_send, pair_recv) = refs[:30]
    place_of = places()
    core, rings, lines, toward = place_of
    scatter = Scatter(kinds, pages, lands, finals, owners, refs[30:], place_of)
    rows, width = top.shape
    half = rows // 2
    first = low_place(lines[0]) == 0
    tiles = expand_hbm.shape[1] // 256
    lead = 4 * width - WIDE
    edge = 3 * width

    def tile_at(i):
        return pl.ds(pl.multiple_of(i * 256, 256), 256)

    def reduce_copy(i):
        slot = lax.rem(i, 3)
        return pltpu.make_async_copy(reduce_hbm.at[tile_at(i)], reduce_ring.at[slot], reduce_sem.at[slot])

    def expand_copy(i, source):
        slot = lax.rem(i, 3)
        return pltpu.make_async_copy(source.at[:, tile_at(i)], expand_ring.at[slot], expand_sem.at[slot])

    def wide_copy(i, target):
        slot = lax.rem(i, 2)
        return pltpu.make_async_copy(stage_wide.at[slot], target.at[:, :, tile_at(i)], wide_sem.at[slot])

    def tall_copy(i):
        slot = lax.rem(i, 2)
        return pltpu.make_async_copy(stage_tall.at[slot], page_reduce.at[tile_at(i)], tall_sem.at[slot])

    for i in range(3):
        reduce_copy(i).start()
        expand_copy(i, expand_hbm).start()
    output_copy = pltpu.make_async_copy(page_hbm.at[:, pl.ds(lead, WIDE)], output, output_sem)
    output_copy.start()
    greet(toward)
    todo = []

    def progress(count):
        for _ in range(count):
            if todo:
                todo.pop(0)()

    if carried:
        steps = [scatter.steps(t) for t in range(n)]
        todo += steps[0][0] + steps[0][1] + steps[0][2]
    progress(4)
    left_one[...] = second[...].T
    second_sum[...] = jnp.zeros_like(second_sum)

    def feed_tile(i, _):
        at = tile_at(i)
        slot, side = lax.rem(i, 3), lax.rem(i, 2)
        reduce_copy(i).wait()
        hidden = (mm_nt(top[...], reduce_ring[slot]) * slope[:, at].astype(F32)).astype(LOW)
        wide_sum[0:1, at] = jnp.sum(hidden.astype(F32), axis=0, keepdims=True)
        expand_copy(i, expand_hbm).wait()
        second_sum[...] += mm_nt(hidden, expand_ring[slot])

        @pl.when(i + 3 < tiles)
        def _():
            reduce_copy(i + 3).start()
            expand_copy(i + 3, expand_hbm).start()

        @pl.when(i >= 2)
        def _():
            wide_copy(i - 2, page_expand).wait()
            tall_copy(i - 2).wait()

        stage_wide[side] = mm(left_one[...], hidden).reshape(16, 72, 256).astype(LOW)
        stage_tall[side] = mm_tn(active[:, at], top[...]).astype(LOW)
        wide_copy(i, page_expand).start()
        tall_copy(i).start()
        return 0

    for begin_at in range(0, tiles, 3):
        lax.fori_loop(begin_at, min(begin_at + 3, tiles), feed_tile, 0)
        progress(3)
    for i in (tiles - 2, tiles - 1):
        wide_copy(i, page_expand).wait()
        tall_copy(i).wait()
    if carried:
        todo += steps[1][0] + steps[2][0] + steps[1][1] + steps[0][3] + steps[1][2] + steps[2][1] + steps[0][4]
        todo += steps[1][3] + steps[2][2] + steps[1][4] + steps[2][3] + steps[2][4]
    else:
        steps = [scatter.steps(t) for t in range(n)]
        todo += steps[0][0] + steps[1][0] + steps[0][1] + steps[0][2] + steps[1][1] + steps[0][3] + steps[1][2]
        todo += steps[0][4] + steps[1][3] + steps[1][4]
    progress(8)
    for i in range(3):
        expand_copy(i, page_hbm).start()

    def row(value):
        return jnp.sum(value, axis=0, keepdims=True)

    upstream = top[...].astype(F32)
    grad_second = close_up(second_sum[...], table[...])
    unit, inverse = normal_parts(middle[...])
    sums[6:7] = row(grad_second * unit)
    sums[7:8] = row(grad_second)
    sums[5:6] = row(upstream)
    value = upstream + normal_back(grad_second * vectors[6:7], unit, inverse)
    grad_middle[...] = value
    branch = value.astype(LOW)
    sums[4:5] = row(branch.astype(F32))
    progress(2)
    mixture[:, edge:] = branch.astype(F32)
    output_copy.wait()
    full = jnp.concatenate([jnp.zeros((rows, edge - lead), LOW), branch], axis=1)
    pulled = mm_nt(full, output[...]).astype(LOW)
    grad_attended[:, :width] = mm_nt(pulled, table[...]).astype(LOW)
    grad_attended[:, width:] = jnp.zeros((rows, WIDE - width), LOW)
    progress(2)

    def rows_of(place, at, p):
        part = slice(place * half, (place + 1) * half)
        product = (grad_attended[part, at].astype(F32) * attended[part, at]).T
        delta = jnp.concatenate([row(product[:HDIM]), row(product[HDIM:])], axis=1)
        return head_pair(query[part, at]), head_pair(grad_attended[part, at]), logs[p, place : place + 1], delta

    def block(kind, near, part, at):
        rows_at = pl.ds(part * half, half)
        one, two = (here, beside) if near == 0 else (away, corner)
        return jnp.concatenate([one[kind, rows_at, at], two[kind, rows_at, at]], axis=0)

    def back(own, keys, values):
        queries, grads, log, delta = own
        weights = jnp.exp(mm_nt(keys, queries) - log)
        lowered = (weights * (mm_nt(values, grads) - delta)).astype(LOW)
        return mm_tn(keys, lowered), mm(lowered, queries), mm(weights.astype(LOW), grads)

    def put(one, two, part, at, grads):
        rows_at = pl.ds(part * half, half)
        for kind, value in enumerate(grads):
            one[kind, rows_at, at] = value[:half].astype(one.dtype)
            two[kind, rows_at, at] = value[half:].astype(two.dtype)

    def far_pair(p, _):
        at = pl.ds(pl.multiple_of(p * 128, 128), 128)
        low, high = rows_of(0, at, p), rows_of(1, at, p)
        last_rows = tuple(jnp.where(first, b, a) for a, b in zip(low, high))
        keys, values = block(0, 1, 0, at), block(1, 1, 0, at)
        high_query, keys_a, values_a = back(high, keys, values)
        last_keys = jnp.where(first, block(0, 1, 1, at), keys)
        last_values = jnp.where(first, block(1, 1, 1, at), values)
        more, keys_b, values_b = back(last_rows, last_keys, last_values)
        zero, empty = jnp.zeros_like(keys_b), jnp.zeros_like(more)
        put(away_give, corner_give, 0, at,
            (keys_a + jnp.where(first, zero, keys_b), values_a + jnp.where(first, zero, values_b)))
        put(away_give, corner_give, 1, at, (jnp.where(first, keys_b, zero), jnp.where(first, values_b, zero)))
        query_sum[:half, at] = from_pair(jnp.where(first, empty, more))
        query_sum[half:, at] = from_pair(high_query + jnp.where(first, more, empty))
        return 0

    for begin_at in (0, 3, 6):
        lax.fori_loop(begin_at, begin_at + 3, far_pair, 0)
        progress(2)

    def pair_copy(source, target, to, number):
        return remote_copy(source, target, pair_send.at[number], pair_recv.at[number], toward[to])

    to_corner = pair_copy(corner_give, corner_got, SIBLING, 0)
    to_away = pair_copy(away_give, away_got, (LEVEL, 1), 1)
    to_beside = pair_copy(beside_give, beside_got, SIBLING, 2)
    to_corner.start()

    def near_pair(p, _):
        at = pl.ds(pl.multiple_of(p * 128, 128), 128)
        low, high = rows_of(0, at, p), rows_of(1, at, p)
        keys, values = block(0, 0, 0, at), block(1, 0, 0, at)
        low_query, keys_a, values_a = back(low, keys, values)
        high_query, keys_b, values_b = back(high, keys, values)
        put(here_sum, beside_give, 0, at, (keys_a + keys_b, values_a + values_b))
        more, keys_a, values_a = back(high, block(0, 0, 1, at), block(1, 0, 1, at))
        put(here_sum, beside_give, 1, at, (keys_a, values_a))
        query_sum[:half, at] += from_pair(low_query)
        query_sum[half:, at] += from_pair(high_query + more)
        return 0

    lax.fori_loop(0, 3, near_pair, 0)
    to_corner.wait_recv()
    for kind in (0, 1):
        away_give[kind] = (away_give[kind].astype(F32) + corner_got[kind].astype(F32)).astype(LOW)
    to_away.start()
    progress(2)
    for begin_at in (3, 6):
        lax.fori_loop(begin_at, begin_at + 3, near_pair, 0)
        progress(2)
    to_beside.start()
    mixture[:, :width] = (query_sum[:, :width] * HDIM ** (-0.5)).astype(LOW).astype(F32)
    sums[2:3] = row(mixture[:, :width])
    left_one[...] = normed_in[...].T
    left_two[...] = attended_low[...].T
    second_sum[...] = jnp.zeros_like(second_sum)
    progress(4)
    to_beside.wait_recv()
    to_away.wait_recv()
    for kind in (0, 1):
        value = here_sum[kind] + beside_got[kind].astype(F32) + away_got[kind].astype(F32)
        mixture[:, (1 + kind) * width : (2 + kind) * width] = value[:, :width].astype(LOW).astype(F32)
    sums[3:4] = row(mixture[:, 2 * width : edge])

    def project_tile(i, _):
        at = tile_at(i)
        slot = lax.rem(i, 3)
        column = i * 256 + lax.broadcasted_iota(jnp.int32, (rows, 256), 1)
        part = jnp.where(column < edge, mixture[:, at], 0.0).astype(LOW)
        expand_copy(i, page_hbm).wait()
        second_sum[...] += mm_nt(part, expand_ring[slot])

        @pl.when(i + 3 < 13)
        def _():
            expand_copy(i + 3, page_hbm).start()

        return 0

    for begin_at, end in ((0, 4), (4, 8), (8, 13)):
        lax.fori_loop(begin_at, end, project_tile, 0)
        progress(2)
    grad_normed = close_up(second_sum[...], table[...])
    unit, inverse = normal_parts(x[...].astype(F32))
    sums[0:1] = row(grad_normed * unit)
    sums[1:2] = row(grad_normed)
    result_out[...] = (grad_middle[...] + normal_back(grad_normed * vectors[0:1], unit, inverse)).astype(LOW)
    progress(2)

    def page_tile(number, i):
        side = lax.rem(i, 2)
        at = tile_at(i)

        @pl.when(i >= 2)
        def _():
            wide_copy(i - 2, page_attention).wait()

        part = mixture[:, at]
        if number == 1:
            value = mm(left_one[...], part.astype(LOW))
        elif number == 2:
            value = mm(left_two[...], part.astype(LOW))
        else:
            column = i * 256 + lax.broadcasted_iota(jnp.int32, (rows, 256), 1)
            value = mm(left_one[...], jnp.where(column < edge, part, 0.0).astype(LOW))
            value = value + mm(left_two[...], jnp.where(column < edge, 0.0, part).astype(LOW))
        stage_wide[side] = value.reshape(16, 72, 256).astype(LOW)
        wide_copy(i, page_attention).start()

    def page_loop(number, begin_at, end):
        def step(i, _):
            page_tile(number, i)
            return 0

        lax.fori_loop(begin_at, end, step, 0)

    whole_tiles = edge // 256
    for begin_at in range(0, whole_tiles, 4):
        page_loop(1, begin_at, begin_at + 4)
        progress(2)
    page_loop(3, whole_tiles, whole_tiles + 1)
    page_loop(2, whole_tiles + 1, tiles)
    small[...] = jnp.zeros_like(small)
    for shard in range(16):
        small[shard, 0:8, 0:68] = sums[:, shard * 68 : (shard + 1) * 68]
        for part in range(4):
            begin_at = shard * 272 + part * 68
            small[shard, 8 + part : 9 + part, 0:68] = wide_sum[0:1, begin_at : begin_at + 68]
    small_copy = pltpu.make_async_copy(small, page_small, output_sem)
    small_copy.start()
    for i in (tiles - 2, tiles - 1):
        wide_copy(i, page_attention).wait()
    small_copy.wait()
    tiny = steps[n - 1]
    if carried:
        own = steps[3]
        todo = own[0] + tiny[0] + todo + own[1] + own[2] + tiny[1] + tiny[2] + own[3] + tiny[3] + tiny[4] + own[4]
    else:
        todo = tiny[0] + todo + tiny[1] + tiny[2] + tiny[3] + tiny[4]
    for task in todo:
        task()
    scatter.drain()
    for copy in (to_corner, to_away, to_beside):
        copy.wait_send()


def backward(top, saved, vectors, table, page, expand, reduce, carried_page=None):
    source, normed, query = saved[:3]
    rows, width = top.shape
    inner = expand.shape[1]
    anywhere = pl.BlockSpec(memory_space=pl.ANY)
    inside = pl.BlockSpec(memory_space=pltpu.VMEM)
    carried = carried_page is not None
    kinds = (COLUMNS, ROWS, COLUMNS, COLUMNS, TINY) if carried else (ROWS, COLUMNS, TINY)
    outs = [
        jax.ShapeDtypeStruct((rows, width), LOW), jax.ShapeDtypeStruct(reduce.shape, LOW),
        jax.ShapeDtypeStruct((16, 72, inner), LOW), jax.ShapeDtypeStruct((16, 72, inner), LOW),
        jax.ShapeDtypeStruct((16, 16, 128), F32),
    ]
    outs += [final_shape(kind) for kind in kinds]
    for kind in kinds:
        outs += landing_shapes(kind)
    pair = pltpu.VMEM((2, rows, WIDE), LOW)
    tall = pltpu.VMEM((WIDE, rows), LOW)
    dma = pltpu.SemaphoreType.DMA
    scratch = [
        pltpu.VMEM((3, 256, width), LOW), pltpu.VMEM((3, WIDE, 256), LOW), pltpu.VMEM((WIDE, WIDE), LOW),
        pltpu.VMEM((rows, WIDE), F32), tall, tall, pltpu.VMEM((2, 16, 72, 256), LOW), pltpu.VMEM((2, 256, width), LOW),
        pltpu.VMEM((8, inner), F32), pltpu.VMEM((rows, WIDE), F32), pltpu.VMEM((2, rows, WIDE), F32),
        pair, pair, pair, pair, pair, pair, pltpu.VMEM((8, 128), F32), pltpu.VMEM((rows, inner), F32),
        pltpu.VMEM((rows, width), F32), pltpu.VMEM((rows, WIDE), LOW), pltpu.VMEM((8, width), F32),
        pltpu.VMEM((16, 16, 128), F32), dma((3,)), dma((3,)), dma(()), dma((2,)), dma((2,)), dma((3,)), dma((3,)),
    ] + work_shapes(kinds)
    res = pl.pallas_call(
        partial(backward_kernel, carried),
        out_shape=tuple(outs),
        in_specs=[inside] * 17 + [anywhere] * (4 if carried else 3),
        out_specs=(inside,) + (anywhere,) * (len(outs) - 1),
        scratch_shapes=scratch,
        compiler_params=pltpu.CompilerParams(
            collective_id=4 if carried else 5, has_side_effects=True, vmem_limit_bytes=62 << 20
        ),
        name="backward_sum" if carried else "backward",
    )(top, source, vectors, table, *saved[1:], page, expand, reduce, *((carried_page,) if carried else ()))
    return res[0], res[3], res[5 : 5 + len(kinds)]


def spread(width):
    row = lax.broadcasted_iota(jnp.int32, (width, 16 * 72), 0)
    column = lax.broadcasted_iota(jnp.int32, (width, 16 * 72), 1)
    same = (row // 68 == column // 72) & (row % 68 == column % 72)
    return same.astype(LOW)


def small_of(page):
    part = page[:, 68, : 12 * 68].astype(F32).reshape(16, 12, 68).transpose(1, 0, 2)
    return part[:8].reshape(8, -1), part[8:].transpose(1, 0, 2).reshape(1, -1)


def layer_forward(source, small, wide, weights, table, shards=None):
    saved, gathered = forward(source, small, wide, table, *weights, shards=shards)
    return saved[13], (source,) + tuple(saved[:13]), gathered


def four_by_four(
    inputs,
    cotangent,
    first_gain,
    first_shift,
    joint_weight,
    query_bias,
    value_bias,
    output_weight,
    output_bias,
    second_gain,
    second_shift,
    expand_weight,
    expand_bias,
    reduce_weight,
    reduce_bias,
):
    core = lax.axis_index(SECTION)
    line = lax.axis_index(LINE)
    low_chunk = jnp.where(line < 2, line, 3 - line)
    width = HEADS * HDIM
    packed = jnp.concatenate(
        [
            first_gain[0],
            first_shift[0],
            query_bias[0],
            value_bias[0],
            output_bias[0],
            reduce_bias[0],
            second_gain[0],
            second_shift[0],
            expand_bias[0],
        ]
    )
    packed = jnp.pad(packed[None], ((0, 3), (0, 4 * width - packed.shape[0])))
    attention_shard = jnp.concatenate(
        [jnp.concatenate([joint_weight[0], output_weight[0]], axis=1), packed], axis=0
    )
    expand_shard = jnp.pad(expand_weight[0], ((0, 4), (0, 0)))
    other = swapped(jnp.where(core == 0, expand_shard, attention_shard), SECTION, 1)
    lower = jnp.where(core == 0, attention_shard, other)
    upper = jnp.where(core == 0, other, expand_shard)
    reduce_other = swapped(reduce_weight[0], SECTION, 1)
    lower_reduce = jnp.where(core == 0, reduce_weight[0], reduce_other)
    upper_reduce = jnp.where(core == 0, reduce_other, reduce_weight[0])
    rows = to_rows(inputs, core, line)
    top = to_rows(cotangent, core, line)
    table = spread(width)

    def prepared(pages):
        small, wide = small_of(pages[0])
        weights = (
            pages[0].reshape(-1, 4 * width),
            pages[1].reshape(-1, 4 * width),
            pages[2].reshape(-1, width),
        )
        return small, wide, weights

    layers = [prepared(gather_pages((lower, lower_reduce)))]
    small, wide, weights = layers[0]
    middle_rows, saved_lower, upper_pages = layer_forward(
        rows, small, wide, weights, table, (upper, upper_reduce)
    )
    layers.append(prepared(upper_pages))
    small, wide, weights = layers[1]
    final_rows, saved_upper, _ = layer_forward(middle_rows, small, wide, weights, table)
    layer_outputs = from_rows(middle_rows, final_rows, core, line)
    upper_grad, upper_attention, upper_sums = backward(top, saved_upper, small, table, *weights)
    small, wide, weights = layers[0]
    lower_grad, _, lower_sums = backward(
        upper_grad, saved_lower, small, table, *weights, carried_page=upper_attention
    )
    input_grads = from_rows(lower_grad, upper_grad, core, line)
    own = core == 0
    attention_sum = jnp.where(own, lower_sums[3], lower_sums[0])
    expand_sum = jnp.where(own, lower_sums[2], upper_sums[1])
    reduce_sum = jnp.where(own, lower_sums[1], upper_sums[0])
    vectors = jnp.where(own, lower_sums[4], upper_sums[2])[:12, :68]
    return (
        layer_outputs,
        input_grads,
        vectors[0][None],
        vectors[1][None],
        attention_sum[None, :68, : 3 * width],
        vectors[2][None],
        vectors[3][None],
        attention_sum[None, :68, 3 * width :],
        vectors[4][None],
        vectors[6][None],
        vectors[7][None],
        expand_sum[None, :68],
        vectors[8:].reshape(1, -1),
        reduce_sum[None],
        vectors[5][None],
    )


def fits(mesh):
    return dict(mesh.shape) == {SECTION: 2, RING: 4, LINE: 4}


def solution(mesh):
    return jax.shard_map(
        four_by_four if fits(mesh) else body,
        mesh=mesh,
        in_specs=(
            P(RING, LINE, None),
            P(RING, LINE, None),
            P(SECTION, OWNERS),
            P(SECTION, OWNERS),
            P(SECTION, OWNERS, None),
            P(SECTION, OWNERS),
            P(SECTION, OWNERS),
            P(SECTION, OWNERS, None),
            P(SECTION, OWNERS),
            P(SECTION, OWNERS),
            P(SECTION, OWNERS),
            P(SECTION, OWNERS, None),
            P(SECTION, OWNERS),
            P(SECTION, OWNERS, None),
            P(SECTION, OWNERS),
        ),
        out_specs=(
            P(SECTION, RING, LINE, None),
            P(SECTION, RING, LINE, None),
            P(SECTION, OWNERS),
            P(SECTION, OWNERS),
            P(SECTION, OWNERS, None),
            P(SECTION, OWNERS),
            P(SECTION, OWNERS),
            P(SECTION, OWNERS, None),
            P(SECTION, OWNERS),
            P(SECTION, OWNERS),
            P(SECTION, OWNERS),
            P(SECTION, OWNERS, None),
            P(SECTION, OWNERS),
            P(SECTION, OWNERS, None),
            P(SECTION, OWNERS),
        ),
        check_vma=False,
    )
```

```python
from functools import partial

import jax
import jax.numpy as jnp
from jax import lax
from jax.experimental import pallas as pl
from jax.experimental.pallas import tpu as pltpu
from jax.sharding import PartitionSpec as P

HEADS = 17
HDIM = 64
BLK = 256
WIDE = 1152
F32, LOW = jnp.float32, jnp.bfloat16
SECTION, RING, LINE = "section", "dp", "seq"
OWNERS = (RING, LINE)
EAST, NORTH, LEVEL, SIBLING, CORNER, ONCE, UP, DOWN = range(8)


epsilon = 1e-05
far_below = -1e30


def passed_along(value, axis, steps):
    count = lax.axis_size(axis)
    first, last = (max(0, -steps), min(count, count - steps))
    return lax.ppermute(value, axis, [(source, source + steps) for source in range(first, last)])


def normalize(values, scales, offsets):
    centre = jnp.mean(values, axis=-1, keepdims=True)
    centred = values - centre
    inverse = lax.rsqrt(jnp.mean(centred * centred, axis=-1, keepdims=True) + epsilon)
    unit_rows = centred * inverse
    return (unit_rows * scales + offsets, unit_rows, inverse)


def normalize_back(upstream, unit_rows, inverse):
    return inverse * (
        upstream
        - jnp.mean(upstream, axis=-1, keepdims=True)
        - unit_rows * jnp.mean(upstream * unit_rows, axis=-1, keepdims=True)
    )


def score_block(query, key_block, block_index, row_block):
    scores = jnp.einsum(
        "qhd,khd->qhk", query, key_block, preferred_element_type=jnp.float32
    ) * HDIM ** (-0.5)
    highest = jnp.max(scores, axis=-1)
    allowed = (block_index <= row_block)[:, None]
    exponent = jnp.exp(scores - highest[..., None]) * allowed[..., None].astype(jnp.float32)
    levels = jnp.where(allowed, highest, far_below)
    return (exponent, levels)


def attend_forward(query, keys_all, values_all, row_block):
    length = keys_all.shape[0]
    row_count = query.shape[0]
    key_shaped = keys_all.reshape(length, HEADS, HDIM)
    value_shaped = values_all.reshape(length, HEADS, HDIM)
    block_limit = row_block[-1] + 1

    def advance(block_index, carried):
        running_peak, running_sum, weighted = carried
        key_block = lax.dynamic_slice_in_dim(key_shaped, block_index * BLK, BLK, 0)
        value_block = lax.dynamic_slice_in_dim(value_shaped, block_index * BLK, BLK, 0)
        exponent, levels = score_block(query, key_block, block_index, row_block)
        weights = exponent.astype(jnp.bfloat16)
        block_out = jnp.einsum(
            "qhk,khd->qhd", weights, value_block, preferred_element_type=jnp.float32
        )
        newest_peak = jnp.maximum(running_peak, levels)
        shrink_old = jnp.exp(running_peak - newest_peak)
        shrink_new = jnp.exp(levels - newest_peak)
        running_sum = running_sum * shrink_old + shrink_new * jnp.sum(exponent, axis=-1)
        weighted = weighted * shrink_old[..., None] + shrink_new[..., None] * block_out
        return (newest_peak, running_sum, weighted)

    initial = (
        jnp.full((row_count, HEADS), far_below, jnp.float32),
        jnp.zeros((row_count, HEADS), jnp.float32),
        jnp.zeros((row_count, HEADS, HDIM), jnp.float32),
    )
    running_peak, running_sum, weighted = lax.fori_loop(0, block_limit, advance, initial)
    return (weighted / running_sum[..., None], running_peak + jnp.log(running_sum))


def attend_backward(query, keys_all, values_all, row_block, attended, log_total, grad_attended):
    length = keys_all.shape[0]
    key_shaped = keys_all.reshape(length, HEADS, HDIM)
    value_shaped = values_all.reshape(length, HEADS, HDIM)
    block_limit = row_block[-1] + 1
    delta = jnp.sum(grad_attended * attended, axis=-1)

    def advance(block_index, carried):
        grad_query, grad_keys, grad_values = carried
        key_block = lax.dynamic_slice_in_dim(key_shaped, block_index * BLK, BLK, 0)
        value_block = lax.dynamic_slice_in_dim(value_shaped, block_index * BLK, BLK, 0)
        exponent, levels = score_block(query, key_block, block_index, row_block)
        weights = exponent.astype(jnp.bfloat16)
        factor = jnp.exp(levels - log_total)
        scaled = (factor[..., None] * grad_attended).astype(jnp.bfloat16)
        grad_weights = jnp.einsum(
            "qhd,khd->qhk", scaled, value_block, preferred_element_type=jnp.float32
        )
        grad_scores = (exponent * (grad_weights - (factor * delta)[..., None])).astype(jnp.bfloat16)
        grad_query = grad_query + jnp.einsum(
            "qhk,khd->qhd", grad_scores, key_block, preferred_element_type=jnp.float32
        )
        grad_key = jnp.einsum(
            "qhk,qhd->khd", grad_scores, query, preferred_element_type=jnp.float32
        )
        grad_value = jnp.einsum("qhk,qhd->khd", weights, scaled, preferred_element_type=jnp.float32)
        grad_keys = lax.dynamic_update_slice_in_dim(grad_keys, grad_key, block_index * BLK, 0)
        grad_values = lax.dynamic_update_slice_in_dim(grad_values, grad_value, block_index * BLK, 0)
        return (grad_query, grad_keys, grad_values)

    initial = (
        jnp.zeros(query.shape, jnp.float32),
        jnp.zeros((length, HEADS, HDIM), jnp.float32),
        jnp.zeros((length, HEADS, HDIM), jnp.float32),
    )
    grad_query, grad_keys, grad_values = lax.fori_loop(0, block_limit, advance, initial)
    return (
        grad_query,
        grad_keys.reshape(length, HEADS * HDIM),
        grad_values.reshape(length, HEADS * HDIM),
    )


def project(source, params):
    feature_width = HEADS * HDIM
    normed, unit_rows, inverse = normalize(
        source, params[0].astype(jnp.float32), params[1].astype(jnp.float32)
    )
    normed_low = normed.astype(jnp.bfloat16)
    mixture = jnp.dot(normed_low, params[2], preferred_element_type=jnp.float32)
    query_low = (mixture[:, :feature_width] + params[3].astype(jnp.float32)).astype(jnp.bfloat16)
    keys_low = mixture[:, feature_width : 2 * feature_width].astype(jnp.bfloat16)
    values_low = (mixture[:, 2 * feature_width :] + params[4].astype(jnp.float32)).astype(
        jnp.bfloat16
    )
    return (unit_rows, inverse, normed_low, query_low, keys_low, values_low)


def complete(source, params, projected, gathered, row_block):
    row_count = source.shape[0]
    query = projected[3].reshape(row_count, HEADS, HDIM)
    attended, log_total = attend_forward(query, gathered[0], gathered[1], row_block)
    attended_low = attended.reshape(row_count, HEADS * HDIM).astype(jnp.bfloat16)
    middle = source + (
        jnp.dot(attended_low, params[5], preferred_element_type=jnp.float32)
        + params[6].astype(jnp.float32)
    )
    second, unit_second, inverse_second = normalize(
        middle, params[7].astype(jnp.float32), params[8].astype(jnp.float32)
    )
    second_low = second.astype(jnp.bfloat16)
    hidden = jnp.dot(second_low, params[9], preferred_element_type=jnp.float32) + params[10].astype(
        jnp.float32
    )
    active, gelu_pull = jax.vjp(partial(jax.nn.gelu, approximate=False), hidden)
    active_low = active.astype(jnp.bfloat16)
    result = middle + (
        jnp.dot(active_low, params[11], preferred_element_type=jnp.float32)
        + params[12].astype(jnp.float32)
    )
    saved = (
        query,
        attended,
        log_total,
        attended_low,
        unit_second,
        inverse_second,
        second_low,
        gelu_pull,
        active_low,
    )
    return (result, saved)


def layer_backward(source, upstream, params, projected, gathered, row_block):
    unit_first, inverse_first, normed_low, query_low, keys_low, values_low = projected
    row_count = source.shape[0]
    feature_width = HEADS * HDIM
    result, saved = complete(source, params, projected, gathered, row_block)
    (
        query,
        attended,
        log_total,
        attended_low,
        unit_second,
        inverse_second,
        second_low,
        gelu_pull,
        active_low,
    ) = saved
    top_low = upstream.astype(jnp.bfloat16)
    grad_reduce_bias = jnp.sum(top_low.astype(jnp.float32), axis=0)
    grad_reduce_weight = jnp.einsum(
        "tf,td->fd", active_low, top_low, preferred_element_type=jnp.float32
    )
    grad_active = jnp.einsum("td,fd->tf", top_low, params[11], preferred_element_type=jnp.float32)
    grad_hidden_low = gelu_pull(grad_active)[0].astype(jnp.bfloat16)
    grad_expand_bias = jnp.sum(grad_hidden_low.astype(jnp.float32), axis=0)
    grad_expand_weight = jnp.einsum(
        "td,tf->df", second_low, grad_hidden_low, preferred_element_type=jnp.float32
    )
    grad_second = jnp.einsum(
        "tf,df->td", grad_hidden_low, params[9], preferred_element_type=jnp.float32
    )
    grad_second_gain = jnp.sum(grad_second * unit_second, axis=0)
    grad_second_shift = jnp.sum(grad_second, axis=0)
    grad_middle = upstream + normalize_back(
        grad_second * params[7].astype(jnp.float32), unit_second, inverse_second
    )
    branch_low = grad_middle.astype(jnp.bfloat16)
    grad_output_bias = jnp.sum(branch_low.astype(jnp.float32), axis=0)
    grad_output_weight = jnp.einsum(
        "td,te->de", attended_low, branch_low, preferred_element_type=jnp.float32
    )
    grad_attended = jnp.einsum(
        "te,de->td", branch_low, params[5], preferred_element_type=jnp.float32
    )
    grad_query, grad_keys_full, grad_values_full = attend_backward(
        query,
        gathered[0],
        gathered[1],
        row_block,
        attended,
        log_total,
        grad_attended.reshape(row_count, HEADS, HDIM),
    )
    grad_keys, grad_values = (
        lax.psum_scatter(grad_keys_full, LINE, scatter_dimension=0, tiled=True),
        lax.psum_scatter(grad_values_full, LINE, scatter_dimension=0, tiled=True),
    )
    scale_factor = HDIM ** (-0.5)
    grad_mixture = jnp.concatenate(
        [
            grad_query.reshape(row_count, feature_width) * scale_factor,
            grad_keys * scale_factor,
            grad_values,
        ],
        axis=1,
    ).astype(jnp.bfloat16)
    grad_query_bias = jnp.sum(grad_mixture[:, :feature_width].astype(jnp.float32), axis=0)
    grad_value_bias = jnp.sum(grad_mixture[:, 2 * feature_width :].astype(jnp.float32), axis=0)
    grad_joint_weight = jnp.einsum(
        "td,te->de", normed_low, grad_mixture, preferred_element_type=jnp.float32
    )
    grad_normed = jnp.einsum(
        "te,de->td", grad_mixture, params[2], preferred_element_type=jnp.float32
    )
    grad_first_gain = jnp.sum(grad_normed * unit_first, axis=0)
    grad_first_shift = jnp.sum(grad_normed, axis=0)
    grad_source = grad_middle + normalize_back(
        grad_normed * params[0].astype(jnp.float32), unit_first, inverse_first
    )
    grads = (
        grad_first_gain,
        grad_first_shift,
        grad_joint_weight,
        grad_query_bias,
        grad_value_bias,
        grad_output_weight,
        grad_output_bias,
        grad_second_gain,
        grad_second_shift,
        grad_expand_weight,
        grad_expand_bias,
        grad_reduce_weight,
        grad_reduce_bias,
    )
    return (grad_source.astype(jnp.bfloat16), grads)


def body(
    inputs,
    cotangent,
    first_gain,
    first_shift,
    joint_weight,
    query_bias,
    value_bias,
    output_weight,
    output_bias,
    second_gain,
    second_shift,
    expand_weight,
    expand_bias,
    reduce_weight,
    reduce_bias,
):
    section_index = lax.axis_index(SECTION)
    micro_count = inputs.shape[0]
    row_count = inputs.shape[1]
    first_row = lax.axis_index(LINE) * row_count
    row_block = (first_row + jnp.arange(row_count, dtype=jnp.int32)) // BLK
    owned = (
        first_gain[0],
        first_shift[0],
        joint_weight[0],
        query_bias[0],
        value_bias[0],
        output_weight[0],
        output_bias[0],
        second_gain[0],
        second_shift[0],
        expand_weight[0],
        expand_bias[0],
        reduce_weight[0],
        reduce_bias[0],
    )
    forward_params = (
        lax.all_gather(first_gain[0], OWNERS, axis=0, tiled=True),
        lax.all_gather(first_shift[0], OWNERS, axis=0, tiled=True),
        lax.all_gather(joint_weight[0], OWNERS, axis=0, tiled=True),
        lax.all_gather(query_bias[0], OWNERS, axis=0, tiled=True),
        lax.all_gather(value_bias[0], OWNERS, axis=0, tiled=True),
        lax.all_gather(output_weight[0], OWNERS, axis=0, tiled=True),
        lax.all_gather(output_bias[0], OWNERS, axis=0, tiled=True),
        lax.all_gather(second_gain[0], OWNERS, axis=0, tiled=True),
        lax.all_gather(second_shift[0], OWNERS, axis=0, tiled=True),
        lax.all_gather(expand_weight[0], OWNERS, axis=0, tiled=True),
        lax.all_gather(expand_bias[0], OWNERS, axis=0, tiled=True),
        lax.all_gather(reduce_weight[0], OWNERS, axis=0, tiled=True),
        lax.all_gather(reduce_bias[0], OWNERS, axis=0, tiled=True),
    )
    incoming = jnp.zeros(inputs.shape[1:], jnp.bfloat16)
    section_inputs = []
    produced = []
    key_sets = []
    for tick_index in range(micro_count + 1):
        section_input = jnp.where(
            section_index == 0, inputs[min(tick_index, micro_count - 1)], incoming
        )
        source = section_input.astype(jnp.float32)
        projected = project(source, forward_params)
        gathered = (
            lax.all_gather(projected[4], LINE, axis=0, tiled=True),
            lax.all_gather(projected[5], LINE, axis=0, tiled=True),
        )
        result, unused = complete(source, forward_params, projected, gathered, row_block)
        result_low = result.astype(jnp.bfloat16)
        section_inputs.append(section_input)
        produced.append(result_low)
        key_sets.append(gathered)
        if tick_index < micro_count:
            incoming = passed_along(result_low, SECTION, 1)
    backward_params = (
        lax.all_gather(first_gain[0], OWNERS, axis=0, tiled=True),
        lax.all_gather(first_shift[0], OWNERS, axis=0, tiled=True),
        lax.all_gather(joint_weight[0], OWNERS, axis=0, tiled=True),
        lax.all_gather(query_bias[0], OWNERS, axis=0, tiled=True),
        lax.all_gather(value_bias[0], OWNERS, axis=0, tiled=True),
        lax.all_gather(output_weight[0], OWNERS, axis=0, tiled=True),
        lax.all_gather(output_bias[0], OWNERS, axis=0, tiled=True),
        lax.all_gather(second_gain[0], OWNERS, axis=0, tiled=True),
        lax.all_gather(second_shift[0], OWNERS, axis=0, tiled=True),
        lax.all_gather(expand_weight[0], OWNERS, axis=0, tiled=True),
        lax.all_gather(expand_bias[0], OWNERS, axis=0, tiled=True),
        lax.all_gather(reduce_weight[0], OWNERS, axis=0, tiled=True),
        lax.all_gather(reduce_bias[0], OWNERS, axis=0, tiled=True),
    )
    totals = tuple((jnp.zeros(piece.shape, jnp.float32) for piece in backward_params))
    shares = tuple((jnp.zeros(piece.shape, jnp.float32) for piece in owned))
    returning = jnp.zeros(inputs.shape[1:], jnp.bfloat16)
    sent_back = []
    for tick_index in range(micro_count + 1):
        upper_pick = min(tick_index + 1, micro_count)
        lower_pick = max(tick_index - 1, 0)
        section_input = jnp.where(
            section_index == 1, section_inputs[upper_pick], section_inputs[lower_pick]
        )
        upstream = jnp.where(
            section_index == 1, cotangent[min(tick_index, micro_count - 1)], returning
        ).astype(jnp.float32)
        weight_valid = jnp.where(
            section_index == 1,
            1.0 if tick_index < micro_count else 0.0,
            1.0 if tick_index >= 1 else 0.0,
        ).astype(jnp.float32)
        source = section_input.astype(jnp.float32)
        projected = project(source, backward_params)
        gathered = (
            lax.all_gather(projected[4], LINE, axis=0, tiled=True),
            lax.all_gather(projected[5], LINE, axis=0, tiled=True),
        )
        grad_source, grads = layer_backward(
            source, upstream, backward_params, projected, gathered, row_block
        )
        masked = tuple((update * weight_valid for update in grads))
        totals = tuple((running + update for running, update in zip(totals, masked)))
        sent_back.append(grad_source)
        if tick_index < micro_count:
            returning = passed_along(grad_source, SECTION, -1)
    layer_outputs = jnp.stack(
        [
            jnp.where(section_index == 0, produced[position], produced[position + 1])
            for position in range(micro_count)
        ]
    )[None]
    input_grads = jnp.stack(
        [
            jnp.where(section_index == 1, sent_back[position], sent_back[position + 1])
            for position in range(micro_count)
        ]
    )[None]
    (
        sum_first_gain,
        sum_first_shift,
        sum_joint_weight,
        sum_query_bias,
        sum_value_bias,
        sum_output_weight,
        sum_output_bias,
        sum_second_gain,
        sum_second_shift,
        sum_expand_weight,
        sum_expand_bias,
        sum_reduce_weight,
        sum_reduce_bias,
    ) = totals
    shares = (
        lax.psum_scatter(sum_first_gain, OWNERS, scatter_dimension=0, tiled=True),
        lax.psum_scatter(sum_first_shift, OWNERS, scatter_dimension=0, tiled=True),
        lax.psum_scatter(sum_joint_weight, OWNERS, scatter_dimension=0, tiled=True),
        lax.psum_scatter(sum_query_bias, OWNERS, scatter_dimension=0, tiled=True),
        lax.psum_scatter(sum_value_bias, OWNERS, scatter_dimension=0, tiled=True),
        lax.psum_scatter(sum_output_weight, OWNERS, scatter_dimension=0, tiled=True),
        lax.psum_scatter(sum_output_bias, OWNERS, scatter_dimension=0, tiled=True),
        lax.psum_scatter(sum_second_gain, OWNERS, scatter_dimension=0, tiled=True),
        lax.psum_scatter(sum_second_shift, OWNERS, scatter_dimension=0, tiled=True),
        lax.psum_scatter(sum_expand_weight, OWNERS, scatter_dimension=0, tiled=True),
        lax.psum_scatter(sum_expand_bias, OWNERS, scatter_dimension=0, tiled=True),
        lax.psum_scatter(sum_reduce_weight, OWNERS, scatter_dimension=0, tiled=True),
        lax.psum_scatter(sum_reduce_bias, OWNERS, scatter_dimension=0, tiled=True),
    )
    return (layer_outputs, input_grads) + tuple((portion[None] for portion in shares))


def flip(place, bits):
    return {1: place + 1 - 2 * (place % 2), 2: (place + 2) % 4, 3: 3 - place}[bits]


def places():
    core, ring, line = (lax.axis_index(name) for name in (SECTION, RING, LINE))
    rings = [ring] + [flip(ring, bits) for bits in (1, 2, 3)]
    lines = [line] + [flip(line, bits) for bits in (1, 2, 3)]
    toward = {
        EAST: {RING: rings[1]},
        NORTH: {RING: rings[2]},
        (LEVEL, 1): {LINE: lines[1]},
        (LEVEL, 2): {LINE: lines[2]},
        (LEVEL, 3): {LINE: lines[3]},
        (CORNER, 3): {SECTION: 1 - core, LINE: lines[3]},
        (LEVEL, UP): {LINE: (line + 1) % 4},
        (LEVEL, DOWN): {LINE: (line + 3) % 4},
        SIBLING: {SECTION: 1 - core},
    }
    return core, rings, lines, toward


def greet(toward):
    barrier = pltpu.get_barrier_semaphore()
    partners = [to for name, to in toward.items() if name not in ((LEVEL, UP), (LEVEL, DOWN))]
    for to in partners:
        pl.semaphore_signal(barrier, inc=1, device_id=to, device_id_type=pl.DeviceIdType.MESH)
    pl.semaphore_wait(barrier, len(partners))


def remote_copy(source, target, send_sem, recv_sem, to):
    return pltpu.make_async_remote_copy(
        src_ref=source,
        dst_ref=target,
        send_sem=send_sem,
        recv_sem=recv_sem,
        device_id=to,
        device_id_type=pl.DeviceIdType.MESH,
    )


def per_core(core, act):
    for index in (0, 1):

        @pl.when(core == index)
        def _():
            act(index)


GATHER_KINDS = (UP, DOWN, EAST, NORTH, CORNER, SIBLING)
GATHER_NUMBER = {kind: 4 * index for index, kind in enumerate(GATHER_KINDS)}
GATHER_SPAN = 4 * len(GATHER_KINDS)


def mm(left, right):
    return jnp.dot(left, right, preferred_element_type=F32)


def mm_nt(left, right):
    return lax.dot_general(left, right, (((1,), (1,)), ((), ())), preferred_element_type=F32)


def mm_tn(left, right):
    return lax.dot_general(left, right, (((0,), (0,)), ((), ())), preferred_element_type=F32)


def normal_parts(values):
    centre = jnp.mean(values, axis=-1, keepdims=True)
    centred = values - centre
    inverse = lax.rsqrt(jnp.mean(centred * centred, axis=-1, keepdims=True) + epsilon)
    return centred * inverse, inverse


def normal_back(upstream, unit, inverse):
    return inverse * (
        upstream
        - jnp.mean(upstream, axis=-1, keepdims=True)
        - unit * jnp.mean(upstream * unit, axis=-1, keepdims=True)
    )


def close_up(rows, table):
    high = rows.astype(LOW)
    rest = (rows - high.astype(F32)).astype(LOW)
    return mm_nt(high, table) + mm_nt(rest, table)


def head_pair(rows):
    lane = lax.broadcasted_iota(jnp.int32, rows.shape, 1)
    zero = jnp.zeros_like(rows)
    return jnp.concatenate(
        [jnp.where(lane < HDIM, rows, zero), jnp.where(lane < HDIM, zero, rows)], axis=0
    )


def from_pair(turned):
    n = turned.shape[1] // 2
    own = jnp.concatenate([turned[:HDIM, :n], turned[HDIM:, n:]], axis=0)
    return own.T


LEAD_ROWS = 144
HALF = 2176


def gather_tasks(slots, send_sem, recv_sem, copy_sem, land_sem, place_of):
    core, rings, lines, toward = place_of
    line = lines[0]
    drains = []

    def cut(t, part):
        if slots[t][1]:
            return (slice(None), pl.ds(HALF * part if isinstance(part, int) else pl.multiple_of(part * HALF, 128), HALF))
        rows = slots[t][2].shape[0]
        return (pl.ds(0, LEAD_ROWS) if part == 0 else pl.ds(LEAD_ROWS, rows - LEAD_ROWS),)

    def landed(t, part):
        _, by_columns, shard, _, land = slots[t]
        return land if by_columns else land.at[pl.ds(0, LEAD_ROWS if part == 0 else shard.shape[0] - LEAD_ROWS)]

    def run(t, act):
        if slots[t][1]:
            act(core)
        else:
            per_core(core, act)

    def place(t, part, dd, j):
        return slots[t][3].at[(rings[dd] * 4 + j,) + cut(t, part)]

    def group(t, part, dd):
        return slots[t][3].at[(pl.ds(rings[dd] * 4, 4),) + cut(t, part)]

    def copy_of(t, source, target, to, kind, j):
        index = t * GATHER_SPAN + GATHER_NUMBER[kind] + j
        return remote_copy(source, target, send_sem.at[index], recv_sem.at[index], toward[to])

    def guarded(valid, act):
        if valid is None:
            act()
        else:
            pl.when(valid)(act)

    def send(t, dd, j, to, kind, valid=None, mine=False):
        def start(part):
            target = place(t, part, dd, j)
            copy_of(t, target, target, to, kind, j).start()

        def start_mine(index):
            shard = slots[t][2].at[cut(t, index)] if index == slots[t][0] else landed(t, index)
            copy_of(t, shard, place(t, index, dd, j), to, kind, j).start()

        def finish(part):
            target = place(t, part, dd, j)
            copy_of(t, target, target, to, kind, j).wait_send()

        if mine:
            guarded(valid, lambda: per_core(core, start_mine))
        else:
            guarded(valid, lambda: run(t, start))
        drains.append(lambda: guarded(valid, lambda: run(t, finish)))

    def arrive(t, dd, j, to, kind, valid=None):
        def act(part):
            target = place(t, part, dd, j)
            copy_of(t, target, target, to, kind, j).wait_recv()

        guarded(valid, lambda: run(t, act))

    def both(one, two):
        return two if one is None else one & two

    def onward(t, j, valid, up, down, mine=False):
        if up:
            send(t, 0, j, (LEVEL, UP), UP, both(valid, line < 3), mine)
        if down:
            send(t, 0, j, (LEVEL, DOWN), DOWN, both(valid, line > 0), mine)
        send(t, 0, j, EAST, EAST, valid, mine)
        send(t, 0, j, NORTH, NORTH, valid, mine)

    def prelude():
        def give(index):
            for t, (owner, _, shard, _, land) in enumerate(slots):
                if index == owner:
                    source = shard.at[cut(t, 1 - index)]
                    remote_copy(source, landed(t, 1 - index), land_sem.at[t], land_sem.at[len(slots) + t], toward[SIBLING]).start()

        per_core(core, give)

    def taken(t):
        owner, shard = slots[t][0], slots[t][2]

        def act(index):
            target = landed(t, 1 - owner)
            copy = remote_copy(target, target, land_sem.at[t], land_sem.at[len(slots) + t], toward[SIBLING])
            if index == owner:
                copy.wait_send()
            else:
                copy.wait_recv()

        per_core(core, act)

    def local(t, index):
        source = slots[t][2].at[cut(t, index)] if index == slots[t][0] else landed(t, index)
        return pltpu.make_async_copy(source, place(t, index, 0, line), copy_sem.at[t])

    def begin(t):
        taken(t)
        onward(t, line, None, True, True, mine=True)
        per_core(core, lambda index: local(t, index).start())

    def own_ready(t):
        per_core(core, lambda index: local(t, index).wait())

    def from_line(t, offset):
        j = line + offset
        valid = j >= 0 if offset < 0 else j <= 3
        kind = UP if offset < 0 else DOWN
        arrive(t, 0, j, (LEVEL, DOWN if offset < 0 else UP), kind, valid)
        onward(t, j, valid, offset < 0, offset > 0)

    def from_side(t, offset):
        j = line + offset
        valid = None if offset == 0 else (j >= 0 if offset < 0 else j <= 3)
        even, odd = both(valid, j % 2 == 0), both(valid, j % 2 == 1)
        arrive(t, 1, j, EAST, EAST, valid)
        send(t, 1, j, NORTH, CORNER, even)
        arrive(t, 2, j, NORTH, NORTH, valid)
        send(t, 2, j, EAST, CORNER, odd)

    def from_corner(t, j):
        arrive(t, 3, j, NORTH if j % 2 == 0 else EAST, CORNER)

    def sibling(t, dd):
        def copy(part):
            return copy_of(t, group(t, part, dd), group(t, part, dd), SIBLING, SIBLING, dd)

        run(t, lambda part: copy(part).start())
        drains.append(lambda: run(t, lambda part: copy(part).wait_send()))

    def last(t):
        def act(part):
            for dd in range(4):
                target = group(t, 1 - part, dd)
                copy_of(t, target, target, SIBLING, SIBLING, dd).wait_recv()

        run(t, act)

    tasks = []

    def then(function, *given):
        tasks.append((given[0] if given else 0, lambda: function(*given)))

    count = len(slots)
    heads, tails = [], []
    for t in range(count):
        then(from_line, t, -1)
        then(from_line, t, 1)
        then(from_side, t, 0)
        for far in (2, 3):
            then(from_line, t, -far)
            then(from_line, t, far)
            then(from_side, t, 1 - far)
            then(from_side, t, far - 1)
        then(own_ready, t)
        then(sibling, t, 0)
        then(from_side, t, -3)
        then(from_side, t, 3)
        then(sibling, t, 1)
        then(sibling, t, 2)
        heads.append(list(tasks))
        tasks.clear()
        for j in range(4):
            then(from_corner, t, j)
        then(sibling, t, 3)
        then(last, t)
        tails.append(list(tasks))
        tasks.clear()
    then(prelude)
    then(begin, 0)
    if count > 1:
        then(begin, 1)
    for t in range(count):
        tasks += heads[t][:7]
        if t > 0:
            tasks += tails[t - 1]
        if t + 2 < count:
            then(begin, t + 2)
        tasks += heads[t][7:]
    tasks += tails[count - 1]

    def drain():
        for act in drains:
            act()

    return tasks, drain


def gather_outs(shards):
    shapes = []
    for _, by_columns, shard in shards:
        rows, columns = shard.shape
        land = (rows, HALF) if by_columns else (LEAD_ROWS, columns)
        shapes += [jax.ShapeDtypeStruct((16, rows, columns), LOW), jax.ShapeDtypeStruct(land, LOW)]
    return shapes


def gather_slots(forms, shards, outs):
    return [form + (shards[t], outs[2 * t], outs[2 * t + 1]) for t, form in enumerate(forms)]


def gather_semaphores(count):
    dma = pltpu.SemaphoreType.DMA
    return [dma((count * GATHER_SPAN,)), dma((count * GATHER_SPAN,)), dma((count,)), dma((2 * count,))]


def row_copies(place_of, source, target, send_sem, recv_sem, local_sem):
    core, _, lines, toward = place_of
    half = target.shape[0] // 2
    which = lines[0] // 2
    from_here = pl.ds(pl.multiple_of(core * half, half), half)
    to_there = pl.ds(pl.multiple_of(which * half, half), half)
    return (
        pltpu.make_async_copy(source.at[which, from_here], target.at[to_there], local_sem),
        remote_copy(source.at[1 - which, from_here], target.at[to_there], send_sem, recv_sem, toward[(LEVEL, 3)]),
    )


def gather_kernel(shard, *refs):
    source, outs, moved, refs = refs[0], refs[1:3], refs[3], refs[4:]
    sems, row_sems = refs[:4], refs[4:]
    place_of = places()
    greet(place_of[3])
    tasks, drain = gather_tasks(gather_slots(((0, True),), (shard,), outs), *sems, place_of)
    for _, task in tasks[:11]:
        task()
    copies = row_copies(place_of, source, moved, *row_sems)
    for copy in copies:
        copy.start()
    for _, task in tasks[11:]:
        task()
    drain()
    for copy in copies:
        copy.wait()


def gather_page(shard, source):
    anywhere = pl.BlockSpec(memory_space=pl.ANY)
    outs = gather_outs(((0, True, shard),)) + [jax.ShapeDtypeStruct(source.shape[1:], LOW)]
    dma = pltpu.SemaphoreType.DMA
    res = pl.pallas_call(
        gather_kernel,
        out_shape=tuple(outs),
        in_specs=[anywhere] * 2,
        out_specs=(anywhere,) * len(outs),
        scratch_shapes=gather_semaphores(1) + [dma(())] * 3,
        compiler_params=pltpu.CompilerParams(collective_id=0, has_side_effects=True),
        name="gather_page",
    )(shard, source)
    return res[0], res[2]


def low_place(line):
    return jnp.where(line < 2, line, 3 - line)


def forward_kernel(forms, *refs):
    count = len(forms)
    moving = count == 2
    x, vectors, wide, table, page_hbm = refs[:5]
    shards, refs = refs[5 : 5 + count], refs[5 + count :]
    if moving:
        row_source, refs = refs[0], refs[1:]
    (normed_out, query_out, here, beside, away, corner, attended_out, log_out, attended_low, middle_out,
     second_out, active_out, slope_out, result_out) = refs[:14]
    outs, refs = refs[14 : 14 + 2 * count], refs[14 + 2 * count :]
    if moving:
        row_target, row_sems, refs = refs[0], refs[-3:], refs[1:-3]
    page, expand, reduce, mixture, result, mixed, stats, page_sem, expand_sem, reduce_sem, pair_send, pair_recv = refs[:12]
    place_of = places()
    core, rings, lines, toward = place_of
    rows, width = x.shape
    half = rows // 2
    first = low_place(lines[0]) == 0

    def page_copy(i):
        at = pl.ds(pl.multiple_of(i * 256, 256), 256)
        return pltpu.make_async_copy(page_hbm.at[:, at], page.at[:, at], page_sem.at[i])

    def expand_copy(i):
        at = pl.ds(pl.multiple_of(i * 256, 256), 256)
        return pltpu.make_async_copy(outs[0].at[:, :, at], expand.at[:, :, at], expand_sem.at[i])

    def reduce_copy(i):
        rows_at = pl.ds(pl.multiple_of(i * 272, 16), 272)
        return pltpu.make_async_copy(outs[2].at[i], reduce.at[rows_at], reduce_sem.at[i])

    tiles = page.shape[1] // 256

    def begin(make, steps):
        def step(i, _):
            make(i).start()
            return 0

        lax.fori_loop(0, steps, step, 0)

    begin(page_copy, tiles)
    greet(toward)
    todo, drain = gather_tasks(gather_slots(forms, shards, outs), *refs[12:], place_of)

    def progress(many):
        for _ in range(many):
            if todo:
                todo.pop(0)[1]()

    def complete(t):
        while any(slot <= t for slot, _ in todo):
            progress(1)

    progress(2)
    unit, _ = normal_parts(x[...].astype(F32))
    normed = (unit * vectors[0:1] + vectors[1:2]).astype(LOW)
    normed_out[...] = mm(normed, table[...]).astype(LOW)

    def column(i, _):
        page_copy(i).wait()
        at = pl.ds(pl.multiple_of(i * 256, 256), 256)
        mixture[:, at] = mm(normed_out[...], page[:, at])
        return 0

    for begin_at, end in ((0, 4), (4, 8), (8, 13)):
        lax.fori_loop(begin_at, end, column, 0)
        progress(2)
    blank = jnp.zeros((rows, WIDE - width), LOW)
    here[0, :, :width] = mixture[:, width : 2 * width].astype(LOW)
    here[0, :, width:] = blank
    here[1, :, :width] = (mixture[:, 2 * width : 3 * width] + vectors[3:4]).astype(LOW)
    here[1, :, width:] = blank

    def pair_copy(source, target, to, number):
        return remote_copy(source, target, pair_send.at[number], pair_recv.at[number], toward[to])

    to_away = pair_copy(here, away, (LEVEL, 1), 0)
    to_beside = pair_copy(here, beside, SIBLING, 1)
    to_corner = pair_copy(away, corner, SIBLING, 2)
    to_away.start()
    to_beside.start()
    query = ((mixture[:, :width] + vectors[2:3]).astype(LOW).astype(F32) * HDIM ** (-0.5)).astype(LOW)
    query_out[:, :width] = query
    query_out[:, width:] = blank
    progress(1)
    to_beside.wait_recv()

    def block(kind, near, part, at):
        rows_at = pl.ds(part * half, half)
        one, two = (here, beside) if near == 0 else (away, corner)
        return jnp.concatenate([one[kind, rows_at, at], two[kind, rows_at, at]], axis=0)

    def one_unit(queries, keys, values):
        scores = mm_nt(keys, queries)
        level = jnp.max(scores, axis=0, keepdims=True)
        exponent = jnp.exp(scores - level)
        return level, jnp.sum(exponent, axis=0, keepdims=True), mm_tn(values, exponent.astype(LOW))

    def merge(units):
        peak = units[0][0]
        for level, _, _ in units[1:]:
            peak = jnp.maximum(peak, level)
        total, out = 0.0, 0.0
        for level, sums, part in units:
            share = jnp.exp(level - peak)
            total = total + share * sums
            out = out + share * part
        return peak, total, out

    def local_pair(p, _):
        at = pl.ds(pl.multiple_of(p * 128, 128), 128)
        low, high = head_pair(query_out[:half, at]), head_pair(query_out[half:, at])
        keys, values = block(0, 0, 0, at), block(1, 0, 0, at)
        bottom = one_unit(low, keys, values)
        top = merge([one_unit(high, keys, values), one_unit(high, block(0, 0, 1, at), block(1, 0, 1, at))])
        for place, (level, sums, out) in enumerate((bottom, top)):
            stats[p, 2 * place : 2 * place + 1] = level
            stats[p, 2 * place + 1 : 2 * place + 2] = sums
            mixed[p, place] = out
        return 0

    for begin_at in (0, 3, 6):
        lax.fori_loop(begin_at, begin_at + 3, local_pair, 0)
        progress(2)
    progress(8)
    to_away.wait_recv()
    to_corner.start()
    progress(2)
    to_corner.wait_recv()

    def far_pair(p, _):
        at = pl.ds(pl.multiple_of(p * 128, 128), 128)
        low, high = head_pair(query_out[:half, at]), head_pair(query_out[half:, at])
        keys, values = block(0, 1, 0, at), block(1, 1, 0, at)
        last_keys = jnp.where(first, block(0, 1, 1, at), keys)
        last_values = jnp.where(first, block(1, 1, 1, at), values)
        near = one_unit(high, keys, values)
        last = one_unit(jnp.where(first, high, low), last_keys, last_values)
        low_last = (jnp.where(first, far_below, last[0]),) + last[1:]
        high_last = (jnp.where(first, last[0], far_below),) + last[1:]

        def before(place):
            return (stats[p, 2 * place : 2 * place + 1], stats[p, 2 * place + 1 : 2 * place + 2], mixed[p, place])

        for place, units in enumerate(([before(0), low_last], [before(1), near, high_last])):
            peak, total, out = merge(units)
            attended_out[place * half : (place + 1) * half, at] = from_pair(out / total)
            log_out[p, place : place + 1] = peak + jnp.log(total)
        return 0

    for begin_at in (0, 3, 6):
        lax.fori_loop(begin_at, begin_at + 3, far_pair, 0)
        progress(2)

    def late(i, _):
        page_copy(i).wait()
        return 0

    lax.fori_loop(13, tiles, late, 0)
    lead = 4 * width - WIDE
    attended_low[...] = mm(attended_out[:, :width].astype(LOW), table[...]).astype(LOW)
    blended = mm(attended_low[...], page[:, lead:])
    middle = x[...].astype(F32) + (blended[:, 3 * width - lead :] + vectors[4:5])
    middle_out[...] = middle
    progress(2)
    unit, _ = normal_parts(middle)
    second = (unit * vectors[6:7] + vectors[7:8]).astype(LOW)
    second_out[...] = mm(second, table[...]).astype(LOW)
    result[...] = middle + vectors[5:6]

    complete(0)
    begin(expand_copy, tiles)
    if moving:
        for copy in row_copies(place_of, row_source, row_target, *row_sems):
            copy.start()

    def inner(i, _):
        at = pl.ds(pl.multiple_of(i * 256, 256), 256)
        expand_copy(i).wait()
        weights = expand[:, :, at].astype(F32).reshape(WIDE, 256).astype(LOW)
        hidden = mm(second_out[...], weights) + wide[:, at]
        below = 0.5 + 0.5 * lax.erf(hidden * 0.7071067811865476)
        active_out[:, at] = (hidden * below).astype(LOW)
        slope_out[:, at] = (below + hidden * (0.3989422804014327 * jnp.exp(-0.5 * hidden * hidden))).astype(LOW)
        return 0

    for begin_at in range(0, tiles, 2):
        lax.fori_loop(begin_at, min(begin_at + 2, tiles), inner, 0)
        progress(3)
    complete(1)
    begin(reduce_copy, 16)

    def landed(i, _):
        reduce_copy(i).wait()
        return 0

    lax.fori_loop(0, 16, landed, 0)

    def outer(i, _):
        at = pl.ds(pl.multiple_of(i * 256, 256), 256)
        result[...] += mm(active_out[:, at], reduce[at])
        return 0

    lax.fori_loop(0, tiles, outer, 0)
    result_out[...] = result[...].astype(LOW)
    progress(len(todo))
    drain()
    if moving:
        for copy in row_copies(place_of, row_source, row_target, *row_sems):
            copy.wait()
    for copy in (to_away, to_beside, to_corner):
        copy.wait_send()


def forward(x, vectors, wide, table, page, shards, moved=()):
    rows, width = x.shape
    inner = page.shape[1]
    pairs = WIDE // 128
    anywhere = pl.BlockSpec(memory_space=pl.ANY)
    inside = pl.BlockSpec(memory_space=pltpu.VMEM)

    def shape(*dims, kind=LOW):
        return jax.ShapeDtypeStruct(dims, kind)

    pair = shape(2, rows, WIDE)
    outs = [
        shape(rows, WIDE), shape(rows, WIDE), pair, pair, pair, pair, shape(rows, WIDE, kind=F32),
        shape(pairs, 2, rows, kind=F32), shape(rows, WIDE), shape(rows, width, kind=F32),
        shape(rows, WIDE), shape(rows, inner), shape(rows, inner), shape(rows, width),
    ]
    count = len(outs)
    dma = pltpu.SemaphoreType.DMA
    scratch = [
        pltpu.VMEM(page.shape, LOW), pltpu.VMEM((16, 72, inner), LOW), pltpu.VMEM((inner, width), LOW),
        pltpu.VMEM((rows, 13 * 256), F32), pltpu.VMEM((rows, width), F32),
        pltpu.VMEM((pairs, 2, 128, rows), F32), pltpu.VMEM((pairs, 4, rows), F32),
        dma((inner // 256,)), dma((inner // 256,)), dma((16,)), dma((3,)), dma((3,)),
    ] + gather_semaphores(len(shards))
    outs += gather_outs(shards)
    gathered = len(outs)
    outs += [jax.ShapeDtypeStruct(source.shape[1:], LOW) for source in moved]
    scratch += [dma(())] * (3 * len(moved))
    forms = tuple(shard[:2] for shard in shards)
    res = pl.pallas_call(
        partial(forward_kernel, forms),
        out_shape=tuple(outs),
        in_specs=[inside] * 4 + [anywhere] * (1 + len(shards) + len(moved)),
        out_specs=(inside,) * count + (anywhere,) * (len(outs) - count),
        scratch_shapes=scratch,
        compiler_params=pltpu.CompilerParams(
            collective_id=len(shards), has_side_effects=True, vmem_limit_bytes=60 << 20
        ),
        name="forward",
    )(x, vectors, wide, table, page, *(shard[2] for shard in shards), *moved)
    return res[:count], res[count:gathered:2], res[gathered:]


COLUMNS, ROWS = range(2)
SIZES = {COLUMNS: (72, 2176), ROWS: (144, 1088)}
DEPTH = 6
EASTWARD = (3, 0)
SCATTER_KINDS = (
    [(SIBLING, dd) for dd in range(4)]
    + [(ONCE, k) for k in range(4)]
    + [(EAST, k) for k in range(4)]
    + [(NORTH, k) for k in range(4)]
    + [(LEVEL, k) for k in (1, 2, 3)]
    + [(CORNER, 0)]
)
SCATTER_NUMBER = {kind: index for index, kind in enumerate(SCATTER_KINDS)}


def landing_shapes(kind):
    return [jax.ShapeDtypeStruct((many,) + SIZES[kind], LOW) for many in (16, 4, 4, 4, 4)]


def final_shape(kind):
    return jax.ShapeDtypeStruct({COLUMNS: (72, 4352), ROWS: (272, 1088)}[kind], F32)


def work_shapes(kinds):
    shapes = []
    for kind in sorted(set(kinds)):
        size = SIZES[kind]
        shapes += [pltpu.VMEM((2, 4) + size, LOW), pltpu.VMEM((DEPTH,) + size, LOW), pltpu.VMEM(size, F32)]
    count = len(kinds) * len(SCATTER_KINDS)
    return shapes + [
        pltpu.SemaphoreType.DMA((count,)), pltpu.SemaphoreType.DMA((count,)),
        pltpu.SemaphoreType.DMA((8,)), pltpu.SemaphoreType.DMA(()),
    ]


class Scatter:
    def __init__(self, kinds, pages, lands, finals, owners, refs, place_of):
        self.kinds, self.pages, self.lands, self.finals, self.owners = kinds, pages, lands, finals, owners
        self.core, self.rings, self.lines, self.toward = place_of
        self.work = {}
        for index, kind in enumerate(sorted(set(kinds))):
            self.work[kind] = refs[3 * index : 3 * index + 3]
        self.send_sem, self.recv_sem, self.load_sem, self.out_sem = refs[3 * len(self.work) :]
        self.turn = 0
        self.used = {kind: [None] * DEPTH for kind in self.work}
        self.count = {kind: 0 for kind in self.work}
        self.given, self.final_sent = [], []

    def remote(self, t, source, target, to, kind):
        index = t * len(SCATTER_KINDS) + SCATTER_NUMBER[kind]
        return remote_copy(source, target, self.send_sem.at[index], self.recv_sem.at[index], self.toward[to])

    def part(self, t, core, index, many=None):
        page, at = self.pages[t], index if many is None else pl.ds(index, many)
        if self.kinds[t] == COLUMNS:
            return page.at[at, :, pl.ds(pl.multiple_of(core * 2176, 128), 2176)]
        return page.at[pl.ds(pl.multiple_of(index * 272 + core * 128, 16), 144)]

    def landed(self, t, dd):
        return self.lands[t][0].at[pl.ds(self.rings[dd] * 4, 4)]

    def give(self, t, dd):
        base = self.rings[dd] * 4
        if self.kinds[t] == ROWS:
            for k in range(4):
                self.remote(t, self.part(t, 1 - self.core, base + k), self.lands[t][0].at[base + k], SIBLING, (SIBLING, dd)).start()
        else:
            self.remote(t, self.part(t, 1 - self.core, base, 4), self.landed(t, dd), SIBLING, (SIBLING, dd)).start()
        self.given.append(self.remote(t, self.landed(t, dd), self.landed(t, dd), SIBLING, (SIBLING, dd)))

    def arrived(self, t, ref, to, kind):
        self.remote(t, ref, ref, to, kind).wait_recv()

    def load(self, t, sources):
        loads = self.work[self.kinds[t]][0]
        slot = self.turn % 2
        self.turn += 1
        copies = []
        for j, source in enumerate(sources):
            copies.append(pltpu.make_async_copy(source, loads.at[slot, j], self.load_sem.at[slot * 4 + j]))
        for copy in copies:
            copy.start()
        return loads, slot, copies

    def add_up(self, t, loaded, store):
        loads, slot, copies = loaded
        terms = len(copies)
        for copy in copies:
            copy.wait()
        rows, columns = SIZES[self.kinds[t]]
        wide = self.kinds[t] != ROWS
        piece = min(256, columns) if wide else 16

        def step(i, _):
            at = pl.ds(pl.multiple_of(i * piece, piece), piece)
            where = (slice(None), at) if wide else (at, slice(None))
            value = loads[(slot, 0) + where].astype(F32)
            for j in range(1, terms):
                value = value + loads[(slot, j) + where].astype(F32)
            store(where, value)
            return 0

        steps = (columns if wide else rows) // piece
        lax.fori_loop(0, steps, step, 0)
        if wide and steps * piece < columns:
            where = (slice(None), pl.ds(steps * piece, columns - steps * piece))
            value = loads[(slot, 0) + where].astype(F32)
            for j in range(1, terms):
                value = value + loads[(slot, j) + where].astype(F32)
            store(where, value)

    def sources(self, t, dd, k, extra):
        index = self.rings[dd] * 4 + self.lines[k]
        return [self.part(t, self.core, index), self.lands[t][0].at[index]] + extra

    def sum_and_send(self, t, dd, k, extra, target, to, kind):
        form = self.kinds[t]
        loaded = self.load(t, self.sources(t, dd, k, extra))

        def finish():
            place = self.count[form] % DEPTH
            self.count[form] += 1
            if self.used[form][place] is not None:
                self.used[form][place].wait_send()
            out = self.work[form][1]

            def store(where, value):
                out[(place,) + where] = value.astype(out.dtype)

            self.add_up(t, loaded, store)
            copy = self.remote(t, out.at[place], target, to, kind)
            copy.start()
            self.used[form][place] = copy

        return finish

    def first(self, t, k):
        if k == 3:
            self.arrived(t, self.landed(t, 3), SIBLING, (SIBLING, 3))
        to = EAST if k in EASTWARD else NORTH
        return self.sum_and_send(t, 3, k, [], self.lands[t][1].at[k], to, (ONCE, k))

    def second(self, t, dd, k):
        if (dd, k) in ((1, 3), (2, 2)):
            self.arrived(t, self.landed(t, dd), SIBLING, (SIBLING, dd))
        to, land = (EAST, self.lands[t][2]) if dd == 1 else (NORTH, self.lands[t][3])
        extra = []
        if (dd == 1) != (k in EASTWARD):
            one = self.lands[t][1].at[k]
            self.arrived(t, one, EAST if k in EASTWARD else NORTH, (ONCE, k))
            extra = [one]
        return self.sum_and_send(t, dd, k, extra, land.at[k], to, (to, k))

    def third(self, t, k):
        if k == 3:
            self.arrived(t, self.landed(t, 0), SIBLING, (SIBLING, 0))
        extra = []
        for to, land in ((EAST, self.lands[t][2]), (NORTH, self.lands[t][3])):
            self.arrived(t, land.at[k], to, (to, k))
            extra.append(land.at[k])
        if k:
            return self.sum_and_send(t, 0, k, extra, self.lands[t][4].at[k], (LEVEL, k), (LEVEL, k))
        loaded = self.load(t, self.sources(t, 0, 0, extra))
        total = self.work[self.kinds[t]][2]

        def store(where, value):
            total[where] = value

        return lambda: self.add_up(t, loaded, store)

    def final_part(self, t, core):
        if self.kinds[t] == COLUMNS:
            return (slice(None), slice(None)), (slice(None), pl.ds(2176 * core, 2176))
        return (pl.ds(16 * core, 144 - 16 * core),), (pl.ds(144 * core, 144 - 16 * core),)

    def last(self, t):
        land = self.lands[t][4]
        for k in (1, 2, 3):
            self.arrived(t, land.at[k], (LEVEL, k), (LEVEL, k))
        loaded = self.load(t, [land.at[k] for k in (1, 2, 3)])
        total = self.work[self.kinds[t]][2]
        owner = self.owners[t]

        def store(where, value):
            total[where] = total[where] + value

        def act(core):
            inner, outer = self.final_part(t, core)
            source, target = total.at[inner], self.finals[t].at[outer]
            if core == owner:
                copy = pltpu.make_async_copy(source, target, self.out_sem)
                copy.start()
                copy.wait()
                theirs = self.finals[t].at[self.final_part(t, 1 - core)[1]]
                self.remote(t, theirs, theirs, SIBLING, (CORNER, 0)).wait_recv()
            else:
                copy = self.remote(t, source, target, SIBLING, (CORNER, 0))
                copy.start()
                copy.wait_send()

        def finish():
            self.add_up(t, loaded, store)
            per_core(self.core, act)

        return finish

    def give_all(self, t):
        for dd in (3, 1, 2, 0):
            self.give(t, dd)

    def steps(self, t):
        def of(waits, function, *given):
            return waits, lambda: function(*given)

        ways = ((1, 3), (2, 2), (1, 0), (2, 1), (1, 2), (2, 3), (1, 1), (2, 0))
        return (
            [of(k == 3, self.first, t, k) for k in (3, 2, 0, 1)],
            [of((dd == 1) != (k in EASTWARD), self.second, t, dd, k) for dd, k in ways],
            [of(True, self.third, t, k) for k in (3, 2, 1, 0)],
            [of(True, self.last, t)],
        )

    def drain(self):
        for copy in self.given:
            copy.wait_send()
        for held in self.used.values():
            for copy in held:
                if copy is not None:
                    copy.wait_send()


def in_turn(earlier, later, done=()):
    return later[0] + earlier[2][:2] + later[1][:4] + earlier[2][2:] + list(done) + later[1][4:]


def tiny_shapes():
    return [
        pltpu.VMEM((16, 16, 128), F32), pltpu.VMEM((16, 16, 128), F32), pltpu.VMEM((2, 4, 16, 128), F32),
        pltpu.VMEM((4, 16, 128), F32), pltpu.VMEM((3, 16, 128), F32),
        pltpu.SemaphoreType.DMA((7,)), pltpu.SemaphoreType.DMA((7,)),
    ]


def tiny_steps(both, final, refs, place_of):
    total, land, land_east, land_north, land_line, send_sem, recv_sem = refs
    core, rings, lines, toward = place_of
    blocks = [pl.ds(rings[dd] * 4, 4) for dd in range(4)]

    def copy(number, source, target, to):
        return remote_copy(source, target, send_sem.at[number], recv_sem.at[number], toward[to])

    over = copy(0, both.at[1 - core], land, SIBLING)
    east = [copy(1 + i, total.at[blocks[dd]], land_east.at[i], EAST) for i, dd in enumerate((1, 3))]
    north = copy(3, total.at[blocks[2]], land_north, NORTH)
    line = [copy(3 + k, total.at[rings[0] * 4 + lines[k]], land_line.at[k - 1], (LEVEL, k)) for k in (1, 2, 3)]

    def zero():
        over.start()
        return lambda: None

    def one():
        over.wait_recv()
        total[...] = both[core] + land[...]
        for each in east:
            each.start()
        return lambda: None

    def two():
        for i, each in enumerate(east):
            each.wait_recv()
            total[blocks[2 * i]] = total[blocks[2 * i]] + land_east[i]
        north.start()
        return lambda: None

    def three():
        north.wait_recv()
        total[blocks[0]] = total[blocks[0]] + land_north[...]
        for each in line:
            each.start()
        return lambda: None

    def four():
        value = total[rings[0] * 4 + lines[0]]
        for i, each in enumerate(line):
            each.wait_recv()
            value = value + land_line[i]
        final[...] = value
        for each in [over, north] + east + line:
            each.wait_send()
        return lambda: None

    return [(True, step) for step in (zero, one, two, three, four)]


def backward_kernel(carried, *refs):
    (top, x, vectors, table, normed_in, query, here, beside, away, corner, attended, logs, attended_low, middle,
     second, active, slope) = refs[:17]
    page_hbm, expand_hbm, reduce_hbm = refs[17:20]
    refs = refs[20:]
    passed, refs = refs[0], refs[1:]
    if carried:
        passed_small, refs = refs[0], refs[1:]
    result_out, small_out, page_reduce, page_expand, page_attention, shipped = refs[:6]
    refs = refs[6:]
    kinds = (COLUMNS, ROWS, COLUMNS, COLUMNS) if carried else (ROWS, COLUMNS)
    owners = (1, 0, 0, 0) if carried else (1, 1)
    pages = (page_reduce, page_expand)
    if carried:
        pages = (passed, page_reduce, page_expand, page_attention)
    n = len(kinds)
    finals, refs = refs[:n], refs[n:]
    lands, refs = [refs[5 * t : 5 * t + 5] for t in range(n)], refs[5 * n :]
    (reduce_ring, expand_ring, output, second_sum, left_one, left_two, stage_wide, stage_tall, wide_sum, query_sum,
     here_sum, beside_give, away_give, corner_give, beside_got, away_got, corner_got, hidden_all, mixture, grad_middle,
     grad_attended, sums, both, reduce_sem, expand_sem, output_sem, wide_sem, tall_sem, pair_send, pair_recv, ship_send, ship_recv, ship_sem) = refs[:33]
    place_of = places()
    core, rings, lines, toward = place_of
    tiny_refs, refs = refs[33:40], refs[40:]
    scatter = Scatter(kinds, pages, lands, finals, owners, refs, place_of)
    rows, width = top.shape
    half = rows // 2
    first = low_place(lines[0]) == 0
    tiles = expand_hbm.shape[1] // 256
    lead = 4 * width - WIDE
    edge = 3 * width

    def tile_at(i):
        return pl.ds(pl.multiple_of(i * 256, 256), 256)

    def reduce_copy(i):
        slot = lax.rem(i, 3)
        return pltpu.make_async_copy(reduce_hbm.at[tile_at(i)], reduce_ring.at[slot], reduce_sem.at[slot])

    def expand_copy(i, source):
        slot = lax.rem(i, 3)
        return pltpu.make_async_copy(source.at[:, tile_at(i)], expand_ring.at[slot], expand_sem.at[slot])

    def wide_copy(i, target):
        slot = lax.rem(i, 2)
        return pltpu.make_async_copy(stage_wide.at[slot], target.at[:, :, tile_at(i)], wide_sem.at[slot])

    def tall_copy(i):
        slot = lax.rem(i, 2)
        return pltpu.make_async_copy(stage_tall.at[slot], page_reduce.at[tile_at(i)], tall_sem.at[slot])

    for i in range(3):
        reduce_copy(i).start()
        expand_copy(i, expand_hbm).start()
    output_copy = pltpu.make_async_copy(page_hbm.at[:, pl.ds(lead, WIDE)], output, output_sem)
    output_copy.start()
    greet(toward)
    todo, open_ends = [], []

    def progress(count):
        for _ in range(count):
            if todo:
                waits, begin = todo.pop(0)
                if waits and open_ends:
                    open_ends.pop()()
                ended = begin()
                if open_ends:
                    open_ends.pop()()
                open_ends.append(ended)

    which = lines[0] // 2
    mine = pl.ds(pl.multiple_of(core * half, half), half)
    other = pl.ds(pl.multiple_of((1 - core) * half, half), half)
    near_rows = pl.ds(pl.multiple_of(which * half, half), half)
    far_rows = pl.ds(pl.multiple_of((1 - which) * half, half), half)

    def ship_copies(rows_ref):
        target = shipped.at[which, mine]
        near, away = rows_ref.at[near_rows], rows_ref.at[far_rows]
        ways = ((near, SIBLING), (away, (LEVEL, 3)), (away, (CORNER, 3)))
        remote = [
            remote_copy(source, target, ship_send.at[index], ship_recv.at[index], toward[to])
            for index, (source, to) in enumerate(ways)
        ]
        return pltpu.make_async_copy(near, target, ship_sem), remote

    def ship(layer, rows_ref):
        local, remote = ship_copies(rows_ref)

        def act(index):
            for copy in (local, remote[1]) if index == layer else (remote[0], remote[2]):
                copy.start()

        per_core(core, act)

    def shipped_all():
        local, remote = ship_copies(top)
        local.wait()
        for index, (sequence, part) in enumerate(((which, other), (1 - which, mine), (1 - which, other))):
            remote[index].wait_send()
            ref = shipped.at[sequence, part]
            remote_copy(ref, ref, ship_send.at[index], ship_recv.at[index], toward[SIBLING]).wait_recv()

    steps = [scatter.steps(t) for t in range(n)]
    if carried:
        scatter.give_all(0)
        todo += steps[0][0] + steps[0][1]
        ship(1, top)
    else:
        ship(0, x)
        ship(1, passed)
    second_sum[...] = jnp.zeros_like(second_sum)

    def tall_tile(i, _):
        side = lax.rem(i, 2)

        @pl.when(i >= 2)
        def _():
            tall_copy(i - 2).wait()

        stage_tall[side] = mm_tn(active[:, tile_at(i)], top[...]).astype(LOW)
        tall_copy(i).start()
        return 0

    def tall_page(t):
        for begin_at in range(0, tiles, 6):
            lax.fori_loop(begin_at, min(begin_at + 6, tiles), tall_tile, 0)
            progress(1)
        for i in (tiles - 2, tiles - 1):
            tall_copy(i).wait()
        scatter.give_all(t)

    def wide_tile(i, _):
        side = lax.rem(i, 2)

        @pl.when(i >= 2)
        def _():
            wide_copy(i - 2, page_expand).wait()

        stage_wide[side] = mm(left_one[...], hidden_all[:, tile_at(i)]).reshape(16, 72, 256).astype(LOW)
        wide_copy(i, page_expand).start()
        return 0

    def wide_page(t):
        for begin_at in range(0, tiles, 5):
            lax.fori_loop(begin_at, min(begin_at + 5, tiles), wide_tile, 0)
            progress(1)
        for i in (tiles - 2, tiles - 1):
            wide_copy(i, page_expand).wait()
        scatter.give_all(t)

    if not carried:
        tall_page(0)
        todo += steps[0][0] + steps[0][1]
    left_one[...] = second[...].T

    def feed_tile(i, _):
        at = tile_at(i)
        slot = lax.rem(i, 3)
        reduce_copy(i).wait()
        hidden = (mm_nt(top[...], reduce_ring[slot]) * slope[:, at].astype(F32)).astype(LOW)
        wide_sum[0:1, at] = jnp.sum(hidden.astype(F32), axis=0, keepdims=True)
        hidden_all[:, at] = hidden
        expand_copy(i, expand_hbm).wait()
        second_sum[...] += mm_nt(hidden, expand_ring[slot])

        @pl.when(i + 3 < tiles)
        def _():
            reduce_copy(i + 3).start()
            expand_copy(i + 3, expand_hbm).start()

        return 0

    for begin_at in range(0, tiles, 3):
        lax.fori_loop(begin_at, min(begin_at + 3, tiles), feed_tile, 0)
        progress(1)
    for i in range(3):
        expand_copy(i, page_hbm).start()

    def row(value):
        return jnp.sum(value, axis=0, keepdims=True)

    upstream = top[...].astype(F32)
    grad_second = close_up(second_sum[...], table[...])
    unit, inverse = normal_parts(middle[...])
    sums[6:7] = row(grad_second * unit)
    sums[7:8] = row(grad_second)
    sums[5:6] = row(upstream)
    value = upstream + normal_back(grad_second * vectors[6:7], unit, inverse)
    grad_middle[...] = value
    branch = value.astype(LOW)
    sums[4:5] = row(branch.astype(F32))
    progress(1)
    mixture[:, edge:] = branch
    output_copy.wait()
    full = jnp.concatenate([jnp.zeros((rows, edge - lead), LOW), branch], axis=1)
    pulled = mm_nt(full, output[...]).astype(LOW)
    grad_attended[:, :width] = mm_nt(pulled, table[...]).astype(LOW)
    grad_attended[:, width:] = jnp.zeros((rows, WIDE - width), LOW)
    progress(1)

    def rows_of(place, at, p):
        part = slice(place * half, (place + 1) * half)
        product = (grad_attended[part, at].astype(F32) * attended[part, at]).T
        delta = jnp.concatenate([row(product[:HDIM]), row(product[HDIM:])], axis=1)
        return head_pair(query[part, at]), head_pair(grad_attended[part, at]), logs[p, place : place + 1], delta

    def block(kind, near, part, at):
        rows_at = pl.ds(part * half, half)
        one, two = (here, beside) if near == 0 else (away, corner)
        return jnp.concatenate([one[kind, rows_at, at], two[kind, rows_at, at]], axis=0)

    def back(own, keys, values):
        queries, grads, log, delta = own
        weights = jnp.exp(mm_nt(keys, queries) - log)
        lowered = (weights * (mm_nt(values, grads) - delta)).astype(LOW)
        return mm_tn(keys, lowered), mm(lowered, queries), mm(weights.astype(LOW), grads)

    def put(one, two, part, at, grads):
        rows_at = pl.ds(part * half, half)
        for kind, value in enumerate(grads):
            one[kind, rows_at, at] = value[:half].astype(one.dtype)
            two[kind, rows_at, at] = value[half:].astype(two.dtype)

    def far_pair(p, _):
        at = pl.ds(pl.multiple_of(p * 128, 128), 128)
        low, high = rows_of(0, at, p), rows_of(1, at, p)
        last_rows = tuple(jnp.where(first, b, a) for a, b in zip(low, high))
        keys, values = block(0, 1, 0, at), block(1, 1, 0, at)
        high_query, keys_a, values_a = back(high, keys, values)
        last_keys = jnp.where(first, block(0, 1, 1, at), keys)
        last_values = jnp.where(first, block(1, 1, 1, at), values)
        more, keys_b, values_b = back(last_rows, last_keys, last_values)
        zero, empty = jnp.zeros_like(keys_b), jnp.zeros_like(more)
        put(away_give, corner_give, 0, at,
            (keys_a + jnp.where(first, zero, keys_b), values_a + jnp.where(first, zero, values_b)))
        put(away_give, corner_give, 1, at, (jnp.where(first, keys_b, zero), jnp.where(first, values_b, zero)))
        query_sum[:half, at] = from_pair(jnp.where(first, empty, more))
        query_sum[half:, at] = from_pair(high_query + jnp.where(first, more, empty))
        return 0

    for begin_at in (0, 3, 6):
        lax.fori_loop(begin_at, begin_at + 3, far_pair, 0)
        progress(1)

    def pair_copy(source, target, to, number):
        return remote_copy(source, target, pair_send.at[number], pair_recv.at[number], toward[to])

    to_corner = pair_copy(corner_give, corner_got, SIBLING, 0)
    to_away = pair_copy(away_give, away_got, (LEVEL, 1), 1)
    to_beside = pair_copy(beside_give, beside_got, SIBLING, 2)
    to_corner.start()

    def near_pair(p, _):
        at = pl.ds(pl.multiple_of(p * 128, 128), 128)
        low, high = rows_of(0, at, p), rows_of(1, at, p)
        keys, values = block(0, 0, 0, at), block(1, 0, 0, at)
        low_query, keys_a, values_a = back(low, keys, values)
        high_query, keys_b, values_b = back(high, keys, values)
        put(here_sum, beside_give, 0, at, (keys_a + keys_b, values_a + values_b))
        more, keys_a, values_a = back(high, block(0, 0, 1, at), block(1, 0, 1, at))
        put(here_sum, beside_give, 1, at, (keys_a, values_a))
        query_sum[:half, at] += from_pair(low_query)
        query_sum[half:, at] += from_pair(high_query + more)
        return 0

    lax.fori_loop(0, 2, near_pair, 0)
    to_corner.wait_recv()
    for kind in (0, 1):
        away_give[kind] = (away_give[kind].astype(F32) + corner_got[kind].astype(F32)).astype(LOW)
    to_away.start()
    progress(1)
    for begin_at, end in ((2, 5), (5, 9)):
        lax.fori_loop(begin_at, end, near_pair, 0)
        progress(1)
    to_beside.start()
    if carried:
        tall_page(1)
        todo += in_turn(steps[0], steps[1])
        wide_page(2)
        todo += in_turn(steps[1], steps[2], steps[0][3])
    else:
        wide_page(1)
        todo += in_turn(steps[0], steps[1])
    low = (query_sum[:, :width] * HDIM ** (-0.5)).astype(LOW)
    mixture[:, :width] = low
    sums[2:3] = row(low.astype(F32))
    left_one[...] = normed_in[...].T
    left_two[...] = attended_low[...].T
    second_sum[...] = jnp.zeros_like(second_sum)
    progress(4)
    to_beside.wait_recv()
    to_away.wait_recv()
    for kind in (0, 1):
        value = here_sum[kind] + beside_got[kind].astype(F32) + away_got[kind].astype(F32)
        low = value[:, :width].astype(LOW)
        mixture[:, (1 + kind) * width : (2 + kind) * width] = low
    sums[3:4] = row(low.astype(F32))

    def project_tile(i, _):
        at = tile_at(i)
        slot = lax.rem(i, 3)
        column = i * 256 + lax.broadcasted_iota(jnp.int32, (rows, 256), 1)
        part = mixture[:, at]
        part = jnp.where(column < edge, part, jnp.zeros_like(part))
        expand_copy(i, page_hbm).wait()
        second_sum[...] += mm_nt(part, expand_ring[slot])

        @pl.when(i + 3 < 13)
        def _():
            expand_copy(i + 3, page_hbm).start()

        return 0

    for begin_at, end in ((0, 4), (4, 8), (8, 13)):
        lax.fori_loop(begin_at, end, project_tile, 0)
        progress(1)
    grad_normed = close_up(second_sum[...], table[...])
    unit, inverse = normal_parts(x[...].astype(F32))
    sums[0:1] = row(grad_normed * unit)
    sums[1:2] = row(grad_normed)
    result_out[...] = (grad_middle[...] + normal_back(grad_normed * vectors[0:1], unit, inverse)).astype(LOW)
    if carried:
        ship(0, result_out)
    progress(2)

    def page_tile(number, i):
        side = lax.rem(i, 2)
        at = tile_at(i)

        @pl.when(i >= 2)
        def _():
            wide_copy(i - 2, page_attention).wait()

        part = mixture[:, at]
        if number == 1:
            value = mm(left_one[...], part)
        elif number == 2:
            value = mm(left_two[...], part)
        else:
            column = i * 256 + lax.broadcasted_iota(jnp.int32, (rows, 256), 1)
            zero = jnp.zeros_like(part)
            value = mm(left_one[...], jnp.where(column < edge, part, zero))
            value = value + mm(left_two[...], jnp.where(column < edge, zero, part))
        stage_wide[side] = value.reshape(16, 72, 256).astype(LOW)
        wide_copy(i, page_attention).start()

    def page_loop(number, begin_at, end):
        def step(i, _):
            page_tile(number, i)
            return 0

        lax.fori_loop(begin_at, end, step, 0)

    whole_tiles = edge // 256
    for begin_at in range(0, whole_tiles, 4):
        page_loop(1, begin_at, begin_at + 4)
        progress(1)
    page_loop(3, whole_tiles, whole_tiles + 1)
    page_loop(2, whole_tiles + 1, tiles)
    for i in (tiles - 2, tiles - 1):
        wide_copy(i, page_attention).wait()
    if carried:
        scatter.give_all(3)
    small = both.at[0] if carried else small_out
    small[...] = jnp.zeros(small.shape, F32)
    for shard in range(16):
        small[shard, 0:8, 0:68] = sums[:, shard * 68 : (shard + 1) * 68]
        for part in range(4):
            begin_at = shard * 272 + part * 68
            small[shard, 8 + part : 9 + part, 0:68] = wide_sum[0:1, begin_at : begin_at + 68]
    if carried:
        both[1] = passed_small[...]
        tiny, own = tiny_steps(both, small_out, tiny_refs, place_of), steps[3]
        todo += in_turn(steps[2], own, steps[1][3])
        todo = tiny[:1] + todo[:3] + tiny[1:2] + todo[3:6] + tiny[2:3] + todo[6:9] + tiny[3:4] + todo[9:12] + tiny[4:] + todo[12:]
        todo = todo + own[2][:3] + steps[2][3] + own[2][3:] + own[3]
    else:
        todo += steps[1][2] + steps[0][3] + steps[1][3]
    progress(len(todo))
    open_ends.pop()()
    scatter.drain()
    shipped_all()
    for copy in (to_corner, to_away, to_beside):
        copy.wait_send()


def backward(top, saved, vectors, table, page, expand, reduce, *passed):
    source, normed, query = saved[:3]
    rows, width = top.shape
    inner = expand.shape[1]
    anywhere = pl.BlockSpec(memory_space=pl.ANY)
    inside = pl.BlockSpec(memory_space=pltpu.VMEM)
    carried = len(passed) == 2
    kinds = (COLUMNS, ROWS, COLUMNS, COLUMNS) if carried else (ROWS, COLUMNS)
    outs = [
        jax.ShapeDtypeStruct((rows, width), LOW), jax.ShapeDtypeStruct((16, 128) if carried else (16, 16, 128), F32),
        jax.ShapeDtypeStruct(reduce.shape, LOW), jax.ShapeDtypeStruct((16, 72, inner), LOW),
        jax.ShapeDtypeStruct((16, 72, inner), LOW), jax.ShapeDtypeStruct((2, rows, width), LOW),
    ]
    outs += [final_shape(kind) for kind in kinds]
    for kind in kinds:
        outs += landing_shapes(kind)
    pair = pltpu.VMEM((2, rows, WIDE), LOW)
    tall = pltpu.VMEM((WIDE, rows), LOW)
    dma = pltpu.SemaphoreType.DMA
    scratch = [
        pltpu.VMEM((3, 256, width), LOW), pltpu.VMEM((3, WIDE, 256), LOW), pltpu.VMEM((WIDE, WIDE), LOW),
        pltpu.VMEM((rows, WIDE), F32), tall, tall, pltpu.VMEM((2, 16, 72, 256), LOW), pltpu.VMEM((2, 256, width), LOW),
        pltpu.VMEM((8, inner), F32), pltpu.VMEM((rows, WIDE), F32), pltpu.VMEM((2, rows, WIDE), F32),
        pair, pair, pair, pair, pair, pair, pltpu.VMEM((rows, inner), LOW), pltpu.VMEM((rows, inner), LOW),
        pltpu.VMEM((rows, width), F32), pltpu.VMEM((rows, WIDE), LOW), pltpu.VMEM((8, width), F32),
        pltpu.VMEM((2, 16, 16, 128), F32), dma((3,)), dma((3,)), dma(()), dma((2,)), dma((2,)), dma((3,)), dma((3,)),
        dma((3,)), dma((3,)), dma(()),
    ] + tiny_shapes() + work_shapes(kinds)
    res = pl.pallas_call(
        partial(backward_kernel, carried),
        out_shape=tuple(outs),
        in_specs=[inside] * 17 + [anywhere] * 4 + [inside] * (len(passed) - 1),
        out_specs=(inside,) * 2 + (anywhere,) * (len(outs) - 2),
        scratch_shapes=scratch,
        compiler_params=pltpu.CompilerParams(
            collective_id=4 if carried else 5, has_side_effects=True, vmem_limit_bytes=62 << 20
        ),
        name="backward_sum" if carried else "backward",
    )(top, source, vectors, table, *saved[1:], page, expand, reduce, *passed)
    return res[0], (res[4], res[1]), res[5][None], res[6 : 6 + len(kinds)]


def spread(width):
    row = lax.broadcasted_iota(jnp.int32, (width, 16 * 72), 0)
    column = lax.broadcasted_iota(jnp.int32, (width, 16 * 72), 1)
    same = (row // 68 == column // 72) & (row % 68 == column % 72)
    return same.astype(LOW)


def small_of(page):
    part = page[:, 68, : 12 * 68].astype(F32).reshape(16, 12, 68).transpose(1, 0, 2)
    return part[:8].reshape(8, -1), part[8:].transpose(1, 0, 2).reshape(1, -1)


def four_by_four(
    inputs,
    cotangent,
    first_gain,
    first_shift,
    joint_weight,
    query_bias,
    value_bias,
    output_weight,
    output_bias,
    second_gain,
    second_shift,
    expand_weight,
    expand_bias,
    reduce_weight,
    reduce_bias,
):
    core = lax.axis_index(SECTION)
    width = HEADS * HDIM
    packed = jnp.concatenate(
        [
            first_gain[0],
            first_shift[0],
            query_bias[0],
            value_bias[0],
            output_bias[0],
            reduce_bias[0],
            second_gain[0],
            second_shift[0],
            expand_bias[0],
        ]
    )
    packed = jnp.pad(packed[None], ((0, 3), (0, 4 * width - packed.shape[0])))
    attention_shard = jnp.concatenate(
        [jnp.concatenate([joint_weight[0], output_weight[0]], axis=1), packed], axis=0
    )
    expand_shard = jnp.pad(expand_weight[0], ((0, 4), (0, 0)))
    reduce_shard = reduce_weight[0]
    table = spread(width)

    def flat(page):
        return page.reshape(-1, page.shape[2])

    lower_page, rows = gather_page(attention_shard, inputs)
    small, wide = small_of(lower_page)
    shards = ((0, True, expand_shard), (0, False, reduce_shard), (1, True, attention_shard))
    saved, (lower_expand, lower_reduce, upper_page), _ = forward(rows, small, wide, table, flat(lower_page), shards)
    weights = (flat(lower_page), flat(lower_expand), flat(lower_reduce))
    saved_lower, middle_rows = (rows,) + tuple(saved[:13]), saved[13]
    upper_small, upper_wide = small_of(upper_page)
    shards = ((1, True, expand_shard), (1, False, reduce_shard))
    saved, (upper_expand, upper_reduce), (top,) = forward(
        middle_rows, upper_small, upper_wide, table, flat(upper_page), shards, (cotangent,)
    )
    upper_weights = (flat(upper_page), flat(upper_expand), flat(upper_reduce))
    saved_upper, final_rows = (middle_rows,) + tuple(saved[:13]), saved[13]
    upper_grad, upper_pages, layer_outputs, upper_sums = backward(
        top, saved_upper, upper_small, table, *upper_weights, final_rows
    )
    _, (_, vectors), input_grads, lower_sums = backward(
        upper_grad, saved_lower, small, table, *weights, *upper_pages
    )
    own = core == 0
    attention_sum = jnp.where(own, lower_sums[3], lower_sums[0])
    expand_sum = jnp.where(own, lower_sums[2], upper_sums[1])
    reduce_sum = jnp.where(own, lower_sums[1], upper_sums[0])
    vectors = vectors[:12, :68]
    return (
        layer_outputs,
        input_grads,
        vectors[0][None],
        vectors[1][None],
        attention_sum[None, :68, : 3 * width],
        vectors[2][None],
        vectors[3][None],
        attention_sum[None, :68, 3 * width :],
        vectors[4][None],
        vectors[6][None],
        vectors[7][None],
        expand_sum[None, :68],
        vectors[8:].reshape(1, -1),
        reduce_sum[None],
        vectors[5][None],
    )


def fits(mesh):
    return dict(mesh.shape) == {SECTION: 2, RING: 4, LINE: 4}


def solution(mesh):
    return jax.shard_map(
        four_by_four if fits(mesh) else body,
        mesh=mesh,
        in_specs=(
            P(RING, LINE, None),
            P(RING, LINE, None),
            P(SECTION, OWNERS),
            P(SECTION, OWNERS),
            P(SECTION, OWNERS, None),
            P(SECTION, OWNERS),
            P(SECTION, OWNERS),
            P(SECTION, OWNERS, None),
            P(SECTION, OWNERS),
            P(SECTION, OWNERS),
            P(SECTION, OWNERS),
            P(SECTION, OWNERS, None),
            P(SECTION, OWNERS),
            P(SECTION, OWNERS, None),
            P(SECTION, OWNERS),
        ),
        out_specs=(
            P(SECTION, RING, LINE, None),
            P(SECTION, RING, LINE, None),
            P(SECTION, OWNERS),
            P(SECTION, OWNERS),
            P(SECTION, OWNERS, None),
            P(SECTION, OWNERS),
            P(SECTION, OWNERS),
            P(SECTION, OWNERS, None),
            P(SECTION, OWNERS),
            P(SECTION, OWNERS),
            P(SECTION, OWNERS),
            P(SECTION, OWNERS, None),
            P(SECTION, OWNERS),
            P(SECTION, OWNERS, None),
            P(SECTION, OWNERS),
        ),
        check_vma=False,
    )
```

```python
from functools import partial

import jax
import jax.numpy as jnp
import numpy as np
from jax import lax
from jax.experimental import pallas as pl
from jax.experimental.pallas import tpu as pltpu
from jax.sharding import PartitionSpec as P

HEADS = 17
HDIM = 64
BLK = 256
WIDE = 1152
F32, LOW = jnp.float32, jnp.bfloat16
SECTION, RING, LINE = "section", "dp", "seq"
OWNERS = (RING, LINE)
EAST, NORTH, LEVEL, SIBLING, CORNER, ONCE, UP, DOWN = range(8)


epsilon = 1e-05
far_below = -1e30


def passed_along(value, axis, steps):
    count = lax.axis_size(axis)
    first, last = (max(0, -steps), min(count, count - steps))
    return lax.ppermute(value, axis, [(source, source + steps) for source in range(first, last)])


def normalize(values, scales, offsets):
    centre = jnp.mean(values, axis=-1, keepdims=True)
    centred = values - centre
    inverse = lax.rsqrt(jnp.mean(centred * centred, axis=-1, keepdims=True) + epsilon)
    unit_rows = centred * inverse
    return (unit_rows * scales + offsets, unit_rows, inverse)


def normalize_back(upstream, unit_rows, inverse):
    return inverse * (
        upstream
        - jnp.mean(upstream, axis=-1, keepdims=True)
        - unit_rows * jnp.mean(upstream * unit_rows, axis=-1, keepdims=True)
    )


def score_block(query, key_block, block_index, row_block):
    scores = jnp.einsum(
        "qhd,khd->qhk", query, key_block, preferred_element_type=jnp.float32
    ) * HDIM ** (-0.5)
    highest = jnp.max(scores, axis=-1)
    allowed = (block_index <= row_block)[:, None]
    exponent = jnp.exp(scores - highest[..., None]) * allowed[..., None].astype(jnp.float32)
    levels = jnp.where(allowed, highest, far_below)
    return (exponent, levels)


def attend_forward(query, keys_all, values_all, row_block):
    length = keys_all.shape[0]
    row_count = query.shape[0]
    key_shaped = keys_all.reshape(length, HEADS, HDIM)
    value_shaped = values_all.reshape(length, HEADS, HDIM)
    block_limit = row_block[-1] + 1

    def advance(block_index, carried):
        running_peak, running_sum, weighted = carried
        key_block = lax.dynamic_slice_in_dim(key_shaped, block_index * BLK, BLK, 0)
        value_block = lax.dynamic_slice_in_dim(value_shaped, block_index * BLK, BLK, 0)
        exponent, levels = score_block(query, key_block, block_index, row_block)
        weights = exponent.astype(jnp.bfloat16)
        block_out = jnp.einsum(
            "qhk,khd->qhd", weights, value_block, preferred_element_type=jnp.float32
        )
        newest_peak = jnp.maximum(running_peak, levels)
        shrink_old = jnp.exp(running_peak - newest_peak)
        shrink_new = jnp.exp(levels - newest_peak)
        running_sum = running_sum * shrink_old + shrink_new * jnp.sum(exponent, axis=-1)
        weighted = weighted * shrink_old[..., None] + shrink_new[..., None] * block_out
        return (newest_peak, running_sum, weighted)

    initial = (
        jnp.full((row_count, HEADS), far_below, jnp.float32),
        jnp.zeros((row_count, HEADS), jnp.float32),
        jnp.zeros((row_count, HEADS, HDIM), jnp.float32),
    )
    running_peak, running_sum, weighted = lax.fori_loop(0, block_limit, advance, initial)
    return (weighted / running_sum[..., None], running_peak + jnp.log(running_sum))


def attend_backward(query, keys_all, values_all, row_block, attended, log_total, grad_attended):
    length = keys_all.shape[0]
    key_shaped = keys_all.reshape(length, HEADS, HDIM)
    value_shaped = values_all.reshape(length, HEADS, HDIM)
    block_limit = row_block[-1] + 1
    delta = jnp.sum(grad_attended * attended, axis=-1)

    def advance(block_index, carried):
        grad_query, grad_keys, grad_values = carried
        key_block = lax.dynamic_slice_in_dim(key_shaped, block_index * BLK, BLK, 0)
        value_block = lax.dynamic_slice_in_dim(value_shaped, block_index * BLK, BLK, 0)
        exponent, levels = score_block(query, key_block, block_index, row_block)
        weights = exponent.astype(jnp.bfloat16)
        factor = jnp.exp(levels - log_total)
        scaled = (factor[..., None] * grad_attended).astype(jnp.bfloat16)
        grad_weights = jnp.einsum(
            "qhd,khd->qhk", scaled, value_block, preferred_element_type=jnp.float32
        )
        grad_scores = (exponent * (grad_weights - (factor * delta)[..., None])).astype(jnp.bfloat16)
        grad_query = grad_query + jnp.einsum(
            "qhk,khd->qhd", grad_scores, key_block, preferred_element_type=jnp.float32
        )
        grad_key = jnp.einsum(
            "qhk,qhd->khd", grad_scores, query, preferred_element_type=jnp.float32
        )
        grad_value = jnp.einsum("qhk,qhd->khd", weights, scaled, preferred_element_type=jnp.float32)
        grad_keys = lax.dynamic_update_slice_in_dim(grad_keys, grad_key, block_index * BLK, 0)
        grad_values = lax.dynamic_update_slice_in_dim(grad_values, grad_value, block_index * BLK, 0)
        return (grad_query, grad_keys, grad_values)

    initial = (
        jnp.zeros(query.shape, jnp.float32),
        jnp.zeros((length, HEADS, HDIM), jnp.float32),
        jnp.zeros((length, HEADS, HDIM), jnp.float32),
    )
    grad_query, grad_keys, grad_values = lax.fori_loop(0, block_limit, advance, initial)
    return (
        grad_query,
        grad_keys.reshape(length, HEADS * HDIM),
        grad_values.reshape(length, HEADS * HDIM),
    )


def project(source, params):
    feature_width = HEADS * HDIM
    normed, unit_rows, inverse = normalize(
        source, params[0].astype(jnp.float32), params[1].astype(jnp.float32)
    )
    normed_low = normed.astype(jnp.bfloat16)
    mixture = jnp.dot(normed_low, params[2], preferred_element_type=jnp.float32)
    query_low = (mixture[:, :feature_width] + params[3].astype(jnp.float32)).astype(jnp.bfloat16)
    keys_low = mixture[:, feature_width : 2 * feature_width].astype(jnp.bfloat16)
    values_low = (mixture[:, 2 * feature_width :] + params[4].astype(jnp.float32)).astype(
        jnp.bfloat16
    )
    return (unit_rows, inverse, normed_low, query_low, keys_low, values_low)


def complete(source, params, projected, gathered, row_block):
    row_count = source.shape[0]
    query = projected[3].reshape(row_count, HEADS, HDIM)
    attended, log_total = attend_forward(query, gathered[0], gathered[1], row_block)
    attended_low = attended.reshape(row_count, HEADS * HDIM).astype(jnp.bfloat16)
    middle = source + (
        jnp.dot(attended_low, params[5], preferred_element_type=jnp.float32)
        + params[6].astype(jnp.float32)
    )
    second, unit_second, inverse_second = normalize(
        middle, params[7].astype(jnp.float32), params[8].astype(jnp.float32)
    )
    second_low = second.astype(jnp.bfloat16)
    hidden = jnp.dot(second_low, params[9], preferred_element_type=jnp.float32) + params[10].astype(
        jnp.float32
    )
    active, gelu_pull = jax.vjp(partial(jax.nn.gelu, approximate=False), hidden)
    active_low = active.astype(jnp.bfloat16)
    result = middle + (
        jnp.dot(active_low, params[11], preferred_element_type=jnp.float32)
        + params[12].astype(jnp.float32)
    )
    saved = (
        query,
        attended,
        log_total,
        attended_low,
        unit_second,
        inverse_second,
        second_low,
        gelu_pull,
        active_low,
    )
    return (result, saved)


def layer_backward(source, upstream, params, projected, gathered, row_block):
    unit_first, inverse_first, normed_low, query_low, keys_low, values_low = projected
    row_count = source.shape[0]
    feature_width = HEADS * HDIM
    result, saved = complete(source, params, projected, gathered, row_block)
    (
        query,
        attended,
        log_total,
        attended_low,
        unit_second,
        inverse_second,
        second_low,
        gelu_pull,
        active_low,
    ) = saved
    top_low = upstream.astype(jnp.bfloat16)
    grad_reduce_bias = jnp.sum(top_low.astype(jnp.float32), axis=0)
    grad_reduce_weight = jnp.einsum(
        "tf,td->fd", active_low, top_low, preferred_element_type=jnp.float32
    )
    grad_active = jnp.einsum("td,fd->tf", top_low, params[11], preferred_element_type=jnp.float32)
    grad_hidden_low = gelu_pull(grad_active)[0].astype(jnp.bfloat16)
    grad_expand_bias = jnp.sum(grad_hidden_low.astype(jnp.float32), axis=0)
    grad_expand_weight = jnp.einsum(
        "td,tf->df", second_low, grad_hidden_low, preferred_element_type=jnp.float32
    )
    grad_second = jnp.einsum(
        "tf,df->td", grad_hidden_low, params[9], preferred_element_type=jnp.float32
    )
    grad_second_gain = jnp.sum(grad_second * unit_second, axis=0)
    grad_second_shift = jnp.sum(grad_second, axis=0)
    grad_middle = upstream + normalize_back(
        grad_second * params[7].astype(jnp.float32), unit_second, inverse_second
    )
    branch_low = grad_middle.astype(jnp.bfloat16)
    grad_output_bias = jnp.sum(branch_low.astype(jnp.float32), axis=0)
    grad_output_weight = jnp.einsum(
        "td,te->de", attended_low, branch_low, preferred_element_type=jnp.float32
    )
    grad_attended = jnp.einsum(
        "te,de->td", branch_low, params[5], preferred_element_type=jnp.float32
    )
    grad_query, grad_keys_full, grad_values_full = attend_backward(
        query,
        gathered[0],
        gathered[1],
        row_block,
        attended,
        log_total,
        grad_attended.reshape(row_count, HEADS, HDIM),
    )
    grad_keys, grad_values = (
        lax.psum_scatter(grad_keys_full, LINE, scatter_dimension=0, tiled=True),
        lax.psum_scatter(grad_values_full, LINE, scatter_dimension=0, tiled=True),
    )
    scale_factor = HDIM ** (-0.5)
    grad_mixture = jnp.concatenate(
        [
            grad_query.reshape(row_count, feature_width) * scale_factor,
            grad_keys * scale_factor,
            grad_values,
        ],
        axis=1,
    ).astype(jnp.bfloat16)
    grad_query_bias = jnp.sum(grad_mixture[:, :feature_width].astype(jnp.float32), axis=0)
    grad_value_bias = jnp.sum(grad_mixture[:, 2 * feature_width :].astype(jnp.float32), axis=0)
    grad_joint_weight = jnp.einsum(
        "td,te->de", normed_low, grad_mixture, preferred_element_type=jnp.float32
    )
    grad_normed = jnp.einsum(
        "te,de->td", grad_mixture, params[2], preferred_element_type=jnp.float32
    )
    grad_first_gain = jnp.sum(grad_normed * unit_first, axis=0)
    grad_first_shift = jnp.sum(grad_normed, axis=0)
    grad_source = grad_middle + normalize_back(
        grad_normed * params[0].astype(jnp.float32), unit_first, inverse_first
    )
    grads = (
        grad_first_gain,
        grad_first_shift,
        grad_joint_weight,
        grad_query_bias,
        grad_value_bias,
        grad_output_weight,
        grad_output_bias,
        grad_second_gain,
        grad_second_shift,
        grad_expand_weight,
        grad_expand_bias,
        grad_reduce_weight,
        grad_reduce_bias,
    )
    return (grad_source.astype(jnp.bfloat16), grads)


def body(
    inputs,
    cotangent,
    first_gain,
    first_shift,
    joint_weight,
    query_bias,
    value_bias,
    output_weight,
    output_bias,
    second_gain,
    second_shift,
    expand_weight,
    expand_bias,
    reduce_weight,
    reduce_bias,
):
    section_index = lax.axis_index(SECTION)
    micro_count = inputs.shape[0]
    row_count = inputs.shape[1]
    first_row = lax.axis_index(LINE) * row_count
    row_block = (first_row + jnp.arange(row_count, dtype=jnp.int32)) // BLK
    owned = (
        first_gain[0],
        first_shift[0],
        joint_weight[0],
        query_bias[0],
        value_bias[0],
        output_weight[0],
        output_bias[0],
        second_gain[0],
        second_shift[0],
        expand_weight[0],
        expand_bias[0],
        reduce_weight[0],
        reduce_bias[0],
    )
    forward_params = (
        lax.all_gather(first_gain[0], OWNERS, axis=0, tiled=True),
        lax.all_gather(first_shift[0], OWNERS, axis=0, tiled=True),
        lax.all_gather(joint_weight[0], OWNERS, axis=0, tiled=True),
        lax.all_gather(query_bias[0], OWNERS, axis=0, tiled=True),
        lax.all_gather(value_bias[0], OWNERS, axis=0, tiled=True),
        lax.all_gather(output_weight[0], OWNERS, axis=0, tiled=True),
        lax.all_gather(output_bias[0], OWNERS, axis=0, tiled=True),
        lax.all_gather(second_gain[0], OWNERS, axis=0, tiled=True),
        lax.all_gather(second_shift[0], OWNERS, axis=0, tiled=True),
        lax.all_gather(expand_weight[0], OWNERS, axis=0, tiled=True),
        lax.all_gather(expand_bias[0], OWNERS, axis=0, tiled=True),
        lax.all_gather(reduce_weight[0], OWNERS, axis=0, tiled=True),
        lax.all_gather(reduce_bias[0], OWNERS, axis=0, tiled=True),
    )
    incoming = jnp.zeros(inputs.shape[1:], jnp.bfloat16)
    section_inputs = []
    produced = []
    key_sets = []
    for tick_index in range(micro_count + 1):
        section_input = jnp.where(
            section_index == 0, inputs[min(tick_index, micro_count - 1)], incoming
        )
        source = section_input.astype(jnp.float32)
        projected = project(source, forward_params)
        gathered = (
            lax.all_gather(projected[4], LINE, axis=0, tiled=True),
            lax.all_gather(projected[5], LINE, axis=0, tiled=True),
        )
        result, unused = complete(source, forward_params, projected, gathered, row_block)
        result_low = result.astype(jnp.bfloat16)
        section_inputs.append(section_input)
        produced.append(result_low)
        key_sets.append(gathered)
        if tick_index < micro_count:
            incoming = passed_along(result_low, SECTION, 1)
    backward_params = (
        lax.all_gather(first_gain[0], OWNERS, axis=0, tiled=True),
        lax.all_gather(first_shift[0], OWNERS, axis=0, tiled=True),
        lax.all_gather(joint_weight[0], OWNERS, axis=0, tiled=True),
        lax.all_gather(query_bias[0], OWNERS, axis=0, tiled=True),
        lax.all_gather(value_bias[0], OWNERS, axis=0, tiled=True),
        lax.all_gather(output_weight[0], OWNERS, axis=0, tiled=True),
        lax.all_gather(output_bias[0], OWNERS, axis=0, tiled=True),
        lax.all_gather(second_gain[0], OWNERS, axis=0, tiled=True),
        lax.all_gather(second_shift[0], OWNERS, axis=0, tiled=True),
        lax.all_gather(expand_weight[0], OWNERS, axis=0, tiled=True),
        lax.all_gather(expand_bias[0], OWNERS, axis=0, tiled=True),
        lax.all_gather(reduce_weight[0], OWNERS, axis=0, tiled=True),
        lax.all_gather(reduce_bias[0], OWNERS, axis=0, tiled=True),
    )
    totals = tuple((jnp.zeros(piece.shape, jnp.float32) for piece in backward_params))
    shares = tuple((jnp.zeros(piece.shape, jnp.float32) for piece in owned))
    returning = jnp.zeros(inputs.shape[1:], jnp.bfloat16)
    sent_back = []
    for tick_index in range(micro_count + 1):
        upper_pick = min(tick_index + 1, micro_count)
        lower_pick = max(tick_index - 1, 0)
        section_input = jnp.where(
            section_index == 1, section_inputs[upper_pick], section_inputs[lower_pick]
        )
        upstream = jnp.where(
            section_index == 1, cotangent[min(tick_index, micro_count - 1)], returning
        ).astype(jnp.float32)
        weight_valid = jnp.where(
            section_index == 1,
            1.0 if tick_index < micro_count else 0.0,
            1.0 if tick_index >= 1 else 0.0,
        ).astype(jnp.float32)
        source = section_input.astype(jnp.float32)
        projected = project(source, backward_params)
        gathered = (
            lax.all_gather(projected[4], LINE, axis=0, tiled=True),
            lax.all_gather(projected[5], LINE, axis=0, tiled=True),
        )
        grad_source, grads = layer_backward(
            source, upstream, backward_params, projected, gathered, row_block
        )
        masked = tuple((update * weight_valid for update in grads))
        totals = tuple((running + update for running, update in zip(totals, masked)))
        sent_back.append(grad_source)
        if tick_index < micro_count:
            returning = passed_along(grad_source, SECTION, -1)
    layer_outputs = jnp.stack(
        [
            jnp.where(section_index == 0, produced[position], produced[position + 1])
            for position in range(micro_count)
        ]
    )[None]
    input_grads = jnp.stack(
        [
            jnp.where(section_index == 1, sent_back[position], sent_back[position + 1])
            for position in range(micro_count)
        ]
    )[None]
    (
        sum_first_gain,
        sum_first_shift,
        sum_joint_weight,
        sum_query_bias,
        sum_value_bias,
        sum_output_weight,
        sum_output_bias,
        sum_second_gain,
        sum_second_shift,
        sum_expand_weight,
        sum_expand_bias,
        sum_reduce_weight,
        sum_reduce_bias,
    ) = totals
    shares = (
        lax.psum_scatter(sum_first_gain, OWNERS, scatter_dimension=0, tiled=True),
        lax.psum_scatter(sum_first_shift, OWNERS, scatter_dimension=0, tiled=True),
        lax.psum_scatter(sum_joint_weight, OWNERS, scatter_dimension=0, tiled=True),
        lax.psum_scatter(sum_query_bias, OWNERS, scatter_dimension=0, tiled=True),
        lax.psum_scatter(sum_value_bias, OWNERS, scatter_dimension=0, tiled=True),
        lax.psum_scatter(sum_output_weight, OWNERS, scatter_dimension=0, tiled=True),
        lax.psum_scatter(sum_output_bias, OWNERS, scatter_dimension=0, tiled=True),
        lax.psum_scatter(sum_second_gain, OWNERS, scatter_dimension=0, tiled=True),
        lax.psum_scatter(sum_second_shift, OWNERS, scatter_dimension=0, tiled=True),
        lax.psum_scatter(sum_expand_weight, OWNERS, scatter_dimension=0, tiled=True),
        lax.psum_scatter(sum_expand_bias, OWNERS, scatter_dimension=0, tiled=True),
        lax.psum_scatter(sum_reduce_weight, OWNERS, scatter_dimension=0, tiled=True),
        lax.psum_scatter(sum_reduce_bias, OWNERS, scatter_dimension=0, tiled=True),
    )
    return (layer_outputs, input_grads) + tuple((portion[None] for portion in shares))


def flip(place, bits):
    return {1: place + 1 - 2 * (place % 2), 2: (place + 2) % 4, 3: 3 - place}[bits]


def places():
    core, ring, line = (lax.axis_index(name) for name in (SECTION, RING, LINE))
    rings = [ring] + [flip(ring, bits) for bits in (1, 2, 3)]
    lines = [line] + [flip(line, bits) for bits in (1, 2, 3)]
    toward = {
        EAST: {RING: rings[1]},
        NORTH: {RING: rings[2]},
        (LEVEL, 1): {LINE: lines[1]},
        (LEVEL, 2): {LINE: lines[2]},
        (LEVEL, 3): {LINE: lines[3]},
        (CORNER, 3): {SECTION: 1 - core, LINE: lines[3]},
        (LEVEL, UP): {LINE: (line + 1) % 4},
        (LEVEL, DOWN): {LINE: (line + 3) % 4},
        SIBLING: {SECTION: 1 - core},
    }
    return core, rings, lines, toward


def greet(toward):
    barrier = pltpu.get_barrier_semaphore()
    partners = [to for name, to in toward.items() if name not in ((LEVEL, UP), (LEVEL, DOWN))]
    for to in partners:
        pl.semaphore_signal(barrier, inc=1, device_id=to, device_id_type=pl.DeviceIdType.MESH)
    pl.semaphore_wait(barrier, len(partners))


def remote_copy(source, target, send_sem, recv_sem, to):
    return pltpu.make_async_remote_copy(
        src_ref=source,
        dst_ref=target,
        send_sem=send_sem,
        recv_sem=recv_sem,
        device_id=to,
        device_id_type=pl.DeviceIdType.MESH,
    )


def per_core(core, act):
    for index in (0, 1):

        @pl.when(core == index)
        def _():
            act(index)


GATHER_KINDS = (UP, DOWN, EAST, NORTH, CORNER, SIBLING)
GATHER_NUMBER = {kind: 4 * index for index, kind in enumerate(GATHER_KINDS)}
GATHER_SPAN = 4 * len(GATHER_KINDS)


def mm(left, right):
    return jnp.dot(left, right, preferred_element_type=F32)


def mm_nt(left, right):
    return lax.dot_general(left, right, (((1,), (1,)), ((), ())), preferred_element_type=F32)


def mm_tn(left, right):
    return lax.dot_general(left, right, (((0,), (0,)), ((), ())), preferred_element_type=F32)


def normal_parts(values):
    centre = jnp.mean(values, axis=-1, keepdims=True)
    centred = values - centre
    inverse = lax.rsqrt(jnp.mean(centred * centred, axis=-1, keepdims=True) + epsilon)
    return centred * inverse, inverse


def normal_back(upstream, unit, inverse):
    return inverse * (
        upstream
        - jnp.mean(upstream, axis=-1, keepdims=True)
        - unit * jnp.mean(upstream * unit, axis=-1, keepdims=True)
    )


def close_up(rows, table):
    high = rows.astype(LOW)
    rest = (rows - high.astype(F32)).astype(LOW)
    return mm_nt(high, table) + mm_nt(rest, table)


def head_pair(rows):
    lane = lax.broadcasted_iota(jnp.int32, rows.shape, 1)
    zero = jnp.zeros_like(rows)
    return jnp.concatenate(
        [jnp.where(lane < HDIM, rows, zero), jnp.where(lane < HDIM, zero, rows)], axis=0
    )


def from_pair(turned):
    n = turned.shape[1] // 2
    own = jnp.concatenate([turned[:HDIM, :n], turned[HDIM:, n:]], axis=0)
    return own.T


LEAD_ROWS = 144
HALF = 2176


def gather_tasks(slots, send_sem, recv_sem, copy_sem, land_sem, place_of):
    core, rings, lines, toward = place_of
    line = lines[0]
    drains = []

    def cut(t, part):
        if slots[t][1]:
            return (slice(None), pl.ds(HALF * part if isinstance(part, int) else pl.multiple_of(part * HALF, 128), HALF))
        rows = slots[t][2].shape[0]
        return (pl.ds(0, LEAD_ROWS) if part == 0 else pl.ds(LEAD_ROWS, rows - LEAD_ROWS),)

    def landed(t, part):
        _, by_columns, shard, _, land = slots[t]
        return land if by_columns else land.at[pl.ds(0, LEAD_ROWS if part == 0 else shard.shape[0] - LEAD_ROWS)]

    def run(t, act):
        if slots[t][1]:
            act(core)
        else:
            per_core(core, act)

    def place(t, part, dd, j):
        return slots[t][3].at[(rings[dd] * 4 + j,) + cut(t, part)]

    def group(t, part, dd):
        return slots[t][3].at[(pl.ds(rings[dd] * 4, 4),) + cut(t, part)]

    def copy_of(t, source, target, to, kind, j):
        index = t * GATHER_SPAN + GATHER_NUMBER[kind] + j
        return remote_copy(source, target, send_sem.at[index], recv_sem.at[index], toward[to])

    def guarded(valid, act):
        if valid is None:
            act()
        else:
            pl.when(valid)(act)

    def send(t, dd, j, to, kind, valid=None, mine=False):
        def start(part):
            target = place(t, part, dd, j)
            copy_of(t, target, target, to, kind, j).start()

        def start_mine(index):
            shard = slots[t][2].at[cut(t, index)] if index == slots[t][0] else landed(t, index)
            copy_of(t, shard, place(t, index, dd, j), to, kind, j).start()

        def finish(part):
            target = place(t, part, dd, j)
            copy_of(t, target, target, to, kind, j).wait_send()

        if mine:
            guarded(valid, lambda: per_core(core, start_mine))
        else:
            guarded(valid, lambda: run(t, start))
        drains.append(lambda: guarded(valid, lambda: run(t, finish)))

    def arrive(t, dd, j, to, kind, valid=None):
        def act(part):
            target = place(t, part, dd, j)
            copy_of(t, target, target, to, kind, j).wait_recv()

        guarded(valid, lambda: run(t, act))

    def both(one, two):
        return two if one is None else one & two

    def onward(t, j, valid, up, down, mine=False):
        if up:
            send(t, 0, j, (LEVEL, UP), UP, both(valid, line < 3), mine)
        if down:
            send(t, 0, j, (LEVEL, DOWN), DOWN, both(valid, line > 0), mine)
        send(t, 0, j, EAST, EAST, valid, mine)
        send(t, 0, j, NORTH, NORTH, valid, mine)

    def prelude():
        def give(index):
            for t, (owner, _, shard, _, land) in enumerate(slots):
                if index == owner:
                    source = shard.at[cut(t, 1 - index)]
                    remote_copy(source, landed(t, 1 - index), land_sem.at[t], land_sem.at[len(slots) + t], toward[SIBLING]).start()

        per_core(core, give)

    def taken(t):
        owner, shard = slots[t][0], slots[t][2]

        def act(index):
            target = landed(t, 1 - owner)
            copy = remote_copy(target, target, land_sem.at[t], land_sem.at[len(slots) + t], toward[SIBLING])
            if index == owner:
                copy.wait_send()
            else:
                copy.wait_recv()

        per_core(core, act)

    def local(t, index):
        source = slots[t][2].at[cut(t, index)] if index == slots[t][0] else landed(t, index)
        return pltpu.make_async_copy(source, place(t, index, 0, line), copy_sem.at[t])

    def begin(t):
        taken(t)
        onward(t, line, None, True, True, mine=True)
        per_core(core, lambda index: local(t, index).start())

    def own_ready(t):
        per_core(core, lambda index: local(t, index).wait())

    def from_line(t, offset):
        j = line + offset
        valid = j >= 0 if offset < 0 else j <= 3
        kind = UP if offset < 0 else DOWN
        arrive(t, 0, j, (LEVEL, DOWN if offset < 0 else UP), kind, valid)
        onward(t, j, valid, offset < 0, offset > 0)

    def from_side(t, offset):
        j = line + offset
        valid = None if offset == 0 else (j >= 0 if offset < 0 else j <= 3)
        even, odd = both(valid, j % 2 == 0), both(valid, j % 2 == 1)
        arrive(t, 1, j, EAST, EAST, valid)
        send(t, 1, j, NORTH, CORNER, even)
        arrive(t, 2, j, NORTH, NORTH, valid)
        send(t, 2, j, EAST, CORNER, odd)

    def from_corner(t, j):
        arrive(t, 3, j, NORTH if j % 2 == 0 else EAST, CORNER)

    def sibling(t, dd):
        def copy(part):
            return copy_of(t, group(t, part, dd), group(t, part, dd), SIBLING, SIBLING, dd)

        run(t, lambda part: copy(part).start())
        drains.append(lambda: run(t, lambda part: copy(part).wait_send()))

    def last(t):
        def act(part):
            for dd in range(4):
                target = group(t, 1 - part, dd)
                copy_of(t, target, target, SIBLING, SIBLING, dd).wait_recv()

        run(t, act)

    tasks = []

    def then(function, *given):
        tasks.append((given[0] if given else 0, lambda: function(*given)))

    count = len(slots)
    heads, tails = [], []
    for t in range(count):
        then(from_line, t, -1)
        then(from_line, t, 1)
        then(from_side, t, 0)
        for far in (2, 3):
            then(from_line, t, -far)
            then(from_line, t, far)
            then(from_side, t, 1 - far)
            then(from_side, t, far - 1)
        then(own_ready, t)
        then(sibling, t, 0)
        then(from_side, t, -3)
        then(from_side, t, 3)
        then(sibling, t, 1)
        then(sibling, t, 2)
        heads.append(list(tasks))
        tasks.clear()
        for j in range(4):
            then(from_corner, t, j)
        then(sibling, t, 3)
        then(last, t)
        tails.append(list(tasks))
        tasks.clear()
    then(prelude)
    then(begin, 0)
    if count > 1:
        then(begin, 1)
    for t in range(count):
        tasks += heads[t][:7]
        if t > 0:
            tasks += tails[t - 1]
        if t + 2 < count:
            then(begin, t + 2)
        tasks += heads[t][7:]
    tasks += tails[count - 1]

    def drain():
        for act in drains:
            act()

    return tasks, drain


def gather_outs(shards):
    shapes = []
    for _, by_columns, shard in shards:
        rows, columns = shard.shape
        land = (rows, HALF) if by_columns else (LEAD_ROWS, columns)
        shapes += [jax.ShapeDtypeStruct((16, rows, columns), LOW), jax.ShapeDtypeStruct(land, LOW)]
    return shapes


def gather_slots(forms, shards, outs):
    return [form + (shards[t], outs[2 * t], outs[2 * t + 1]) for t, form in enumerate(forms)]


def gather_semaphores(count):
    dma = pltpu.SemaphoreType.DMA
    return [dma((count * GATHER_SPAN,)), dma((count * GATHER_SPAN,)), dma((count,)), dma((2 * count,))]


def row_copies(place_of, source, target, send_sem, recv_sem, local_sem):
    core, _, lines, toward = place_of
    half = target.shape[0] // 2
    which = lines[0] // 2
    from_here = pl.ds(pl.multiple_of(core * half, half), half)
    to_there = pl.ds(pl.multiple_of(which * half, half), half)
    return (
        pltpu.make_async_copy(source.at[which, from_here], target.at[to_there], local_sem),
        remote_copy(source.at[1 - which, from_here], target.at[to_there], send_sem, recv_sem, toward[(LEVEL, 3)]),
    )


def gather_kernel(shard, *refs):
    source, outs, moved, refs = refs[0], refs[1:3], refs[3], refs[4:]
    sems, row_sems = refs[:4], refs[4:]
    place_of = places()
    greet(place_of[3])
    tasks, drain = gather_tasks(gather_slots(((0, True),), (shard,), outs), *sems, place_of)
    for _, task in tasks[:11]:
        task()
    copies = row_copies(place_of, source, moved, *row_sems)
    for copy in copies:
        copy.start()
    for _, task in tasks[11:]:
        task()
    drain()
    for copy in copies:
        copy.wait()


def gather_page(shard, source):
    anywhere = pl.BlockSpec(memory_space=pl.ANY)
    outs = gather_outs(((0, True, shard),)) + [jax.ShapeDtypeStruct(source.shape[1:], LOW)]
    dma = pltpu.SemaphoreType.DMA
    res = pl.pallas_call(
        gather_kernel,
        out_shape=tuple(outs),
        in_specs=[anywhere] * 2,
        out_specs=(anywhere,) * len(outs),
        scratch_shapes=gather_semaphores(1) + [dma(())] * 3,
        compiler_params=pltpu.CompilerParams(collective_id=0, has_side_effects=True),
        name="gather_page",
    )(shard, source)
    return res[0], res[2]


def low_place(line):
    return jnp.where(line < 2, line, 3 - line)


def forward_kernel(forms, *refs):
    count = len(forms)
    moving = count == 2
    x, vectors, wide, table, page_hbm = refs[:5]
    shards, refs = refs[5 : 5 + count], refs[5 + count :]
    if moving:
        row_source, refs = refs[0], refs[1:]
    stored, refs = refs[:14], refs[14:]
    outs, refs = refs[: 2 * count], refs[2 * count :]
    if moving:
        row_target, row_sems, refs = refs[0], refs[-3:], refs[1:-3]
    held, store_sem, refs = refs[:14], refs[14], refs[15:]
    (normed_out, query_out, here, beside, away, corner, attended_out, log_out, attended_low, middle_out,
     second_out, active_out, slope_out, result_out) = held
    page, expand, reduce, mixture, result, mixed, stats, page_sem, expand_sem, reduce_sem, pair_send, pair_recv = refs[:12]
    place_of = places()
    core, rings, lines, toward = place_of
    rows, width = x.shape
    half = rows // 2
    first = low_place(lines[0]) == 0

    def store_copy(i):
        return pltpu.make_async_copy(held[i], stored[i], store_sem.at[i])

    def store(*numbers):
        for i in numbers:
            store_copy(i).start()

    def page_copy(i):
        at = pl.ds(pl.multiple_of(i * 256, 256), 256)
        return pltpu.make_async_copy(page_hbm.at[:, at], page.at[:, at], page_sem.at[i])

    def expand_copy(i):
        at = pl.ds(pl.multiple_of(i * 256, 256), 256)
        return pltpu.make_async_copy(outs[0].at[:, :, at], expand.at[:, :, at], expand_sem.at[i])

    def reduce_copy(i):
        rows_at = pl.ds(pl.multiple_of(i * 272, 16), 272)
        return pltpu.make_async_copy(outs[2].at[i], reduce.at[rows_at], reduce_sem.at[i])

    tiles = page.shape[1] // 256

    def begin(make, steps):
        def step(i, _):
            make(i).start()
            return 0

        lax.fori_loop(0, steps, step, 0)

    begin(page_copy, tiles)
    greet(toward)
    todo, drain = gather_tasks(gather_slots(forms, shards, outs), *refs[12:], place_of)

    def progress(many):
        for _ in range(many):
            if todo:
                todo.pop(0)[1]()

    def complete(t):
        while any(slot <= t for slot, _ in todo):
            progress(1)

    progress(2)
    unit, _ = normal_parts(x[...].astype(F32))
    normed = (unit * vectors[0:1] + vectors[1:2]).astype(LOW)
    normed_out[...] = mm(normed, table[...]).astype(LOW)
    store(0)

    def column(i, _):
        page_copy(i).wait()
        at = pl.ds(pl.multiple_of(i * 256, 256), 256)
        mixture[:, at] = mm(normed_out[...], page[:, at])
        return 0

    for begin_at, end in ((0, 4), (4, 8), (8, 13)):
        lax.fori_loop(begin_at, end, column, 0)
        progress(2)
    blank = jnp.zeros((rows, WIDE - width), LOW)
    here[0, :, :width] = mixture[:, width : 2 * width].astype(LOW)
    here[0, :, width:] = blank
    here[1, :, :width] = (mixture[:, 2 * width : 3 * width] + vectors[3:4]).astype(LOW)
    here[1, :, width:] = blank

    def pair_copy(source, target, to, number):
        return remote_copy(source, target, pair_send.at[number], pair_recv.at[number], toward[to])

    to_away = pair_copy(here, away, (LEVEL, 1), 0)
    to_beside = pair_copy(here, beside, SIBLING, 1)
    to_corner = pair_copy(away, corner, SIBLING, 2)
    to_away.start()
    to_beside.start()
    query = ((mixture[:, :width] + vectors[2:3]).astype(LOW).astype(F32) * HDIM ** (-0.5)).astype(LOW)
    query_out[:, :width] = query
    query_out[:, width:] = blank
    store(1, 2)
    progress(1)
    to_beside.wait_recv()
    store(3)

    def block(kind, near, part, at):
        rows_at = pl.ds(part * half, half)
        one, two = (here, beside) if near == 0 else (away, corner)
        return jnp.concatenate([one[kind, rows_at, at], two[kind, rows_at, at]], axis=0)

    def one_unit(queries, keys, values):
        scores = mm_nt(keys, queries)
        level = jnp.max(scores, axis=0, keepdims=True)
        exponent = jnp.exp(scores - level)
        return level, jnp.sum(exponent, axis=0, keepdims=True), mm_tn(values, exponent.astype(LOW))

    def merge(units):
        peak = units[0][0]
        for level, _, _ in units[1:]:
            peak = jnp.maximum(peak, level)
        total, out = 0.0, 0.0
        for level, sums, part in units:
            share = jnp.exp(level - peak)
            total = total + share * sums
            out = out + share * part
        return peak, total, out

    def local_pair(p, _):
        at = pl.ds(pl.multiple_of(p * 128, 128), 128)
        low, high = head_pair(query_out[:half, at]), head_pair(query_out[half:, at])
        keys, values = block(0, 0, 0, at), block(1, 0, 0, at)
        bottom = one_unit(low, keys, values)
        top = merge([one_unit(high, keys, values), one_unit(high, block(0, 0, 1, at), block(1, 0, 1, at))])
        for place, (level, sums, out) in enumerate((bottom, top)):
            stats[p, 2 * place : 2 * place + 1] = level
            stats[p, 2 * place + 1 : 2 * place + 2] = sums
            mixed[p, place] = out
        return 0

    for begin_at in (0, 3, 6):
        lax.fori_loop(begin_at, begin_at + 3, local_pair, 0)
        progress(2)
    progress(8)
    to_away.wait_recv()
    to_corner.start()
    store(4)
    progress(2)
    to_corner.wait_recv()
    store(5)

    def far_pair(p, _):
        at = pl.ds(pl.multiple_of(p * 128, 128), 128)
        low, high = head_pair(query_out[:half, at]), head_pair(query_out[half:, at])
        keys, values = block(0, 1, 0, at), block(1, 1, 0, at)
        last_keys = jnp.where(first, block(0, 1, 1, at), keys)
        last_values = jnp.where(first, block(1, 1, 1, at), values)
        near = one_unit(high, keys, values)
        last = one_unit(jnp.where(first, high, low), last_keys, last_values)
        low_last = (jnp.where(first, far_below, last[0]),) + last[1:]
        high_last = (jnp.where(first, last[0], far_below),) + last[1:]

        def before(place):
            return (stats[p, 2 * place : 2 * place + 1], stats[p, 2 * place + 1 : 2 * place + 2], mixed[p, place])

        for place, units in enumerate(([before(0), low_last], [before(1), near, high_last])):
            peak, total, out = merge(units)
            attended_out[place * half : (place + 1) * half, at] = from_pair(out / total)
            log_out[p, place : place + 1] = peak + jnp.log(total)
        return 0

    for begin_at in (0, 3, 6):
        lax.fori_loop(begin_at, begin_at + 3, far_pair, 0)
        progress(2)

    def late(i, _):
        page_copy(i).wait()
        return 0

    lax.fori_loop(13, tiles, late, 0)
    lead = 4 * width - WIDE
    store(6, 7)
    attended_low[...] = mm(attended_out[:, :width].astype(LOW), table[...]).astype(LOW)
    store(8)
    blended = mm(attended_low[...], page[:, lead:])
    middle = x[...].astype(F32) + (blended[:, 3 * width - lead :] + vectors[4:5])
    middle_out[...] = middle
    store(9)
    progress(2)
    unit, _ = normal_parts(middle)
    second = (unit * vectors[6:7] + vectors[7:8]).astype(LOW)
    second_out[...] = mm(second, table[...]).astype(LOW)
    store(10)
    result[...] = middle + vectors[5:6]

    complete(0)
    begin(expand_copy, tiles)
    if moving:
        for copy in row_copies(place_of, row_source, row_target, *row_sems):
            copy.start()

    def inner(i, _):
        at = pl.ds(pl.multiple_of(i * 256, 256), 256)
        expand_copy(i).wait()
        weights = expand[:, :, at].astype(F32).reshape(WIDE, 256).astype(LOW)
        hidden = mm(second_out[...], weights) + wide[:, at]
        below = 0.5 + 0.5 * lax.erf(hidden * 0.7071067811865476)
        active_out[:, at] = (hidden * below).astype(LOW)
        slope_out[:, at] = (below + hidden * (0.3989422804014327 * jnp.exp(-0.5 * hidden * hidden))).astype(LOW)
        return 0

    for begin_at in range(0, tiles, 2):
        lax.fori_loop(begin_at, min(begin_at + 2, tiles), inner, 0)
        progress(3)
    store(11, 12)
    complete(1)
    begin(reduce_copy, 16)

    def landed(i, _):
        reduce_copy(i).wait()
        return 0

    lax.fori_loop(0, 16, landed, 0)

    def outer(i, _):
        at = pl.ds(pl.multiple_of(i * 256, 256), 256)
        result[...] += mm(active_out[:, at], reduce[at])
        return 0

    lax.fori_loop(0, tiles, outer, 0)
    result_out[...] = result[...].astype(LOW)
    store(13)
    progress(len(todo))
    drain()
    for i in range(14):
        store_copy(i).wait()
    if moving:
        for copy in row_copies(place_of, row_source, row_target, *row_sems):
            copy.wait()
    for copy in (to_away, to_beside, to_corner):
        copy.wait_send()


def forward(x, vectors, wide, table, page, shards, moved=()):
    rows, width = x.shape
    inner = page.shape[1]
    pairs = WIDE // 128
    anywhere = pl.BlockSpec(memory_space=pl.ANY)
    inside = pl.BlockSpec(memory_space=pltpu.VMEM)

    def shape(*dims, kind=LOW):
        return jax.ShapeDtypeStruct(dims, kind)

    pair = shape(2, rows, WIDE)
    outs = [
        shape(rows, WIDE), shape(rows, WIDE), pair, pair, pair, pair, shape(rows, WIDE, kind=F32),
        shape(pairs, 2, rows, kind=F32), shape(rows, WIDE), shape(rows, width, kind=F32),
        shape(rows, WIDE), shape(rows, inner), shape(rows, inner), shape(rows, width),
    ]
    count = len(outs)
    dma = pltpu.SemaphoreType.DMA
    scratch = [pltpu.VMEM(out.shape, out.dtype) for out in outs] + [
        dma((count,)), pltpu.VMEM(page.shape, LOW), pltpu.VMEM((16, 72, inner), LOW), pltpu.VMEM((inner, width), LOW),
        pltpu.VMEM((rows, 13 * 256), F32), pltpu.VMEM((rows, width), F32),
        pltpu.VMEM((pairs, 2, 128, rows), F32), pltpu.VMEM((pairs, 4, rows), F32),
        dma((inner // 256,)), dma((inner // 256,)), dma((16,)), dma((3,)), dma((3,)),
    ] + gather_semaphores(len(shards))
    outs += gather_outs(shards)
    gathered = len(outs)
    outs += [jax.ShapeDtypeStruct(source.shape[1:], LOW) for source in moved]
    scratch += [dma(())] * (3 * len(moved))
    forms = tuple(shard[:2] for shard in shards)
    res = pl.pallas_call(
        partial(forward_kernel, forms),
        out_shape=tuple(outs),
        in_specs=[inside] * 4 + [anywhere] * (1 + len(shards) + len(moved)),
        out_specs=(anywhere,) * len(outs),
        scratch_shapes=scratch,
        compiler_params=pltpu.CompilerParams(
            collective_id=len(shards), has_side_effects=True, vmem_limit_bytes=60 << 20
        ),
        name="forward",
    )(x, vectors, wide, table, page, *(shard[2] for shard in shards), *moved)
    return res[:count], res[count:gathered:2], res[gathered:]


COLUMNS, ROWS = range(2)
SIZES = {COLUMNS: (72, 2176), ROWS: (144, 1088)}
DEPTH = 6
EASTWARD = (3, 0)
SCATTER_KINDS = (
    [(SIBLING, dd) for dd in range(4)]
    + [(ONCE, k) for k in range(4)]
    + [(EAST, k) for k in range(4)]
    + [(NORTH, k) for k in range(4)]
    + [(LEVEL, k) for k in (1, 2, 3)]
    + [(CORNER, 0)]
)
SCATTER_NUMBER = {kind: index for index, kind in enumerate(SCATTER_KINDS)}


def landing_shapes(kind):
    return [jax.ShapeDtypeStruct((many,) + SIZES[kind], LOW) for many in (16, 4, 4, 4, 4)]


def final_shape(kind):
    return jax.ShapeDtypeStruct({COLUMNS: (72, 4352), ROWS: (272, 1088)}[kind], F32)


def work_shapes(kinds):
    shapes = []
    for kind in sorted(set(kinds)):
        size = SIZES[kind]
        shapes += [pltpu.VMEM((2, 4) + size, LOW), pltpu.VMEM((DEPTH,) + size, LOW), pltpu.VMEM(size, F32)]
    count = len(kinds) * len(SCATTER_KINDS)
    return shapes + [
        pltpu.SemaphoreType.DMA((count,)), pltpu.SemaphoreType.DMA((count,)),
        pltpu.SemaphoreType.DMA((8,)), pltpu.SemaphoreType.DMA(()),
    ]


class Scatter:
    def __init__(self, kinds, pages, lands, finals, owners, refs, place_of):
        self.kinds, self.pages, self.lands, self.finals, self.owners = kinds, pages, lands, finals, owners
        self.core, self.rings, self.lines, self.toward = place_of
        self.work = {}
        for index, kind in enumerate(sorted(set(kinds))):
            self.work[kind] = refs[3 * index : 3 * index + 3]
        self.send_sem, self.recv_sem, self.load_sem, self.out_sem = refs[3 * len(self.work) :]
        self.turn = 0
        self.used = {kind: [None] * DEPTH for kind in self.work}
        self.count = {kind: 0 for kind in self.work}
        self.given, self.final_sent = [], []

    def remote(self, t, source, target, to, kind):
        index = t * len(SCATTER_KINDS) + SCATTER_NUMBER[kind]
        return remote_copy(source, target, self.send_sem.at[index], self.recv_sem.at[index], self.toward[to])

    def part(self, t, core, index, many=None):
        page, at = self.pages[t], index if many is None else pl.ds(index, many)
        if self.kinds[t] == COLUMNS:
            return page.at[at, :, pl.ds(pl.multiple_of(core * 2176, 128), 2176)]
        return page.at[pl.ds(pl.multiple_of(index * 272 + core * 128, 16), 144)]

    def landed(self, t, dd):
        return self.lands[t][0].at[pl.ds(self.rings[dd] * 4, 4)]

    def give(self, t, dd):
        base = self.rings[dd] * 4
        if self.kinds[t] == ROWS:
            for k in range(4):
                self.remote(t, self.part(t, 1 - self.core, base + k), self.lands[t][0].at[base + k], SIBLING, (SIBLING, dd)).start()
        else:
            self.remote(t, self.part(t, 1 - self.core, base, 4), self.landed(t, dd), SIBLING, (SIBLING, dd)).start()
        self.given.append(self.remote(t, self.landed(t, dd), self.landed(t, dd), SIBLING, (SIBLING, dd)))

    def arrived(self, t, ref, to, kind):
        self.remote(t, ref, ref, to, kind).wait_recv()

    def load(self, t, sources):
        loads = self.work[self.kinds[t]][0]
        slot = self.turn % 2
        self.turn += 1
        copies = []
        for j, source in enumerate(sources):
            copies.append(pltpu.make_async_copy(source, loads.at[slot, j], self.load_sem.at[slot * 4 + j]))
        for copy in copies:
            copy.start()
        return loads, slot, copies

    def add_up(self, t, loaded, store):
        loads, slot, copies = loaded
        terms = len(copies)
        for copy in copies:
            copy.wait()
        rows, columns = SIZES[self.kinds[t]]
        wide = self.kinds[t] != ROWS
        piece = min(256, columns) if wide else 16

        def step(i, _):
            at = pl.ds(pl.multiple_of(i * piece, piece), piece)
            where = (slice(None), at) if wide else (at, slice(None))
            value = loads[(slot, 0) + where].astype(F32)
            for j in range(1, terms):
                value = value + loads[(slot, j) + where].astype(F32)
            store(where, value)
            return 0

        steps = (columns if wide else rows) // piece
        lax.fori_loop(0, steps, step, 0)
        if wide and steps * piece < columns:
            where = (slice(None), pl.ds(steps * piece, columns - steps * piece))
            value = loads[(slot, 0) + where].astype(F32)
            for j in range(1, terms):
                value = value + loads[(slot, j) + where].astype(F32)
            store(where, value)

    def sources(self, t, dd, k, extra):
        index = self.rings[dd] * 4 + self.lines[k]
        return [self.part(t, self.core, index), self.lands[t][0].at[index]] + extra

    def sum_and_send(self, t, dd, k, extra, target, to, kind):
        form = self.kinds[t]
        loaded = self.load(t, self.sources(t, dd, k, extra))

        def finish():
            place = self.count[form] % DEPTH
            self.count[form] += 1
            if self.used[form][place] is not None:
                self.used[form][place].wait_send()
            out = self.work[form][1]

            def store(where, value):
                out[(place,) + where] = value.astype(out.dtype)

            self.add_up(t, loaded, store)
            copy = self.remote(t, out.at[place], target, to, kind)
            copy.start()
            self.used[form][place] = copy

        return finish

    def first(self, t, k):
        if k == 3:
            self.arrived(t, self.landed(t, 3), SIBLING, (SIBLING, 3))
        to = EAST if k in EASTWARD else NORTH
        return self.sum_and_send(t, 3, k, [], self.lands[t][1].at[k], to, (ONCE, k))

    def second(self, t, dd, k):
        if (dd, k) in ((1, 3), (2, 2)):
            self.arrived(t, self.landed(t, dd), SIBLING, (SIBLING, dd))
        to, land = (EAST, self.lands[t][2]) if dd == 1 else (NORTH, self.lands[t][3])
        extra = []
        if (dd == 1) != (k in EASTWARD):
            one = self.lands[t][1].at[k]
            self.arrived(t, one, EAST if k in EASTWARD else NORTH, (ONCE, k))
            extra = [one]
        return self.sum_and_send(t, dd, k, extra, land.at[k], to, (to, k))

    def third(self, t, k):
        if k == 3:
            self.arrived(t, self.landed(t, 0), SIBLING, (SIBLING, 0))
        extra = []
        for to, land in ((EAST, self.lands[t][2]), (NORTH, self.lands[t][3])):
            self.arrived(t, land.at[k], to, (to, k))
            extra.append(land.at[k])
        if k:
            return self.sum_and_send(t, 0, k, extra, self.lands[t][4].at[k], (LEVEL, k), (LEVEL, k))
        loaded = self.load(t, self.sources(t, 0, 0, extra))
        total = self.work[self.kinds[t]][2]

        def store(where, value):
            total[where] = value

        return lambda: self.add_up(t, loaded, store)

    def final_part(self, t, core):
        if self.kinds[t] == COLUMNS:
            return (slice(None), slice(None)), (slice(None), pl.ds(2176 * core, 2176))
        return (pl.ds(16 * core, 144 - 16 * core),), (pl.ds(144 * core, 144 - 16 * core),)

    def last(self, t):
        land = self.lands[t][4]
        for k in (1, 2, 3):
            self.arrived(t, land.at[k], (LEVEL, k), (LEVEL, k))
        loaded = self.load(t, [land.at[k] for k in (1, 2, 3)])
        total = self.work[self.kinds[t]][2]
        owner = self.owners[t]

        def store(where, value):
            total[where] = total[where] + value

        def act(core):
            inner, outer = self.final_part(t, core)
            source, target = total.at[inner], self.finals[t].at[outer]
            if core == owner:
                copy = pltpu.make_async_copy(source, target, self.out_sem)
                copy.start()
                copy.wait()
                theirs = self.finals[t].at[self.final_part(t, 1 - core)[1]]
                self.remote(t, theirs, theirs, SIBLING, (CORNER, 0)).wait_recv()
            else:
                copy = self.remote(t, source, target, SIBLING, (CORNER, 0))
                copy.start()
                copy.wait_send()

        def finish():
            self.add_up(t, loaded, store)
            per_core(self.core, act)

        return finish

    def give_all(self, t):
        for dd in (3, 1, 2, 0):
            self.give(t, dd)

    def steps(self, t):
        def of(waits, function, *given):
            return waits, lambda: function(*given)

        ways = ((1, 3), (2, 2), (1, 0), (2, 1), (1, 2), (2, 3), (1, 1), (2, 0))
        return (
            [of(k == 3, self.first, t, k) for k in (3, 2, 0, 1)],
            [of((dd == 1) != (k in EASTWARD), self.second, t, dd, k) for dd, k in ways],
            [of(True, self.third, t, k) for k in (3, 2, 1, 0)],
            [of(True, self.last, t)],
        )

    def drain(self):
        for copy in self.given:
            copy.wait_send()
        for held in self.used.values():
            for copy in held:
                if copy is not None:
                    copy.wait_send()


def in_turn(earlier, later, done=()):
    return later[0] + earlier[2][:2] + later[1][:4] + list(done) + earlier[2][2:] + later[1][4:]


def tiny_shapes():
    return [
        pltpu.VMEM((16, 16, 128), F32), pltpu.VMEM((16, 16, 128), F32), pltpu.VMEM((2, 4, 16, 128), F32),
        pltpu.VMEM((4, 16, 128), F32), pltpu.VMEM((3, 16, 128), F32),
        pltpu.SemaphoreType.DMA((7,)), pltpu.SemaphoreType.DMA((7,)),
    ]


def tiny_steps(both, final, refs, place_of):
    total, land, land_east, land_north, land_line, send_sem, recv_sem = refs
    core, rings, lines, toward = place_of
    blocks = [pl.ds(rings[dd] * 4, 4) for dd in range(4)]

    def copy(number, source, target, to):
        return remote_copy(source, target, send_sem.at[number], recv_sem.at[number], toward[to])

    over = copy(0, both.at[1 - core], land, SIBLING)
    east = [copy(1 + i, total.at[blocks[dd]], land_east.at[i], EAST) for i, dd in enumerate((1, 3))]
    north = copy(3, total.at[blocks[2]], land_north, NORTH)
    line = [copy(3 + k, total.at[rings[0] * 4 + lines[k]], land_line.at[k - 1], (LEVEL, k)) for k in (1, 2, 3)]

    def zero():
        over.start()
        return lambda: None

    def one():
        over.wait_recv()
        total[...] = both[core] + land[...]
        for each in east:
            each.start()
        return lambda: None

    def two():
        for i, each in enumerate(east):
            each.wait_recv()
            total[blocks[2 * i]] = total[blocks[2 * i]] + land_east[i]
        north.start()
        return lambda: None

    def three():
        north.wait_recv()
        total[blocks[0]] = total[blocks[0]] + land_north[...]
        for each in line:
            each.start()
        return lambda: None

    def four():
        value = total[rings[0] * 4 + lines[0]]
        for i, each in enumerate(line):
            each.wait_recv()
            value = value + land_line[i]
        final[...] = value
        for each in [over, north] + east + line:
            each.wait_send()
        return lambda: None

    return [(True, step) for step in (zero, one, two, three, four)]


def backward_kernel(*refs):
    vectors_of, table, refs = refs[:2], refs[2], refs[3:]
    stored_of, refs = ((None,) + refs[:14], refs[14:29]), refs[29:]
    weights_of, outer_rows, refs = (refs[:3], refs[3:6]), refs[6], refs[7:]
    small_out, refs = refs[0], refs[1:]
    pages_of, refs = (refs[:3], refs[3:6]), refs[6:]
    shipped_of, refs = refs[:2], refs[2:]
    reduce_final, expand_final, attention_final, refs = refs[0], refs[1], refs[2], refs[3:]
    kinds = (ROWS, COLUMNS, COLUMNS) * 2
    owners = (1, 1, 1, 0, 0, 0)
    n = len(kinds)
    lands, refs = [refs[5 * t : 5 * t + 5] for t in range(n)], refs[5 * n :]
    (reduce_ring, expand_ring, output, second_sum, left_one, left_two, stage_wide, stage_tall, wide_sum, query_sum,
     here_sum, beside_give, away_give, corner_give, beside_got, away_got_one, away_got_two, corner_got, hidden_all, mixture,
     grad_middle, grad_attended, sums, both, result_one, result_two, reduce_sem, expand_sem, output_sem, wide_sem, tall_sem,
     pair_send, pair_recv, ship_send, ship_recv, ship_sem) = refs[:36]
    refs = refs[36:]
    tiny_refs, held, load_sem, refs = refs[:7], refs[7:22], refs[22], refs[23:]
    (top, x, normed_in, query, here, beside, away, corner, attended, logs, attended_low, middle, second, active,
     slope) = held
    place_of = places()
    core, rings, lines, toward = place_of
    scatter = Scatter(kinds, pages_of[1] + pages_of[0], lands, (reduce_final, expand_final, attention_final) * 2, owners, refs, place_of)
    steps = [scatter.steps(t) for t in range(n)]
    rows, width = top.shape
    half = rows // 2
    first = low_place(lines[0]) == 0
    tiles = weights_of[0][1].shape[1] // 256
    lead = 4 * width - WIDE
    edge = 3 * width
    todo, open_ends = [], []

    def progress(count):
        for _ in range(count):
            if todo:
                waits, begin = todo.pop(0)
                if waits and open_ends:
                    open_ends.pop()()
                ended = begin()
                if open_ends:
                    open_ends.pop()()
                open_ends.append(ended)

    def row(value):
        return jnp.sum(value, axis=0, keepdims=True)

    which = lines[0] // 2
    mine = pl.ds(pl.multiple_of(core * half, half), half)
    other = pl.ds(pl.multiple_of((1 - core) * half, half), half)
    near_rows = pl.ds(pl.multiple_of(which * half, half), half)
    far_rows = pl.ds(pl.multiple_of((1 - which) * half, half), half)

    def ship_copies(number, rows_ref):
        target = shipped_of[number].at[which, mine]
        near, distant = rows_ref.at[near_rows], rows_ref.at[far_rows]
        ways = ((near, SIBLING), (distant, (LEVEL, 3)), (distant, (CORNER, 3)))
        remote = [
            remote_copy(source, target, ship_send.at[3 * number + index], ship_recv.at[3 * number + index], toward[to])
            for index, (source, to) in enumerate(ways)
        ]
        return pltpu.make_async_copy(near, target, ship_sem.at[number]), remote

    def ship(number, layer, rows_ref):
        local, remote = ship_copies(number, rows_ref)

        def act(index):
            for copy in (local, remote[1]) if index == layer else (remote[0], remote[2]):
                copy.start()

        per_core(core, act)

    def shipped_all(number):
        local, remote = ship_copies(number, result_one)
        local.wait()
        for index, (sequence, part) in enumerate(((which, other), (1 - which, mine), (1 - which, other))):
            remote[index].wait_send()
            ref = shipped_of[number].at[sequence, part]
            place = 3 * number + index
            remote_copy(ref, ref, ship_send.at[place], ship_recv.at[place], toward[SIBLING]).wait_recv()

    def load_copy(layer, i):
        return pltpu.make_async_copy(stored_of[layer][i], held[i], load_sem.at[i])

    def load(layer, *numbers):
        for i in numbers:
            load_copy(layer, i).start()

    def pair_copy(layer, source, target, to, number):
        index = 3 * layer + number
        return remote_copy(source, target, pair_send.at[index], pair_recv.at[index], toward[to])

    def pair_copies(layer):
        away_got = away_got_one if layer == 1 else away_got_two
        return (
            pair_copy(layer, corner_give, corner_got, SIBLING, 0),
            pair_copy(layer, away_give, away_got, (LEVEL, 1), 1),
            pair_copy(layer, beside_give, beside_got, SIBLING, 2),
        )

    def layer_pass(layer):
        page_hbm, expand_hbm, reduce_hbm = weights_of[layer]
        page_reduce, page_expand, page_attention = pages_of[layer]
        vectors = vectors_of[layer]
        away_got = away_got_one if layer == 1 else away_got_two

        def tile_at(i):
            return pl.ds(pl.multiple_of(i * 256, 256), 256)

        def reduce_copy(i):
            slot = lax.rem(i, 3)
            return pltpu.make_async_copy(reduce_hbm.at[tile_at(i)], reduce_ring.at[slot], reduce_sem.at[slot])

        def expand_copy(i, source):
            slot = lax.rem(i, 3)
            return pltpu.make_async_copy(source.at[:, tile_at(i)], expand_ring.at[slot], expand_sem.at[slot])

        def wide_copy(i, target):
            slot = lax.rem(i, 2)
            return pltpu.make_async_copy(stage_wide.at[slot], target.at[:, :, tile_at(i)], wide_sem.at[slot])

        def tall_copy(i):
            slot = lax.rem(i, 2)
            return pltpu.make_async_copy(stage_tall.at[slot], page_reduce.at[tile_at(i)], tall_sem.at[slot])

        def loaded(*numbers):
            for i in numbers:
                load_copy(layer, i).wait()

        for i in range(3):
            reduce_copy(i).start()
            expand_copy(i, expand_hbm).start()
        output_copy = pltpu.make_async_copy(page_hbm.at[:, pl.ds(lead, WIDE)], output, output_sem)
        output_copy.start()
        if layer == 1:
            load(1, 11, 3, 8, 9, 4, 5, 6, 7, 10, 2, 1)
            greet(toward)
            ship(0, 0, stored_of[1][1])
            ship(0, 1, outer_rows)
        else:
            top[...] = result_one[...]
            for copy in pair_copies(1):
                copy.wait_send()
        second_sum[...] = jnp.zeros_like(second_sum)

        def tall_tile(i, _):
            side = lax.rem(i, 2)

            @pl.when(i >= 2)
            def _():
                tall_copy(i - 2).wait()

            stage_tall[side] = mm_tn(active[:, tile_at(i)], top[...]).astype(LOW)
            tall_copy(i).start()
            return 0

        def tall_page(t):
            for begin_at in range(0, tiles, 6):
                lax.fori_loop(begin_at, min(begin_at + 6, tiles), tall_tile, 0)
                progress(1)
            for i in (tiles - 2, tiles - 1):
                tall_copy(i).wait()
            scatter.give_all(t)

        def wide_tile(i, _):
            side = lax.rem(i, 2)

            @pl.when(i >= 2)
            def _():
                wide_copy(i - 2, page_expand).wait()

            stage_wide[side] = mm(left_one[...], hidden_all[:, tile_at(i)]).reshape(16, 72, 256).astype(LOW)
            wide_copy(i, page_expand).start()
            return 0

        def wide_page(t):
            for begin_at in range(0, tiles, 5):
                lax.fori_loop(begin_at, min(begin_at + 5, tiles), wide_tile, 0)
                progress(1)
            for i in (tiles - 2, tiles - 1):
                wide_copy(i, page_expand).wait()
            scatter.give_all(t)

        if layer == 1:
            loaded(0, 13)
            tall_page(0)
            todo.extend(steps[0][0] + steps[0][1])
        loaded(14, 12)
        left_one[...] = second[...].T

        def feed_tile(i, _):
            at = tile_at(i)
            slot = lax.rem(i, 3)
            reduce_copy(i).wait()
            hidden = (mm_nt(top[...], reduce_ring[slot]) * slope[:, at].astype(F32)).astype(LOW)
            wide_sum[0:1, at] = jnp.sum(hidden.astype(F32), axis=0, keepdims=True)
            hidden_all[:, at] = hidden
            expand_copy(i, expand_hbm).wait()
            second_sum[...] += mm_nt(hidden, expand_ring[slot])

            @pl.when(i + 3 < tiles)
            def _():
                reduce_copy(i + 3).start()
                expand_copy(i + 3, expand_hbm).start()

            return 0

        for begin_at in range(0, tiles, 2):
            lax.fori_loop(begin_at, min(begin_at + 2, tiles), feed_tile, 0)
            progress(1)
        for i in range(3):
            expand_copy(i, page_hbm).start()

        loaded(11)
        upstream = top[...].astype(F32)
        grad_second = close_up(second_sum[...], table[...])
        unit, inverse = normal_parts(middle[...])
        sums[6:7] = row(grad_second * unit)
        sums[7:8] = row(grad_second)
        sums[5:6] = row(upstream)
        value = upstream + normal_back(grad_second * vectors[6:7], unit, inverse)
        grad_middle[...] = value
        branch = value.astype(LOW)
        sums[4:5] = row(branch.astype(F32))
        progress(1)
        mixture[:, edge:] = branch
        output_copy.wait()
        full = jnp.concatenate([jnp.zeros((rows, edge - lead), LOW), branch], axis=1)
        pulled = mm_nt(full, output[...]).astype(LOW)
        grad_attended[:, :width] = mm_nt(pulled, table[...]).astype(LOW)
        grad_attended[:, width:] = jnp.zeros((rows, WIDE - width), LOW)
        progress(1)

        loaded(3, 8, 9, 4, 5, 6, 7)

        def rows_of(place, at, p):
            part = slice(place * half, (place + 1) * half)
            product = (grad_attended[part, at].astype(F32) * attended[part, at]).T
            delta = jnp.concatenate([row(product[:HDIM]), row(product[HDIM:])], axis=1)
            return head_pair(query[part, at]), head_pair(grad_attended[part, at]), logs[p, place : place + 1], delta

        def block(kind, near, part, at):
            rows_at = pl.ds(part * half, half)
            one, two = (here, beside) if near == 0 else (away, corner)
            return jnp.concatenate([one[kind, rows_at, at], two[kind, rows_at, at]], axis=0)

        def back(own, keys, values):
            queries, grads, log, delta = own
            weights = jnp.exp(mm_nt(keys, queries) - log)
            lowered = (weights * (mm_nt(values, grads) - delta)).astype(LOW)
            return mm_tn(keys, lowered), mm(lowered, queries), mm(weights.astype(LOW), grads)

        def put(one, two, part, at, grads):
            rows_at = pl.ds(part * half, half)
            for kind, value in enumerate(grads):
                one[kind, rows_at, at] = value[:half].astype(one.dtype)
                two[kind, rows_at, at] = value[half:].astype(two.dtype)

        def far_pair(p, _):
            at = pl.ds(pl.multiple_of(p * 128, 128), 128)
            low, high = rows_of(0, at, p), rows_of(1, at, p)
            last_rows = tuple(jnp.where(first, b, a) for a, b in zip(low, high))
            keys, values = block(0, 1, 0, at), block(1, 1, 0, at)
            high_query, keys_a, values_a = back(high, keys, values)
            last_keys = jnp.where(first, block(0, 1, 1, at), keys)
            last_values = jnp.where(first, block(1, 1, 1, at), values)
            more, keys_b, values_b = back(last_rows, last_keys, last_values)
            zero, empty = jnp.zeros_like(keys_b), jnp.zeros_like(more)
            put(away_give, corner_give, 0, at,
                (keys_a + jnp.where(first, zero, keys_b), values_a + jnp.where(first, zero, values_b)))
            put(away_give, corner_give, 1, at, (jnp.where(first, keys_b, zero), jnp.where(first, values_b, zero)))
            query_sum[:half, at] = from_pair(jnp.where(first, empty, more))
            query_sum[half:, at] = from_pair(high_query + jnp.where(first, more, empty))
            return 0

        for begin_at in (0, 3, 6):
            lax.fori_loop(begin_at, begin_at + 3, far_pair, 0)
            progress(1)

        to_corner, to_away, to_beside = pair_copies(layer)
        to_corner.start()

        def near_pair(p, _):
            at = pl.ds(pl.multiple_of(p * 128, 128), 128)
            low, high = rows_of(0, at, p), rows_of(1, at, p)
            keys, values = block(0, 0, 0, at), block(1, 0, 0, at)
            low_query, keys_a, values_a = back(low, keys, values)
            high_query, keys_b, values_b = back(high, keys, values)
            put(here_sum, beside_give, 0, at, (keys_a + keys_b, values_a + values_b))
            more, keys_a, values_a = back(high, block(0, 0, 1, at), block(1, 0, 1, at))
            put(here_sum, beside_give, 1, at, (keys_a, values_a))
            query_sum[:half, at] += from_pair(low_query)
            query_sum[half:, at] += from_pair(high_query + more)
            return 0

        lax.fori_loop(0, 2, near_pair, 0)
        to_corner.wait_recv()
        for kind in (0, 1):
            away_give[kind] = (away_give[kind].astype(F32) + corner_got[kind].astype(F32)).astype(LOW)
        to_away.start()
        progress(1)
        for begin_at, end in ((2, 5), (5, 9)):
            lax.fori_loop(begin_at, end, near_pair, 0)
            progress(1)
        to_beside.start()
        if layer == 1:
            wide_page(1)
            todo.extend(in_turn(steps[0], steps[1]))
        else:
            loaded(13)
            tall_page(3)
            todo.extend(in_turn(steps[2], steps[3], steps[1][3]))
            wide_page(4)
            todo.extend(in_turn(steps[3], steps[4], steps[2][3]))
        low = (query_sum[:, :width] * HDIM ** (-0.5)).astype(LOW)
        mixture[:, :width] = low
        sums[2:3] = row(low.astype(F32))
        loaded(10, 2, 1)
        left_one[...] = normed_in[...].T
        left_two[...] = attended_low[...].T
        second_sum[...] = jnp.zeros_like(second_sum)
        progress(4)
        to_beside.wait_recv()
        to_away.wait_recv()
        for kind in (0, 1):
            value = here_sum[kind] + beside_got[kind].astype(F32) + away_got[kind].astype(F32)
            low = value[:, :width].astype(LOW)
            mixture[:, (1 + kind) * width : (2 + kind) * width] = low
        sums[3:4] = row(low.astype(F32))

        def project_tile(i, _):
            at = tile_at(i)
            slot = lax.rem(i, 3)
            column = i * 256 + lax.broadcasted_iota(jnp.int32, (rows, 256), 1)
            part = mixture[:, at]
            part = jnp.where(column < edge, part, jnp.zeros_like(part))
            expand_copy(i, page_hbm).wait()
            second_sum[...] += mm_nt(part, expand_ring[slot])

            @pl.when(i + 3 < 13)
            def _():
                expand_copy(i + 3, page_hbm).start()

            return 0

        for begin_at, end in ((0, 4), (4, 8), (8, 13)):
            lax.fori_loop(begin_at, end, project_tile, 0)
            progress(1)
        grad_normed = close_up(second_sum[...], table[...])
        unit, inverse = normal_parts(x[...].astype(F32))
        sums[0:1] = row(grad_normed * unit)
        sums[1:2] = row(grad_normed)
        result = result_one if layer == 1 else result_two
        result[...] = (grad_middle[...] + normal_back(grad_normed * vectors[0:1], unit, inverse)).astype(LOW)
        if layer == 1:
            load(0, 14, 12, 11, 3, 8, 9, 4, 5, 6, 7, 13, 10, 2, 1)
        ship(1, layer, result)
        progress(2)

        def page_tile(number, i):
            side = lax.rem(i, 2)
            at = tile_at(i)

            @pl.when(i >= 2)
            def _():
                wide_copy(i - 2, page_attention).wait()

            part = mixture[:, at]
            if number == 1:
                value = mm(left_one[...], part)
            elif number == 2:
                value = mm(left_two[...], part)
            else:
                column = i * 256 + lax.broadcasted_iota(jnp.int32, (rows, 256), 1)
                zero = jnp.zeros_like(part)
                value = mm(left_one[...], jnp.where(column < edge, part, zero))
                value = value + mm(left_two[...], jnp.where(column < edge, zero, part))
            stage_wide[side] = value.reshape(16, 72, 256).astype(LOW)
            wide_copy(i, page_attention).start()

        def page_loop(number, begin_at, end):
            def step(i, _):
                page_tile(number, i)
                return 0

            lax.fori_loop(begin_at, end, step, 0)

        whole_tiles = edge // 256
        for begin_at in range(0, whole_tiles, 4):
            page_loop(1, begin_at, begin_at + 4)
            progress(1)
        page_loop(3, whole_tiles, whole_tiles + 1)
        page_loop(2, whole_tiles + 1, tiles)
        for i in (tiles - 2, tiles - 1):
            wide_copy(i, page_attention).wait()
        scatter.give_all(2 if layer == 1 else 5)
        if layer == 1:
            todo.extend(in_turn(steps[1], steps[2], steps[0][3]))
        small = both.at[layer]
        small[...] = jnp.zeros(small.shape, F32)
        for shard in range(16):
            small[shard, 0:8, 0:68] = sums[:, shard * 68 : (shard + 1) * 68]
            for part in range(4):
                begin_at = shard * 272 + part * 68
                small[shard, 8 + part : 9 + part, 0:68] = wide_sum[0:1, begin_at : begin_at + 68]

    load(1, 0, 13, 14, 12)
    layer_pass(1)
    layer_pass(0)
    tiny = tiny_steps(both, small_out, tiny_refs, place_of)
    todo += in_turn(steps[4], steps[5], steps[3][3])
    for place, step in enumerate(tiny):
        todo.insert(min(4 * place, len(todo)), step)
    todo += steps[5][2][:3] + steps[4][3] + steps[5][2][3:] + steps[5][3]
    progress(len(todo))
    open_ends.pop()()
    scatter.drain()
    shipped_all(0)
    shipped_all(1)
    for copy in pair_copies(0):
        copy.wait_send()


def backward(top, saved, vectors, table, weights, outer_rows):
    rows, width = top.shape
    inner = weights[0][1].shape[1]
    anywhere = pl.BlockSpec(memory_space=pl.ANY)
    inside = pl.BlockSpec(memory_space=pltpu.VMEM)
    kinds = (ROWS, COLUMNS, COLUMNS) * 2
    page = jax.ShapeDtypeStruct((16, 72, inner), LOW)
    outs = [jax.ShapeDtypeStruct((16, 128), F32)]
    outs += [jax.ShapeDtypeStruct((inner, width), LOW), page, page] * 2
    outs += [jax.ShapeDtypeStruct((2, rows, width), LOW)] * 2
    outs += [final_shape(kind) for kind in kinds[:3]]
    for kind in kinds:
        outs += landing_shapes(kind)
    pair = pltpu.VMEM((2, rows, WIDE), LOW)
    tall = pltpu.VMEM((WIDE, rows), LOW)
    flat = pltpu.VMEM((rows, width), LOW)
    dma = pltpu.SemaphoreType.DMA
    scratch = [
        pltpu.VMEM((3, 256, width), LOW), pltpu.VMEM((3, WIDE, 256), LOW), pltpu.VMEM((WIDE, WIDE), LOW),
        pltpu.VMEM((rows, WIDE), F32), tall, tall, pltpu.VMEM((2, 16, 72, 256), LOW), pltpu.VMEM((2, 256, width), LOW),
        pltpu.VMEM((8, inner), F32), pltpu.VMEM((rows, WIDE), F32), pltpu.VMEM((2, rows, WIDE), F32),
        pair, pair, pair, pair, pair, pair, pair, pltpu.VMEM((rows, inner), LOW), pltpu.VMEM((rows, inner), LOW),
        pltpu.VMEM((rows, width), F32), pltpu.VMEM((rows, WIDE), LOW), pltpu.VMEM((8, width), F32),
        pltpu.VMEM((2, 16, 16, 128), F32), flat, flat, dma((3,)), dma((3,)), dma(()), dma((2,)), dma((2,)),
        dma((6,)), dma((6,)), dma((6,)), dma((6,)), dma((2,)),
    ] + tiny_shapes() + [pltpu.VMEM(value.shape, value.dtype) for value in (top,) + saved[1]] + [dma((15,))] + work_shapes(kinds)
    res = pl.pallas_call(
        backward_kernel,
        out_shape=tuple(outs),
        in_specs=[inside] * 3 + [anywhere] * (29 + 7),
        out_specs=(inside,) + (anywhere,) * (len(outs) - 1),
        scratch_shapes=scratch,
        compiler_params=pltpu.CompilerParams(collective_id=4, has_side_effects=True, vmem_limit_bytes=63 << 20),
        name="backward",
    )(*vectors, table, *saved[0], top, *saved[1], *weights[0], *weights[1], outer_rows)
    return res[0], res[7][None], res[8][None], res[9:12]


def spread(width):
    feature = np.arange(width)
    table = np.zeros((width, 16 * 72), np.float32)
    table[feature, feature // 68 * 72 + feature % 68] = 1
    return jnp.asarray(table, LOW)


def small_of(page):
    row = page[:, 68].astype(F32)
    vectors = row[:, : 8 * 128].reshape(16, 8, 128)[:, :, :68].transpose(1, 0, 2)
    return vectors.reshape(8, -1), row[:, 8 * 128 : 8 * 128 + 4 * 68].reshape(1, -1)


def four_by_four(
    inputs,
    cotangent,
    first_gain,
    first_shift,
    joint_weight,
    query_bias,
    value_bias,
    output_weight,
    output_bias,
    second_gain,
    second_shift,
    expand_weight,
    expand_bias,
    reduce_weight,
    reduce_bias,
):
    core = lax.axis_index(SECTION)
    width = HEADS * HDIM
    vectors = (
        first_gain,
        first_shift,
        query_bias,
        value_bias,
        output_bias,
        reduce_bias,
        second_gain,
        second_shift,
        expand_bias,
    )
    packed = sum(
        jnp.pad(vector, ((0, 3), (128 * place, 4 * width - 128 * place - vector.shape[1])))
        for place, vector in enumerate(vectors)
    )
    attention_shard = jnp.concatenate(
        [jnp.concatenate([joint_weight[0], output_weight[0]], axis=1), packed], axis=0
    )
    expand_shard = jnp.pad(expand_weight[0], ((0, 4), (0, 0)))
    reduce_shard = reduce_weight[0]
    table = spread(width)

    def flat(page):
        return page.reshape(-1, page.shape[2])

    lower_page, rows = gather_page(attention_shard, inputs)
    small, wide = small_of(lower_page)
    shards = ((0, True, expand_shard), (0, False, reduce_shard), (1, True, attention_shard))
    saved, (lower_expand, lower_reduce, upper_page), _ = forward(rows, small, wide, table, flat(lower_page), shards)
    weights = (flat(lower_page), flat(lower_expand), flat(lower_reduce))
    saved_lower, middle_rows = (rows,) + tuple(saved[:13]), saved[13]
    upper_small, upper_wide = small_of(upper_page)
    shards = ((1, True, expand_shard), (1, False, reduce_shard))
    saved, (upper_expand, upper_reduce), (top,) = forward(
        middle_rows, upper_small, upper_wide, table, flat(upper_page), shards, (cotangent,)
    )
    upper_weights = (flat(upper_page), flat(upper_expand), flat(upper_reduce))
    saved_upper, final_rows = (middle_rows,) + tuple(saved[:13]), saved[13]
    vectors, layer_outputs, input_grads, (reduce_sum, expand_sum, attention_sum) = backward(
        top, (saved_lower, saved_upper), (small, upper_small), table, (weights, upper_weights), final_rows
    )
    vectors = vectors[:12, :68]
    return (
        layer_outputs,
        input_grads,
        vectors[0][None],
        vectors[1][None],
        attention_sum[None, :68, : 3 * width],
        vectors[2][None],
        vectors[3][None],
        attention_sum[None, :68, 3 * width :],
        vectors[4][None],
        vectors[6][None],
        vectors[7][None],
        expand_sum[None, :68],
        vectors[8:].reshape(1, -1),
        reduce_sum[None],
        vectors[5][None],
    )


def fits(mesh):
    return dict(mesh.shape) == {SECTION: 2, RING: 4, LINE: 4}


def solution(mesh):
    return jax.shard_map(
        four_by_four if fits(mesh) else body,
        mesh=mesh,
        in_specs=(
            P(RING, LINE, None),
            P(RING, LINE, None),
            P(SECTION, OWNERS),
            P(SECTION, OWNERS),
            P(SECTION, OWNERS, None),
            P(SECTION, OWNERS),
            P(SECTION, OWNERS),
            P(SECTION, OWNERS, None),
            P(SECTION, OWNERS),
            P(SECTION, OWNERS),
            P(SECTION, OWNERS),
            P(SECTION, OWNERS, None),
            P(SECTION, OWNERS),
            P(SECTION, OWNERS, None),
            P(SECTION, OWNERS),
        ),
        out_specs=(
            P(SECTION, RING, LINE, None),
            P(SECTION, RING, LINE, None),
            P(SECTION, OWNERS),
            P(SECTION, OWNERS),
            P(SECTION, OWNERS, None),
            P(SECTION, OWNERS),
            P(SECTION, OWNERS),
            P(SECTION, OWNERS, None),
            P(SECTION, OWNERS),
            P(SECTION, OWNERS),
            P(SECTION, OWNERS),
            P(SECTION, OWNERS, None),
            P(SECTION, OWNERS),
            P(SECTION, OWNERS, None),
            P(SECTION, OWNERS),
        ),
        check_vma=False,
    )
```

```python
from functools import partial

import jax
import jax.numpy as jnp
import numpy as np
from jax import lax
from jax.experimental import pallas as pl
from jax.experimental.pallas import tpu as pltpu
from jax.sharding import PartitionSpec as P

HEADS = 17
HDIM = 64
BLK = 256
WIDE = 1152
F32, LOW = jnp.float32, jnp.bfloat16
SECTION, RING, LINE = "section", "dp", "seq"
OWNERS = (RING, LINE)
EAST, NORTH, LEVEL, SIBLING, CORNER, ONCE, UP, DOWN = range(8)


epsilon = 1e-05
far_below = -1e30


def passed_along(value, axis, steps):
    count = lax.axis_size(axis)
    first, last = (max(0, -steps), min(count, count - steps))
    return lax.ppermute(value, axis, [(source, source + steps) for source in range(first, last)])


def normalize(values, scales, offsets):
    centre = jnp.mean(values, axis=-1, keepdims=True)
    centred = values - centre
    inverse = lax.rsqrt(jnp.mean(centred * centred, axis=-1, keepdims=True) + epsilon)
    unit_rows = centred * inverse
    return (unit_rows * scales + offsets, unit_rows, inverse)


def normalize_back(upstream, unit_rows, inverse):
    return inverse * (
        upstream
        - jnp.mean(upstream, axis=-1, keepdims=True)
        - unit_rows * jnp.mean(upstream * unit_rows, axis=-1, keepdims=True)
    )


def score_block(query, key_block, block_index, row_block):
    scores = jnp.einsum(
        "qhd,khd->qhk", query, key_block, preferred_element_type=jnp.float32
    ) * HDIM ** (-0.5)
    highest = jnp.max(scores, axis=-1)
    allowed = (block_index <= row_block)[:, None]
    exponent = jnp.exp(scores - highest[..., None]) * allowed[..., None].astype(jnp.float32)
    levels = jnp.where(allowed, highest, far_below)
    return (exponent, levels)


def attend_forward(query, keys_all, values_all, row_block):
    length = keys_all.shape[0]
    row_count = query.shape[0]
    key_shaped = keys_all.reshape(length, HEADS, HDIM)
    value_shaped = values_all.reshape(length, HEADS, HDIM)
    block_limit = row_block[-1] + 1

    def advance(block_index, carried):
        running_peak, running_sum, weighted = carried
        key_block = lax.dynamic_slice_in_dim(key_shaped, block_index * BLK, BLK, 0)
        value_block = lax.dynamic_slice_in_dim(value_shaped, block_index * BLK, BLK, 0)
        exponent, levels = score_block(query, key_block, block_index, row_block)
        weights = exponent.astype(jnp.bfloat16)
        block_out = jnp.einsum(
            "qhk,khd->qhd", weights, value_block, preferred_element_type=jnp.float32
        )
        newest_peak = jnp.maximum(running_peak, levels)
        shrink_old = jnp.exp(running_peak - newest_peak)
        shrink_new = jnp.exp(levels - newest_peak)
        running_sum = running_sum * shrink_old + shrink_new * jnp.sum(exponent, axis=-1)
        weighted = weighted * shrink_old[..., None] + shrink_new[..., None] * block_out
        return (newest_peak, running_sum, weighted)

    initial = (
        jnp.full((row_count, HEADS), far_below, jnp.float32),
        jnp.zeros((row_count, HEADS), jnp.float32),
        jnp.zeros((row_count, HEADS, HDIM), jnp.float32),
    )
    running_peak, running_sum, weighted = lax.fori_loop(0, block_limit, advance, initial)
    return (weighted / running_sum[..., None], running_peak + jnp.log(running_sum))


def attend_backward(query, keys_all, values_all, row_block, attended, log_total, grad_attended):
    length = keys_all.shape[0]
    key_shaped = keys_all.reshape(length, HEADS, HDIM)
    value_shaped = values_all.reshape(length, HEADS, HDIM)
    block_limit = row_block[-1] + 1
    delta = jnp.sum(grad_attended * attended, axis=-1)

    def advance(block_index, carried):
        grad_query, grad_keys, grad_values = carried
        key_block = lax.dynamic_slice_in_dim(key_shaped, block_index * BLK, BLK, 0)
        value_block = lax.dynamic_slice_in_dim(value_shaped, block_index * BLK, BLK, 0)
        exponent, levels = score_block(query, key_block, block_index, row_block)
        weights = exponent.astype(jnp.bfloat16)
        factor = jnp.exp(levels - log_total)
        scaled = (factor[..., None] * grad_attended).astype(jnp.bfloat16)
        grad_weights = jnp.einsum(
            "qhd,khd->qhk", scaled, value_block, preferred_element_type=jnp.float32
        )
        grad_scores = (exponent * (grad_weights - (factor * delta)[..., None])).astype(jnp.bfloat16)
        grad_query = grad_query + jnp.einsum(
            "qhk,khd->qhd", grad_scores, key_block, preferred_element_type=jnp.float32
        )
        grad_key = jnp.einsum(
            "qhk,qhd->khd", grad_scores, query, preferred_element_type=jnp.float32
        )
        grad_value = jnp.einsum("qhk,qhd->khd", weights, scaled, preferred_element_type=jnp.float32)
        grad_keys = lax.dynamic_update_slice_in_dim(grad_keys, grad_key, block_index * BLK, 0)
        grad_values = lax.dynamic_update_slice_in_dim(grad_values, grad_value, block_index * BLK, 0)
        return (grad_query, grad_keys, grad_values)

    initial = (
        jnp.zeros(query.shape, jnp.float32),
        jnp.zeros((length, HEADS, HDIM), jnp.float32),
        jnp.zeros((length, HEADS, HDIM), jnp.float32),
    )
    grad_query, grad_keys, grad_values = lax.fori_loop(0, block_limit, advance, initial)
    return (
        grad_query,
        grad_keys.reshape(length, HEADS * HDIM),
        grad_values.reshape(length, HEADS * HDIM),
    )


def project(source, params):
    feature_width = HEADS * HDIM
    normed, unit_rows, inverse = normalize(
        source, params[0].astype(jnp.float32), params[1].astype(jnp.float32)
    )
    normed_low = normed.astype(jnp.bfloat16)
    mixture = jnp.dot(normed_low, params[2], preferred_element_type=jnp.float32)
    query_low = (mixture[:, :feature_width] + params[3].astype(jnp.float32)).astype(jnp.bfloat16)
    keys_low = mixture[:, feature_width : 2 * feature_width].astype(jnp.bfloat16)
    values_low = (mixture[:, 2 * feature_width :] + params[4].astype(jnp.float32)).astype(
        jnp.bfloat16
    )
    return (unit_rows, inverse, normed_low, query_low, keys_low, values_low)


def complete(source, params, projected, gathered, row_block):
    row_count = source.shape[0]
    query = projected[3].reshape(row_count, HEADS, HDIM)
    attended, log_total = attend_forward(query, gathered[0], gathered[1], row_block)
    attended_low = attended.reshape(row_count, HEADS * HDIM).astype(jnp.bfloat16)
    middle = source + (
        jnp.dot(attended_low, params[5], preferred_element_type=jnp.float32)
        + params[6].astype(jnp.float32)
    )
    second, unit_second, inverse_second = normalize(
        middle, params[7].astype(jnp.float32), params[8].astype(jnp.float32)
    )
    second_low = second.astype(jnp.bfloat16)
    hidden = jnp.dot(second_low, params[9], preferred_element_type=jnp.float32) + params[10].astype(
        jnp.float32
    )
    active, gelu_pull = jax.vjp(partial(jax.nn.gelu, approximate=False), hidden)
    active_low = active.astype(jnp.bfloat16)
    result = middle + (
        jnp.dot(active_low, params[11], preferred_element_type=jnp.float32)
        + params[12].astype(jnp.float32)
    )
    saved = (
        query,
        attended,
        log_total,
        attended_low,
        unit_second,
        inverse_second,
        second_low,
        gelu_pull,
        active_low,
    )
    return (result, saved)


def layer_backward(source, upstream, params, projected, gathered, row_block):
    unit_first, inverse_first, normed_low, query_low, keys_low, values_low = projected
    row_count = source.shape[0]
    feature_width = HEADS * HDIM
    result, saved = complete(source, params, projected, gathered, row_block)
    (
        query,
        attended,
        log_total,
        attended_low,
        unit_second,
        inverse_second,
        second_low,
        gelu_pull,
        active_low,
    ) = saved
    top_low = upstream.astype(jnp.bfloat16)
    grad_reduce_bias = jnp.sum(top_low.astype(jnp.float32), axis=0)
    grad_reduce_weight = jnp.einsum(
        "tf,td->fd", active_low, top_low, preferred_element_type=jnp.float32
    )
    grad_active = jnp.einsum("td,fd->tf", top_low, params[11], preferred_element_type=jnp.float32)
    grad_hidden_low = gelu_pull(grad_active)[0].astype(jnp.bfloat16)
    grad_expand_bias = jnp.sum(grad_hidden_low.astype(jnp.float32), axis=0)
    grad_expand_weight = jnp.einsum(
        "td,tf->df", second_low, grad_hidden_low, preferred_element_type=jnp.float32
    )
    grad_second = jnp.einsum(
        "tf,df->td", grad_hidden_low, params[9], preferred_element_type=jnp.float32
    )
    grad_second_gain = jnp.sum(grad_second * unit_second, axis=0)
    grad_second_shift = jnp.sum(grad_second, axis=0)
    grad_middle = upstream + normalize_back(
        grad_second * params[7].astype(jnp.float32), unit_second, inverse_second
    )
    branch_low = grad_middle.astype(jnp.bfloat16)
    grad_output_bias = jnp.sum(branch_low.astype(jnp.float32), axis=0)
    grad_output_weight = jnp.einsum(
        "td,te->de", attended_low, branch_low, preferred_element_type=jnp.float32
    )
    grad_attended = jnp.einsum(
        "te,de->td", branch_low, params[5], preferred_element_type=jnp.float32
    )
    grad_query, grad_keys_full, grad_values_full = attend_backward(
        query,
        gathered[0],
        gathered[1],
        row_block,
        attended,
        log_total,
        grad_attended.reshape(row_count, HEADS, HDIM),
    )
    grad_keys, grad_values = (
        lax.psum_scatter(grad_keys_full, LINE, scatter_dimension=0, tiled=True),
        lax.psum_scatter(grad_values_full, LINE, scatter_dimension=0, tiled=True),
    )
    scale_factor = HDIM ** (-0.5)
    grad_mixture = jnp.concatenate(
        [
            grad_query.reshape(row_count, feature_width) * scale_factor,
            grad_keys * scale_factor,
            grad_values,
        ],
        axis=1,
    ).astype(jnp.bfloat16)
    grad_query_bias = jnp.sum(grad_mixture[:, :feature_width].astype(jnp.float32), axis=0)
    grad_value_bias = jnp.sum(grad_mixture[:, 2 * feature_width :].astype(jnp.float32), axis=0)
    grad_joint_weight = jnp.einsum(
        "td,te->de", normed_low, grad_mixture, preferred_element_type=jnp.float32
    )
    grad_normed = jnp.einsum(
        "te,de->td", grad_mixture, params[2], preferred_element_type=jnp.float32
    )
    grad_first_gain = jnp.sum(grad_normed * unit_first, axis=0)
    grad_first_shift = jnp.sum(grad_normed, axis=0)
    grad_source = grad_middle + normalize_back(
        grad_normed * params[0].astype(jnp.float32), unit_first, inverse_first
    )
    grads = (
        grad_first_gain,
        grad_first_shift,
        grad_joint_weight,
        grad_query_bias,
        grad_value_bias,
        grad_output_weight,
        grad_output_bias,
        grad_second_gain,
        grad_second_shift,
        grad_expand_weight,
        grad_expand_bias,
        grad_reduce_weight,
        grad_reduce_bias,
    )
    return (grad_source.astype(jnp.bfloat16), grads)


def body(
    inputs,
    cotangent,
    first_gain,
    first_shift,
    joint_weight,
    query_bias,
    value_bias,
    output_weight,
    output_bias,
    second_gain,
    second_shift,
    expand_weight,
    expand_bias,
    reduce_weight,
    reduce_bias,
):
    section_index = lax.axis_index(SECTION)
    micro_count = inputs.shape[0]
    row_count = inputs.shape[1]
    first_row = lax.axis_index(LINE) * row_count
    row_block = (first_row + jnp.arange(row_count, dtype=jnp.int32)) // BLK
    owned = (
        first_gain[0],
        first_shift[0],
        joint_weight[0],
        query_bias[0],
        value_bias[0],
        output_weight[0],
        output_bias[0],
        second_gain[0],
        second_shift[0],
        expand_weight[0],
        expand_bias[0],
        reduce_weight[0],
        reduce_bias[0],
    )
    forward_params = (
        lax.all_gather(first_gain[0], OWNERS, axis=0, tiled=True),
        lax.all_gather(first_shift[0], OWNERS, axis=0, tiled=True),
        lax.all_gather(joint_weight[0], OWNERS, axis=0, tiled=True),
        lax.all_gather(query_bias[0], OWNERS, axis=0, tiled=True),
        lax.all_gather(value_bias[0], OWNERS, axis=0, tiled=True),
        lax.all_gather(output_weight[0], OWNERS, axis=0, tiled=True),
        lax.all_gather(output_bias[0], OWNERS, axis=0, tiled=True),
        lax.all_gather(second_gain[0], OWNERS, axis=0, tiled=True),
        lax.all_gather(second_shift[0], OWNERS, axis=0, tiled=True),
        lax.all_gather(expand_weight[0], OWNERS, axis=0, tiled=True),
        lax.all_gather(expand_bias[0], OWNERS, axis=0, tiled=True),
        lax.all_gather(reduce_weight[0], OWNERS, axis=0, tiled=True),
        lax.all_gather(reduce_bias[0], OWNERS, axis=0, tiled=True),
    )
    incoming = jnp.zeros(inputs.shape[1:], jnp.bfloat16)
    section_inputs = []
    produced = []
    key_sets = []
    for tick_index in range(micro_count + 1):
        section_input = jnp.where(
            section_index == 0, inputs[min(tick_index, micro_count - 1)], incoming
        )
        source = section_input.astype(jnp.float32)
        projected = project(source, forward_params)
        gathered = (
            lax.all_gather(projected[4], LINE, axis=0, tiled=True),
            lax.all_gather(projected[5], LINE, axis=0, tiled=True),
        )
        result, unused = complete(source, forward_params, projected, gathered, row_block)
        result_low = result.astype(jnp.bfloat16)
        section_inputs.append(section_input)
        produced.append(result_low)
        key_sets.append(gathered)
        if tick_index < micro_count:
            incoming = passed_along(result_low, SECTION, 1)
    backward_params = (
        lax.all_gather(first_gain[0], OWNERS, axis=0, tiled=True),
        lax.all_gather(first_shift[0], OWNERS, axis=0, tiled=True),
        lax.all_gather(joint_weight[0], OWNERS, axis=0, tiled=True),
        lax.all_gather(query_bias[0], OWNERS, axis=0, tiled=True),
        lax.all_gather(value_bias[0], OWNERS, axis=0, tiled=True),
        lax.all_gather(output_weight[0], OWNERS, axis=0, tiled=True),
        lax.all_gather(output_bias[0], OWNERS, axis=0, tiled=True),
        lax.all_gather(second_gain[0], OWNERS, axis=0, tiled=True),
        lax.all_gather(second_shift[0], OWNERS, axis=0, tiled=True),
        lax.all_gather(expand_weight[0], OWNERS, axis=0, tiled=True),
        lax.all_gather(expand_bias[0], OWNERS, axis=0, tiled=True),
        lax.all_gather(reduce_weight[0], OWNERS, axis=0, tiled=True),
        lax.all_gather(reduce_bias[0], OWNERS, axis=0, tiled=True),
    )
    totals = tuple((jnp.zeros(piece.shape, jnp.float32) for piece in backward_params))
    shares = tuple((jnp.zeros(piece.shape, jnp.float32) for piece in owned))
    returning = jnp.zeros(inputs.shape[1:], jnp.bfloat16)
    sent_back = []
    for tick_index in range(micro_count + 1):
        upper_pick = min(tick_index + 1, micro_count)
        lower_pick = max(tick_index - 1, 0)
        section_input = jnp.where(
            section_index == 1, section_inputs[upper_pick], section_inputs[lower_pick]
        )
        upstream = jnp.where(
            section_index == 1, cotangent[min(tick_index, micro_count - 1)], returning
        ).astype(jnp.float32)
        weight_valid = jnp.where(
            section_index == 1,
            1.0 if tick_index < micro_count else 0.0,
            1.0 if tick_index >= 1 else 0.0,
        ).astype(jnp.float32)
        source = section_input.astype(jnp.float32)
        projected = project(source, backward_params)
        gathered = (
            lax.all_gather(projected[4], LINE, axis=0, tiled=True),
            lax.all_gather(projected[5], LINE, axis=0, tiled=True),
        )
        grad_source, grads = layer_backward(
            source, upstream, backward_params, projected, gathered, row_block
        )
        masked = tuple((update * weight_valid for update in grads))
        totals = tuple((running + update for running, update in zip(totals, masked)))
        sent_back.append(grad_source)
        if tick_index < micro_count:
            returning = passed_along(grad_source, SECTION, -1)
    layer_outputs = jnp.stack(
        [
            jnp.where(section_index == 0, produced[position], produced[position + 1])
            for position in range(micro_count)
        ]
    )[None]
    input_grads = jnp.stack(
        [
            jnp.where(section_index == 1, sent_back[position], sent_back[position + 1])
            for position in range(micro_count)
        ]
    )[None]
    (
        sum_first_gain,
        sum_first_shift,
        sum_joint_weight,
        sum_query_bias,
        sum_value_bias,
        sum_output_weight,
        sum_output_bias,
        sum_second_gain,
        sum_second_shift,
        sum_expand_weight,
        sum_expand_bias,
        sum_reduce_weight,
        sum_reduce_bias,
    ) = totals
    shares = (
        lax.psum_scatter(sum_first_gain, OWNERS, scatter_dimension=0, tiled=True),
        lax.psum_scatter(sum_first_shift, OWNERS, scatter_dimension=0, tiled=True),
        lax.psum_scatter(sum_joint_weight, OWNERS, scatter_dimension=0, tiled=True),
        lax.psum_scatter(sum_query_bias, OWNERS, scatter_dimension=0, tiled=True),
        lax.psum_scatter(sum_value_bias, OWNERS, scatter_dimension=0, tiled=True),
        lax.psum_scatter(sum_output_weight, OWNERS, scatter_dimension=0, tiled=True),
        lax.psum_scatter(sum_output_bias, OWNERS, scatter_dimension=0, tiled=True),
        lax.psum_scatter(sum_second_gain, OWNERS, scatter_dimension=0, tiled=True),
        lax.psum_scatter(sum_second_shift, OWNERS, scatter_dimension=0, tiled=True),
        lax.psum_scatter(sum_expand_weight, OWNERS, scatter_dimension=0, tiled=True),
        lax.psum_scatter(sum_expand_bias, OWNERS, scatter_dimension=0, tiled=True),
        lax.psum_scatter(sum_reduce_weight, OWNERS, scatter_dimension=0, tiled=True),
        lax.psum_scatter(sum_reduce_bias, OWNERS, scatter_dimension=0, tiled=True),
    )
    return (layer_outputs, input_grads) + tuple((portion[None] for portion in shares))


def flip(place, bits):
    return {1: place + 1 - 2 * (place % 2), 2: (place + 2) % 4, 3: 3 - place}[bits]


def places():
    core, ring, line = (lax.axis_index(name) for name in (SECTION, RING, LINE))
    rings = [ring] + [flip(ring, bits) for bits in (1, 2, 3)]
    lines = [line] + [flip(line, bits) for bits in (1, 2, 3)]
    toward = {
        EAST: {RING: rings[1]},
        NORTH: {RING: rings[2]},
        (LEVEL, 1): {LINE: lines[1]},
        (LEVEL, 2): {LINE: lines[2]},
        (LEVEL, 3): {LINE: lines[3]},
        (CORNER, 3): {SECTION: 1 - core, LINE: lines[3]},
        (LEVEL, UP): {LINE: (line + 1) % 4},
        (LEVEL, DOWN): {LINE: (line + 3) % 4},
        SIBLING: {SECTION: 1 - core},
    }
    return core, rings, lines, toward


def greet(toward):
    barrier = pltpu.get_barrier_semaphore()
    partners = [to for name, to in toward.items() if name not in ((LEVEL, UP), (LEVEL, DOWN))]
    for to in partners:
        pl.semaphore_signal(barrier, inc=1, device_id=to, device_id_type=pl.DeviceIdType.MESH)
    pl.semaphore_wait(barrier, len(partners))


def remote_copy(source, target, send_sem, recv_sem, to):
    return pltpu.make_async_remote_copy(
        src_ref=source,
        dst_ref=target,
        send_sem=send_sem,
        recv_sem=recv_sem,
        device_id=to,
        device_id_type=pl.DeviceIdType.MESH,
    )


def per_core(core, act):
    for index in (0, 1):

        @pl.when(core == index)
        def _():
            act(index)


GATHER_KINDS = (UP, DOWN, EAST, NORTH, CORNER, SIBLING)
GATHER_NUMBER = {kind: 4 * index for index, kind in enumerate(GATHER_KINDS)}
GATHER_SPAN = 4 * len(GATHER_KINDS)


def mm(left, right):
    return jnp.dot(left, right, preferred_element_type=F32)


def mm_nt(left, right):
    return lax.dot_general(left, right, (((1,), (1,)), ((), ())), preferred_element_type=F32)


def mm_tn(left, right):
    return lax.dot_general(left, right, (((0,), (0,)), ((), ())), preferred_element_type=F32)


def normal_parts(values):
    centre = jnp.mean(values, axis=-1, keepdims=True)
    centred = values - centre
    inverse = lax.rsqrt(jnp.mean(centred * centred, axis=-1, keepdims=True) + epsilon)
    return centred * inverse, inverse


def normal_back(upstream, unit, inverse):
    return inverse * (
        upstream
        - jnp.mean(upstream, axis=-1, keepdims=True)
        - unit * jnp.mean(upstream * unit, axis=-1, keepdims=True)
    )


def close_up(rows, table):
    high = rows.astype(LOW)
    rest = (rows - high.astype(F32)).astype(LOW)
    return mm_nt(high, table) + mm_nt(rest, table)


def head_pair(rows):
    lane = lax.broadcasted_iota(jnp.int32, rows.shape, 1)
    zero = jnp.zeros_like(rows)
    return jnp.concatenate(
        [jnp.where(lane < HDIM, rows, zero), jnp.where(lane < HDIM, zero, rows)], axis=0
    )


def from_pair(turned):
    n = turned.shape[1] // 2
    own = jnp.concatenate([turned[:HDIM, :n], turned[HDIM:, n:]], axis=0)
    return own.T


LEAD_ROWS = 144
HALF = 2176


def gather_tasks(slots, send_sem, recv_sem, copy_sem, land_sem, place_of):
    core, rings, lines, toward = place_of
    line = lines[0]
    drains = []

    def cut(t, part):
        if slots[t][1]:
            return (slice(None), pl.ds(HALF * part if isinstance(part, int) else pl.multiple_of(part * HALF, 128), HALF))
        rows = slots[t][2].shape[0]
        return (pl.ds(0, LEAD_ROWS) if part == 0 else pl.ds(LEAD_ROWS, rows - LEAD_ROWS),)

    def landed(t, part):
        _, by_columns, shard, _, land = slots[t]
        return land if by_columns else land.at[pl.ds(0, LEAD_ROWS if part == 0 else shard.shape[0] - LEAD_ROWS)]

    def run(t, act):
        if slots[t][1]:
            act(core)
        else:
            per_core(core, act)

    def place(t, part, dd, j):
        return slots[t][3].at[(rings[dd] * 4 + j,) + cut(t, part)]

    def group(t, part, dd):
        return slots[t][3].at[(pl.ds(rings[dd] * 4, 4),) + cut(t, part)]

    def copy_of(t, source, target, to, kind, j):
        index = t * GATHER_SPAN + GATHER_NUMBER[kind] + j
        return remote_copy(source, target, send_sem.at[index], recv_sem.at[index], toward[to])

    def guarded(valid, act):
        if valid is None:
            act()
        else:
            pl.when(valid)(act)

    def send(t, dd, j, to, kind, valid=None, mine=False):
        def start(part):
            target = place(t, part, dd, j)
            copy_of(t, target, target, to, kind, j).start()

        def start_mine(index):
            shard = slots[t][2].at[cut(t, index)] if index == slots[t][0] else landed(t, index)
            copy_of(t, shard, place(t, index, dd, j), to, kind, j).start()

        def finish(part):
            target = place(t, part, dd, j)
            copy_of(t, target, target, to, kind, j).wait_send()

        if mine:
            guarded(valid, lambda: per_core(core, start_mine))
        else:
            guarded(valid, lambda: run(t, start))
        drains.append(lambda: guarded(valid, lambda: run(t, finish)))

    def arrive(t, dd, j, to, kind, valid=None):
        def act(part):
            target = place(t, part, dd, j)
            copy_of(t, target, target, to, kind, j).wait_recv()

        guarded(valid, lambda: run(t, act))

    def both(one, two):
        return two if one is None else one & two

    def onward(t, j, valid, up, down, mine=False):
        if up:
            send(t, 0, j, (LEVEL, UP), UP, both(valid, line < 3), mine)
        if down:
            send(t, 0, j, (LEVEL, DOWN), DOWN, both(valid, line > 0), mine)
        send(t, 0, j, EAST, EAST, valid, mine)
        send(t, 0, j, NORTH, NORTH, valid, mine)

    def prelude():
        def give(index):
            for t, (owner, _, shard, _, land) in enumerate(slots):
                if index == owner:
                    source = shard.at[cut(t, 1 - index)]
                    remote_copy(source, landed(t, 1 - index), land_sem.at[t], land_sem.at[len(slots) + t], toward[SIBLING]).start()

        per_core(core, give)

    def taken(t):
        owner, shard = slots[t][0], slots[t][2]

        def act(index):
            target = landed(t, 1 - owner)
            copy = remote_copy(target, target, land_sem.at[t], land_sem.at[len(slots) + t], toward[SIBLING])
            if index == owner:
                copy.wait_send()
            else:
                copy.wait_recv()

        per_core(core, act)

    def local(t, index):
        source = slots[t][2].at[cut(t, index)] if index == slots[t][0] else landed(t, index)
        return pltpu.make_async_copy(source, place(t, index, 0, line), copy_sem.at[t])

    def begin(t):
        taken(t)
        onward(t, line, None, True, True, mine=True)
        per_core(core, lambda index: local(t, index).start())

    def own_ready(t):
        per_core(core, lambda index: local(t, index).wait())

    def from_line(t, offset):
        j = line + offset
        valid = j >= 0 if offset < 0 else j <= 3
        kind = UP if offset < 0 else DOWN
        arrive(t, 0, j, (LEVEL, DOWN if offset < 0 else UP), kind, valid)
        onward(t, j, valid, offset < 0, offset > 0)

    def from_side(t, offset):
        j = line + offset
        valid = None if offset == 0 else (j >= 0 if offset < 0 else j <= 3)
        even, odd = both(valid, j % 2 == 0), both(valid, j % 2 == 1)
        arrive(t, 1, j, EAST, EAST, valid)
        send(t, 1, j, NORTH, CORNER, even)
        arrive(t, 2, j, NORTH, NORTH, valid)
        send(t, 2, j, EAST, CORNER, odd)

    def from_corner(t, j):
        arrive(t, 3, j, NORTH if j % 2 == 0 else EAST, CORNER)

    def sibling(t, dd):
        def copy(part):
            return copy_of(t, group(t, part, dd), group(t, part, dd), SIBLING, SIBLING, dd)

        run(t, lambda part: copy(part).start())
        drains.append(lambda: run(t, lambda part: copy(part).wait_send()))

    def last(t):
        def act(part):
            for dd in range(4):
                target = group(t, 1 - part, dd)
                copy_of(t, target, target, SIBLING, SIBLING, dd).wait_recv()

        run(t, act)

    tasks = []

    def then(function, *given):
        tasks.append((given[0] if given else 0, lambda: function(*given)))

    count = len(slots)
    heads, tails = [], []
    for t in range(count):
        then(from_line, t, -1)
        then(from_line, t, 1)
        then(from_side, t, 0)
        for far in (2, 3):
            then(from_line, t, -far)
            then(from_line, t, far)
            then(from_side, t, 1 - far)
            then(from_side, t, far - 1)
        then(own_ready, t)
        then(sibling, t, 0)
        then(from_side, t, -3)
        then(from_side, t, 3)
        then(sibling, t, 1)
        then(sibling, t, 2)
        heads.append(list(tasks))
        tasks.clear()
        for j in range(4):
            then(from_corner, t, j)
        then(sibling, t, 3)
        then(last, t)
        tails.append(list(tasks))
        tasks.clear()
    then(prelude)
    then(begin, 0)
    if count > 1:
        then(begin, 1)
    for t in range(count):
        tasks += heads[t][:7]
        if t > 0:
            tasks += tails[t - 1]
        if t + 2 < count:
            then(begin, t + 2)
        tasks += heads[t][7:]
    tasks += tails[count - 1]

    def drain():
        for act in drains:
            act()

    return tasks, drain


def gather_outs(shards):
    shapes = []
    for _, by_columns, shard in shards:
        rows, columns = shard.shape
        land = (rows, HALF) if by_columns else (LEAD_ROWS, columns)
        shapes += [jax.ShapeDtypeStruct((16, rows, columns), LOW), jax.ShapeDtypeStruct(land, LOW)]
    return shapes


def gather_slots(forms, shards, outs):
    return [form + (shards[t], outs[2 * t], outs[2 * t + 1]) for t, form in enumerate(forms)]


def gather_semaphores(count):
    dma = pltpu.SemaphoreType.DMA
    return [dma((count * GATHER_SPAN,)), dma((count * GATHER_SPAN,)), dma((count,)), dma((2 * count,))]


def row_copies(place_of, source, target, send_sem, recv_sem, local_sem):
    core, _, lines, toward = place_of
    half = target.shape[0] // 2
    which = lines[0] // 2
    from_here = pl.ds(pl.multiple_of(core * half, half), half)
    to_there = pl.ds(pl.multiple_of(which * half, half), half)
    return (
        pltpu.make_async_copy(source.at[which, from_here], target.at[to_there], local_sem),
        remote_copy(source.at[1 - which, from_here], target.at[to_there], send_sem, recv_sem, toward[(LEVEL, 3)]),
    )


def gather_kernel(shard, *refs):
    source, outs, moved, refs = refs[0], refs[1:3], refs[3], refs[4:]
    sems, row_sems = refs[:4], refs[4:]
    place_of = places()
    greet(place_of[3])
    tasks, drain = gather_tasks(gather_slots(((0, True),), (shard,), outs), *sems, place_of)
    for _, task in tasks[:11]:
        task()
    copies = row_copies(place_of, source, moved, *row_sems)
    for copy in copies:
        copy.start()
    for _, task in tasks[11:]:
        task()
    drain()
    for copy in copies:
        copy.wait()


def gather_page(shard, source):
    anywhere = pl.BlockSpec(memory_space=pl.ANY)
    outs = gather_outs(((0, True, shard),)) + [jax.ShapeDtypeStruct(source.shape[1:], LOW)]
    dma = pltpu.SemaphoreType.DMA
    res = pl.pallas_call(
        gather_kernel,
        out_shape=tuple(outs),
        in_specs=[anywhere] * 2,
        out_specs=(anywhere,) * len(outs),
        scratch_shapes=gather_semaphores(1) + [dma(())] * 3,
        compiler_params=pltpu.CompilerParams(collective_id=0, has_side_effects=True),
        name="gather_page",
    )(shard, source)
    return res[0], res[2]


def low_place(line):
    return jnp.where(line < 2, line, 3 - line)


def forward_kernel(*refs):
    x_in, vectors_in, wide_in, table, page_hbm, row_source = refs[:6]
    shards, refs = refs[6:11], refs[11:]
    stored_of, refs = (refs[:14], refs[14:28]), refs[28:]
    outs, row_target, vectors_out, refs = refs[:10], refs[10], refs[11], refs[12:]
    held_of, refs = (refs[:14], refs[:3] + refs[14:17] + refs[6:14]), refs[17:]
    (store_sem, big, reduce, mixture, result, mixed, stats, wide_own, page_sem, expand_sem, reduce_sem, pair_send,
     pair_recv) = refs[:13]
    gather_sems, row_sems = refs[13:17], refs[17:]
    place_of = places()
    core, rings, lines, toward = place_of
    rows, width = x_in.shape
    half = rows // 2
    first = low_place(lines[0]) == 0
    tiles = big.shape[2] // 256

    def tile_at(i):
        return pl.ds(pl.multiple_of(i * 256, 256), 256)

    def tile_of(at):
        return big[:, :, at].astype(F32).reshape(WIDE, 256).astype(LOW)

    def begin(make, steps):
        def step(i, _):
            make(i).start()
            return 0

        lax.fori_loop(0, steps, step, 0)

    def pair_copies(layer):
        here, beside, away, corner = held_of[layer][2:6]
        ways = ((here, away, (LEVEL, 1)), (here, beside, SIBLING), (away, corner, SIBLING))
        return [
            remote_copy(source, target, pair_send.at[3 * layer + number], pair_recv.at[3 * layer + number], toward[to])
            for number, (source, target, to) in enumerate(ways)
        ]

    def store_copy(layer, i):
        return pltpu.make_async_copy(held_of[layer][i], stored_of[layer][i], store_sem.at[i])

    todo, drain = gather_tasks(gather_slots(FORMS, shards, outs), *gather_sems, place_of)

    def progress(many):
        for _ in range(many):
            if todo:
                todo.pop(0)[1]()

    def complete(t):
        while any(slot <= t for slot, _ in todo):
            progress(1)

    def one_unit(queries, keys, values):
        scores = mm_nt(keys, queries)
        level = jnp.max(scores, axis=0, keepdims=True)
        exponent = jnp.exp(scores - level)
        return level, jnp.sum(exponent, axis=0, keepdims=True), mm_tn(values, exponent.astype(LOW))

    def merge(units):
        peak = units[0][0]
        for level, _, _ in units[1:]:
            peak = jnp.maximum(peak, level)
        total, out = 0.0, 0.0
        for level, sums, part in units:
            share = jnp.exp(level - peak)
            total = total + share * sums
            out = out + share * part
        return peak, total, out

    def layer_pass(layer):
        (normed_out, query_out, here, beside, away, corner, attended_out, log_out, attended_low, middle_out,
         second_out, active_out, slope_out, result_out) = held_of[layer]
        x = x_in if layer == 0 else result_out
        vectors, wide = (vectors_in, wide_in) if layer == 0 else (vectors_out, wide_own)
        page_source, expand_source, reduce_source = (page_hbm, outs[0], outs[2]) if layer == 0 else (outs[4], outs[6], outs[8])

        def store(*numbers):
            for i in numbers:
                store_copy(layer, i).start()

        def page_copy(i):
            return pltpu.make_async_copy(page_source.at[:, :, tile_at(i)], big.at[:, :, tile_at(i)], page_sem.at[i])

        def expand_copy(i):
            return pltpu.make_async_copy(expand_source.at[:, :, tile_at(i)], big.at[:, :, tile_at(i)], expand_sem.at[i])

        def reduce_copy(i):
            rows_at = pl.ds(pl.multiple_of(i * 272, 16), 272)
            return pltpu.make_async_copy(reduce_source.at[i], reduce.at[rows_at], reduce_sem.at[i])

        if layer == 0:
            begin(page_copy, tiles)
            greet(toward)
            progress(3)
        else:
            complete(2)
            begin(page_copy, tiles)
            for i in range(14):
                store_copy(0, i).wait()
            for copy in pair_copies(0):
                copy.wait_send()

            def arrived(i, _):
                page_copy(i).wait()
                return 0

            lax.fori_loop(0, tiles, arrived, 0)
            for shard in range(16):
                line = big[shard, 64:72, 0:1408].astype(F32)[4:5]
                for place in range(8):
                    vectors[place : place + 1, shard * 68 : (shard + 1) * 68] = line[:, place * 128 : place * 128 + 68]
                wide[0:1, shard * 272 : (shard + 1) * 272] = line[:, 1024:1296]
        unit, _ = normal_parts(x[...].astype(F32))
        normed = (unit * vectors[0:1] + vectors[1:2]).astype(LOW)
        normed_out[...] = mm(normed, table[...]).astype(LOW)
        store(0)

        def column(i, _):
            if layer == 0:
                page_copy(i).wait()
            at = tile_at(i)
            mixture[:, at] = mm(normed_out[...], tile_of(at))
            return 0

        for begin_at, end in ((0, 4), (4, 8), (8, 13)):
            lax.fori_loop(begin_at, end, column, 0)
            progress(2)
        blank = jnp.zeros((rows, WIDE - width), LOW)
        here[0, :, :width] = mixture[:, width : 2 * width].astype(LOW)
        here[0, :, width:] = blank
        here[1, :, :width] = (mixture[:, 2 * width : 3 * width] + vectors[3:4]).astype(LOW)
        here[1, :, width:] = blank

        to_away, to_beside, to_corner = pair_copies(layer)
        to_away.start()
        to_beside.start()
        query = ((mixture[:, :width] + vectors[2:3]).astype(LOW).astype(F32) * HDIM ** (-0.5)).astype(LOW)
        query_out[:, :width] = query
        query_out[:, width:] = blank
        store(1, 2)
        progress(1)
        to_beside.wait_recv()
        store(3)

        def block(kind, near, part, at):
            rows_at = pl.ds(part * half, half)
            one, two = (here, beside) if near == 0 else (away, corner)
            return jnp.concatenate([one[kind, rows_at, at], two[kind, rows_at, at]], axis=0)

        def local_pair(p, _):
            at = pl.ds(pl.multiple_of(p * 128, 128), 128)
            low, high = head_pair(query_out[:half, at]), head_pair(query_out[half:, at])
            keys, values = block(0, 0, 0, at), block(1, 0, 0, at)
            bottom = one_unit(low, keys, values)
            top = merge([one_unit(high, keys, values), one_unit(high, block(0, 0, 1, at), block(1, 0, 1, at))])
            for place, (level, sums, out) in enumerate((bottom, top)):
                stats[p, 2 * place : 2 * place + 1] = level
                stats[p, 2 * place + 1 : 2 * place + 2] = sums
                mixed[p, place] = out
            return 0

        for begin_at in (0, 3, 6):
            lax.fori_loop(begin_at, begin_at + 3, local_pair, 0)
            progress(2)
        progress(8)
        to_away.wait_recv()
        to_corner.start()
        store(4)
        progress(2)
        to_corner.wait_recv()
        store(5)

        def far_pair(p, _):
            at = pl.ds(pl.multiple_of(p * 128, 128), 128)
            low, high = head_pair(query_out[:half, at]), head_pair(query_out[half:, at])
            keys, values = block(0, 1, 0, at), block(1, 1, 0, at)
            last_keys = jnp.where(first, block(0, 1, 1, at), keys)
            last_values = jnp.where(first, block(1, 1, 1, at), values)
            near = one_unit(high, keys, values)
            last = one_unit(jnp.where(first, high, low), last_keys, last_values)
            low_last = (jnp.where(first, far_below, last[0]),) + last[1:]
            high_last = (jnp.where(first, last[0], far_below),) + last[1:]

            def before(place):
                return (stats[p, 2 * place : 2 * place + 1], stats[p, 2 * place + 1 : 2 * place + 2], mixed[p, place])

            for place, units in enumerate(([before(0), low_last], [before(1), near, high_last])):
                peak, total, out = merge(units)
                attended_out[place * half : (place + 1) * half, at] = from_pair(out / total)
                log_out[p, place : place + 1] = peak + jnp.log(total)
            return 0

        for begin_at in (0, 3, 6):
            lax.fori_loop(begin_at, begin_at + 3, far_pair, 0)
            progress(2)

        def late(i, _):
            page_copy(i).wait()
            return 0

        if layer == 0:
            lax.fori_loop(13, tiles, late, 0)
        lead = 4 * width - WIDE
        store(6, 7)
        attended_low[...] = mm(attended_out[:, :width].astype(LOW), table[...]).astype(LOW)
        store(8)

        def blend(i, _):
            at = pl.ds(pl.multiple_of(lead + i * 128, 128), 128)
            weights = big[:, :, at].astype(F32).reshape(WIDE, 128).astype(LOW)
            mixture[:, pl.ds(pl.multiple_of(i * 128, 128), 128)] = mm(attended_low[...], weights)
            return 0

        lax.fori_loop(0, WIDE // 128, blend, 0)
        middle = x[...].astype(F32) + (mixture[:, 3 * width - lead : WIDE] + vectors[4:5])
        middle_out[...] = middle
        store(9)
        progress(2)
        unit, _ = normal_parts(middle)
        second = (unit * vectors[6:7] + vectors[7:8]).astype(LOW)
        second_out[...] = mm(second, table[...]).astype(LOW)
        store(10)
        result[...] = middle + vectors[5:6]

        complete(3 * layer)
        begin(expand_copy, tiles)
        if layer == 1:
            for copy in row_copies(place_of, row_source, row_target, *row_sems):
                copy.start()

        def inner(i, _):
            at = tile_at(i)
            expand_copy(i).wait()
            hidden = mm(second_out[...], tile_of(at)) + wide[0:1, at]
            below = 0.5 + 0.5 * lax.erf(hidden * 0.7071067811865476)
            active_out[:, at] = (hidden * below).astype(LOW)
            slope_out[:, at] = (below + hidden * (0.3989422804014327 * jnp.exp(-0.5 * hidden * hidden))).astype(LOW)
            return 0

        for begin_at in range(0, tiles, 2):
            lax.fori_loop(begin_at, min(begin_at + 2, tiles), inner, 0)
            progress(3)
        store(11, 12)
        complete(1 + 3 * layer)
        begin(reduce_copy, 16)

        def landed(i, _):
            reduce_copy(i).wait()
            return 0

        lax.fori_loop(0, 16, landed, 0)

        def outer(i, _):
            at = pl.ds(pl.multiple_of(i * 256, 256), 256)
            result[...] += mm(active_out[:, at], reduce[at])
            return 0

        lax.fori_loop(0, tiles, outer, 0)
        result_out[...] = result[...].astype(LOW)
        store(13)

    layer_pass(0)
    layer_pass(1)
    progress(len(todo))
    drain()
    for i in range(14):
        store_copy(1, i).wait()
    for copy in row_copies(place_of, row_source, row_target, *row_sems):
        copy.wait()
    for copy in pair_copies(1):
        copy.wait_send()


FORMS = ((0, True), (0, False), (1, True), (1, True), (1, False))


def forward(x, vectors, wide, table, page, row_source, shards):
    rows, width = x.shape
    inner = page.shape[2]
    pairs = WIDE // 128
    anywhere = pl.BlockSpec(memory_space=pl.ANY)
    inside = pl.BlockSpec(memory_space=pltpu.VMEM)

    def shape(*dims, kind=LOW):
        return jax.ShapeDtypeStruct(dims, kind)

    pair = shape(2, rows, WIDE)
    kept = [
        shape(rows, WIDE), shape(rows, WIDE), pair, pair, pair, pair, shape(rows, WIDE, kind=F32),
        shape(pairs, 2, rows, kind=F32), shape(rows, WIDE), shape(rows, width, kind=F32),
        shape(rows, WIDE), shape(rows, inner), shape(rows, inner), shape(rows, width),
    ]
    outs = kept * 2 + gather_outs(tuple(form + (shard,) for form, shard in zip(FORMS, shards)))
    outs += [shape(rows, width), shape(8, width, kind=F32)]
    dma = pltpu.SemaphoreType.DMA
    scratch = [pltpu.VMEM(out.shape, out.dtype) for out in kept + [pair] * 3] + [
        dma((14,)), pltpu.VMEM((16, 72, inner), LOW), pltpu.VMEM((inner, width), LOW),
        pltpu.VMEM((rows, 13 * 256), F32), pltpu.VMEM((rows, width), F32),
        pltpu.VMEM((pairs, 2, 128, rows), F32), pltpu.VMEM((pairs, 4, rows), F32), pltpu.VMEM((8, inner), F32),
        dma((inner // 256,)), dma((inner // 256,)), dma((16,)), dma((6,)), dma((6,)),
    ] + gather_semaphores(len(shards)) + [dma(())] * 3
    res = pl.pallas_call(
        forward_kernel,
        out_shape=tuple(outs),
        in_specs=[inside] * 4 + [anywhere] * (2 + len(shards)),
        out_specs=(anywhere,) * (len(outs) - 1) + (inside,),
        scratch_shapes=scratch,
        compiler_params=pltpu.CompilerParams(collective_id=3, has_side_effects=True, vmem_limit_bytes=62 << 20),
        name="forward",
    )(x, vectors, wide, table, page, row_source, *shards)
    return res[:14], res[14:28], res[28:38:2], res[38], res[39]


COLUMNS, ROWS = range(2)
SIZES = {COLUMNS: (72, 2176), ROWS: (144, 1088)}
DEPTH = 8
EASTWARD = (3, 0)
SCATTER_KINDS = (
    [(SIBLING, dd) for dd in range(4)]
    + [(ONCE, k) for k in range(4)]
    + [(EAST, k) for k in range(4)]
    + [(NORTH, k) for k in range(4)]
    + [(LEVEL, k) for k in (1, 2, 3)]
    + [(CORNER, 0)]
)
SCATTER_NUMBER = {kind: index for index, kind in enumerate(SCATTER_KINDS)}


def landing_shapes(kind):
    return [jax.ShapeDtypeStruct((many,) + SIZES[kind], LOW) for many in (16, 4, 4, 4, 4)]


def final_shape(kind):
    return jax.ShapeDtypeStruct({COLUMNS: (72, 4352), ROWS: (272, 1088)}[kind], F32)


def work_shapes(kinds):
    shapes = []
    for kind in sorted(set(kinds)):
        size = SIZES[kind]
        shapes += [pltpu.VMEM((2, 4) + size, LOW), pltpu.VMEM((DEPTH,) + size, LOW), pltpu.VMEM(size, F32)]
    count = len(kinds) * len(SCATTER_KINDS)
    return shapes + [
        pltpu.SemaphoreType.DMA((count,)), pltpu.SemaphoreType.DMA((count,)),
        pltpu.SemaphoreType.DMA((8,)), pltpu.SemaphoreType.DMA(()),
    ]


class Scatter:
    def __init__(self, kinds, pages, lands, finals, owners, refs, place_of):
        self.kinds, self.pages, self.lands, self.finals, self.owners = kinds, pages, lands, finals, owners
        self.core, self.rings, self.lines, self.toward = place_of
        self.work = {}
        for index, kind in enumerate(sorted(set(kinds))):
            self.work[kind] = refs[3 * index : 3 * index + 3]
        self.send_sem, self.recv_sem, self.load_sem, self.out_sem = refs[3 * len(self.work) :]
        self.turn = 0
        self.used = {kind: [None] * DEPTH for kind in self.work}
        self.count = {kind: 0 for kind in self.work}
        self.given, self.final_sent = [], []

    def remote(self, t, source, target, to, kind):
        index = t * len(SCATTER_KINDS) + SCATTER_NUMBER[kind]
        return remote_copy(source, target, self.send_sem.at[index], self.recv_sem.at[index], self.toward[to])

    def part(self, t, core, index, many=None):
        page, at = self.pages[t], index if many is None else pl.ds(index, many)
        if self.kinds[t] == COLUMNS:
            return page.at[at, :, pl.ds(pl.multiple_of(core * 2176, 128), 2176)]
        return page.at[pl.ds(pl.multiple_of(index * 272 + core * 128, 16), 144)]

    def landed(self, t, dd):
        return self.lands[t][0].at[pl.ds(self.rings[dd] * 4, 4)]

    def give(self, t, dd):
        base = self.rings[dd] * 4
        if self.kinds[t] == ROWS:
            for k in range(4):
                self.remote(t, self.part(t, 1 - self.core, base + k), self.lands[t][0].at[base + k], SIBLING, (SIBLING, dd)).start()
        else:
            self.remote(t, self.part(t, 1 - self.core, base, 4), self.landed(t, dd), SIBLING, (SIBLING, dd)).start()
        self.given.append(self.remote(t, self.landed(t, dd), self.landed(t, dd), SIBLING, (SIBLING, dd)))

    def arrived(self, t, ref, to, kind):
        self.remote(t, ref, ref, to, kind).wait_recv()

    def load(self, t, sources):
        loads = self.work[self.kinds[t]][0]
        slot = self.turn % 2
        self.turn += 1
        copies = []
        for j, source in enumerate(sources):
            copies.append(pltpu.make_async_copy(source, loads.at[slot, j], self.load_sem.at[slot * 4 + j]))
        for copy in copies:
            copy.start()
        return loads, slot, copies

    def add_up(self, t, loaded, store):
        loads, slot, copies = loaded
        terms = len(copies)
        for copy in copies:
            copy.wait()
        rows, columns = SIZES[self.kinds[t]]
        wide = self.kinds[t] != ROWS
        piece = min(256, columns) if wide else 16

        def step(i, _):
            at = pl.ds(pl.multiple_of(i * piece, piece), piece)
            where = (slice(None), at) if wide else (at, slice(None))
            value = loads[(slot, 0) + where].astype(F32)
            for j in range(1, terms):
                value = value + loads[(slot, j) + where].astype(F32)
            store(where, value)
            return 0

        steps = (columns if wide else rows) // piece
        lax.fori_loop(0, steps, step, 0)
        if wide and steps * piece < columns:
            where = (slice(None), pl.ds(steps * piece, columns - steps * piece))
            value = loads[(slot, 0) + where].astype(F32)
            for j in range(1, terms):
                value = value + loads[(slot, j) + where].astype(F32)
            store(where, value)

    def sources(self, t, dd, k, extra):
        index = self.rings[dd] * 4 + self.lines[k]
        return [self.part(t, self.core, index), self.lands[t][0].at[index]] + extra

    def sum_and_send(self, t, dd, k, extra, target, to, kind):
        form = self.kinds[t]
        loaded = self.load(t, self.sources(t, dd, k, extra))

        def finish():
            place = self.count[form] % DEPTH
            self.count[form] += 1
            if self.used[form][place] is not None:
                self.used[form][place].wait_send()
            out = self.work[form][1]

            def store(where, value):
                out[(place,) + where] = value.astype(out.dtype)

            self.add_up(t, loaded, store)
            copy = self.remote(t, out.at[place], target, to, kind)
            copy.start()
            self.used[form][place] = copy

        return finish

    def first(self, t, k):
        if k == 3:
            self.arrived(t, self.landed(t, 3), SIBLING, (SIBLING, 3))
        to = EAST if k in EASTWARD else NORTH
        return self.sum_and_send(t, 3, k, [], self.lands[t][1].at[k], to, (ONCE, k))

    def second(self, t, dd, k):
        if (dd, k) in ((1, 3), (2, 2)):
            self.arrived(t, self.landed(t, dd), SIBLING, (SIBLING, dd))
        to, land = (EAST, self.lands[t][2]) if dd == 1 else (NORTH, self.lands[t][3])
        extra = []
        if (dd == 1) != (k in EASTWARD):
            one = self.lands[t][1].at[k]
            self.arrived(t, one, EAST if k in EASTWARD else NORTH, (ONCE, k))
            extra = [one]
        return self.sum_and_send(t, dd, k, extra, land.at[k], to, (to, k))

    def third(self, t, k):
        if k == 3:
            self.arrived(t, self.landed(t, 0), SIBLING, (SIBLING, 0))
        extra = []
        for to, land in ((EAST, self.lands[t][2]), (NORTH, self.lands[t][3])):
            self.arrived(t, land.at[k], to, (to, k))
            extra.append(land.at[k])
        if k:
            return self.sum_and_send(t, 0, k, extra, self.lands[t][4].at[k], (LEVEL, k), (LEVEL, k))
        loaded = self.load(t, self.sources(t, 0, 0, extra))
        total = self.work[self.kinds[t]][2]

        def store(where, value):
            total[where] = value

        return lambda: self.add_up(t, loaded, store)

    def final_part(self, t, core):
        if self.kinds[t] == COLUMNS:
            return (slice(None), slice(None)), (slice(None), pl.ds(2176 * core, 2176))
        return (pl.ds(16 * core, 144 - 16 * core),), (pl.ds(144 * core, 144 - 16 * core),)

    def last(self, t):
        land = self.lands[t][4]
        for k in (1, 2, 3):
            self.arrived(t, land.at[k], (LEVEL, k), (LEVEL, k))
        loaded = self.load(t, [land.at[k] for k in (1, 2, 3)])
        total = self.work[self.kinds[t]][2]
        owner = self.owners[t]

        def store(where, value):
            total[where] = total[where] + value

        def act(core):
            inner, outer = self.final_part(t, core)
            source, target = total.at[inner], self.finals[t].at[outer]
            if core == owner:
                copy = pltpu.make_async_copy(source, target, self.out_sem)
                copy.start()
                copy.wait()
                theirs = self.finals[t].at[self.final_part(t, 1 - core)[1]]
                self.remote(t, theirs, theirs, SIBLING, (CORNER, 0)).wait_recv()
            else:
                copy = self.remote(t, source, target, SIBLING, (CORNER, 0))
                copy.start()
                copy.wait_send()

        def finish():
            self.add_up(t, loaded, store)
            per_core(self.core, act)

        return finish

    def give_all(self, t):
        for dd in (3, 1, 2, 0):
            self.give(t, dd)

    def steps(self, t):
        def of(waits, function, *given):
            return waits, lambda: function(*given)

        ways = ((1, 3), (2, 2), (1, 0), (2, 1), (1, 2), (2, 3), (1, 1), (2, 0))
        return (
            [of(k == 3, self.first, t, k) for k in (3, 2, 0, 1)],
            [of((dd == 1) != (k in EASTWARD), self.second, t, dd, k) for dd, k in ways],
            [of(True, self.third, t, k) for k in (3, 2, 1, 0)],
            [of(True, self.last, t)],
        )

    def drain(self):
        for copy in self.given:
            copy.wait_send()
        for held in self.used.values():
            for copy in held:
                if copy is not None:
                    copy.wait_send()


def in_turn(earlier, later, done=()):
    return later[0] + earlier[2][:2] + later[1][:4] + list(done) + earlier[2][2:] + later[1][4:]


def tiny_shapes():
    return [
        pltpu.VMEM((16, 16, 128), F32), pltpu.VMEM((16, 16, 128), F32), pltpu.VMEM((2, 4, 16, 128), F32),
        pltpu.VMEM((4, 16, 128), F32), pltpu.VMEM((3, 16, 128), F32),
        pltpu.SemaphoreType.DMA((7,)), pltpu.SemaphoreType.DMA((7,)),
    ]


def tiny_steps(both, final, refs, place_of):
    total, land, land_east, land_north, land_line, send_sem, recv_sem = refs
    core, rings, lines, toward = place_of
    blocks = [pl.ds(rings[dd] * 4, 4) for dd in range(4)]

    def copy(number, source, target, to):
        return remote_copy(source, target, send_sem.at[number], recv_sem.at[number], toward[to])

    over = copy(0, both.at[1 - core], land, SIBLING)
    east = [copy(1 + i, total.at[blocks[dd]], land_east.at[i], EAST) for i, dd in enumerate((1, 3))]
    north = copy(3, total.at[blocks[2]], land_north, NORTH)
    line = [copy(3 + k, total.at[rings[0] * 4 + lines[k]], land_line.at[k - 1], (LEVEL, k)) for k in (1, 2, 3)]

    def zero():
        over.start()
        return lambda: None

    def one():
        over.wait_recv()
        total[...] = both[core] + land[...]
        for each in east:
            each.start()
        return lambda: None

    def two():
        for i, each in enumerate(east):
            each.wait_recv()
            total[blocks[2 * i]] = total[blocks[2 * i]] + land_east[i]
        north.start()
        return lambda: None

    def three():
        north.wait_recv()
        total[blocks[0]] = total[blocks[0]] + land_north[...]
        for each in line:
            each.start()
        return lambda: None

    def four():
        value = total[rings[0] * 4 + lines[0]]
        for i, each in enumerate(line):
            each.wait_recv()
            value = value + land_line[i]
        final[...] = value
        for each in [over, north] + east + line:
            each.wait_send()
        return lambda: None

    return [(True, step) for step in (zero, one, two, three, four)]


def backward_kernel(*refs):
    vectors_of, table, refs = refs[:2], refs[2], refs[3:]
    stored_of, refs = ((None,) + refs[:14], refs[14:29]), refs[29:]
    weights_of, outer_rows, refs = (refs[:3], refs[3:6]), refs[6], refs[7:]
    small_out, refs = refs[0], refs[1:]
    pages_of, refs = (refs[:3], refs[3:6]), refs[6:]
    shipped_of, refs = refs[:2], refs[2:]
    reduce_final, expand_final, attention_final, refs = refs[0], refs[1], refs[2], refs[3:]
    kinds = (ROWS, COLUMNS, COLUMNS) * 2
    owners = (1, 1, 1, 0, 0, 0)
    n = len(kinds)
    lands, refs = [refs[5 * t : 5 * t + 5] for t in range(n)], refs[5 * n :]
    (reduce_ring, expand_ring, output, second_sum, left_one, left_two, stage_wide, stage_tall, wide_sum, query_sum,
     here_sum, beside_give, away_give, corner_give, beside_got, away_got_one, away_got_two, corner_got, hidden_all, mixture,
     grad_middle, grad_attended, sums, both, result_one, result_two, reduce_sem, expand_sem, output_sem, wide_sem, tall_sem,
     pair_send, pair_recv, ship_send, ship_recv, ship_sem) = refs[:36]
    refs = refs[36:]
    tiny_refs, held, load_sem, refs = refs[:7], refs[7:22], refs[22], refs[23:]
    (top, x, normed_in, query, here, beside, away, corner, attended, logs, attended_low, middle, second, active,
     slope) = held
    place_of = places()
    core, rings, lines, toward = place_of
    scatter = Scatter(kinds, pages_of[1] + pages_of[0], lands, (reduce_final, expand_final, attention_final) * 2, owners, refs, place_of)
    steps = [scatter.steps(t) for t in range(n)]
    rows, width = top.shape
    half = rows // 2
    first = low_place(lines[0]) == 0
    tiles = weights_of[0][1].shape[1] // 256
    lead = 4 * width - WIDE
    edge = 3 * width
    todo, open_ends = [], []

    def progress(count):
        for _ in range(count):
            if todo:
                waits, begin = todo.pop(0)
                if waits and open_ends:
                    open_ends.pop()()
                ended = begin()
                if open_ends:
                    open_ends.pop()()
                open_ends.append(ended)

    def row(value):
        return jnp.sum(value, axis=0, keepdims=True)

    which = lines[0] // 2
    mine = pl.ds(pl.multiple_of(core * half, half), half)
    other = pl.ds(pl.multiple_of((1 - core) * half, half), half)
    near_rows = pl.ds(pl.multiple_of(which * half, half), half)
    far_rows = pl.ds(pl.multiple_of((1 - which) * half, half), half)

    def ship_copies(number, rows_ref):
        target = shipped_of[number].at[which, mine]
        near, distant = rows_ref.at[near_rows], rows_ref.at[far_rows]
        ways = ((near, SIBLING), (distant, (LEVEL, 3)), (distant, (CORNER, 3)))
        remote = [
            remote_copy(source, target, ship_send.at[3 * number + index], ship_recv.at[3 * number + index], toward[to])
            for index, (source, to) in enumerate(ways)
        ]
        return pltpu.make_async_copy(near, target, ship_sem.at[number]), remote

    def ship(number, layer, rows_ref):
        local, remote = ship_copies(number, rows_ref)

        def act(index):
            for copy in (local, remote[1]) if index == layer else (remote[0], remote[2]):
                copy.start()

        per_core(core, act)

    def shipped_all(number):
        local, remote = ship_copies(number, result_one)
        local.wait()
        for index, (sequence, part) in enumerate(((which, other), (1 - which, mine), (1 - which, other))):
            remote[index].wait_send()
            ref = shipped_of[number].at[sequence, part]
            place = 3 * number + index
            remote_copy(ref, ref, ship_send.at[place], ship_recv.at[place], toward[SIBLING]).wait_recv()

    def load_copy(layer, i):
        return pltpu.make_async_copy(stored_of[layer][i], held[i], load_sem.at[i])

    def load(layer, *numbers):
        for i in numbers:
            load_copy(layer, i).start()

    def pair_copy(layer, source, target, to, number):
        index = 3 * layer + number
        return remote_copy(source, target, pair_send.at[index], pair_recv.at[index], toward[to])

    def pair_copies(layer):
        away_got = away_got_one if layer == 1 else away_got_two
        return (
            pair_copy(layer, corner_give, corner_got, SIBLING, 0),
            pair_copy(layer, away_give, away_got, (LEVEL, 1), 1),
            pair_copy(layer, beside_give, beside_got, SIBLING, 2),
        )

    def layer_pass(layer):
        page_hbm, expand_hbm, reduce_hbm = weights_of[layer]
        page_reduce, page_expand, page_attention = pages_of[layer]
        vectors = vectors_of[layer]
        away_got = away_got_one if layer == 1 else away_got_two

        def tile_at(i):
            return pl.ds(pl.multiple_of(i * 256, 256), 256)

        def reduce_copy(i):
            slot = lax.rem(i, 3)
            return pltpu.make_async_copy(reduce_hbm.at[tile_at(i)], reduce_ring.at[slot], reduce_sem.at[slot])

        def expand_copy(i, source):
            slot = lax.rem(i, 3)
            return pltpu.make_async_copy(source.at[:, tile_at(i)], expand_ring.at[slot], expand_sem.at[slot])

        def wide_copy(i, target):
            slot = lax.rem(i, 2)
            return pltpu.make_async_copy(stage_wide.at[slot], target.at[:, :, tile_at(i)], wide_sem.at[slot])

        def tall_copy(i):
            slot = lax.rem(i, 2)
            return pltpu.make_async_copy(stage_tall.at[slot], page_reduce.at[tile_at(i)], tall_sem.at[slot])

        def loaded(*numbers):
            for i in numbers:
                load_copy(layer, i).wait()

        for i in range(3):
            reduce_copy(i).start()
            expand_copy(i, expand_hbm).start()
        output_copy = pltpu.make_async_copy(page_hbm.at[:, pl.ds(lead, WIDE)], output, output_sem)
        output_copy.start()
        if layer == 1:
            load(1, 11, 3, 8, 9, 4, 5, 6, 7, 10, 2, 1)
            greet(toward)
            ship(0, 0, stored_of[1][1])
            ship(0, 1, outer_rows)
        else:
            top[...] = result_one[...]
            for copy in pair_copies(1):
                copy.wait_send()
        second_sum[...] = jnp.zeros_like(second_sum)

        def tall_tile(i, _):
            side = lax.rem(i, 2)

            @pl.when(i >= 2)
            def _():
                tall_copy(i - 2).wait()

            stage_tall[side] = mm_tn(active[:, tile_at(i)], top[...]).astype(LOW)
            tall_copy(i).start()
            return 0

        def tall_page(t):
            for begin_at in range(0, tiles, 6):
                lax.fori_loop(begin_at, min(begin_at + 6, tiles), tall_tile, 0)
                progress(1)
            for i in (tiles - 2, tiles - 1):
                tall_copy(i).wait()
            scatter.give_all(t)

        def wide_tile(i, _):
            side = lax.rem(i, 2)

            @pl.when(i >= 2)
            def _():
                wide_copy(i - 2, page_expand).wait()

            stage_wide[side] = mm(left_one[...], hidden_all[:, tile_at(i)]).reshape(16, 72, 256).astype(LOW)
            wide_copy(i, page_expand).start()
            return 0

        def wide_page(t):
            for begin_at in range(0, tiles, 5):
                lax.fori_loop(begin_at, min(begin_at + 5, tiles), wide_tile, 0)
                progress(1)
            for i in (tiles - 2, tiles - 1):
                wide_copy(i, page_expand).wait()
            scatter.give_all(t)

        if layer == 1:
            loaded(0, 13)
            tall_page(0)
            todo.extend(steps[0][0] + steps[0][1])
        loaded(14, 12)
        left_one[...] = second[...].T

        def feed_tile(i, _):
            at = tile_at(i)
            slot = lax.rem(i, 3)
            reduce_copy(i).wait()
            hidden = (mm_nt(top[...], reduce_ring[slot]) * slope[:, at].astype(F32)).astype(LOW)
            wide_sum[0:1, at] = jnp.sum(hidden.astype(F32), axis=0, keepdims=True)
            hidden_all[:, at] = hidden
            expand_copy(i, expand_hbm).wait()
            second_sum[...] += mm_nt(hidden, expand_ring[slot])

            @pl.when(i + 3 < tiles)
            def _():
                reduce_copy(i + 3).start()
                expand_copy(i + 3, expand_hbm).start()

            return 0

        for begin_at in range(0, tiles, 3):
            lax.fori_loop(begin_at, min(begin_at + 3, tiles), feed_tile, 0)
            progress(1)
        for i in range(3):
            expand_copy(i, page_hbm).start()

        loaded(11)
        upstream = top[...].astype(F32)
        grad_second = close_up(second_sum[...], table[...])
        unit, inverse = normal_parts(middle[...])
        sums[6:7] = row(grad_second * unit)
        sums[7:8] = row(grad_second)
        sums[5:6] = row(upstream)
        value = upstream + normal_back(grad_second * vectors[6:7], unit, inverse)
        grad_middle[...] = value
        branch = value.astype(LOW)
        sums[4:5] = row(branch.astype(F32))
        progress(1)
        mixture[:, edge:] = branch
        output_copy.wait()
        full = jnp.concatenate([jnp.zeros((rows, edge - lead), LOW), branch], axis=1)
        pulled = mm_nt(full, output[...]).astype(LOW)
        grad_attended[:, :width] = mm_nt(pulled, table[...]).astype(LOW)
        grad_attended[:, width:] = jnp.zeros((rows, WIDE - width), LOW)
        progress(1)

        loaded(3, 8, 9, 4, 5, 6, 7)

        def rows_of(place, at, p):
            part = slice(place * half, (place + 1) * half)
            product = (grad_attended[part, at].astype(F32) * attended[part, at]).T
            delta = jnp.concatenate([row(product[:HDIM]), row(product[HDIM:])], axis=1)
            return head_pair(query[part, at]), head_pair(grad_attended[part, at]), logs[p, place : place + 1], delta

        def block(kind, near, part, at):
            rows_at = pl.ds(part * half, half)
            one, two = (here, beside) if near == 0 else (away, corner)
            return jnp.concatenate([one[kind, rows_at, at], two[kind, rows_at, at]], axis=0)

        def back(own, keys, values):
            queries, grads, log, delta = own
            weights = jnp.exp(mm_nt(keys, queries) - log)
            lowered = (weights * (mm_nt(values, grads) - delta)).astype(LOW)
            return mm_tn(keys, lowered), mm(lowered, queries), mm(weights.astype(LOW), grads)

        def put(one, two, part, at, grads):
            rows_at = pl.ds(part * half, half)
            for kind, value in enumerate(grads):
                one[kind, rows_at, at] = value[:half].astype(one.dtype)
                two[kind, rows_at, at] = value[half:].astype(two.dtype)

        def far_pair(p, _):
            at = pl.ds(pl.multiple_of(p * 128, 128), 128)
            low, high = rows_of(0, at, p), rows_of(1, at, p)
            last_rows = tuple(jnp.where(first, b, a) for a, b in zip(low, high))
            keys, values = block(0, 1, 0, at), block(1, 1, 0, at)
            high_query, keys_a, values_a = back(high, keys, values)
            last_keys = jnp.where(first, block(0, 1, 1, at), keys)
            last_values = jnp.where(first, block(1, 1, 1, at), values)
            more, keys_b, values_b = back(last_rows, last_keys, last_values)
            zero, empty = jnp.zeros_like(keys_b), jnp.zeros_like(more)
            put(away_give, corner_give, 0, at,
                (keys_a + jnp.where(first, zero, keys_b), values_a + jnp.where(first, zero, values_b)))
            put(away_give, corner_give, 1, at, (jnp.where(first, keys_b, zero), jnp.where(first, values_b, zero)))
            query_sum[:half, at] = from_pair(jnp.where(first, empty, more))
            query_sum[half:, at] = from_pair(high_query + jnp.where(first, more, empty))
            return 0

        for begin_at in (0, 3, 6):
            lax.fori_loop(begin_at, begin_at + 3, far_pair, 0)
            progress(1)

        to_corner, to_away, to_beside = pair_copies(layer)
        to_corner.start()

        def near_pair(p, _):
            at = pl.ds(pl.multiple_of(p * 128, 128), 128)
            low, high = rows_of(0, at, p), rows_of(1, at, p)
            keys, values = block(0, 0, 0, at), block(1, 0, 0, at)
            low_query, keys_a, values_a = back(low, keys, values)
            high_query, keys_b, values_b = back(high, keys, values)
            put(here_sum, beside_give, 0, at, (keys_a + keys_b, values_a + values_b))
            more, keys_a, values_a = back(high, block(0, 0, 1, at), block(1, 0, 1, at))
            put(here_sum, beside_give, 1, at, (keys_a, values_a))
            query_sum[:half, at] += from_pair(low_query)
            query_sum[half:, at] += from_pair(high_query + more)
            return 0

        lax.fori_loop(0, 2, near_pair, 0)
        to_corner.wait_recv()
        for kind in (0, 1):
            away_give[kind] = (away_give[kind].astype(F32) + corner_got[kind].astype(F32)).astype(LOW)
        to_away.start()
        progress(1)
        for begin_at, end in ((2, 5), (5, 9)):
            lax.fori_loop(begin_at, end, near_pair, 0)
            progress(1)
        to_beside.start()
        if layer == 1:
            wide_page(1)
            todo.extend(in_turn(steps[0], steps[1]))
        else:
            loaded(13)
            tall_page(3)
            todo.extend(in_turn(steps[2], steps[3], steps[1][3]))
            wide_page(4)
            todo.extend(in_turn(steps[3], steps[4], steps[2][3]))
        low = (query_sum[:, :width] * HDIM ** (-0.5)).astype(LOW)
        mixture[:, :width] = low
        sums[2:3] = row(low.astype(F32))
        loaded(10, 2, 1)
        left_one[...] = normed_in[...].T
        left_two[...] = attended_low[...].T
        second_sum[...] = jnp.zeros_like(second_sum)
        progress(4)
        to_beside.wait_recv()
        to_away.wait_recv()
        for kind in (0, 1):
            value = here_sum[kind] + beside_got[kind].astype(F32) + away_got[kind].astype(F32)
            low = value[:, :width].astype(LOW)
            mixture[:, (1 + kind) * width : (2 + kind) * width] = low
        sums[3:4] = row(low.astype(F32))

        def project_tile(i, _):
            at = tile_at(i)
            slot = lax.rem(i, 3)
            column = i * 256 + lax.broadcasted_iota(jnp.int32, (rows, 256), 1)
            part = mixture[:, at]
            part = jnp.where(column < edge, part, jnp.zeros_like(part))
            expand_copy(i, page_hbm).wait()
            second_sum[...] += mm_nt(part, expand_ring[slot])

            @pl.when(i + 3 < 13)
            def _():
                expand_copy(i + 3, page_hbm).start()

            return 0

        for begin_at, end in ((0, 4), (4, 8), (8, 13)):
            lax.fori_loop(begin_at, end, project_tile, 0)
            progress(1)
        grad_normed = close_up(second_sum[...], table[...])
        unit, inverse = normal_parts(x[...].astype(F32))
        sums[0:1] = row(grad_normed * unit)
        sums[1:2] = row(grad_normed)
        result = result_one if layer == 1 else result_two
        result[...] = (grad_middle[...] + normal_back(grad_normed * vectors[0:1], unit, inverse)).astype(LOW)
        if layer == 1:
            load(0, 14, 12, 11, 3, 8, 9, 4, 5, 6, 7, 13, 10, 2, 1)
        ship(1, layer, result)
        progress(2)

        def page_tile(number, i):
            side = lax.rem(i, 2)
            at = tile_at(i)

            @pl.when(i >= 2)
            def _():
                wide_copy(i - 2, page_attention).wait()

            part = mixture[:, at]
            if number == 1:
                value = mm(left_one[...], part)
            elif number == 2:
                value = mm(left_two[...], part)
            else:
                column = i * 256 + lax.broadcasted_iota(jnp.int32, (rows, 256), 1)
                zero = jnp.zeros_like(part)
                value = mm(left_one[...], jnp.where(column < edge, part, zero))
                value = value + mm(left_two[...], jnp.where(column < edge, zero, part))
            stage_wide[side] = value.reshape(16, 72, 256).astype(LOW)
            wide_copy(i, page_attention).start()

        def page_loop(number, begin_at, end):
            def step(i, _):
                page_tile(number, i)
                return 0

            lax.fori_loop(begin_at, end, step, 0)

        whole_tiles = edge // 256
        for begin_at in range(0, whole_tiles, 4):
            page_loop(1, begin_at, begin_at + 4)
            progress(1)
        page_loop(3, whole_tiles, whole_tiles + 1)
        page_loop(2, whole_tiles + 1, tiles)
        for i in (tiles - 2, tiles - 1):
            wide_copy(i, page_attention).wait()
        scatter.give_all(2 if layer == 1 else 5)
        if layer == 1:
            todo.extend(in_turn(steps[1], steps[2], steps[0][3]))
        small = both.at[layer]
        small[...] = jnp.zeros(small.shape, F32)
        for shard in range(16):
            small[shard, 0:8, 0:68] = sums[:, shard * 68 : (shard + 1) * 68]
            for part in range(4):
                begin_at = shard * 272 + part * 68
                small[shard, 8 + part : 9 + part, 0:68] = wide_sum[0:1, begin_at : begin_at + 68]

    load(1, 0, 13, 14, 12)
    layer_pass(1)
    layer_pass(0)
    tiny = tiny_steps(both, small_out, tiny_refs, place_of)
    todo += in_turn(steps[4], steps[5], steps[3][3])
    for place, step in enumerate(tiny):
        todo.insert(min(4 * place, len(todo)), step)
    todo += steps[5][2][:3] + steps[4][3] + steps[5][2][3:] + steps[5][3]
    progress(len(todo))
    open_ends.pop()()
    scatter.drain()
    shipped_all(0)
    shipped_all(1)
    for copy in pair_copies(0):
        copy.wait_send()


def backward(top, saved, vectors, table, weights, outer_rows):
    rows, width = top.shape
    inner = weights[0][1].shape[1]
    anywhere = pl.BlockSpec(memory_space=pl.ANY)
    inside = pl.BlockSpec(memory_space=pltpu.VMEM)
    kinds = (ROWS, COLUMNS, COLUMNS) * 2
    page = jax.ShapeDtypeStruct((16, 72, inner), LOW)
    outs = [jax.ShapeDtypeStruct((16, 128), F32)]
    outs += [jax.ShapeDtypeStruct((inner, width), LOW), page, page] * 2
    outs += [jax.ShapeDtypeStruct((2, rows, width), LOW)] * 2
    outs += [final_shape(kind) for kind in kinds[:3]]
    for kind in kinds:
        outs += landing_shapes(kind)
    pair = pltpu.VMEM((2, rows, WIDE), LOW)
    tall = pltpu.VMEM((WIDE, rows), LOW)
    flat = pltpu.VMEM((rows, width), LOW)
    dma = pltpu.SemaphoreType.DMA
    scratch = [
        pltpu.VMEM((3, 256, width), LOW), pltpu.VMEM((3, WIDE, 256), LOW), pltpu.VMEM((WIDE, WIDE), LOW),
        pltpu.VMEM((rows, WIDE), F32), tall, tall, pltpu.VMEM((2, 16, 72, 256), LOW), pltpu.VMEM((2, 256, width), LOW),
        pltpu.VMEM((8, inner), F32), pltpu.VMEM((rows, WIDE), F32), pltpu.VMEM((2, rows, WIDE), F32),
        pair, pair, pair, pair, pair, pair, pair, pltpu.VMEM((rows, inner), LOW), pltpu.VMEM((rows, inner), LOW),
        pltpu.VMEM((rows, width), F32), pltpu.VMEM((rows, WIDE), LOW), pltpu.VMEM((8, width), F32),
        pltpu.VMEM((2, 16, 16, 128), F32), flat, flat, dma((3,)), dma((3,)), dma(()), dma((2,)), dma((2,)),
        dma((6,)), dma((6,)), dma((6,)), dma((6,)), dma((2,)),
    ] + tiny_shapes() + [pltpu.VMEM(value.shape, value.dtype) for value in (top,) + saved[1]] + [dma((15,))] + work_shapes(kinds)
    res = pl.pallas_call(
        backward_kernel,
        out_shape=tuple(outs),
        in_specs=[inside] * 3 + [anywhere] * (29 + 7),
        out_specs=(inside,) + (anywhere,) * (len(outs) - 1),
        scratch_shapes=scratch,
        compiler_params=pltpu.CompilerParams(collective_id=4, has_side_effects=True, vmem_limit_bytes=63 << 20),
        name="backward",
    )(*vectors, table, *saved[0], top, *saved[1], *weights[0], *weights[1], outer_rows)
    return res[0], res[7][None], res[8][None], res[9:12]


def spread(width):
    feature = np.arange(width)
    table = np.zeros((width, 16 * 72), np.float32)
    table[feature, feature // 68 * 72 + feature % 68] = 1
    return jnp.asarray(table, LOW)


def small_of(page):
    row = page[:, 68].astype(F32)
    vectors = row[:, : 8 * 128].reshape(16, 8, 128)[:, :, :68].transpose(1, 0, 2)
    return vectors.reshape(8, -1), row[:, 8 * 128 : 8 * 128 + 4 * 68].reshape(1, -1)


def four_by_four(
    inputs,
    cotangent,
    first_gain,
    first_shift,
    joint_weight,
    query_bias,
    value_bias,
    output_weight,
    output_bias,
    second_gain,
    second_shift,
    expand_weight,
    expand_bias,
    reduce_weight,
    reduce_bias,
):
    core = lax.axis_index(SECTION)
    width = HEADS * HDIM
    vectors = (
        first_gain,
        first_shift,
        query_bias,
        value_bias,
        output_bias,
        reduce_bias,
        second_gain,
        second_shift,
        expand_bias,
    )
    packed = sum(
        jnp.pad(vector, ((0, 3), (128 * place, 4 * width - 128 * place - vector.shape[1])))
        for place, vector in enumerate(vectors)
    )
    attention_shard = jnp.concatenate(
        [jnp.concatenate([joint_weight[0], output_weight[0]], axis=1), packed], axis=0
    )
    expand_shard = jnp.pad(expand_weight[0], ((0, 4), (0, 0)))
    reduce_shard = reduce_weight[0]
    table = spread(width)

    def flat(page):
        return page.reshape(-1, page.shape[2])

    lower_page, rows = gather_page(attention_shard, inputs)
    small, wide = small_of(lower_page)
    shards = (expand_shard, reduce_shard, attention_shard, expand_shard, reduce_shard)
    saved, saved_upper, gathered, top, upper_small = forward(
        rows, small, wide, table, lower_page, cotangent, shards
    )
    lower_expand, lower_reduce, upper_page, upper_expand, upper_reduce = gathered
    weights = (flat(lower_page), flat(lower_expand), flat(lower_reduce))
    upper_weights = (flat(upper_page), flat(upper_expand), flat(upper_reduce))
    middle_rows, final_rows = saved[13], saved_upper[13]
    saved_lower, saved_upper = (rows,) + tuple(saved[:13]), (middle_rows,) + tuple(saved_upper[:13])
    vectors, layer_outputs, input_grads, (reduce_sum, expand_sum, attention_sum) = backward(
        top, (saved_lower, saved_upper), (small, upper_small), table, (weights, upper_weights), final_rows
    )
    vectors = vectors[:12, :68]
    return (
        layer_outputs,
        input_grads,
        vectors[0][None],
        vectors[1][None],
        attention_sum[None, :68, : 3 * width],
        vectors[2][None],
        vectors[3][None],
        attention_sum[None, :68, 3 * width :],
        vectors[4][None],
        vectors[6][None],
        vectors[7][None],
        expand_sum[None, :68],
        vectors[8:].reshape(1, -1),
        reduce_sum[None],
        vectors[5][None],
    )


def fits(mesh):
    return dict(mesh.shape) == {SECTION: 2, RING: 4, LINE: 4}


def solution(mesh):
    return jax.shard_map(
        four_by_four if fits(mesh) else body,
        mesh=mesh,
        in_specs=(
            P(RING, LINE, None),
            P(RING, LINE, None),
            P(SECTION, OWNERS),
            P(SECTION, OWNERS),
            P(SECTION, OWNERS, None),
            P(SECTION, OWNERS),
            P(SECTION, OWNERS),
            P(SECTION, OWNERS, None),
            P(SECTION, OWNERS),
            P(SECTION, OWNERS),
            P(SECTION, OWNERS),
            P(SECTION, OWNERS, None),
            P(SECTION, OWNERS),
            P(SECTION, OWNERS, None),
            P(SECTION, OWNERS),
        ),
        out_specs=(
            P(SECTION, RING, LINE, None),
            P(SECTION, RING, LINE, None),
            P(SECTION, OWNERS),
            P(SECTION, OWNERS),
            P(SECTION, OWNERS, None),
            P(SECTION, OWNERS),
            P(SECTION, OWNERS),
            P(SECTION, OWNERS, None),
            P(SECTION, OWNERS),
            P(SECTION, OWNERS),
            P(SECTION, OWNERS),
            P(SECTION, OWNERS, None),
            P(SECTION, OWNERS),
            P(SECTION, OWNERS, None),
            P(SECTION, OWNERS),
        ),
        check_vma=False,
    )
```

```python
from functools import partial

import jax
import jax.numpy as jnp
import numpy as np
from jax import lax
from jax.experimental import pallas as pl
from jax.experimental.pallas import tpu as pltpu
from jax.sharding import PartitionSpec as P

HEADS = 17
HDIM = 64
BLK = 256
WIDE = 1152
F32, LOW = jnp.float32, jnp.bfloat16
SECTION, RING, LINE = "section", "dp", "seq"
OWNERS = (RING, LINE)
EAST, NORTH, LEVEL, SIBLING, CORNER, ONCE, UP, DOWN = range(8)


epsilon = 1e-05
far_below = -1e30


def passed_along(value, axis, steps):
    count = lax.axis_size(axis)
    first, last = (max(0, -steps), min(count, count - steps))
    return lax.ppermute(value, axis, [(source, source + steps) for source in range(first, last)])


def normalize(values, scales, offsets):
    centre = jnp.mean(values, axis=-1, keepdims=True)
    centred = values - centre
    inverse = lax.rsqrt(jnp.mean(centred * centred, axis=-1, keepdims=True) + epsilon)
    unit_rows = centred * inverse
    return (unit_rows * scales + offsets, unit_rows, inverse)


def normalize_back(upstream, unit_rows, inverse):
    return inverse * (
        upstream
        - jnp.mean(upstream, axis=-1, keepdims=True)
        - unit_rows * jnp.mean(upstream * unit_rows, axis=-1, keepdims=True)
    )


def score_block(query, key_block, block_index, row_block):
    scores = jnp.einsum(
        "qhd,khd->qhk", query, key_block, preferred_element_type=jnp.float32
    ) * HDIM ** (-0.5)
    highest = jnp.max(scores, axis=-1)
    allowed = (block_index <= row_block)[:, None]
    exponent = jnp.exp(scores - highest[..., None]) * allowed[..., None].astype(jnp.float32)
    levels = jnp.where(allowed, highest, far_below)
    return (exponent, levels)


def attend_forward(query, keys_all, values_all, row_block):
    length = keys_all.shape[0]
    row_count = query.shape[0]
    key_shaped = keys_all.reshape(length, HEADS, HDIM)
    value_shaped = values_all.reshape(length, HEADS, HDIM)
    block_limit = row_block[-1] + 1

    def advance(block_index, carried):
        running_peak, running_sum, weighted = carried
        key_block = lax.dynamic_slice_in_dim(key_shaped, block_index * BLK, BLK, 0)
        value_block = lax.dynamic_slice_in_dim(value_shaped, block_index * BLK, BLK, 0)
        exponent, levels = score_block(query, key_block, block_index, row_block)
        weights = exponent.astype(jnp.bfloat16)
        block_out = jnp.einsum(
            "qhk,khd->qhd", weights, value_block, preferred_element_type=jnp.float32
        )
        newest_peak = jnp.maximum(running_peak, levels)
        shrink_old = jnp.exp(running_peak - newest_peak)
        shrink_new = jnp.exp(levels - newest_peak)
        running_sum = running_sum * shrink_old + shrink_new * jnp.sum(exponent, axis=-1)
        weighted = weighted * shrink_old[..., None] + shrink_new[..., None] * block_out
        return (newest_peak, running_sum, weighted)

    initial = (
        jnp.full((row_count, HEADS), far_below, jnp.float32),
        jnp.zeros((row_count, HEADS), jnp.float32),
        jnp.zeros((row_count, HEADS, HDIM), jnp.float32),
    )
    running_peak, running_sum, weighted = lax.fori_loop(0, block_limit, advance, initial)
    return (weighted / running_sum[..., None], running_peak + jnp.log(running_sum))


def attend_backward(query, keys_all, values_all, row_block, attended, log_total, grad_attended):
    length = keys_all.shape[0]
    key_shaped = keys_all.reshape(length, HEADS, HDIM)
    value_shaped = values_all.reshape(length, HEADS, HDIM)
    block_limit = row_block[-1] + 1
    delta = jnp.sum(grad_attended * attended, axis=-1)

    def advance(block_index, carried):
        grad_query, grad_keys, grad_values = carried
        key_block = lax.dynamic_slice_in_dim(key_shaped, block_index * BLK, BLK, 0)
        value_block = lax.dynamic_slice_in_dim(value_shaped, block_index * BLK, BLK, 0)
        exponent, levels = score_block(query, key_block, block_index, row_block)
        weights = exponent.astype(jnp.bfloat16)
        factor = jnp.exp(levels - log_total)
        scaled = (factor[..., None] * grad_attended).astype(jnp.bfloat16)
        grad_weights = jnp.einsum(
            "qhd,khd->qhk", scaled, value_block, preferred_element_type=jnp.float32
        )
        grad_scores = (exponent * (grad_weights - (factor * delta)[..., None])).astype(jnp.bfloat16)
        grad_query = grad_query + jnp.einsum(
            "qhk,khd->qhd", grad_scores, key_block, preferred_element_type=jnp.float32
        )
        grad_key = jnp.einsum(
            "qhk,qhd->khd", grad_scores, query, preferred_element_type=jnp.float32
        )
        grad_value = jnp.einsum("qhk,qhd->khd", weights, scaled, preferred_element_type=jnp.float32)
        grad_keys = lax.dynamic_update_slice_in_dim(grad_keys, grad_key, block_index * BLK, 0)
        grad_values = lax.dynamic_update_slice_in_dim(grad_values, grad_value, block_index * BLK, 0)
        return (grad_query, grad_keys, grad_values)

    initial = (
        jnp.zeros(query.shape, jnp.float32),
        jnp.zeros((length, HEADS, HDIM), jnp.float32),
        jnp.zeros((length, HEADS, HDIM), jnp.float32),
    )
    grad_query, grad_keys, grad_values = lax.fori_loop(0, block_limit, advance, initial)
    return (
        grad_query,
        grad_keys.reshape(length, HEADS * HDIM),
        grad_values.reshape(length, HEADS * HDIM),
    )


def project(source, params):
    feature_width = HEADS * HDIM
    normed, unit_rows, inverse = normalize(
        source, params[0].astype(jnp.float32), params[1].astype(jnp.float32)
    )
    normed_low = normed.astype(jnp.bfloat16)
    mixture = jnp.dot(normed_low, params[2], preferred_element_type=jnp.float32)
    query_low = (mixture[:, :feature_width] + params[3].astype(jnp.float32)).astype(jnp.bfloat16)
    keys_low = mixture[:, feature_width : 2 * feature_width].astype(jnp.bfloat16)
    values_low = (mixture[:, 2 * feature_width :] + params[4].astype(jnp.float32)).astype(
        jnp.bfloat16
    )
    return (unit_rows, inverse, normed_low, query_low, keys_low, values_low)


def complete(source, params, projected, gathered, row_block):
    row_count = source.shape[0]
    query = projected[3].reshape(row_count, HEADS, HDIM)
    attended, log_total = attend_forward(query, gathered[0], gathered[1], row_block)
    attended_low = attended.reshape(row_count, HEADS * HDIM).astype(jnp.bfloat16)
    middle = source + (
        jnp.dot(attended_low, params[5], preferred_element_type=jnp.float32)
        + params[6].astype(jnp.float32)
    )
    second, unit_second, inverse_second = normalize(
        middle, params[7].astype(jnp.float32), params[8].astype(jnp.float32)
    )
    second_low = second.astype(jnp.bfloat16)
    hidden = jnp.dot(second_low, params[9], preferred_element_type=jnp.float32) + params[10].astype(
        jnp.float32
    )
    active, gelu_pull = jax.vjp(partial(jax.nn.gelu, approximate=False), hidden)
    active_low = active.astype(jnp.bfloat16)
    result = middle + (
        jnp.dot(active_low, params[11], preferred_element_type=jnp.float32)
        + params[12].astype(jnp.float32)
    )
    saved = (
        query,
        attended,
        log_total,
        attended_low,
        unit_second,
        inverse_second,
        second_low,
        gelu_pull,
        active_low,
    )
    return (result, saved)


def layer_backward(source, upstream, params, projected, gathered, row_block):
    unit_first, inverse_first, normed_low, query_low, keys_low, values_low = projected
    row_count = source.shape[0]
    feature_width = HEADS * HDIM
    result, saved = complete(source, params, projected, gathered, row_block)
    (
        query,
        attended,
        log_total,
        attended_low,
        unit_second,
        inverse_second,
        second_low,
        gelu_pull,
        active_low,
    ) = saved
    top_low = upstream.astype(jnp.bfloat16)
    grad_reduce_bias = jnp.sum(top_low.astype(jnp.float32), axis=0)
    grad_reduce_weight = jnp.einsum(
        "tf,td->fd", active_low, top_low, preferred_element_type=jnp.float32
    )
    grad_active = jnp.einsum("td,fd->tf", top_low, params[11], preferred_element_type=jnp.float32)
    grad_hidden_low = gelu_pull(grad_active)[0].astype(jnp.bfloat16)
    grad_expand_bias = jnp.sum(grad_hidden_low.astype(jnp.float32), axis=0)
    grad_expand_weight = jnp.einsum(
        "td,tf->df", second_low, grad_hidden_low, preferred_element_type=jnp.float32
    )
    grad_second = jnp.einsum(
        "tf,df->td", grad_hidden_low, params[9], preferred_element_type=jnp.float32
    )
    grad_second_gain = jnp.sum(grad_second * unit_second, axis=0)
    grad_second_shift = jnp.sum(grad_second, axis=0)
    grad_middle = upstream + normalize_back(
        grad_second * params[7].astype(jnp.float32), unit_second, inverse_second
    )
    branch_low = grad_middle.astype(jnp.bfloat16)
    grad_output_bias = jnp.sum(branch_low.astype(jnp.float32), axis=0)
    grad_output_weight = jnp.einsum(
        "td,te->de", attended_low, branch_low, preferred_element_type=jnp.float32
    )
    grad_attended = jnp.einsum(
        "te,de->td", branch_low, params[5], preferred_element_type=jnp.float32
    )
    grad_query, grad_keys_full, grad_values_full = attend_backward(
        query,
        gathered[0],
        gathered[1],
        row_block,
        attended,
        log_total,
        grad_attended.reshape(row_count, HEADS, HDIM),
    )
    grad_keys, grad_values = (
        lax.psum_scatter(grad_keys_full, LINE, scatter_dimension=0, tiled=True),
        lax.psum_scatter(grad_values_full, LINE, scatter_dimension=0, tiled=True),
    )
    scale_factor = HDIM ** (-0.5)
    grad_mixture = jnp.concatenate(
        [
            grad_query.reshape(row_count, feature_width) * scale_factor,
            grad_keys * scale_factor,
            grad_values,
        ],
        axis=1,
    ).astype(jnp.bfloat16)
    grad_query_bias = jnp.sum(grad_mixture[:, :feature_width].astype(jnp.float32), axis=0)
    grad_value_bias = jnp.sum(grad_mixture[:, 2 * feature_width :].astype(jnp.float32), axis=0)
    grad_joint_weight = jnp.einsum(
        "td,te->de", normed_low, grad_mixture, preferred_element_type=jnp.float32
    )
    grad_normed = jnp.einsum(
        "te,de->td", grad_mixture, params[2], preferred_element_type=jnp.float32
    )
    grad_first_gain = jnp.sum(grad_normed * unit_first, axis=0)
    grad_first_shift = jnp.sum(grad_normed, axis=0)
    grad_source = grad_middle + normalize_back(
        grad_normed * params[0].astype(jnp.float32), unit_first, inverse_first
    )
    grads = (
        grad_first_gain,
        grad_first_shift,
        grad_joint_weight,
        grad_query_bias,
        grad_value_bias,
        grad_output_weight,
        grad_output_bias,
        grad_second_gain,
        grad_second_shift,
        grad_expand_weight,
        grad_expand_bias,
        grad_reduce_weight,
        grad_reduce_bias,
    )
    return (grad_source.astype(jnp.bfloat16), grads)


def body(
    inputs,
    cotangent,
    first_gain,
    first_shift,
    joint_weight,
    query_bias,
    value_bias,
    output_weight,
    output_bias,
    second_gain,
    second_shift,
    expand_weight,
    expand_bias,
    reduce_weight,
    reduce_bias,
):
    section_index = lax.axis_index(SECTION)
    micro_count = inputs.shape[0]
    row_count = inputs.shape[1]
    first_row = lax.axis_index(LINE) * row_count
    row_block = (first_row + jnp.arange(row_count, dtype=jnp.int32)) // BLK
    owned = (
        first_gain[0],
        first_shift[0],
        joint_weight[0],
        query_bias[0],
        value_bias[0],
        output_weight[0],
        output_bias[0],
        second_gain[0],
        second_shift[0],
        expand_weight[0],
        expand_bias[0],
        reduce_weight[0],
        reduce_bias[0],
    )
    forward_params = (
        lax.all_gather(first_gain[0], OWNERS, axis=0, tiled=True),
        lax.all_gather(first_shift[0], OWNERS, axis=0, tiled=True),
        lax.all_gather(joint_weight[0], OWNERS, axis=0, tiled=True),
        lax.all_gather(query_bias[0], OWNERS, axis=0, tiled=True),
        lax.all_gather(value_bias[0], OWNERS, axis=0, tiled=True),
        lax.all_gather(output_weight[0], OWNERS, axis=0, tiled=True),
        lax.all_gather(output_bias[0], OWNERS, axis=0, tiled=True),
        lax.all_gather(second_gain[0], OWNERS, axis=0, tiled=True),
        lax.all_gather(second_shift[0], OWNERS, axis=0, tiled=True),
        lax.all_gather(expand_weight[0], OWNERS, axis=0, tiled=True),
        lax.all_gather(expand_bias[0], OWNERS, axis=0, tiled=True),
        lax.all_gather(reduce_weight[0], OWNERS, axis=0, tiled=True),
        lax.all_gather(reduce_bias[0], OWNERS, axis=0, tiled=True),
    )
    incoming = jnp.zeros(inputs.shape[1:], jnp.bfloat16)
    section_inputs = []
    produced = []
    key_sets = []
    for tick_index in range(micro_count + 1):
        section_input = jnp.where(
            section_index == 0, inputs[min(tick_index, micro_count - 1)], incoming
        )
        source = section_input.astype(jnp.float32)
        projected = project(source, forward_params)
        gathered = (
            lax.all_gather(projected[4], LINE, axis=0, tiled=True),
            lax.all_gather(projected[5], LINE, axis=0, tiled=True),
        )
        result, unused = complete(source, forward_params, projected, gathered, row_block)
        result_low = result.astype(jnp.bfloat16)
        section_inputs.append(section_input)
        produced.append(result_low)
        key_sets.append(gathered)
        if tick_index < micro_count:
            incoming = passed_along(result_low, SECTION, 1)
    backward_params = (
        lax.all_gather(first_gain[0], OWNERS, axis=0, tiled=True),
        lax.all_gather(first_shift[0], OWNERS, axis=0, tiled=True),
        lax.all_gather(joint_weight[0], OWNERS, axis=0, tiled=True),
        lax.all_gather(query_bias[0], OWNERS, axis=0, tiled=True),
        lax.all_gather(value_bias[0], OWNERS, axis=0, tiled=True),
        lax.all_gather(output_weight[0], OWNERS, axis=0, tiled=True),
        lax.all_gather(output_bias[0], OWNERS, axis=0, tiled=True),
        lax.all_gather(second_gain[0], OWNERS, axis=0, tiled=True),
        lax.all_gather(second_shift[0], OWNERS, axis=0, tiled=True),
        lax.all_gather(expand_weight[0], OWNERS, axis=0, tiled=True),
        lax.all_gather(expand_bias[0], OWNERS, axis=0, tiled=True),
        lax.all_gather(reduce_weight[0], OWNERS, axis=0, tiled=True),
        lax.all_gather(reduce_bias[0], OWNERS, axis=0, tiled=True),
    )
    totals = tuple((jnp.zeros(piece.shape, jnp.float32) for piece in backward_params))
    shares = tuple((jnp.zeros(piece.shape, jnp.float32) for piece in owned))
    returning = jnp.zeros(inputs.shape[1:], jnp.bfloat16)
    sent_back = []
    for tick_index in range(micro_count + 1):
        upper_pick = min(tick_index + 1, micro_count)
        lower_pick = max(tick_index - 1, 0)
        section_input = jnp.where(
            section_index == 1, section_inputs[upper_pick], section_inputs[lower_pick]
        )
        upstream = jnp.where(
            section_index == 1, cotangent[min(tick_index, micro_count - 1)], returning
        ).astype(jnp.float32)
        weight_valid = jnp.where(
            section_index == 1,
            1.0 if tick_index < micro_count else 0.0,
            1.0 if tick_index >= 1 else 0.0,
        ).astype(jnp.float32)
        source = section_input.astype(jnp.float32)
        projected = project(source, backward_params)
        gathered = (
            lax.all_gather(projected[4], LINE, axis=0, tiled=True),
            lax.all_gather(projected[5], LINE, axis=0, tiled=True),
        )
        grad_source, grads = layer_backward(
            source, upstream, backward_params, projected, gathered, row_block
        )
        masked = tuple((update * weight_valid for update in grads))
        totals = tuple((running + update for running, update in zip(totals, masked)))
        sent_back.append(grad_source)
        if tick_index < micro_count:
            returning = passed_along(grad_source, SECTION, -1)
    layer_outputs = jnp.stack(
        [
            jnp.where(section_index == 0, produced[position], produced[position + 1])
            for position in range(micro_count)
        ]
    )[None]
    input_grads = jnp.stack(
        [
            jnp.where(section_index == 1, sent_back[position], sent_back[position + 1])
            for position in range(micro_count)
        ]
    )[None]
    (
        sum_first_gain,
        sum_first_shift,
        sum_joint_weight,
        sum_query_bias,
        sum_value_bias,
        sum_output_weight,
        sum_output_bias,
        sum_second_gain,
        sum_second_shift,
        sum_expand_weight,
        sum_expand_bias,
        sum_reduce_weight,
        sum_reduce_bias,
    ) = totals
    shares = (
        lax.psum_scatter(sum_first_gain, OWNERS, scatter_dimension=0, tiled=True),
        lax.psum_scatter(sum_first_shift, OWNERS, scatter_dimension=0, tiled=True),
        lax.psum_scatter(sum_joint_weight, OWNERS, scatter_dimension=0, tiled=True),
        lax.psum_scatter(sum_query_bias, OWNERS, scatter_dimension=0, tiled=True),
        lax.psum_scatter(sum_value_bias, OWNERS, scatter_dimension=0, tiled=True),
        lax.psum_scatter(sum_output_weight, OWNERS, scatter_dimension=0, tiled=True),
        lax.psum_scatter(sum_output_bias, OWNERS, scatter_dimension=0, tiled=True),
        lax.psum_scatter(sum_second_gain, OWNERS, scatter_dimension=0, tiled=True),
        lax.psum_scatter(sum_second_shift, OWNERS, scatter_dimension=0, tiled=True),
        lax.psum_scatter(sum_expand_weight, OWNERS, scatter_dimension=0, tiled=True),
        lax.psum_scatter(sum_expand_bias, OWNERS, scatter_dimension=0, tiled=True),
        lax.psum_scatter(sum_reduce_weight, OWNERS, scatter_dimension=0, tiled=True),
        lax.psum_scatter(sum_reduce_bias, OWNERS, scatter_dimension=0, tiled=True),
    )
    return (layer_outputs, input_grads) + tuple((portion[None] for portion in shares))


def flip(place, bits):
    return {1: place + 1 - 2 * (place % 2), 2: (place + 2) % 4, 3: 3 - place}[bits]


def places():
    core, ring, line = (lax.axis_index(name) for name in (SECTION, RING, LINE))
    rings = [ring] + [flip(ring, bits) for bits in (1, 2, 3)]
    lines = [line] + [flip(line, bits) for bits in (1, 2, 3)]
    toward = {
        EAST: {RING: rings[1]},
        NORTH: {RING: rings[2]},
        (LEVEL, 1): {LINE: lines[1]},
        (LEVEL, 2): {LINE: lines[2]},
        (LEVEL, 3): {LINE: lines[3]},
        (CORNER, 3): {SECTION: 1 - core, LINE: lines[3]},
        (LEVEL, UP): {LINE: (line + 1) % 4},
        (LEVEL, DOWN): {LINE: (line + 3) % 4},
        SIBLING: {SECTION: 1 - core},
    }
    return core, rings, lines, toward


def greet(toward):
    barrier = pltpu.get_barrier_semaphore()
    partners = [to for name, to in toward.items() if name not in ((LEVEL, UP), (LEVEL, DOWN))]
    for to in partners:
        pl.semaphore_signal(barrier, inc=1, device_id=to, device_id_type=pl.DeviceIdType.MESH)
    pl.semaphore_wait(barrier, len(partners))


def remote_copy(source, target, send_sem, recv_sem, to):
    return pltpu.make_async_remote_copy(
        src_ref=source,
        dst_ref=target,
        send_sem=send_sem,
        recv_sem=recv_sem,
        device_id=to,
        device_id_type=pl.DeviceIdType.MESH,
    )


def per_core(core, act):
    for index in (0, 1):

        @pl.when(core == index)
        def _():
            act(index)


GATHER_KINDS = (UP, DOWN, EAST, NORTH, CORNER, SIBLING)
GATHER_NUMBER = {kind: 4 * index for index, kind in enumerate(GATHER_KINDS)}
GATHER_SPAN = 4 * len(GATHER_KINDS)


def mm(left, right):
    return jnp.dot(left, right, preferred_element_type=F32)


def mm_nt(left, right):
    return lax.dot_general(left, right, (((1,), (1,)), ((), ())), preferred_element_type=F32)


def mm_tn(left, right):
    return lax.dot_general(left, right, (((0,), (0,)), ((), ())), preferred_element_type=F32)


def normal_parts(values):
    centre = jnp.mean(values, axis=-1, keepdims=True)
    centred = values - centre
    inverse = lax.rsqrt(jnp.mean(centred * centred, axis=-1, keepdims=True) + epsilon)
    return centred * inverse, inverse


def normal_back(upstream, unit, inverse):
    return inverse * (
        upstream
        - jnp.mean(upstream, axis=-1, keepdims=True)
        - unit * jnp.mean(upstream * unit, axis=-1, keepdims=True)
    )


def close_up(rows, table):
    high = rows.astype(LOW)
    rest = (rows - high.astype(F32)).astype(LOW)
    return mm_nt(high, table) + mm_nt(rest, table)


def head_pair(rows):
    lane = lax.broadcasted_iota(jnp.int32, rows.shape, 1)
    zero = jnp.zeros_like(rows)
    return jnp.concatenate(
        [jnp.where(lane < HDIM, rows, zero), jnp.where(lane < HDIM, zero, rows)], axis=0
    )


def from_pair(turned):
    n = turned.shape[1] // 2
    own = jnp.concatenate([turned[:HDIM, :n], turned[HDIM:, n:]], axis=0)
    return own.T


LEAD_ROWS = 144
HALF = 2176


def gather_tasks(slots, send_sem, recv_sem, copy_sem, land_sem, place_of):
    core, rings, lines, toward = place_of
    line = lines[0]
    drains = []

    def cut(t, part):
        if slots[t][1]:
            return (slice(None), pl.ds(HALF * part if isinstance(part, int) else pl.multiple_of(part * HALF, 128), HALF))
        rows = slots[t][2].shape[0]
        return (pl.ds(0, LEAD_ROWS) if part == 0 else pl.ds(LEAD_ROWS, rows - LEAD_ROWS),)

    def landed(t, part):
        _, by_columns, shard, _, land = slots[t]
        return land if by_columns else land.at[pl.ds(0, LEAD_ROWS if part == 0 else shard.shape[0] - LEAD_ROWS)]

    def run(t, act):
        if slots[t][1]:
            act(core)
        else:
            per_core(core, act)

    def place(t, part, dd, j):
        return slots[t][3].at[(rings[dd] * 4 + j,) + cut(t, part)]

    def group(t, part, dd):
        return slots[t][3].at[(pl.ds(rings[dd] * 4, 4),) + cut(t, part)]

    def copy_of(t, source, target, to, kind, j):
        index = t * GATHER_SPAN + GATHER_NUMBER[kind] + j
        return remote_copy(source, target, send_sem.at[index], recv_sem.at[index], toward[to])

    def guarded(valid, act):
        if valid is None:
            act()
        else:
            pl.when(valid)(act)

    def send(t, dd, j, to, kind, valid=None, mine=False):
        def start(part):
            target = place(t, part, dd, j)
            copy_of(t, target, target, to, kind, j).start()

        def start_mine(index):
            shard = slots[t][2].at[cut(t, index)] if index == slots[t][0] else landed(t, index)
            copy_of(t, shard, place(t, index, dd, j), to, kind, j).start()

        def finish(part):
            target = place(t, part, dd, j)
            copy_of(t, target, target, to, kind, j).wait_send()

        if mine:
            guarded(valid, lambda: per_core(core, start_mine))
        else:
            guarded(valid, lambda: run(t, start))
        drains.append(lambda: guarded(valid, lambda: run(t, finish)))

    def arrive(t, dd, j, to, kind, valid=None):
        def act(part):
            target = place(t, part, dd, j)
            copy_of(t, target, target, to, kind, j).wait_recv()

        guarded(valid, lambda: run(t, act))

    def both(one, two):
        return two if one is None else one & two

    def onward(t, j, valid, up, down, mine=False):
        if up:
            send(t, 0, j, (LEVEL, UP), UP, both(valid, line < 3), mine)
        if down:
            send(t, 0, j, (LEVEL, DOWN), DOWN, both(valid, line > 0), mine)
        send(t, 0, j, EAST, EAST, valid, mine)
        send(t, 0, j, NORTH, NORTH, valid, mine)

    def prelude():
        def give(index):
            for t, (owner, _, shard, _, land) in enumerate(slots):
                if index == owner:
                    source = shard.at[cut(t, 1 - index)]
                    remote_copy(source, landed(t, 1 - index), land_sem.at[t], land_sem.at[len(slots) + t], toward[SIBLING]).start()

        per_core(core, give)

    def taken(t):
        owner, shard = slots[t][0], slots[t][2]

        def act(index):
            target = landed(t, 1 - owner)
            copy = remote_copy(target, target, land_sem.at[t], land_sem.at[len(slots) + t], toward[SIBLING])
            if index == owner:
                copy.wait_send()
            else:
                copy.wait_recv()

        per_core(core, act)

    def local(t, index):
        source = slots[t][2].at[cut(t, index)] if index == slots[t][0] else landed(t, index)
        return pltpu.make_async_copy(source, place(t, index, 0, line), copy_sem.at[t])

    def begin(t):
        taken(t)
        onward(t, line, None, True, True, mine=True)
        per_core(core, lambda index: local(t, index).start())

    def own_ready(t):
        per_core(core, lambda index: local(t, index).wait())

    def from_line(t, offset):
        j = line + offset
        valid = j >= 0 if offset < 0 else j <= 3
        kind = UP if offset < 0 else DOWN
        arrive(t, 0, j, (LEVEL, DOWN if offset < 0 else UP), kind, valid)
        onward(t, j, valid, offset < 0, offset > 0)

    def from_side(t, offset):
        j = line + offset
        valid = None if offset == 0 else (j >= 0 if offset < 0 else j <= 3)
        even, odd = both(valid, j % 2 == 0), both(valid, j % 2 == 1)
        arrive(t, 1, j, EAST, EAST, valid)
        send(t, 1, j, NORTH, CORNER, even)
        arrive(t, 2, j, NORTH, NORTH, valid)
        send(t, 2, j, EAST, CORNER, odd)

    def from_corner(t, j):
        arrive(t, 3, j, NORTH if j % 2 == 0 else EAST, CORNER)

    def sibling(t, dd):
        def copy(part):
            return copy_of(t, group(t, part, dd), group(t, part, dd), SIBLING, SIBLING, dd)

        run(t, lambda part: copy(part).start())
        drains.append(lambda: run(t, lambda part: copy(part).wait_send()))

    def last(t):
        def act(part):
            for dd in range(4):
                target = group(t, 1 - part, dd)
                copy_of(t, target, target, SIBLING, SIBLING, dd).wait_recv()

        run(t, act)

    tasks = []

    def then(function, *given):
        tasks.append((given[0] if given else 0, lambda: function(*given)))

    count = len(slots)
    heads, tails = [], []
    for t in range(count):
        then(from_line, t, -1)
        then(from_line, t, 1)
        then(from_side, t, 0)
        for far in (2, 3):
            then(from_line, t, -far)
            then(from_line, t, far)
            then(from_side, t, 1 - far)
            then(from_side, t, far - 1)
        then(own_ready, t)
        then(sibling, t, 0)
        then(from_side, t, -3)
        then(from_side, t, 3)
        then(sibling, t, 1)
        then(sibling, t, 2)
        heads.append(list(tasks))
        tasks.clear()
        for j in range(4):
            then(from_corner, t, j)
        then(sibling, t, 3)
        then(last, t)
        tails.append(list(tasks))
        tasks.clear()
    then(prelude)
    then(begin, 0)
    for t in range(count):
        tasks += heads[t][:7]
        if t > 0:
            tasks += tails[t - 1]
        if t == 0:
            then(begin, 1)
        if t + 2 < count:
            then(begin, t + 2)
        tasks += heads[t][7:]
    tasks += tails[count - 1]

    def drain():
        for act in drains:
            act()

    return tasks, drain


def gather_outs(shards):
    shapes = []
    for _, by_columns, shard in shards:
        rows, columns = shard.shape
        land = (rows, HALF) if by_columns else (LEAD_ROWS, columns)
        shapes += [jax.ShapeDtypeStruct((16, rows, columns), LOW), jax.ShapeDtypeStruct(land, LOW)]
    return shapes


def gather_slots(forms, shards, outs):
    return [form + (shards[t], outs[2 * t], outs[2 * t + 1]) for t, form in enumerate(forms)]


def gather_semaphores(count):
    dma = pltpu.SemaphoreType.DMA
    return [dma((count * GATHER_SPAN,)), dma((count * GATHER_SPAN,)), dma((count,)), dma((2 * count,))]


def row_copies(place_of, source, target, send_sem, recv_sem, local_sem):
    core, _, lines, toward = place_of
    half = target.shape[0] // 2
    which = lines[0] // 2
    from_here = pl.ds(pl.multiple_of(core * half, half), half)
    to_there = pl.ds(pl.multiple_of(which * half, half), half)
    return (
        pltpu.make_async_copy(source.at[which, from_here], target.at[to_there], local_sem),
        remote_copy(source.at[1 - which, from_here], target.at[to_there], send_sem, recv_sem, toward[(LEVEL, 3)]),
    )


def low_place(line):
    return jnp.where(line < 2, line, 3 - line)


def forward_kernel(*refs):
    table, row_sources, shards, refs = refs[0], refs[1:3], refs[3:9], refs[9:]
    stored_of, refs = (refs[:14], refs[14:28]), refs[28:]
    outs, row_targets, vectors_of, refs = refs[:12], refs[12:14], refs[14:16], refs[16:]
    held_of, refs = (refs[:14], refs[:3] + refs[14:17] + refs[6:14]), refs[17:]
    (store_sem, big, reduce, mixture, result, mixed, stats, wide, x_in, page_sem, expand_sem, reduce_sem, pair_send,
     pair_recv, x_sem) = refs[:15]
    gather_sems, row_sems = refs[15:19], refs[19:]
    place_of = places()
    core, rings, lines, toward = place_of
    rows, width = x_in.shape
    half = rows // 2
    first = low_place(lines[0]) == 0
    tiles = big.shape[2] // 256

    def tile_at(i):
        return pl.ds(pl.multiple_of(i * 256, 256), 256)

    def tile_of(at):
        return big[:, :, at].astype(F32).reshape(WIDE, 256).astype(LOW)

    def begin(make, steps):
        def step(i, _):
            make(i).start()
            return 0

        lax.fori_loop(0, steps, step, 0)

    def pair_copies(layer):
        here, beside, away, corner = held_of[layer][2:6]
        ways = ((here, away, (LEVEL, 1)), (here, beside, SIBLING), (away, corner, SIBLING))
        return [
            remote_copy(source, target, pair_send.at[3 * layer + number], pair_recv.at[3 * layer + number], toward[to])
            for number, (source, target, to) in enumerate(ways)
        ]

    def rows_of(layer):
        return row_copies(place_of, row_sources[layer], row_targets[layer], *row_sems[3 * layer : 3 * layer + 3])

    def store_copy(layer, i):
        return pltpu.make_async_copy(held_of[layer][i], stored_of[layer][i], store_sem.at[i])

    todo, drain = gather_tasks(gather_slots(FORMS, shards, outs), *gather_sems, place_of)

    def progress(many):
        for _ in range(many):
            if todo:
                todo.pop(0)[1]()

    def complete(t):
        while any(slot <= t for slot, _ in todo):
            progress(1)

    def one_unit(queries, keys, values):
        scores = mm_nt(keys, queries)
        level = jnp.max(scores, axis=0, keepdims=True)
        exponent = jnp.exp(scores - level)
        return level, jnp.sum(exponent, axis=0, keepdims=True), mm_tn(values, exponent.astype(LOW))

    def merge(units):
        peak = units[0][0]
        for level, _, _ in units[1:]:
            peak = jnp.maximum(peak, level)
        total, out = 0.0, 0.0
        for level, sums, part in units:
            share = jnp.exp(level - peak)
            total = total + share * sums
            out = out + share * part
        return peak, total, out

    def layer_pass(layer):
        (normed_out, query_out, here, beside, away, corner, attended_out, log_out, attended_low, middle_out,
         second_out, active_out, slope_out, result_out) = held_of[layer]
        x = x_in if layer == 0 else result_out
        vectors = vectors_of[layer]
        page_source, expand_source, reduce_source = outs[6 * layer : 6 * layer + 6 : 2]

        def store(*numbers):
            for i in numbers:
                store_copy(layer, i).start()

        def page_copy(i):
            return pltpu.make_async_copy(page_source.at[:, :, tile_at(i)], big.at[:, :, tile_at(i)], page_sem.at[i])

        def expand_copy(i):
            return pltpu.make_async_copy(expand_source.at[:, :, tile_at(i)], big.at[:, :, tile_at(i)], expand_sem.at[i])

        def reduce_copy(i):
            rows_at = pl.ds(pl.multiple_of(i * 272, 16), 272)
            return pltpu.make_async_copy(reduce_source.at[i], reduce.at[rows_at], reduce_sem.at[i])

        if layer == 0:
            greet(toward)
            progress(12)
            for copy in rows_of(0):
                copy.start()
        complete(3 * layer)
        begin(page_copy, tiles)
        if layer == 0:
            for copy in rows_of(0):
                copy.wait()
            x_copy = pltpu.make_async_copy(row_targets[0], x_in, x_sem)
            x_copy.start()
            x_copy.wait()
        else:
            for i in range(14):
                store_copy(0, i).wait()
            for copy in pair_copies(0):
                copy.wait_send()

        def arrived(i, _):
            page_copy(i).wait()
            return 0

        lax.fori_loop(0, tiles, arrived, 0)
        for shard in range(16):
            line = big[shard, 64:72, 0:1408].astype(F32)[4:5]
            for place in range(8):
                vectors[place : place + 1, shard * 68 : (shard + 1) * 68] = line[:, place * 128 : place * 128 + 68]
            wide[0:1, shard * 272 : (shard + 1) * 272] = line[:, 1024:1296]
        unit, _ = normal_parts(x[...].astype(F32))
        normed = (unit * vectors[0:1] + vectors[1:2]).astype(LOW)
        normed_out[...] = mm(normed, table[...]).astype(LOW)
        store(0)

        def column(i, _):
            at = tile_at(i)
            mixture[:, at] = mm(normed_out[...], tile_of(at))
            return 0

        for begin_at, end in ((0, 4), (4, 8), (8, 13)):
            lax.fori_loop(begin_at, end, column, 0)
            progress(2)
        blank = jnp.zeros((rows, WIDE - width), LOW)
        here[0, :, :width] = mixture[:, width : 2 * width].astype(LOW)
        here[0, :, width:] = blank
        here[1, :, :width] = (mixture[:, 2 * width : 3 * width] + vectors[3:4]).astype(LOW)
        here[1, :, width:] = blank

        to_away, to_beside, to_corner = pair_copies(layer)
        to_away.start()
        to_beside.start()
        query = ((mixture[:, :width] + vectors[2:3]).astype(LOW).astype(F32) * HDIM ** (-0.5)).astype(LOW)
        query_out[:, :width] = query
        query_out[:, width:] = blank
        store(1, 2)
        progress(1)
        to_beside.wait_recv()
        store(3)

        def block(kind, near, part, at):
            rows_at = pl.ds(part * half, half)
            one, two = (here, beside) if near == 0 else (away, corner)
            return jnp.concatenate([one[kind, rows_at, at], two[kind, rows_at, at]], axis=0)

        def local_pair(p, _):
            at = pl.ds(pl.multiple_of(p * 128, 128), 128)
            low, high = head_pair(query_out[:half, at]), head_pair(query_out[half:, at])
            keys, values = block(0, 0, 0, at), block(1, 0, 0, at)
            bottom = one_unit(low, keys, values)
            top = merge([one_unit(high, keys, values), one_unit(high, block(0, 0, 1, at), block(1, 0, 1, at))])
            for place, (level, sums, out) in enumerate((bottom, top)):
                stats[p, 2 * place : 2 * place + 1] = level
                stats[p, 2 * place + 1 : 2 * place + 2] = sums
                mixed[p, place] = out
            return 0

        for begin_at in (0, 3, 6):
            lax.fori_loop(begin_at, begin_at + 3, local_pair, 0)
            progress(2)
        progress(8)
        to_away.wait_recv()
        to_corner.start()
        store(4)
        progress(2)
        to_corner.wait_recv()
        store(5)

        def far_pair(p, _):
            at = pl.ds(pl.multiple_of(p * 128, 128), 128)
            low, high = head_pair(query_out[:half, at]), head_pair(query_out[half:, at])
            keys, values = block(0, 1, 0, at), block(1, 1, 0, at)
            last_keys = jnp.where(first, block(0, 1, 1, at), keys)
            last_values = jnp.where(first, block(1, 1, 1, at), values)
            near = one_unit(high, keys, values)
            last = one_unit(jnp.where(first, high, low), last_keys, last_values)
            low_last = (jnp.where(first, far_below, last[0]),) + last[1:]
            high_last = (jnp.where(first, last[0], far_below),) + last[1:]

            def before(place):
                return (stats[p, 2 * place : 2 * place + 1], stats[p, 2 * place + 1 : 2 * place + 2], mixed[p, place])

            for place, units in enumerate(([before(0), low_last], [before(1), near, high_last])):
                peak, total, out = merge(units)
                attended_out[place * half : (place + 1) * half, at] = from_pair(out / total)
                log_out[p, place : place + 1] = peak + jnp.log(total)
            return 0

        for begin_at in (0, 3, 6):
            lax.fori_loop(begin_at, begin_at + 3, far_pair, 0)
            progress(2)

        lead = 4 * width - WIDE
        store(6, 7)
        attended_low[...] = mm(attended_out[:, :width].astype(LOW), table[...]).astype(LOW)
        store(8)

        def blend(i, _):
            at = pl.ds(pl.multiple_of(lead + i * 128, 128), 128)
            weights = big[:, :, at].astype(F32).reshape(WIDE, 128).astype(LOW)
            mixture[:, pl.ds(pl.multiple_of(i * 128, 128), 128)] = mm(attended_low[...], weights)
            return 0

        lax.fori_loop(0, WIDE // 128, blend, 0)
        middle = x[...].astype(F32) + (mixture[:, 3 * width - lead : WIDE] + vectors[4:5])
        middle_out[...] = middle
        store(9)
        progress(2)
        unit, _ = normal_parts(middle)
        second = (unit * vectors[6:7] + vectors[7:8]).astype(LOW)
        second_out[...] = mm(second, table[...]).astype(LOW)
        store(10)
        result[...] = middle + vectors[5:6]

        complete(1 + 3 * layer)
        begin(expand_copy, tiles)
        if layer == 1:
            for copy in rows_of(1):
                copy.start()

        def inner(i, _):
            at = tile_at(i)
            expand_copy(i).wait()
            hidden = mm(second_out[...], tile_of(at)) + wide[0:1, at]
            below = 0.5 + 0.5 * lax.erf(hidden * 0.7071067811865476)
            active_out[:, at] = (hidden * below).astype(LOW)
            slope_out[:, at] = (below + hidden * (0.3989422804014327 * jnp.exp(-0.5 * hidden * hidden))).astype(LOW)
            return 0

        for begin_at in range(0, tiles, 2):
            lax.fori_loop(begin_at, min(begin_at + 2, tiles), inner, 0)
            progress(2)
        store(11, 12)
        complete(2 + 3 * layer)
        begin(reduce_copy, 16)

        def landed(i, _):
            reduce_copy(i).wait()
            return 0

        lax.fori_loop(0, 16, landed, 0)

        def outer(i, _):
            at = pl.ds(pl.multiple_of(i * 256, 256), 256)
            result[...] += mm(active_out[:, at], reduce[at])
            return 0

        lax.fori_loop(0, tiles, outer, 0)
        result_out[...] = result[...].astype(LOW)
        store(13)

    layer_pass(0)
    layer_pass(1)
    progress(len(todo))
    drain()
    for i in range(14):
        store_copy(1, i).wait()
    for copy in rows_of(1):
        copy.wait()
    for copy in pair_copies(1):
        copy.wait_send()


FORMS = ((0, True), (0, True), (0, False), (1, True), (1, True), (1, False))


def forward(table, row_sources, shards):
    rows, width = row_sources[0].shape[1:]
    inner = shards[0].shape[1]
    pairs = WIDE // 128
    anywhere = pl.BlockSpec(memory_space=pl.ANY)
    inside = pl.BlockSpec(memory_space=pltpu.VMEM)

    def shape(*dims, kind=LOW):
        return jax.ShapeDtypeStruct(dims, kind)

    pair = shape(2, rows, WIDE)
    kept = [
        shape(rows, WIDE), shape(rows, WIDE), pair, pair, pair, pair, shape(rows, WIDE, kind=F32),
        shape(pairs, 2, rows, kind=F32), shape(rows, WIDE), shape(rows, width, kind=F32),
        shape(rows, WIDE), shape(rows, inner), shape(rows, inner), shape(rows, width),
    ]
    outs = kept * 2 + gather_outs(tuple(form + (shard,) for form, shard in zip(FORMS, shards)))
    outs += [shape(rows, width)] * 2 + [shape(8, width, kind=F32)] * 2
    dma = pltpu.SemaphoreType.DMA
    scratch = [pltpu.VMEM(out.shape, out.dtype) for out in kept + [pair] * 3] + [
        dma((14,)), pltpu.VMEM((16, 72, inner), LOW), pltpu.VMEM((inner, width), LOW),
        pltpu.VMEM((rows, 13 * 256), F32), pltpu.VMEM((rows, width), F32),
        pltpu.VMEM((pairs, 2, 128, rows), F32), pltpu.VMEM((pairs, 4, rows), F32), pltpu.VMEM((8, inner), F32),
        pltpu.VMEM((rows, width), LOW), dma((inner // 256,)), dma((inner // 256,)), dma((16,)), dma((6,)), dma((6,)), dma(()),
    ] + gather_semaphores(len(shards)) + [dma(())] * 6
    res = pl.pallas_call(
        forward_kernel,
        out_shape=tuple(outs),
        in_specs=[inside] + [anywhere] * (2 + len(shards)),
        out_specs=(anywhere,) * (len(outs) - 2) + (inside,) * 2,
        scratch_shapes=scratch,
        compiler_params=pltpu.CompilerParams(collective_id=3, has_side_effects=True, vmem_limit_bytes=62 << 20),
        name="forward",
    )(table, *row_sources, *shards)
    return res[:14], res[14:28], res[28:40:2], res[40:42], res[42:]


COLUMNS, ROWS = range(2)
SIZES = {COLUMNS: (72, 2176), ROWS: (144, 1088)}
DEPTH = 8
EASTWARD = (3, 0)
SCATTER_KINDS = (
    [(SIBLING, dd) for dd in range(4)]
    + [(ONCE, k) for k in range(4)]
    + [(EAST, k) for k in range(4)]
    + [(NORTH, k) for k in range(4)]
    + [(LEVEL, k) for k in (1, 2, 3)]
    + [(CORNER, 0)]
)
SCATTER_NUMBER = {kind: index for index, kind in enumerate(SCATTER_KINDS)}


def landing_shapes(kind):
    return [jax.ShapeDtypeStruct((many,) + SIZES[kind], LOW) for many in (16, 4, 4, 4, 4)]


def final_shape(kind):
    return jax.ShapeDtypeStruct({COLUMNS: (72, 4352), ROWS: (272, 1088)}[kind], F32)


def work_shapes(kinds):
    shapes = []
    for kind in sorted(set(kinds)):
        size = SIZES[kind]
        shapes += [pltpu.VMEM((2, 4) + size, LOW), pltpu.VMEM((DEPTH,) + size, LOW), pltpu.VMEM(size, F32)]
    count = len(kinds) * len(SCATTER_KINDS)
    return shapes + [
        pltpu.SemaphoreType.DMA((count,)), pltpu.SemaphoreType.DMA((count,)),
        pltpu.SemaphoreType.DMA((8,)), pltpu.SemaphoreType.DMA(()),
    ]


class Scatter:
    def __init__(self, kinds, pages, lands, finals, owners, refs, place_of):
        self.kinds, self.pages, self.lands, self.finals, self.owners = kinds, pages, lands, finals, owners
        self.core, self.rings, self.lines, self.toward = place_of
        self.work = {}
        for index, kind in enumerate(sorted(set(kinds))):
            self.work[kind] = refs[3 * index : 3 * index + 3]
        self.send_sem, self.recv_sem, self.load_sem, self.out_sem = refs[3 * len(self.work) :]
        self.turn = 0
        self.used = {kind: [None] * DEPTH for kind in self.work}
        self.count = {kind: 0 for kind in self.work}
        self.given, self.final_sent = [], []

    def remote(self, t, source, target, to, kind):
        index = t * len(SCATTER_KINDS) + SCATTER_NUMBER[kind]
        return remote_copy(source, target, self.send_sem.at[index], self.recv_sem.at[index], self.toward[to])

    def part(self, t, core, index, many=None):
        page, at = self.pages[t], index if many is None else pl.ds(index, many)
        if self.kinds[t] == COLUMNS:
            return page.at[at, :, pl.ds(pl.multiple_of(core * 2176, 128), 2176)]
        return page.at[pl.ds(pl.multiple_of(index * 272 + core * 128, 16), 144)]

    def landed(self, t, dd):
        return self.lands[t][0].at[pl.ds(self.rings[dd] * 4, 4)]

    def give(self, t, dd):
        base = self.rings[dd] * 4
        if self.kinds[t] == ROWS:
            for k in range(4):
                self.remote(t, self.part(t, 1 - self.core, base + k), self.lands[t][0].at[base + k], SIBLING, (SIBLING, dd)).start()
        else:
            self.remote(t, self.part(t, 1 - self.core, base, 4), self.landed(t, dd), SIBLING, (SIBLING, dd)).start()
        self.given.append(self.remote(t, self.landed(t, dd), self.landed(t, dd), SIBLING, (SIBLING, dd)))

    def arrived(self, t, ref, to, kind):
        self.remote(t, ref, ref, to, kind).wait_recv()

    def load(self, t, sources):
        loads = self.work[self.kinds[t]][0]
        slot = self.turn % 2
        self.turn += 1
        copies = []
        for j, source in enumerate(sources):
            copies.append(pltpu.make_async_copy(source, loads.at[slot, j], self.load_sem.at[slot * 4 + j]))
        for copy in copies:
            copy.start()
        return loads, slot, copies

    def add_up(self, t, loaded, store):
        loads, slot, copies = loaded
        terms = len(copies)
        for copy in copies:
            copy.wait()
        rows, columns = SIZES[self.kinds[t]]
        wide = self.kinds[t] != ROWS
        piece = min(256, columns) if wide else 16

        def step(i, _):
            at = pl.ds(pl.multiple_of(i * piece, piece), piece)
            where = (slice(None), at) if wide else (at, slice(None))
            value = loads[(slot, 0) + where].astype(F32)
            for j in range(1, terms):
                value = value + loads[(slot, j) + where].astype(F32)
            store(where, value)
            return 0

        steps = (columns if wide else rows) // piece
        lax.fori_loop(0, steps, step, 0)
        if wide and steps * piece < columns:
            where = (slice(None), pl.ds(steps * piece, columns - steps * piece))
            value = loads[(slot, 0) + where].astype(F32)
            for j in range(1, terms):
                value = value + loads[(slot, j) + where].astype(F32)
            store(where, value)

    def sources(self, t, dd, k, extra):
        index = self.rings[dd] * 4 + self.lines[k]
        return [self.part(t, self.core, index), self.lands[t][0].at[index]] + extra

    def sum_and_send(self, t, dd, k, extra, target, to, kind):
        form = self.kinds[t]
        loaded = self.load(t, self.sources(t, dd, k, extra))

        def finish():
            place = self.count[form] % DEPTH
            self.count[form] += 1
            if self.used[form][place] is not None:
                self.used[form][place].wait_send()
            out = self.work[form][1]

            def store(where, value):
                out[(place,) + where] = value.astype(out.dtype)

            self.add_up(t, loaded, store)
            copy = self.remote(t, out.at[place], target, to, kind)
            copy.start()
            self.used[form][place] = copy

        return finish

    def first(self, t, k):
        if k == 3:
            self.arrived(t, self.landed(t, 3), SIBLING, (SIBLING, 3))
        to = EAST if k in EASTWARD else NORTH
        return self.sum_and_send(t, 3, k, [], self.lands[t][1].at[k], to, (ONCE, k))

    def second(self, t, dd, k):
        if (dd, k) in ((1, 3), (2, 2)):
            self.arrived(t, self.landed(t, dd), SIBLING, (SIBLING, dd))
        to, land = (EAST, self.lands[t][2]) if dd == 1 else (NORTH, self.lands[t][3])
        extra = []
        if (dd == 1) != (k in EASTWARD):
            one = self.lands[t][1].at[k]
            self.arrived(t, one, EAST if k in EASTWARD else NORTH, (ONCE, k))
            extra = [one]
        return self.sum_and_send(t, dd, k, extra, land.at[k], to, (to, k))

    def third(self, t, k):
        if k == 3:
            self.arrived(t, self.landed(t, 0), SIBLING, (SIBLING, 0))
        extra = []
        for to, land in ((EAST, self.lands[t][2]), (NORTH, self.lands[t][3])):
            self.arrived(t, land.at[k], to, (to, k))
            extra.append(land.at[k])
        if k:
            return self.sum_and_send(t, 0, k, extra, self.lands[t][4].at[k], (LEVEL, k), (LEVEL, k))
        loaded = self.load(t, self.sources(t, 0, 0, extra))
        total = self.work[self.kinds[t]][2]

        def store(where, value):
            total[where] = value

        return lambda: self.add_up(t, loaded, store)

    def final_part(self, t, core):
        if self.kinds[t] == COLUMNS:
            return (slice(None), slice(None)), (slice(None), pl.ds(2176 * core, 2176))
        return (pl.ds(16 * core, 144 - 16 * core),), (pl.ds(144 * core, 144 - 16 * core),)

    def last(self, t):
        land = self.lands[t][4]
        for k in (1, 2, 3):
            self.arrived(t, land.at[k], (LEVEL, k), (LEVEL, k))
        loaded = self.load(t, [land.at[k] for k in (1, 2, 3)])
        total = self.work[self.kinds[t]][2]
        owner = self.owners[t]

        def store(where, value):
            total[where] = total[where] + value

        def act(core):
            inner, outer = self.final_part(t, core)
            source, target = total.at[inner], self.finals[t].at[outer]
            if core == owner:
                copy = pltpu.make_async_copy(source, target, self.out_sem)
                copy.start()
                copy.wait()
                theirs = self.finals[t].at[self.final_part(t, 1 - core)[1]]
                self.remote(t, theirs, theirs, SIBLING, (CORNER, 0)).wait_recv()
            else:
                copy = self.remote(t, source, target, SIBLING, (CORNER, 0))
                copy.start()
                copy.wait_send()

        def finish():
            self.add_up(t, loaded, store)
            per_core(self.core, act)

        return finish

    def give_all(self, t):
        for dd in (3, 1, 2, 0):
            self.give(t, dd)

    def steps(self, t):
        def of(waits, function, *given):
            return waits, lambda: function(*given)

        ways = ((1, 3), (2, 2), (1, 0), (2, 1), (1, 2), (2, 3), (1, 1), (2, 0))
        return (
            [of(k == 3, self.first, t, k) for k in (3, 2, 0, 1)],
            [of((dd == 1) != (k in EASTWARD), self.second, t, dd, k) for dd, k in ways],
            [of(True, self.third, t, k) for k in (3, 2, 1, 0)],
            [of(True, self.last, t)],
        )

    def drain(self):
        for copy in self.given:
            copy.wait_send()
        for held in self.used.values():
            for copy in held:
                if copy is not None:
                    copy.wait_send()


def in_turn(earlier, later, done=()):
    return later[0] + earlier[2][:2] + later[1][:4] + list(done) + earlier[2][2:] + later[1][4:]


def tiny_shapes():
    return [
        pltpu.VMEM((16, 16, 128), F32), pltpu.VMEM((16, 16, 128), F32), pltpu.VMEM((2, 4, 16, 128), F32),
        pltpu.VMEM((4, 16, 128), F32), pltpu.VMEM((3, 16, 128), F32),
        pltpu.SemaphoreType.DMA((7,)), pltpu.SemaphoreType.DMA((7,)),
    ]


def tiny_steps(both, final, refs, place_of):
    total, land, land_east, land_north, land_line, send_sem, recv_sem = refs
    core, rings, lines, toward = place_of
    blocks = [pl.ds(rings[dd] * 4, 4) for dd in range(4)]

    def copy(number, source, target, to):
        return remote_copy(source, target, send_sem.at[number], recv_sem.at[number], toward[to])

    over = copy(0, both.at[1 - core], land, SIBLING)
    east = [copy(1 + i, total.at[blocks[dd]], land_east.at[i], EAST) for i, dd in enumerate((1, 3))]
    north = copy(3, total.at[blocks[2]], land_north, NORTH)
    line = [copy(3 + k, total.at[rings[0] * 4 + lines[k]], land_line.at[k - 1], (LEVEL, k)) for k in (1, 2, 3)]

    def zero():
        over.start()
        return lambda: None

    def one():
        over.wait_recv()
        total[...] = both[core] + land[...]
        for each in east:
            each.start()
        return lambda: None

    def two():
        for i, each in enumerate(east):
            each.wait_recv()
            total[blocks[2 * i]] = total[blocks[2 * i]] + land_east[i]
        north.start()
        return lambda: None

    def three():
        north.wait_recv()
        total[blocks[0]] = total[blocks[0]] + land_north[...]
        for each in line:
            each.start()
        return lambda: None

    def four():
        value = total[rings[0] * 4 + lines[0]]
        for i, each in enumerate(line):
            each.wait_recv()
            value = value + land_line[i]
        final[...] = value
        for each in [over, north] + east + line:
            each.wait_send()
        return lambda: None

    return [(True, step) for step in (zero, one, two, three, four)]


def backward_kernel(*refs):
    vectors_of, table, refs = refs[:2], refs[2], refs[3:]
    stored_of, refs = ((None,) + refs[:14], refs[14:29]), refs[29:]
    weights_of, outer_rows, refs = (refs[:3], refs[3:6]), refs[6], refs[7:]
    small_out, refs = refs[0], refs[1:]
    pages_of, refs = (refs[:3], refs[3:6]), refs[6:]
    shipped_of, refs = refs[:2], refs[2:]
    reduce_final, expand_final, attention_final, refs = refs[0], refs[1], refs[2], refs[3:]
    kinds = (ROWS, COLUMNS, COLUMNS) * 2
    owners = (1, 1, 1, 0, 0, 0)
    n = len(kinds)
    lands, refs = [refs[5 * t : 5 * t + 5] for t in range(n)], refs[5 * n :]
    (reduce_ring, expand_ring, output, second_sum, left_one, left_two, stage_wide, stage_tall, wide_sum, query_sum,
     here_sum, beside_give, away_give, corner_give, beside_got, away_got_one, away_got_two, corner_got, hidden_all, mixture,
     grad_middle, grad_attended, sums, both, result_one, result_two, reduce_sem, expand_sem, output_sem, wide_sem, tall_sem,
     pair_send, pair_recv, ship_send, ship_recv, ship_sem) = refs[:36]
    refs = refs[36:]
    tiny_refs, held, load_sem, refs = refs[:7], refs[7:22], refs[22], refs[23:]
    (top, x, normed_in, query, here, beside, away, corner, attended, logs, attended_low, middle, second, active,
     slope) = held
    place_of = places()
    core, rings, lines, toward = place_of
    scatter = Scatter(kinds, pages_of[1] + pages_of[0], lands, (reduce_final, expand_final, attention_final) * 2, owners, refs, place_of)
    steps = [scatter.steps(t) for t in range(n)]
    rows, width = top.shape
    half = rows // 2
    first = low_place(lines[0]) == 0
    tiles = weights_of[0][1].shape[1] // 256
    lead = 4 * width - WIDE
    edge = 3 * width
    todo, open_ends = [], []

    def progress(count):
        for _ in range(count):
            if todo:
                waits, begin = todo.pop(0)
                if waits and open_ends:
                    open_ends.pop()()
                ended = begin()
                if open_ends:
                    open_ends.pop()()
                open_ends.append(ended)

    def row(value):
        return jnp.sum(value, axis=0, keepdims=True)

    which = lines[0] // 2
    mine = pl.ds(pl.multiple_of(core * half, half), half)
    other = pl.ds(pl.multiple_of((1 - core) * half, half), half)
    near_rows = pl.ds(pl.multiple_of(which * half, half), half)
    far_rows = pl.ds(pl.multiple_of((1 - which) * half, half), half)

    def ship_copies(number, rows_ref):
        target = shipped_of[number].at[which, mine]
        near, distant = rows_ref.at[near_rows], rows_ref.at[far_rows]
        ways = ((near, SIBLING), (distant, (LEVEL, 3)), (distant, (CORNER, 3)))
        remote = [
            remote_copy(source, target, ship_send.at[3 * number + index], ship_recv.at[3 * number + index], toward[to])
            for index, (source, to) in enumerate(ways)
        ]
        return pltpu.make_async_copy(near, target, ship_sem.at[number]), remote

    def ship(number, layer, rows_ref):
        local, remote = ship_copies(number, rows_ref)

        def act(index):
            for copy in (local, remote[1]) if index == layer else (remote[0], remote[2]):
                copy.start()

        per_core(core, act)

    def shipped_all(number):
        local, remote = ship_copies(number, result_one)
        local.wait()
        for index, (sequence, part) in enumerate(((which, other), (1 - which, mine), (1 - which, other))):
            remote[index].wait_send()
            ref = shipped_of[number].at[sequence, part]
            place = 3 * number + index
            remote_copy(ref, ref, ship_send.at[place], ship_recv.at[place], toward[SIBLING]).wait_recv()

    def load_copy(layer, i):
        return pltpu.make_async_copy(stored_of[layer][i], held[i], load_sem.at[i])

    def load(layer, *numbers):
        for i in numbers:
            load_copy(layer, i).start()

    def pair_copy(layer, source, target, to, number):
        index = 3 * layer + number
        return remote_copy(source, target, pair_send.at[index], pair_recv.at[index], toward[to])

    def pair_copies(layer):
        away_got = away_got_one if layer == 1 else away_got_two
        return (
            pair_copy(layer, corner_give, corner_got, SIBLING, 0),
            pair_copy(layer, away_give, away_got, (LEVEL, 1), 1),
            pair_copy(layer, beside_give, beside_got, SIBLING, 2),
        )

    def layer_pass(layer):
        page_hbm, expand_hbm, reduce_hbm = weights_of[layer]
        page_reduce, page_expand, page_attention = pages_of[layer]
        vectors = vectors_of[layer]
        away_got = away_got_one if layer == 1 else away_got_two

        def tile_at(i):
            return pl.ds(pl.multiple_of(i * 256, 256), 256)

        def reduce_copy(i):
            slot = lax.rem(i, 3)
            return pltpu.make_async_copy(reduce_hbm.at[tile_at(i)], reduce_ring.at[slot], reduce_sem.at[slot])

        def expand_copy(i, source):
            slot = lax.rem(i, 3)
            return pltpu.make_async_copy(source.at[:, tile_at(i)], expand_ring.at[slot], expand_sem.at[slot])

        def wide_copy(i, target):
            slot = lax.rem(i, 2)
            return pltpu.make_async_copy(stage_wide.at[slot], target.at[:, :, tile_at(i)], wide_sem.at[slot])

        def tall_copy(i):
            slot = lax.rem(i, 2)
            return pltpu.make_async_copy(stage_tall.at[slot], page_reduce.at[tile_at(i)], tall_sem.at[slot])

        def loaded(*numbers):
            for i in numbers:
                load_copy(layer, i).wait()

        for i in range(3):
            reduce_copy(i).start()
            expand_copy(i, expand_hbm).start()
        output_copy = pltpu.make_async_copy(page_hbm.at[:, pl.ds(lead, WIDE)], output, output_sem)
        output_copy.start()
        if layer == 1:
            load(1, 11, 3, 8, 9, 4, 5, 6, 7, 10, 2, 1)
            greet(toward)
            ship(0, 0, stored_of[1][1])
            ship(0, 1, outer_rows)
        else:
            top[...] = result_one[...]
            for copy in pair_copies(1):
                copy.wait_send()
        second_sum[...] = jnp.zeros_like(second_sum)

        def tall_tile(i, _):
            side = lax.rem(i, 2)

            @pl.when(i >= 2)
            def _():
                tall_copy(i - 2).wait()

            stage_tall[side] = mm_tn(active[:, tile_at(i)], top[...]).astype(LOW)
            tall_copy(i).start()
            return 0

        def tall_page(t):
            for begin_at in range(0, tiles, 6):
                lax.fori_loop(begin_at, min(begin_at + 6, tiles), tall_tile, 0)
                progress(1)
            for i in (tiles - 2, tiles - 1):
                tall_copy(i).wait()
            scatter.give_all(t)

        def wide_tile(i, _):
            side = lax.rem(i, 2)

            @pl.when(i >= 2)
            def _():
                wide_copy(i - 2, page_expand).wait()

            stage_wide[side] = mm(left_one[...], hidden_all[:, tile_at(i)]).reshape(16, 72, 256).astype(LOW)
            wide_copy(i, page_expand).start()
            return 0

        def wide_page(t):
            for begin_at in range(0, tiles, 5):
                lax.fori_loop(begin_at, min(begin_at + 5, tiles), wide_tile, 0)
                progress(1)
            for i in (tiles - 2, tiles - 1):
                wide_copy(i, page_expand).wait()
            scatter.give_all(t)

        if layer == 1:
            loaded(0, 13)
            tall_page(0)
            todo.extend(steps[0][0] + steps[0][1])
        loaded(14, 12)
        left_one[...] = second[...].T

        def feed_tile(i, _):
            at = tile_at(i)
            slot = lax.rem(i, 3)
            reduce_copy(i).wait()
            hidden = (mm_nt(top[...], reduce_ring[slot]) * slope[:, at].astype(F32)).astype(LOW)
            wide_sum[0:1, at] = jnp.sum(hidden.astype(F32), axis=0, keepdims=True)
            hidden_all[:, at] = hidden
            expand_copy(i, expand_hbm).wait()
            second_sum[...] += mm_nt(hidden, expand_ring[slot])

            @pl.when(i + 3 < tiles)
            def _():
                reduce_copy(i + 3).start()
                expand_copy(i + 3, expand_hbm).start()

            return 0

        for begin_at in range(0, tiles, 3):
            lax.fori_loop(begin_at, min(begin_at + 3, tiles), feed_tile, 0)
            progress(1)
        for i in range(3):
            expand_copy(i, page_hbm).start()

        loaded(11)
        upstream = top[...].astype(F32)
        grad_second = close_up(second_sum[...], table[...])
        unit, inverse = normal_parts(middle[...])
        sums[6:7] = row(grad_second * unit)
        sums[7:8] = row(grad_second)
        sums[5:6] = row(upstream)
        value = upstream + normal_back(grad_second * vectors[6:7], unit, inverse)
        grad_middle[...] = value
        branch = value.astype(LOW)
        sums[4:5] = row(branch.astype(F32))
        progress(1)
        mixture[:, edge:] = branch
        output_copy.wait()
        full = jnp.concatenate([jnp.zeros((rows, edge - lead), LOW), branch], axis=1)
        pulled = mm_nt(full, output[...]).astype(LOW)
        grad_attended[:, :width] = mm_nt(pulled, table[...]).astype(LOW)
        grad_attended[:, width:] = jnp.zeros((rows, WIDE - width), LOW)
        progress(1)

        loaded(3, 8, 9, 4, 5, 6, 7)

        def rows_of(place, at, p):
            part = slice(place * half, (place + 1) * half)
            product = (grad_attended[part, at].astype(F32) * attended[part, at]).T
            delta = jnp.concatenate([row(product[:HDIM]), row(product[HDIM:])], axis=1)
            return head_pair(query[part, at]), head_pair(grad_attended[part, at]), logs[p, place : place + 1], delta

        def block(kind, near, part, at):
            rows_at = pl.ds(part * half, half)
            one, two = (here, beside) if near == 0 else (away, corner)
            return jnp.concatenate([one[kind, rows_at, at], two[kind, rows_at, at]], axis=0)

        def back(own, keys, values):
            queries, grads, log, delta = own
            weights = jnp.exp(mm_nt(keys, queries) - log)
            lowered = (weights * (mm_nt(values, grads) - delta)).astype(LOW)
            return mm_tn(keys, lowered), mm(lowered, queries), mm(weights.astype(LOW), grads)

        def put(one, two, part, at, grads):
            rows_at = pl.ds(part * half, half)
            for kind, value in enumerate(grads):
                one[kind, rows_at, at] = value[:half].astype(one.dtype)
                two[kind, rows_at, at] = value[half:].astype(two.dtype)

        def far_pair(p, _):
            at = pl.ds(pl.multiple_of(p * 128, 128), 128)
            low, high = rows_of(0, at, p), rows_of(1, at, p)
            last_rows = tuple(jnp.where(first, b, a) for a, b in zip(low, high))
            keys, values = block(0, 1, 0, at), block(1, 1, 0, at)
            high_query, keys_a, values_a = back(high, keys, values)
            last_keys = jnp.where(first, block(0, 1, 1, at), keys)
            last_values = jnp.where(first, block(1, 1, 1, at), values)
            more, keys_b, values_b = back(last_rows, last_keys, last_values)
            zero, empty = jnp.zeros_like(keys_b), jnp.zeros_like(more)
            put(away_give, corner_give, 0, at,
                (keys_a + jnp.where(first, zero, keys_b), values_a + jnp.where(first, zero, values_b)))
            put(away_give, corner_give, 1, at, (jnp.where(first, keys_b, zero), jnp.where(first, values_b, zero)))
            query_sum[:half, at] = from_pair(jnp.where(first, empty, more))
            query_sum[half:, at] = from_pair(high_query + jnp.where(first, more, empty))
            return 0

        for begin_at in (0, 3, 6):
            lax.fori_loop(begin_at, begin_at + 3, far_pair, 0)
            progress(1)

        to_corner, to_away, to_beside = pair_copies(layer)
        to_corner.start()

        def near_pair(p, _):
            at = pl.ds(pl.multiple_of(p * 128, 128), 128)
            low, high = rows_of(0, at, p), rows_of(1, at, p)
            keys, values = block(0, 0, 0, at), block(1, 0, 0, at)
            low_query, keys_a, values_a = back(low, keys, values)
            high_query, keys_b, values_b = back(high, keys, values)
            put(here_sum, beside_give, 0, at, (keys_a + keys_b, values_a + values_b))
            more, keys_a, values_a = back(high, block(0, 0, 1, at), block(1, 0, 1, at))
            put(here_sum, beside_give, 1, at, (keys_a, values_a))
            query_sum[:half, at] += from_pair(low_query)
            query_sum[half:, at] += from_pair(high_query + more)
            return 0

        lax.fori_loop(0, 2, near_pair, 0)
        to_corner.wait_recv()
        for kind in (0, 1):
            away_give[kind] = (away_give[kind].astype(F32) + corner_got[kind].astype(F32)).astype(LOW)
        to_away.start()
        progress(1)
        for begin_at, end in ((2, 5), (5, 9)):
            lax.fori_loop(begin_at, end, near_pair, 0)
            progress(1)
        to_beside.start()
        if layer == 1:
            wide_page(1)
            todo.extend(in_turn(steps[0], steps[1]))
        else:
            loaded(13)
            tall_page(3)
            todo.extend(in_turn(steps[2], steps[3], steps[1][3]))
            wide_page(4)
            todo.extend(in_turn(steps[3], steps[4], steps[2][3]))
        low = (query_sum[:, :width] * HDIM ** (-0.5)).astype(LOW)
        mixture[:, :width] = low
        sums[2:3] = row(low.astype(F32))
        loaded(10, 2, 1)
        left_one[...] = normed_in[...].T
        left_two[...] = attended_low[...].T
        second_sum[...] = jnp.zeros_like(second_sum)
        progress(8)
        to_beside.wait_recv()
        to_away.wait_recv()
        for kind in (0, 1):
            value = here_sum[kind] + beside_got[kind].astype(F32) + away_got[kind].astype(F32)
            low = value[:, :width].astype(LOW)
            mixture[:, (1 + kind) * width : (2 + kind) * width] = low
        sums[3:4] = row(low.astype(F32))

        def project_tile(i, _):
            at = tile_at(i)
            slot = lax.rem(i, 3)
            column = i * 256 + lax.broadcasted_iota(jnp.int32, (rows, 256), 1)
            part = mixture[:, at]
            part = jnp.where(column < edge, part, jnp.zeros_like(part))
            expand_copy(i, page_hbm).wait()
            second_sum[...] += mm_nt(part, expand_ring[slot])

            @pl.when(i + 3 < 13)
            def _():
                expand_copy(i + 3, page_hbm).start()

            return 0

        for begin_at, end in ((0, 4), (4, 8), (8, 13)):
            lax.fori_loop(begin_at, end, project_tile, 0)
            progress(2)
        grad_normed = close_up(second_sum[...], table[...])
        unit, inverse = normal_parts(x[...].astype(F32))
        sums[0:1] = row(grad_normed * unit)
        sums[1:2] = row(grad_normed)
        result = result_one if layer == 1 else result_two
        result[...] = (grad_middle[...] + normal_back(grad_normed * vectors[0:1], unit, inverse)).astype(LOW)
        if layer == 1:
            load(0, 14, 12, 11, 3, 8, 9, 4, 5, 6, 7, 13, 10, 2, 1)
        ship(1, layer, result)
        progress(2)

        def page_tile(number, i):
            side = lax.rem(i, 2)
            at = tile_at(i)

            @pl.when(i >= 2)
            def _():
                wide_copy(i - 2, page_attention).wait()

            part = mixture[:, at]
            if number == 1:
                value = mm(left_one[...], part)
            elif number == 2:
                value = mm(left_two[...], part)
            else:
                column = i * 256 + lax.broadcasted_iota(jnp.int32, (rows, 256), 1)
                zero = jnp.zeros_like(part)
                value = mm(left_one[...], jnp.where(column < edge, part, zero))
                value = value + mm(left_two[...], jnp.where(column < edge, zero, part))
            stage_wide[side] = value.reshape(16, 72, 256).astype(LOW)
            wide_copy(i, page_attention).start()

        def page_loop(number, begin_at, end):
            def step(i, _):
                page_tile(number, i)
                return 0

            lax.fori_loop(begin_at, end, step, 0)

        whole_tiles = edge // 256
        for begin_at in range(0, whole_tiles, 4):
            page_loop(1, begin_at, begin_at + 4)
            progress(3)
        page_loop(3, whole_tiles, whole_tiles + 1)
        page_loop(2, whole_tiles + 1, tiles)
        for i in (tiles - 2, tiles - 1):
            wide_copy(i, page_attention).wait()
        scatter.give_all(2 if layer == 1 else 5)
        if layer == 1:
            todo.extend(in_turn(steps[1], steps[2], steps[0][3]))
        small = both.at[layer]
        small[...] = jnp.zeros(small.shape, F32)
        for shard in range(16):
            small[shard, 0:8, 0:68] = sums[:, shard * 68 : (shard + 1) * 68]
            for part in range(4):
                begin_at = shard * 272 + part * 68
                small[shard, 8 + part : 9 + part, 0:68] = wide_sum[0:1, begin_at : begin_at + 68]

    load(1, 0, 13, 14, 12)
    layer_pass(1)
    layer_pass(0)
    tiny = tiny_steps(both, small_out, tiny_refs, place_of)
    todo += in_turn(steps[4], steps[5], steps[3][3])
    for place, step in enumerate(tiny):
        todo.insert(min(4 * place, len(todo)), step)
    todo += steps[5][2][:3] + steps[4][3] + steps[5][2][3:] + steps[5][3]
    progress(len(todo))
    open_ends.pop()()
    scatter.drain()
    shipped_all(0)
    shipped_all(1)
    for copy in pair_copies(0):
        copy.wait_send()


def backward(top, saved, vectors, table, weights, outer_rows):
    rows, width = top.shape
    inner = weights[0][1].shape[1]
    anywhere = pl.BlockSpec(memory_space=pl.ANY)
    inside = pl.BlockSpec(memory_space=pltpu.VMEM)
    kinds = (ROWS, COLUMNS, COLUMNS) * 2
    page = jax.ShapeDtypeStruct((16, 72, inner), LOW)
    outs = [jax.ShapeDtypeStruct((16, 128), F32)]
    outs += [jax.ShapeDtypeStruct((inner, width), LOW), page, page] * 2
    outs += [jax.ShapeDtypeStruct((2, rows, width), LOW)] * 2
    outs += [final_shape(kind) for kind in kinds[:3]]
    for kind in kinds:
        outs += landing_shapes(kind)
    pair = pltpu.VMEM((2, rows, WIDE), LOW)
    tall = pltpu.VMEM((WIDE, rows), LOW)
    flat = pltpu.VMEM((rows, width), LOW)
    dma = pltpu.SemaphoreType.DMA
    scratch = [
        pltpu.VMEM((3, 256, width), LOW), pltpu.VMEM((3, WIDE, 256), LOW), pltpu.VMEM((WIDE, WIDE), LOW),
        pltpu.VMEM((rows, WIDE), F32), tall, tall, pltpu.VMEM((2, 16, 72, 256), LOW), pltpu.VMEM((2, 256, width), LOW),
        pltpu.VMEM((8, inner), F32), pltpu.VMEM((rows, WIDE), F32), pltpu.VMEM((2, rows, WIDE), F32),
        pair, pair, pair, pair, pair, pair, pair, pltpu.VMEM((rows, inner), LOW), pltpu.VMEM((rows, inner), LOW),
        pltpu.VMEM((rows, width), F32), pltpu.VMEM((rows, WIDE), LOW), pltpu.VMEM((8, width), F32),
        pltpu.VMEM((2, 16, 16, 128), F32), flat, flat, dma((3,)), dma((3,)), dma(()), dma((2,)), dma((2,)),
        dma((6,)), dma((6,)), dma((6,)), dma((6,)), dma((2,)),
    ] + tiny_shapes() + [pltpu.VMEM(value.shape, value.dtype) for value in (top,) + saved[1]] + [dma((15,))] + work_shapes(kinds)
    res = pl.pallas_call(
        backward_kernel,
        out_shape=tuple(outs),
        in_specs=[inside] * 3 + [anywhere] * (29 + 7),
        out_specs=(inside,) + (anywhere,) * (len(outs) - 1),
        scratch_shapes=scratch,
        compiler_params=pltpu.CompilerParams(collective_id=4, has_side_effects=True, vmem_limit_bytes=63 << 20),
        name="backward",
    )(*vectors, table, *saved[0], top, *saved[1], *weights[0], *weights[1], outer_rows)
    return res[0], res[7][None], res[8][None], res[9:12]


def spread(width):
    feature = np.arange(width)
    table = np.zeros((width, 16 * 72), np.float32)
    table[feature, feature // 68 * 72 + feature % 68] = 1
    return jnp.asarray(table, LOW)


def four_by_four(
    inputs,
    cotangent,
    first_gain,
    first_shift,
    joint_weight,
    query_bias,
    value_bias,
    output_weight,
    output_bias,
    second_gain,
    second_shift,
    expand_weight,
    expand_bias,
    reduce_weight,
    reduce_bias,
):
    core = lax.axis_index(SECTION)
    width = HEADS * HDIM
    vectors = (
        first_gain,
        first_shift,
        query_bias,
        value_bias,
        output_bias,
        reduce_bias,
        second_gain,
        second_shift,
        expand_bias,
    )
    packed = sum(
        jnp.pad(vector, ((0, 3), (128 * place, 4 * width - 128 * place - vector.shape[1])))
        for place, vector in enumerate(vectors)
    )
    attention_shard = jnp.concatenate(
        [jnp.concatenate([joint_weight[0], output_weight[0]], axis=1), packed], axis=0
    )
    expand_shard = jnp.pad(expand_weight[0], ((0, 4), (0, 0)))
    reduce_shard = reduce_weight[0]
    table = spread(width)

    def flat(page):
        return page.reshape(-1, page.shape[2])

    shards = (attention_shard, expand_shard, reduce_shard) * 2
    saved, saved_upper, gathered, (rows, top), smalls = forward(table, (inputs, cotangent), shards)
    lower_page, lower_expand, lower_reduce, upper_page, upper_expand, upper_reduce = gathered
    weights = (flat(lower_page), flat(lower_expand), flat(lower_reduce))
    upper_weights = (flat(upper_page), flat(upper_expand), flat(upper_reduce))
    middle_rows, final_rows = saved[13], saved_upper[13]
    saved_lower, saved_upper = (rows,) + tuple(saved[:13]), (middle_rows,) + tuple(saved_upper[:13])
    vectors, layer_outputs, input_grads, (reduce_sum, expand_sum, attention_sum) = backward(
        top, (saved_lower, saved_upper), smalls, table, (weights, upper_weights), final_rows
    )
    vectors = vectors[:12, :68]
    return (
        layer_outputs,
        input_grads,
        vectors[0][None],
        vectors[1][None],
        attention_sum[None, :68, : 3 * width],
        vectors[2][None],
        vectors[3][None],
        attention_sum[None, :68, 3 * width :],
        vectors[4][None],
        vectors[6][None],
        vectors[7][None],
        expand_sum[None, :68],
        vectors[8:].reshape(1, -1),
        reduce_sum[None],
        vectors[5][None],
    )


def fits(mesh):
    return dict(mesh.shape) == {SECTION: 2, RING: 4, LINE: 4}


def solution(mesh):
    return jax.shard_map(
        four_by_four if fits(mesh) else body,
        mesh=mesh,
        in_specs=(
            P(RING, LINE, None),
            P(RING, LINE, None),
            P(SECTION, OWNERS),
            P(SECTION, OWNERS),
            P(SECTION, OWNERS, None),
            P(SECTION, OWNERS),
            P(SECTION, OWNERS),
            P(SECTION, OWNERS, None),
            P(SECTION, OWNERS),
            P(SECTION, OWNERS),
            P(SECTION, OWNERS),
            P(SECTION, OWNERS, None),
            P(SECTION, OWNERS),
            P(SECTION, OWNERS, None),
            P(SECTION, OWNERS),
        ),
        out_specs=(
            P(SECTION, RING, LINE, None),
            P(SECTION, RING, LINE, None),
            P(SECTION, OWNERS),
            P(SECTION, OWNERS),
            P(SECTION, OWNERS, None),
            P(SECTION, OWNERS),
            P(SECTION, OWNERS),
            P(SECTION, OWNERS, None),
            P(SECTION, OWNERS),
            P(SECTION, OWNERS),
            P(SECTION, OWNERS),
            P(SECTION, OWNERS, None),
            P(SECTION, OWNERS),
            P(SECTION, OWNERS, None),
            P(SECTION, OWNERS),
        ),
        check_vma=False,
    )
```
